256 devices in a mesh: wide: 64 (over x, z, core), narrow: 4 (over y).
Axes of the slice: x: 4, y: 4, z: 8, core: 2. Of those that a mesh axis runs over, the one named last changes fastest.
Arguments:
- source: float32 [256, 256, 256], P('wide', 'narrow'), may hold values from -6 to 6
- coef_first: float32 [256, 256, 256], P('wide', 'narrow'), may hold values from 0.25 to 4
- coef_second: float32 [256, 256, 256], P('wide', 'narrow'), may hold values from 0.25 to 4
- coef_third: float32 [256, 256, 256], P('wide', 'narrow'), may hold values from 0.25 to 4
Outputs:
- correction: float32 [256, 256, 256], P('wide', 'narrow')
The draws below stay inside these ranges and needn't reach their ends.
All inputs are finite; a program needn't handle non-finite values.
Results may differ from the reference program's by a relative error of at most 0.00002.
Values sent between devices are 32-bit elements; how exact they have to be, the bound alone decides.
No kernel may reach another device: no remote copies, remote signals or barrier semaphores. Data moves between devices by JAX's collectives and lax.ppermute only.
A program may use at most 128 MiB of HBM per device.

```python
import math
import jax
import jax.numpy as jnp

NY = 256
LEVELS = 5
SWEEPS = 2
COARSE_SWEEPS = 4
NX = 256
NZ = 256


def steps_of(key, shape, pieces, least, top_value):
    factor_of, own = 1.0, jax.random.fold_in(key, 6)
    for position, blocks in pieces:
        steps = jnp.exp(jax.random.uniform(jax.random.fold_in(own, position), (blocks,), jnp.float32, least / len(pieces), top_value / len(pieces)))
        factor_of = factor_of * jnp.repeat(steps, shape[position] // blocks).reshape([-1 if axis == position else 1 for axis in range(len(shape))])
    return factor_of


def scatter_about(key, extent, deviation, limit, pieces=(), dtype=jnp.bfloat16):
    values = jax.random.normal(key, extent, jnp.float32) * deviation
    if len(pieces) > 0:
        values = steps_of(key, extent, pieces, -0.22, 0.18) * values
    return jnp.clip(values, min=-limit, max=limit).astype(dtype)


def setup_inputs(seed: int = 0) -> dict:
    arg_keys = jax.random.split(jax.random.key(seed), 5)
    return {
        "source": scatter_about(arg_keys[0], (NX, NZ, NY), 1.0, 6.0, ((0, 64), (1, 4)), jnp.float32),
        "coef_first": jnp.clip(jnp.exp(math.log(4.0) - 2.7725887 * jax.random.uniform(arg_keys[1], (NX, NZ, NY), jnp.float32) ** steps_of(arg_keys[1], (NX, NZ, NY), ((0, 64), (1, 4)), -0.2, 0.2)), 0.25, 4.0),
        "coef_second": jnp.clip(jnp.exp(math.log(4.0) - 2.7725887 * jax.random.uniform(arg_keys[2], (NX, NZ, NY), jnp.float32) ** steps_of(arg_keys[2], (NX, NZ, NY), ((0, 64), (1, 4)), -0.2, 0.2)), 0.25, 4.0),
        "coef_third": jnp.clip(jnp.exp(math.log(4.0) - 2.7725887 * jax.random.uniform(arg_keys[3], (NX, NZ, NY), jnp.float32) ** steps_of(arg_keys[3], (NX, NZ, NY), ((0, 64), (1, 4)), -0.2, 0.2)), 0.25, 4.0),
    }


LOWER = 0.25
UPPER = 2.0
SIGMA_BASE = 0.0002


def halve(array, axis_pos, mode):
    shape = array.shape
    parts = array.reshape(shape[:axis_pos] + (shape[axis_pos] // 2, 2) + shape[axis_pos + 1:])
    first = jnp.take(parts, 0, axis=axis_pos + 1)
    if mode == "even":
        return first
    return first + jnp.take(parts, 1, axis=axis_pos + 1)


def level_ops(coefs, level):
    sig = SIGMA_BASE * 4.0 ** level
    coef_a, coef_b, coef_c = coefs
    high_a = jnp.roll(coef_a, -1, 0)
    high_b = jnp.roll(coef_b, -1, 1)
    high_c = jnp.roll(coef_c, -1, 2)
    diag = sig + coef_a + high_a + coef_b + high_b + coef_c + high_c
    return (sig, coef_a, coef_b, coef_c, high_a, high_b, high_c, diag)


def apply_from(field, ops, low_a, up_a, low_b, up_b, low_c, up_c):
    sig, coef_a, coef_b, coef_c, high_a, high_b, high_c, diag = ops
    part_a = coef_a * (field - low_a) + high_a * (field - up_a)
    part_b = coef_b * (field - low_b) + high_b * (field - up_b)
    part_c = coef_c * (field - low_c) + high_c * (field - up_c)
    return sig * field + part_a + part_b + part_c


def apply_op(field, ops):
    return apply_from(field, ops, jnp.roll(field, 1, 0), jnp.roll(field, -1, 0),
                      jnp.roll(field, 1, 1), jnp.roll(field, -1, 1),
                      jnp.roll(field, 1, 2), jnp.roll(field, -1, 2))


def smooth(start, forcing, ops, degree):
    diag = ops[7]
    theta = (UPPER + LOWER) / 2.0
    delta = (UPPER - LOWER) / 2.0
    ratio = theta / delta
    rho = 1.0 / ratio
    if start is None:
        resid = forcing / diag
        step = resid / theta
        field = step
    else:
        resid = (forcing - apply_op(start, ops)) / diag
        step = resid / theta
        field = start + step
    for sweep in range(degree - 1):
        resid = (forcing - apply_op(field, ops)) / diag
        rho_new = 1.0 / (2.0 * ratio - rho)
        step = rho_new * rho * step + (2.0 * rho_new / delta) * resid
        field = field + step
        rho = rho_new
    return field


def cycle(level, forcing, coefs):
    ops = level_ops(coefs, level)
    if level == LEVELS - 1:
        return smooth(None, forcing, ops, COARSE_SWEEPS)
    field = smooth(None, forcing, ops, SWEEPS)
    resid = forcing - apply_op(field, ops)
    coarse_f = 0.5 * halve(halve(halve(resid, 0, "sum"), 1, "sum"), 2, "sum")
    coarse_a = 0.25 * halve(halve(halve(coefs[0], 0, "even"), 1, "sum"), 2, "sum")
    coarse_b = 0.25 * halve(halve(halve(coefs[1], 0, "sum"), 1, "even"), 2, "sum")
    coarse_c = 0.25 * halve(halve(halve(coefs[2], 0, "sum"), 1, "sum"), 2, "even")
    coarse_e = cycle(level + 1, coarse_f, (coarse_a, coarse_b, coarse_c))
    fine_e = jnp.repeat(jnp.repeat(jnp.repeat(coarse_e, 2, 0), 2, 1), 2, 2)
    field = field + fine_e
    return smooth(field, forcing, ops, SWEEPS)


def reference(source, coef_first, coef_second, coef_third):
    return cycle(0, source, (coef_first, coef_second, coef_third))
```

```python
import functools

import jax
import jax.numpy as jnp
from jax import lax
from jax.experimental import pallas as pl
from jax.experimental.pallas import tpu as pltpu
from jax.sharding import PartitionSpec as P

THETA = 1.125
DELTA = 0.875
RATIO = THETA / DELTA
SIG = [0.0002 * 4.0**level for level in range(5)]
F32 = jnp.float32
HIGHEST = lax.Precision.HIGHEST


def factors(degree):
    rho, out = 1.0 / RATIO, []
    for _ in range(degree - 1):
        new = 1.0 / (2.0 * RATIO - rho)
        out.append((new * rho, 2.0 * new / DELTA))
        rho = new
    return out


(KEEP, GAIN), = factors(2)


def roll(x, by, axis):
    return pltpu.roll(x, by % x.shape[axis], axis)


def gather_sum(below, here, above, c1, h1, c2, c3):
    first = c1 * below + h1 * above
    second = c2 * roll(here, 1, 0) + roll(c2 * here, -1, 0)
    third = c3 * roll(here, 1, 1) + roll(c3 * here, -1, 1)
    return first + second + third


def diagonal(sig, c1, h1, c2, c3):
    return sig + c1 + h1 + c2 + roll(c2, -1, 0) + c3 + roll(c3, -1, 1)


def iota(shape, dim):
    return lax.broadcasted_iota(jnp.int32, shape, dim)


def pairs_of_lanes(lanes, period, even=False):
    row, col = iota((lanes, 128), 0), iota((lanes, 128), 1) % period
    hit = row == 2 * col if even else row // 2 == col
    return hit.astype(F32)


def copies_of_lanes(lanes_in, lanes_out):
    row, col = iota((lanes_in, lanes_out), 0), iota((lanes_in, lanes_out), 1)
    return (row == col // 2).astype(F32)


def mul(a, b):
    return jnp.dot(a, b, precision=HIGHEST, preferred_element_type=F32)


def pair_rows(x, scratch, start=0, count=None, even=False):
    rows = x.shape[0]
    count = rows // 2 if count is None else count
    scratch[0:rows, :] = x
    first = scratch[pl.ds(start, count, stride=2), :]
    if even:
        return first
    return first + scratch[pl.ds(start + 1, count, stride=2), :]


def twice_rows(x, scratch):
    rows = x.shape[0]
    scratch[pl.ds(0, rows, stride=2), :] = x
    scratch[pl.ds(1, rows, stride=2), :] = x
    return scratch[0 : 2 * rows, :]


def coarse_coefs(planes, scratch, lanes, period, start=0, count=None):
    both = pairs_of_lanes(lanes, period)
    alone = pairs_of_lanes(lanes, period, even=True)
    return (
        0.25 * pair_rows(mul(planes[0], both), scratch, start, count),
        0.25 * pair_rows(mul(planes[1], both), scratch, start, count, even=True),
        0.25 * pair_rows(mul(planes[2], alone), scratch, start, count),
    )


def spread_block(x, block, width):
    lane = iota(x.shape, 1)
    x = jnp.where(lane // width == block, x, 0.0)
    while width < 128:
        x = x + pltpu.roll(x, width, 1)
        width *= 2
    return x


def smooth_two(u1, below, above, f, g, c1, h1, c2, c3):
    near = gather_sum(below, u1, above, c1, h1, c2, c3)
    return (1.0 + KEEP) * u1 + GAIN * (g * (f + near) - u1)


def first_post(v, below, above, f, g, c1, h1, c2, c3):
    near = gather_sum(below, v, above, c1, h1, c2, c3)
    return v + (1.0 / THETA) * (g * (f + near) - v)


def second_post(u, v, below, above, f, g, c1, h1, c2, c3):
    near = gather_sum(below, u, above, c1, h1, c2, c3)
    return u + KEEP * (u - v) + GAIN * (g * (f + near) - u)


def call(kernel, outs, scratch=(), smem=0):
    def run(*args):
        in_specs = [pl.BlockSpec(memory_space=pltpu.SMEM if i < smem else pltpu.VMEM) for i in range(len(args))]
        return pl.pallas_call(
            kernel,
            out_shape=[jax.ShapeDtypeStruct(s, F32) for s in outs],
            in_specs=in_specs,
            out_specs=[pl.BlockSpec(memory_space=pltpu.VMEM)] * len(outs),
            scratch_shapes=[pltpu.VMEM(s, F32) for s in scratch],
            compiler_params=pltpu.CompilerParams(vmem_limit_bytes=40 * 2**20),
        )(*args)

    return run


def start_kernel(f, c1, c2, c3, up, down, coef3, scr):
    for a, ref in enumerate((f, c1, c2, c3)):
        up[4 * a : 4 * a + 4] = ref[:, 56:64, :]
        down[4 * a : 4 * a + 4] = ref[:, 0:8, :]
    k1 = jnp.concatenate([c1[0], c1[2]], axis=0)
    k2 = jnp.concatenate([c2[0] + c2[1], c2[2] + c2[3]], axis=0)
    k3 = jnp.concatenate([c3[0] + c3[1], c3[2] + c3[3]], axis=0)
    k1, k2, k3 = coarse_coefs((k1, k2, k3), scr, 256, 128)
    k1, k2, k3 = k1[:32], k2[:32] + k2[32:], k3[:32] + k3[32:]
    k1, k2, k3 = coarse_coefs((k1, k2, k3), scr, 128, 64)
    k1, k2, k3 = coarse_coefs((k1, k2, k3), scr, 128, 32)
    lane = iota(k1.shape, 1)
    coef3[...] = jnp.where(lane < 32, k1, jnp.where(lane < 64, k2, k3))


def pad_kernel(f, c1, c2, c3, low, high, own, coef1, up, down, scr):
    for a, ref in enumerate((f, c1, c2, c3)):
        for p in range(4):
            own[4 * a + p, 0:8] = low[4 * a + p]
            own[4 * a + p, 8:72] = ref[p]
            own[4 * a + p, 72:80] = high[4 * a + p]
    for p, out, slot in ((1, down, 5), (2, up, 4)):
        diag = diagonal(SIG[0], own[4 + p], own[5 + p], own[8 + p], own[12 + p])
        out[slot] = own[p] / diag / THETA
    for a in range(4):
        up[a] = own[4 * a + 3]
        down[a] = own[4 * a]
    down[4] = own[5]
    k1 = jnp.concatenate([own[4], own[6]], axis=0)
    k2 = jnp.concatenate([own[8] + own[9], own[10] + own[11]], axis=0)
    k3 = jnp.concatenate([own[12] + own[13], own[14] + own[15]], axis=0)
    coarse = coarse_coefs((k1, k2, k3), scr, 256, 128)
    for a in range(3):
        for p in range(2):
            coef1[2 * a + p] = coarse[a][40 * p : 40 * p + 40]
    for out, at in ((up, 5), (down, 6)):
        out[at, 0:40, 0:128] = coef1[0]
        out[at, 0:40, 128:256] = coef1[1]
        out[at, 40:80, 0:128] = coef1[2]
        out[at, 40:80, 128:256] = coef1[3]
        out[at + 1, 0:40, 0:128] = coef1[4]
        out[at + 1, 0:40, 128:256] = coef1[5]
        out[at + 1, 40:80, :] = jnp.zeros((40, 256), F32)


def unpack(ref, at, index):
    plane, slot = at + index // 4, index % 4
    row, lane = 40 * (slot // 2), 128 * (slot % 2)
    return ref[plane, row : row + 40, lane : lane + 128]


CHUNK = 16


def chunked(rows, body):
    for r0 in range(0, rows, CHUNK):
        body(r0, rows)


def near_chunk(u, p, c1, c2, c3, q, r0, rows):
    here = pl.ds(r0, CHUNK)
    x = u[p, here, :]
    if r0 > 0:
        lower = u[p, pl.ds(r0 - 1, CHUNK), :]
    else:
        lower = roll(x, 1, 0)
    if r0 + CHUNK < rows:
        after = pl.ds(r0 + 1, CHUNK)
        upper = c2[q, after, :] * u[p, after, :]
    else:
        upper = roll(c2[q, here, :] * x, -1, 0)
    k3 = c3[q, here, :]
    first = c1[q, here, :] * u[p - 1, here, :] + c1[q + 1, here, :] * u[p + 1, here, :]
    second = c2[q, here, :] * lower + upper
    third = k3 * roll(x, 1, 1) + roll(k3 * x, -1, 1)
    return x, first + second + third


def diag_chunk(c1, c2, c3, q, r0, rows):
    here = pl.ds(r0, CHUNK)
    k2, k3 = c2[q, here, :], c3[q, here, :]
    if r0 + CHUNK < rows:
        h2 = c2[q, pl.ds(r0 + 1, CHUNK), :]
    else:
        h2 = roll(k2, -1, 0)
    return SIG[0] + c1[q, here, :] + c1[q + 1, here, :] + k2 + h2 + k3 + roll(k3, -1, 1)


def fine_pre_kernel(own, coef1, low, high, f, c1, c2, c3, g, u2, w1, g1, msg_up, msg_down, f1, coef2, u1, res, scr):
    for a, ref in enumerate((f, c1, c2, c3)):
        ref[0] = low[a]
        ref[1:5] = own[4 * a : 4 * a + 4]
        ref[5] = high[a]
    c1[6] = high[4]
    u1[0] = low[4]
    u1[7] = high[5]

    def smooth_first(q, carry):
        def rows(r0, n):
            here = pl.ds(r0, CHUNK)
            inverse = 1.0 / diag_chunk(c1, c2, c3, q, r0, n)
            g[q, here, :] = inverse
            u1[q + 1, here, :] = f[q, here, :] * inverse * (1.0 / THETA)

        chunked(80, rows)
        return carry

    lax.fori_loop(0, 6, smooth_first, 0)

    def smooth_second(q, carry):
        def rows(r0, n):
            here = pl.ds(r0, CHUNK)
            x, near = near_chunk(u1, q + 1, c1, c2, c3, q, r0, n)
            u2[q + 1, here, :] = (1.0 + KEEP) * x + GAIN * (g[q, here, :] * (f[q, here, :] + near) - x)

        chunked(80, rows)
        return carry

    lax.fori_loop(0, 6, smooth_second, 0)

    def residual(q, carry):
        def rows(r0, n):
            here = pl.ds(r0, CHUNK)
            x, near = near_chunk(u2, q + 1, c1, c2, c3, q, r0, n)
            res[q - 1, here, :] = f[q, here, :] + near - diag_chunk(c1, c2, c3, q, r0, n) * x

        chunked(80, rows)
        return carry

    lax.fori_loop(1, 5, residual, 0)

    both = pairs_of_lanes(256, 128)
    sums = jnp.concatenate([res[0] + res[1], res[2] + res[3]], axis=0)
    coarse = 0.5 * pair_rows(mul(sums, both), scr)
    f1[0] = coarse[:40]
    f1[1] = coarse[40:]
    for a in range(3):
        for p in range(2):
            w1[6 * a + p] = unpack(low, 5, 2 * a + p)
            w1[6 * a + 2 + p] = coef1[2 * a + p]
            w1[6 * a + 4 + p] = unpack(high, 6, 2 * a + p)
    for k in range(4):
        p = k + 1
        g1[k] = 1.0 / diagonal(SIG[1], w1[p], w1[p + 1], w1[6 + p], w1[12 + p])
    for p in range(2):
        start = f1[p] * g1[1 + p] * (1.0 / THETA)
        for out in (msg_up, msg_down):
            out[p] = f1[p]
            out[2 + p] = start
    for out, plane in ((msg_up, 4), (msg_down, 3)):
        out[4] = u2[plane, 0:40, 0:128]
        out[5] = u2[plane, 0:40, 128:256]
        out[6] = u2[plane, 40:80, 0:128]
        out[7] = u2[plane, 40:80, 128:256]
    k1 = jnp.concatenate([w1[0], w1[2], w1[4]], axis=0)
    k2 = jnp.concatenate([w1[6 + 2 * k] + w1[7 + 2 * k] for k in range(3)], axis=0)
    k3 = jnp.concatenate([w1[12 + 2 * k] + w1[13 + 2 * k] for k in range(3)], axis=0)
    coarse = coarse_coefs((k1, k2, k3), scr, 128, 64)
    for a in range(3):
        for k in range(3):
            coef2[3 * a + k] = coarse[a][20 * k + 2 : 20 * k + 18]


def middle_pre_kernel(own, low, high, w1, g1, f, u2, f2, up, down, u1, scr):
    f[0] = low[1]
    f[1:3] = own[0:2]
    f[3] = high[0]
    u1[0:2] = low[2:4]
    u1[2:4] = own[2:4]
    u1[4:6] = high[2:4]
    u2[0] = jnp.zeros((40, 128), F32)
    u2[5] = jnp.zeros((40, 128), F32)
    for p in range(1, 5):
        u2[p] = smooth_two(u1[p], u1[p - 1], u1[p + 1], f[p - 1], g1[p - 1], w1[p], w1[p + 1], w1[6 + p], w1[12 + p])
    total = 0.0
    for p in (2, 3):
        k1, h1, k2, k3 = w1[p], w1[p + 1], w1[6 + p], w1[12 + p]
        near = gather_sum(u2[p - 1], u2[p], u2[p + 1], k1, h1, k2, k3)
        total = total + (f[p - 1] + near - diagonal(SIG[1], k1, h1, k2, k3) * u2[p])
    coarse = 0.5 * pair_rows(mul(total, pairs_of_lanes(128, 64)), scr, 4, 16)
    f2[...] = coarse
    up[0:16] = coarse
    down[0:16] = coarse
    for p in range(2):
        up[16 + 8 * p : 24 + 8 * p] = u2[2 + p, 28:36]
        down[16 + 8 * p : 24 + 8 * p] = u2[2 + p, 4:12]


def coarse_start_kernel(place, f2, low, high, far, coef2, u2fine, c2w, own, msg, far_msg):
    n = place[1]
    for piece, by in ((f2, 0), (high, 1), (far, 2), (low, 3)):
        at = pl.multiple_of(16 * lax.rem(n + by, 4), 16)
        own[0, pl.ds(at, 16), :] = piece[0:16, :]
    for k in range(9):
        for m in range(4):
            c2w[k, 16 * m : 16 * m + 16] = coef2[9 * m + k]
    g = 1.0 / diagonal(SIG[2], c2w[1], c2w[2], c2w[4], c2w[7])
    own[1] = g
    start = own[0] * g * (1.0 / THETA)
    own[2] = start
    far_msg[...] = start
    msg[0:64] = own[0]
    msg[64:128] = g
    msg[128:192] = c2w[2]
    for p in range(2):
        at = 192 + 40 * p
        msg[at : at + 40] = u2fine[2 + p]
        msg[at : at + 4] = low[20 + 8 * p : 24 + 8 * p]
        msg[at + 36 : at + 40] = high[16 + 8 * p : 20 + 8 * p]


def coarse_pre_kernel(own, c2w, low, high, low2, high2, u2, mine, send, scr):
    f = (low[0:64], own[0], high[0:64])
    g = (low[64:128], own[1], high[64:128])
    u1 = [low2[...], f[0] * g[0] * (1.0 / THETA), own[2], f[2] * g[2] * (1.0 / THETA), high2[...]]
    h1 = (c2w[1], c2w[2], high[128:192])
    for k in range(3):
        u2[k] = smooth_two(u1[k + 1], u1[k], u1[k + 2], f[k], g[k], c2w[k], h1[k], c2w[3 + k], c2w[6 + k])
    mine[...] = u2[1]
    k1, k2, k3 = c2w[1], c2w[4], c2w[7]
    near = gather_sum(u2[0], u2[1], u2[2], k1, h1[1], k2, k3)
    res = f[1] + near - diagonal(SIG[2], k1, h1[1], k2, k3) * u2[1]
    part = 0.5 * pair_rows(mul(res, pairs_of_lanes(128, 32)), scr)
    block = iota((8, 128), 1) // 32
    packed = part[0:8]
    for q in range(1, 4):
        packed = jnp.where(block == q, part[8 * q : 8 * q + 8], packed)
    for w in range(send.shape[0]):
        send[w] = packed


def rows_loop(count, body):
    def step(j, carry):
        body(j)
        return carry

    lax.fori_loop(0, count, step, 0)


def coarse_coef_kernel(coef3, c1, c2, c3, g3, d1, d2, d3, g4, scr):
    n3, n4 = c1.shape[0] - 1, d1.shape[0] - 1

    def unpack_plane(j):
        for m in range(4):
            even, odd = coef3[m, 2 * j], coef3[m, 2 * j + 1]
            rows = pl.ds(8 * m, 8)
            c1[j, rows, :] = spread_block(even, 0, 32)
            c2[j, rows, :] = spread_block(even + odd, 1, 32)
            c3[j, rows, :] = spread_block(even + odd, 2, 32)

    rows_loop(n3, unpack_plane)
    c1[n3] = c1[0]

    def inverse3(j):
        g3[j] = 1.0 / diagonal(SIG[3], c1[j], c1[j + 1], c2[j], c3[j])

    rows_loop(n3, inverse3)
    k1 = jnp.concatenate([c1[2 * j] for j in range(n4)], axis=0)
    k2 = jnp.concatenate([c2[2 * j] + c2[2 * j + 1] for j in range(n4)], axis=0)
    k3 = jnp.concatenate([c3[2 * j] + c3[2 * j + 1] for j in range(n4)], axis=0)
    coarse = coarse_coefs((k1, k2, k3), scr, 128, 16)
    for a, ref in enumerate((d1, d2, d3)):
        for j in range(n4):
            ref[j] = coarse[a][16 * j : 16 * j + 16]
    d1[n4] = d1[0]

    def inverse4(j):
        g4[j] = 1.0 / diagonal(SIG[4], d1[j], d1[j + 1], d2[j], d3[j])

    rows_loop(n4, inverse4)


def around(j, n):
    return lax.rem(j + n, n)


def bottom_kernel(place, parts, c1, c2, c3, g3, d1, d2, d3, g4, own, c2w, low, high, u2w, u2low, u2high, out,
                  f3, u1, u2, res, f4, ua, ub, st, v3, w3, scr):
    n3, n4 = f3.shape[0], f4.shape[0]

    def unpack_plane(j):
        both = parts[2 * j] + parts[2 * j + 1]
        for q in range(4):
            f3[j, 8 * q : 8 * q + 8] = spread_block(both, q, 32)
        u1[j] = f3[j] * g3[j] * (1.0 / THETA)

    rows_loop(n3, unpack_plane)

    def pre(j):
        u2[j] = smooth_two(u1[j], u1[around(j - 1, n3)], u1[around(j + 1, n3)], f3[j], g3[j], c1[j], c1[j + 1], c2[j], c3[j])

    rows_loop(n3, pre)

    def residual(k):
        total = 0.0
        for half in range(2):
            j = 2 * k + half
            near = gather_sum(u2[around(j - 1, n3)], u2[j], u2[around(j + 1, n3)], c1[j], c1[j + 1], c2[j], c3[j])
            total = total + (f3[j] + near - diagonal(SIG[3], c1[j], c1[j + 1], c2[j], c3[j]) * u2[j])
        res[pl.ds(pl.multiple_of(32 * k, 32), 32), :] = total

    rows_loop(n4, residual)
    coarse = 0.5 * pair_rows(mul(res[0 : 32 * n4, :], pairs_of_lanes(128, 16)), scr)
    for k in range(n4):
        f4[k] = coarse[16 * k : 16 * k + 16]

    def first4(k):
        x = f4[k] * g4[k] * (1.0 / THETA)
        ua[k] = x
        st[k] = x

    rows_loop(n4, first4)
    src, dst = ua, ub
    for keep, gain in factors(4):
        def sweep(k, src=src, dst=dst, keep=keep, gain=gain):
            x = src[k]
            near = gather_sum(src[around(k - 1, n4)], x, src[around(k + 1, n4)], d1[k], d1[k + 1], d2[k], d3[k])
            step = keep * st[k] + gain * (g4[k] * (f4[k] + near) - x)
            st[k] = step
            dst[k] = x + step

        rows_loop(n4, sweep)
        src, dst = dst, src

    j0 = around(place[0] - 2, 2 * n3) // 2
    for k in range(5):
        scr[16 * k : 16 * k + 16] = src[around(around(j0 - 2, n3) // 2 + k, n4)]
    e4 = mul(scr[0:80, :], fold_copies(16))
    fine = twice_rows(e4, scr)
    odd = lax.rem(around(j0 - 2, n3), 2)
    for k in range(5):
        res[32 * k : 32 * k + 32] = fine[32 * k : 32 * k + 32]

    def add(k):
        j = around(j0 - 2 + k, n3)
        at = pl.multiple_of(32 * ((odd + k) // 2), 32)
        v3[k] = u2[j] + res[pl.ds(at, 32), :]

    rows_loop(7, add)

    def post1(k):
        j = around(j0 - 2 + k, n3)
        w3[k] = first_post(v3[k], v3[k - 1], v3[k + 1], f3[j], g3[j], c1[j], c1[j + 1], c2[j], c3[j])

    lax.fori_loop(1, 6, lambda k, c: (post1(k), c)[1], 0)
    for k in range(2, 5):
        j = around(j0 - 2 + k, n3)
        x = second_post(w3[k], v3[k], w3[k - 1], w3[k + 1], f3[j], g3[j], c1[j], c1[j + 1], c2[j], c3[j])
        res[32 * (k - 2) : 32 * (k - 2) + 32] = x
    e3 = mul(res[0:96, :], fold_copies(32))
    fine = twice_rows(e3, scr)
    for k in range(3):
        res[64 * k : 64 * k + 64] = fine[64 * k : 64 * k + 64]

    odd = lax.rem(around(place[0] - 2, 2 * n3), 2)
    base = (u2low[...], u2w[0], u2w[1], u2w[2], u2high[...])
    v = [base[k] + res[pl.ds(pl.multiple_of(64 * ((odd + k) // 2), 64), 64), :] for k in range(5)]
    f = (low[0:64], own[0], high[0:64])
    g = (low[64:128], own[1], high[64:128])
    h1 = (c2w[1], c2w[2], high[128:192])
    w = [first_post(v[k + 1], v[k], v[k + 2], f[k], g[k], c2w[k], h1[k], c2w[3 + k], c2w[6 + k]) for k in range(3)]
    out[...] = second_post(w[1], v[2], w[0], w[2], f[1], g[1], c2w[1], h1[1], c2w[4], c2w[7])


def fold_copies(period):
    row, col = iota((128, 128), 0), iota((128, 128), 1) % (2 * period)
    return (row == col // 2).astype(F32)


def middle_post_kernel(place, e2low, e2, e2high, msg, low, high, u2, f, g1, w1, out, up, down, v, w):
    n = place[1]
    row, col = iota((40, 64), 0), iota((40, 64), 1)
    pick = (col == lax.rem(16 * n + (row + 4) // 2 + 60, 64)).astype(F32)
    lanes = copies_of_lanes(128, 128)
    fine = [mul(mul(pick, e[...]), lanes) for e in (e2low, e2, e2high)]
    for p in range(6):
        if p < 2:
            base = low[192 + 40 * p : 232 + 40 * p]
        elif p < 4:
            base = msg[192 + 40 * (p - 2) : 232 + 40 * (p - 2)]
        else:
            base = high[192 + 40 * (p - 4) : 232 + 40 * (p - 4)]
        v[p] = base + fine[p // 2]
    for p in range(1, 5):
        w[p] = first_post(v[p], v[p - 1], v[p + 1], f[p - 1], g1[p - 1], w1[p], w1[p + 1], w1[6 + p], w1[12 + p])
    for p in (2, 3):
        out[p - 2] = second_post(w[p], v[p], w[p - 1], w[p + 1], f[p - 1], g1[p - 1], w1[p], w1[p + 1], w1[6 + p], w1[12 + p])
    up[...] = out[1]
    down[...] = out[0]


def fine_post_kernel(e1, e1low, e1high, low, high, f, c1, c2, c3, g, u2, out, v, w, scr):
    lanes = copies_of_lanes(128, 256)
    rows = twice_rows(jnp.concatenate([e1low[...], e1[0], e1[1], e1high[...]], axis=0), scr)
    fine = mul(rows, lanes)
    for k, ref in ((0, low), (7, high)):
        part = fine[80 * (k // 2) : 80 * (k // 2) + 80]
        v[k, 0:40, 0:128] = ref[4] + part[0:40, 0:128]
        v[k, 0:40, 128:256] = ref[5] + part[0:40, 128:256]
        v[k, 40:80, 0:128] = ref[6] + part[40:80, 0:128]
        v[k, 40:80, 128:256] = ref[7] + part[40:80, 128:256]
    for k in range(1, 7):
        v[k] = u2[k] + fine[80 * (k // 2) : 80 * (k // 2) + 80]

    def post1(q, carry):
        def chunk(r0, n):
            here = pl.ds(r0, CHUNK)
            x, near = near_chunk(v, q + 1, c1, c2, c3, q, r0, n)
            w[q + 1, here, :] = x + (1.0 / THETA) * (g[q, here, :] * (f[q, here, :] + near) - x)

        chunked(80, chunk)
        return carry

    lax.fori_loop(0, 6, post1, 0)

    def post2(q, carry):
        for r0 in range(8, 72, CHUNK):
            here = pl.ds(r0, CHUNK)
            x, near = near_chunk(w, q + 1, c1, c2, c3, q, r0, 80)
            step = KEEP * (x - v[q + 1, here, :]) + GAIN * (g[q, here, :] * (f[q, here, :] + near) - x)
            out[q - 1, pl.ds(r0 - 8, CHUNK), :] = x + step
        return carry

    lax.fori_loop(1, 5, post2, 0)


def shift(x, axis, by):
    count = lax.axis_size(axis)
    return lax.ppermute(x, axis, [(i, (i + by) % count) for i in range(count)])


def body(source, coef_first, coef_second, coef_third):
    wide = lax.axis_size("wide")
    n3, n4 = wide // 2, wide // 4
    place = jnp.stack([lax.axis_index("wide"), lax.axis_index("narrow")]).astype(jnp.int32)
    inputs = (source, coef_first, coef_second, coef_third)
    big = (80, 256)

    up, down, part3 = call(start_kernel, [(16, 8, 256), (16, 8, 256), (8, 128)], [(128, 128)])(*inputs)
    low, high = shift(up, "narrow", 1), shift(down, "narrow", -1)
    coef3 = lax.all_gather(part3, "wide", tiled=True)
    coef3 = lax.all_gather(coef3, "narrow", tiled=True).reshape(4, wide, 8, 128)

    own, coef1, up, down = call(
        pad_kernel, [(16,) + big, (6, 40, 128), (7,) + big, (8,) + big], [(160, 128)]
    )(*inputs, low, high)
    low, high = shift(up, "wide", 1), shift(down, "wide", -1)

    f, c1, c2, c3, g, u2, w1, g1, up, down, f1, coef2 = call(
        fine_pre_kernel,
        [(6,) + big, (7,) + big, (6,) + big, (6,) + big, (6,) + big, (8,) + big]
        + [(18, 40, 128), (4, 40, 128), (8, 40, 128), (8, 40, 128), (2, 40, 128), (9, 16, 128)],
        [(8,) + big, (4,) + big, (160, 128)],
    )(own, coef1, low, high)
    coef2 = lax.all_gather(coef2, "narrow", tiled=True)
    low1, high1 = shift(up, "wide", 1), shift(down, "wide", -1)

    f1w, u2m, f2, up, down = call(
        middle_pre_kernel,
        [(4, 40, 128), (6, 40, 128), (16, 128), (32, 128), (32, 128)],
        [(6, 40, 128), (40, 128)],
    )(up, low1, high1, w1, g1)
    low, high, far = shift(up, "narrow", 1), shift(down, "narrow", -1), shift(f2, "narrow", 2)

    c2w, own2, msg, far_msg = call(
        coarse_start_kernel, [(9, 64, 128), (3, 64, 128), (272, 128), (64, 128)], smem=1
    )(place, f2, low, high, far, coef2, u2m)
    low2, high2 = shift(msg, "wide", 1), shift(msg, "wide", -1)
    low2f, high2f = shift(far_msg, "wide", 2), shift(far_msg, "wide", -2)

    u2w, mine, send = call(
        coarse_pre_kernel, [(3, 64, 128), (64, 128), (wide, 8, 128)], [(64, 128)]
    )(own2, c2w, low2, high2, low2f, high2f)
    u2low, u2high = shift(mine, "wide", 2), shift(mine, "wide", -2)
    parts = lax.all_to_all(send, "wide", split_axis=0, concat_axis=0, tiled=True)

    three, four = (n3, 32, 128), (n4, 16, 128)
    coefs = call(
        coarse_coef_kernel,
        [(n3 + 1, 32, 128), three, three, three, (n4 + 1, 16, 128), four, four, four],
        [(n4 * 32, 128)],
    )(coef3)
    (e2,) = call(
        bottom_kernel,
        [(64, 128)],
        [three, three, three, (max(n4 * 32, 192), 128), four, four, four, four, (7, 32, 128), (7, 32, 128)]
        + [(max(n4 * 32, 192), 128)],
        smem=1,
    )(place, parts, *coefs, own2, c2w, low2, high2, u2w, u2low, u2high)
    e2low, e2high = shift(e2, "wide", 1), shift(e2, "wide", -1)

    e1, up, down = call(
        middle_post_kernel,
        [(2, 40, 128), (40, 128), (40, 128)],
        [(6, 40, 128), (6, 40, 128)],
        smem=1,
    )(place, e2low, e2, e2high, msg, low2, high2, u2m, f1w, g1, w1)
    e1low, e1high = shift(up, "wide", 1), shift(down, "wide", -1)

    (out,) = call(
        fine_post_kernel, [(4, 64, 256)], [(8,) + big, (8,) + big, (320, 128)]
    )(e1, e1low, e1high, low1, high1, f, c1, c2, c3, g, u2)
    return out


def solution(mesh):
    spec = P("wide", "narrow", None)
    return jax.shard_map(body, mesh=mesh, in_specs=(spec,) * 4, out_specs=spec, check_vma=False)
```

```python
import functools

import jax
import jax.numpy as jnp
from jax import lax
from jax.experimental import pallas as pl
from jax.experimental.pallas import tpu as pltpu
from jax.sharding import PartitionSpec as P

THETA = 1.125
DELTA = 0.875
RATIO = THETA / DELTA
SIG = [0.0002 * 4.0**level for level in range(5)]
F32 = jnp.float32
HIGHEST = lax.Precision.HIGHEST


def factors(degree):
    rho, out = 1.0 / RATIO, []
    for _ in range(degree - 1):
        new = 1.0 / (2.0 * RATIO - rho)
        out.append((new * rho, 2.0 * new / DELTA))
        rho = new
    return out


(KEEP, GAIN), = factors(2)


def roll(x, by, axis):
    return pltpu.roll(x, by % x.shape[axis], axis)


def gather_sum(below, here, above, c1, h1, c2, c3):
    first = c1 * below + h1 * above
    second = c2 * roll(here, 1, 0) + roll(c2 * here, -1, 0)
    third = c3 * roll(here, 1, 1) + roll(c3 * here, -1, 1)
    return first + second + third


def diagonal(sig, c1, h1, c2, c3):
    return sig + c1 + h1 + c2 + roll(c2, -1, 0) + c3 + roll(c3, -1, 1)


def iota(shape, dim):
    return lax.broadcasted_iota(jnp.int32, shape, dim)


def pairs_of_lanes(lanes, period, even=False):
    row, col = iota((lanes, 128), 0), iota((lanes, 128), 1) % period
    hit = row == 2 * col if even else row // 2 == col
    return hit.astype(F32)


def copies_of_lanes(lanes_in, lanes_out):
    row, col = iota((lanes_in, lanes_out), 0), iota((lanes_in, lanes_out), 1)
    return (row == col // 2).astype(F32)


def mul(a, b):
    return jnp.dot(a, b, precision=HIGHEST, preferred_element_type=F32)


def pair_rows(x, scratch, start=0, count=None, even=False):
    rows = x.shape[0]
    count = rows // 2 if count is None else count
    scratch[0:rows, :] = x
    first = scratch[pl.ds(start, count, stride=2), :]
    if even:
        return first
    return first + scratch[pl.ds(start + 1, count, stride=2), :]


def twice_rows(x, scratch):
    rows = x.shape[0]
    scratch[pl.ds(0, rows, stride=2), :] = x
    scratch[pl.ds(1, rows, stride=2), :] = x
    return scratch[0 : 2 * rows, :]


def coarse_coefs(planes, scratch, lanes, period, start=0, count=None):
    both = pairs_of_lanes(lanes, period)
    alone = pairs_of_lanes(lanes, period, even=True)
    return (
        0.25 * pair_rows(mul(planes[0], both), scratch, start, count),
        0.25 * pair_rows(mul(planes[1], both), scratch, start, count, even=True),
        0.25 * pair_rows(mul(planes[2], alone), scratch, start, count),
    )


def spread_block(x, block, width):
    lane = iota(x.shape, 1)
    x = jnp.where(lane // width == block, x, 0.0)
    while width < 128:
        x = x + pltpu.roll(x, width, 1)
        width *= 2
    return x


def smooth_two(u1, below, above, f, g, c1, h1, c2, c3):
    near = gather_sum(below, u1, above, c1, h1, c2, c3)
    return (1.0 + KEEP) * u1 + GAIN * (g * (f + near) - u1)


def first_post(v, below, above, f, g, c1, h1, c2, c3):
    near = gather_sum(below, v, above, c1, h1, c2, c3)
    return v + (1.0 / THETA) * (g * (f + near) - v)


def second_post(u, v, below, above, f, g, c1, h1, c2, c3):
    near = gather_sum(below, u, above, c1, h1, c2, c3)
    return u + KEEP * (u - v) + GAIN * (g * (f + near) - u)


def call(kernel, outs, scratch=(), places=(), limit=8, alias=None):
    places = dict(places)

    def run(*args):
        in_specs = [pl.BlockSpec(memory_space=places.get(i, pltpu.VMEM)) for i in range(len(args))]
        return pl.pallas_call(
            kernel,
            out_shape=[jax.ShapeDtypeStruct(s, F32) for s in outs],
            in_specs=in_specs,
            out_specs=[pl.BlockSpec(memory_space=pltpu.VMEM)] * len(outs),
            scratch_shapes=[pltpu.VMEM(s, F32) if isinstance(s, tuple) else s for s in scratch],
            input_output_aliases=alias or {},
            compiler_params=pltpu.CompilerParams(vmem_limit_bytes=limit * 2**20),
        )(*args)

    return run


SCALARS = {0: pltpu.SMEM}


def two_blocks(x):
    half = x.shape[0] // 2
    return jnp.where(iota((half, 128), 1) < 64, x[:half], x[half:])


def start_kernel(f, c1, c2, c3, own, up, down, far, scr, sems):
    copies = []
    for a, ref in enumerate((f, c1, c2, c3)):
        copy = pltpu.make_async_copy(ref, own.at[pl.ds(4 * a, 4), pl.ds(8, 64), :], sems.at[a])
        copy.start()
        copies.append(copy)
    for copy in copies:
        copy.wait()
    inner = pl.ds(8, 64)
    for a in range(16):
        up[a] = own[a, 64:72, :]
        down[a] = own[a, 8:16, :]
    k1 = jnp.concatenate([own[4, inner], own[6, inner]], axis=0)
    k2 = jnp.concatenate([own[8, inner] + own[9, inner], own[10, inner] + own[11, inner]], axis=0)
    k3 = jnp.concatenate([own[12, inner] + own[13, inner], own[14, inner] + own[15, inner]], axis=0)
    k1, k2, k3 = coarse_coefs((k1, k2, k3), scr, 256, 128)
    k1, k2, k3 = k1[:32], k2[:32] + k2[32:], k3[:32] + k3[32:]
    k1, k2, k3 = coarse_coefs((k1, k2, k3), scr, 128, 64)
    far[0, :, 0:128] = two_blocks(k1)
    far[0, :, 128:256] = two_blocks(k2)
    far[1, :, 0:128] = two_blocks(k3)
    far[1, :, 128:256] = jnp.zeros((8, 128), F32)
    both, alone = pairs_of_lanes(128, 32), pairs_of_lanes(128, 32, even=True)
    block = iota((2, 128), 1) // 32
    for a, (k, lanes) in enumerate(((k1, both), (k2, both), (k3, alone))):
        scr[0:16, :] = 0.25 * mul(k, lanes)
        packed = 0.0
        for q in range(4):
            part = scr[pl.ds(2 * q, 2, stride=8), :]
            if a != 1:
                part = part + scr[pl.ds(2 * q + 1, 2, stride=8), :]
            packed = jnp.where(block == q, part, packed)
        far[1, 2 * a : 2 * a + 2, 128:256] = packed
    up[16:18] = far[...]
    down[16:18] = far[...]


def pad_kernel(place, old, low, high, mine, far, own, coef1, coef2, coef3, up, down, scr):
    n = place[1]
    for a in range(16):
        own[a, 0:8] = low[a]
        own[a, 8:72] = old[a, 8:72]
        own[a, 72:80] = high[a]
    row = iota((8, 128), 0)
    coef3[...] = jnp.zeros((32, 128), F32)
    for ref, at, by in ((mine, 0, 0), (high, 16, 1), (far, 0, 2), (low, 16, 3)):
        m = lax.rem(n + by, 4)
        for a in range(3):
            tile = ref[at + a // 2, :, 128 * (a % 2) : 128 * (a % 2) + 128]
            here = pl.multiple_of(16 * m, 16)
            coef2[a, pl.ds(here, 8), :] = spread_block(tile, 0, 64)
            coef2[a, pl.ds(here + 8, 8), :] = spread_block(tile, 1, 64)
            part = pltpu.roll(ref[at + 1, :, 128:256], lax.rem(2 * m + 8 - 2 * a, 8), 0)
            coef3[8 * a : 8 * a + 8] = jnp.where(row // 2 == m, part, coef3[8 * a : 8 * a + 8])
    for p, out, slot in ((1, down, 5), (2, up, 4)):
        diag = diagonal(SIG[0], own[4 + p], own[5 + p], own[8 + p], own[12 + p])
        out[80 * slot : 80 * slot + 80] = own[p] / diag / THETA
    for a in range(4):
        up[80 * a : 80 * a + 80] = own[4 * a + 3]
        down[80 * a : 80 * a + 80] = own[4 * a]
    down[320:400] = own[5]
    k1 = jnp.concatenate([own[4], own[6]], axis=0)
    k2 = jnp.concatenate([own[8] + own[9], own[10] + own[11]], axis=0)
    k3 = jnp.concatenate([own[12] + own[13], own[14] + own[15]], axis=0)
    coarse = coarse_coefs((k1, k2, k3), scr, 256, 128)
    for a in range(3):
        for p in range(2):
            coef1[2 * a + p] = coarse[a][40 * p : 40 * p + 40]
    for out, at in ((up, 400), (down, 480)):
        for k in range(6):
            row, lane = at + 40 * (k // 2), 128 * (k % 2)
            out[row : row + 40, lane : lane + 128] = coef1[k]
        for a in range(3):
            both = two_blocks(coef2[a])
            row = at + 120 + 16 * a
            out[row : row + 16, 0:128] = both[:16]
            out[row : row + 16, 128:256] = both[16:]


def unpack(ref, at, index):
    row, lane = at + 40 * (index // 2), 128 * (index % 2)
    return ref[row : row + 40, lane : lane + 128]


CHUNK = 16


def chunked(rows, body):
    for r0 in range(0, rows, CHUNK):
        body(r0, rows)


def near_chunk(u, p, c1, c2, c3, q, r0, rows):
    here = pl.ds(r0, CHUNK)
    x = u[p, here, :]
    if r0 > 0:
        lower = u[p, pl.ds(r0 - 1, CHUNK), :]
    else:
        lower = roll(x, 1, 0)
    if r0 + CHUNK < rows:
        after = pl.ds(r0 + 1, CHUNK)
        upper = c2[q, after, :] * u[p, after, :]
    else:
        upper = roll(c2[q, here, :] * x, -1, 0)
    k3 = c3[q, here, :]
    first = c1[q, here, :] * u[p - 1, here, :] + c1[q + 1, here, :] * u[p + 1, here, :]
    second = c2[q, here, :] * lower + upper
    third = k3 * roll(x, 1, 1) + roll(k3 * x, -1, 1)
    return x, first + second + third


def diag_chunk(c1, c2, c3, q, r0, rows):
    here = pl.ds(r0, CHUNK)
    k2, k3 = c2[q, here, :], c3[q, here, :]
    if r0 + CHUNK < rows:
        h2 = c2[q, pl.ds(r0 + 1, CHUNK), :]
    else:
        h2 = roll(k2, -1, 0)
    return SIG[0] + c1[q, here, :] + c1[q + 1, here, :] + k2 + h2 + k3 + roll(k3, -1, 1)


def fine_pre_kernel(own, coef1, coef2, low, high, f, c1, c2, c3, g, u2, w1, g1, msg_up, msg_down, c2w, f1, u1, res, scr):
    for a, ref in enumerate((f, c1, c2, c3)):
        ref[0] = low[80 * a : 80 * a + 80]
        ref[1:5] = own[4 * a : 4 * a + 4]
        ref[5] = high[80 * a : 80 * a + 80]
    c1[6] = high[320:400]
    u1[0] = low[320:400]
    u1[7] = high[400:480]

    def smooth_first(q, carry):
        def rows(r0, n):
            here = pl.ds(r0, CHUNK)
            inverse = 1.0 / diag_chunk(c1, c2, c3, q, r0, n)
            g[q, here, :] = inverse
            u1[q + 1, here, :] = f[q, here, :] * inverse * (1.0 / THETA)

        chunked(80, rows)
        return carry

    lax.fori_loop(0, 6, smooth_first, 0)

    def smooth_second(q, carry):
        def rows(r0, n):
            here = pl.ds(r0, CHUNK)
            x, near = near_chunk(u1, q + 1, c1, c2, c3, q, r0, n)
            u2[q + 1, here, :] = (1.0 + KEEP) * x + GAIN * (g[q, here, :] * (f[q, here, :] + near) - x)

        chunked(80, rows)
        return carry

    lax.fori_loop(0, 6, smooth_second, 0)

    def residual(q, carry):
        def rows(r0, n):
            here = pl.ds(r0, CHUNK)
            x, near = near_chunk(u2, q + 1, c1, c2, c3, q, r0, n)
            res[q - 1, here, :] = f[q, here, :] + near - diag_chunk(c1, c2, c3, q, r0, n) * x

        chunked(80, rows)
        return carry

    lax.fori_loop(1, 5, residual, 0)

    both = pairs_of_lanes(256, 128)
    sums = jnp.concatenate([res[0] + res[1], res[2] + res[3]], axis=0)
    coarse = 0.5 * pair_rows(mul(sums, both), scr)
    f1[0] = coarse[:40]
    f1[1] = coarse[40:]
    for a in range(3):
        for p in range(2):
            w1[6 * a + p] = unpack(low, 400, 2 * a + p)
            w1[6 * a + 2 + p] = coef1[2 * a + p]
            w1[6 * a + 4 + p] = unpack(high, 480, 2 * a + p)
    for k in range(4):
        p = k + 1
        g1[k] = 1.0 / diagonal(SIG[1], w1[p], w1[p + 1], w1[6 + p], w1[12 + p])
    for p in range(2):
        start = f1[p] * g1[1 + p] * (1.0 / THETA)
        for out in (msg_up, msg_down):
            out[p] = f1[p]
            out[2 + p] = start
    for out, plane in ((msg_up, 4), (msg_down, 3)):
        out[4] = u2[plane, 0:40, 0:128]
        out[5] = u2[plane, 0:40, 128:256]
        out[6] = u2[plane, 40:80, 0:128]
        out[7] = u2[plane, 40:80, 128:256]
    for a in range(3):
        c2w[3 * a + 1] = coef2[a]
        for k, ref, at in ((0, low, 520), (2, high, 600)):
            row = at + 16 * a
            for half in range(2):
                part = ref[row : row + 16, 128 * half : 128 * half + 128]
                c2w[3 * a + k, 16 * half : 16 * half + 16] = spread_block(part, 0, 64)
                c2w[3 * a + k, 32 + 16 * half : 48 + 16 * half] = spread_block(part, 1, 64)


def middle_pre_kernel(own, low, high, w1, g1, f, u2, f2, up, down, u1, scr):
    f[0] = low[1]
    f[1:3] = own[0:2]
    f[3] = high[0]
    u1[0:2] = low[2:4]
    u1[2:4] = own[2:4]
    u1[4:6] = high[2:4]
    u2[0] = jnp.zeros((40, 128), F32)
    u2[5] = jnp.zeros((40, 128), F32)
    for p in range(1, 5):
        u2[p] = smooth_two(u1[p], u1[p - 1], u1[p + 1], f[p - 1], g1[p - 1], w1[p], w1[p + 1], w1[6 + p], w1[12 + p])
    total = 0.0
    for p in (2, 3):
        k1, h1, k2, k3 = w1[p], w1[p + 1], w1[6 + p], w1[12 + p]
        near = gather_sum(u2[p - 1], u2[p], u2[p + 1], k1, h1, k2, k3)
        total = total + (f[p - 1] + near - diagonal(SIG[1], k1, h1, k2, k3) * u2[p])
    coarse = 0.5 * pair_rows(mul(total, pairs_of_lanes(128, 64)), scr, 4, 16)
    f2[...] = coarse
    up[0:16] = coarse
    down[0:16] = coarse
    for p in range(2):
        up[16 + 8 * p : 24 + 8 * p] = u2[2 + p, 28:36]
        down[16 + 8 * p : 24 + 8 * p] = u2[2 + p, 4:12]


def coarse_start_kernel(place, f2, low, high, far, c2w, u2fine, own, msg, far_msg):
    n = place[1]
    for piece, by in ((f2, 0), (high, 1), (far, 2), (low, 3)):
        at = pl.multiple_of(16 * lax.rem(n + by, 4), 16)
        own[0, pl.ds(at, 16), :] = piece[0:16, :]
    g = 1.0 / diagonal(SIG[2], c2w[1], c2w[2], c2w[4], c2w[7])
    own[1] = g
    start = own[0] * g * (1.0 / THETA)
    own[2] = start
    far_msg[...] = start
    msg[0:64] = own[0]
    msg[64:128] = g
    msg[128:192] = c2w[2]
    for p in range(2):
        at = 192 + 40 * p
        msg[at : at + 40] = u2fine[2 + p]
        msg[at : at + 4] = low[20 + 8 * p : 24 + 8 * p]
        msg[at + 36 : at + 40] = high[16 + 8 * p : 20 + 8 * p]


def coarse_pre_kernel(own, c2w, low, high, low2, high2, u2, mine, send, scr):
    f = (low[0:64], own[0], high[0:64])
    g = (low[64:128], own[1], high[64:128])
    u1 = [low2[...], f[0] * g[0] * (1.0 / THETA), own[2], f[2] * g[2] * (1.0 / THETA), high2[...]]
    h1 = (c2w[1], c2w[2], high[128:192])
    for k in range(3):
        u2[k] = smooth_two(u1[k + 1], u1[k], u1[k + 2], f[k], g[k], c2w[k], h1[k], c2w[3 + k], c2w[6 + k])
    mine[...] = u2[1]
    k1, k2, k3 = c2w[1], c2w[4], c2w[7]
    near = gather_sum(u2[0], u2[1], u2[2], k1, h1[1], k2, k3)
    res = f[1] + near - diagonal(SIG[2], k1, h1[1], k2, k3) * u2[1]
    scr[...] = 0.5 * mul(res, pairs_of_lanes(128, 32))
    block = iota((8, 128), 1) // 32
    packed = 0.0
    for q in range(4):
        part = scr[pl.ds(2 * q, 8, stride=8), :] + scr[pl.ds(2 * q + 1, 8, stride=8), :]
        packed = jnp.where(block == q, part, packed)
    for w in range(send.shape[0]):
        send[w] = packed


def packed_sum(below, x, above, c1, h1, c2, c3, width, blocks):
    lane = iota(x.shape, 2)
    block, inner = lane // width % blocks, lane % width

    def second_down(x):
        x = pltpu.roll(x, width, 2)
        return jnp.where(block == 0, pltpu.roll(x, 1, 1), x)

    def second_up(x):
        x = pltpu.roll(x, 128 - width, 2)
        return jnp.where(block == blocks - 1, pltpu.roll(x, 7, 1), x)

    def third_down(x):
        return jnp.where(inner == 0, pltpu.roll(x, 129 - width, 2), pltpu.roll(x, 1, 2))

    def third_up(x):
        return jnp.where(inner == width - 1, pltpu.roll(x, width - 1, 2), pltpu.roll(x, 127, 2))

    first = c1 * below + h1 * above
    second = c2 * second_down(x) + second_up(c2 * x)
    third = c3 * third_down(x) + third_up(c3 * x)
    return first + second + third


def packed_diagonal(sig, c1, h1, c2, c3, width, blocks):
    lane = iota(c1.shape, 2)
    block, inner = lane // width % blocks, lane % width
    h2 = pltpu.roll(c2, 128 - width, 2)
    h2 = jnp.where(block == blocks - 1, pltpu.roll(h2, 7, 1), h2)
    h3 = jnp.where(inner == width - 1, pltpu.roll(c3, width - 1, 2), pltpu.roll(c3, 127, 2))
    return sig + c1 + h1 + c2 + h2 + c3 + h3


def fold_matrix(even2=False, even3=False):
    k, j = iota((128, 128), 0), iota((128, 128), 1)
    k2, k3, j2, j3 = k // 32, k % 32, j // 16 % 2, j % 16
    hit2 = k2 == 2 * j2 if even2 else k2 // 2 == j2
    hit3 = k3 == 2 * j3 if even3 else k3 // 2 == j3
    return (hit2 & hit3).astype(F32)


def wrap(ref, count):
    ref[0] = ref[count]
    ref[count + 1] = ref[1]


def around(j, n):
    return lax.rem(j + n, n)


STEP = 8
THREE, FOUR = (32, 4), (16, 2)


def bottom_kernel(place, parts, coef3, own, c2w, low, high, u2w, u2low, u2high, out,
                  f3, c1, c2, c3, d3, g3, u1, u2, res, f4, d1, d2, e3, g4, ua, ub, st, scr):
    n3, n4 = f3.shape[0], f4.shape[0]

    def loop(body):
        def step(c, carry):
            body(pl.multiple_of(c * STEP, STEP))
            return carry

        lax.fori_loop(0, n3 // STEP, step, 0)

    def load(j):
        here = pl.ds(j, STEP)
        f3[here] = parts[here, 0] + parts[here, 1]
        c1[here] = coef3[here, 0, 0]
        c2[here] = coef3[here, 0, 1] + coef3[here, 1, 1]
        c3[here] = coef3[here, 0, 2] + coef3[here, 1, 2]

    loop(load)
    c1[n3] = c1[0]

    def start(j):
        here = pl.ds(j, STEP)
        diag = packed_diagonal(SIG[3], c1[here], c1[pl.ds(j + 1, STEP)], c2[here], c3[here], *THREE)
        inverse = 1.0 / diag
        d3[here] = diag
        g3[here] = inverse
        u1[pl.ds(j + 1, STEP)] = f3[here] * inverse * (1.0 / THETA)

    loop(start)
    wrap(u1, n3)

    def near3(u, j):
        here = pl.ds(j, STEP)
        x = u[pl.ds(j + 1, STEP)]
        args = (c1[here], c1[pl.ds(j + 1, STEP)], c2[here], c3[here])
        return here, x, packed_sum(u[here], x, u[pl.ds(j + 2, STEP)], *args, *THREE)

    def pre(j):
        here, x, near = near3(u1, j)
        u2[pl.ds(j + 1, STEP)] = (1.0 + KEEP) * x + GAIN * (g3[here] * (f3[here] + near) - x)

    loop(pre)
    wrap(u2, n3)

    def residual(j):
        here, x, near = near3(u2, j)
        left = (f3[here] + near - d3[here] * x).reshape(STEP // 2, 2, 8, 128)
        res[pl.ds(j // 2, STEP // 2)] = left[:, 0] + left[:, 1]

    loop(residual)

    def fold(x, *even):
        return mul(x.reshape(8 * n4, 128), fold_matrix(*even)).reshape(n4, 8, 128)

    def halves(ref):
        x = ref[0:n3].reshape(n4, 2, 8, 128)
        return x[:, 0], x[:, 1]

    f4[...] = 0.5 * fold(res[...])
    d1[0:n4] = 0.25 * fold(halves(c1)[0])
    d1[n4] = d1[0]
    d2[...] = 0.25 * fold(sum(halves(c2)), True, False)
    e3[...] = 0.25 * fold(sum(halves(c3)), False, True)
    coefs4 = (d1[0:n4], d1[1 : n4 + 1], d2[...], e3[...])
    g4[...] = 1.0 / packed_diagonal(SIG[4], *coefs4, *FOUR)
    x = f4[...] * g4[...] * (1.0 / THETA)
    ua[1 : n4 + 1] = x
    wrap(ua, n4)
    st[...] = x
    src, dst = ua, ub
    for keep, gain in factors(4):
        x = src[1 : n4 + 1]
        near = packed_sum(src[0:n4], x, src[2 : n4 + 2], d1[0:n4], d1[1 : n4 + 1], d2[...], e3[...], *FOUR)
        step = keep * st[...] + gain * (g4[...] * (f4[...] + near) - x)
        st[...] = step
        dst[1 : n4 + 1] = x + step
        wrap(dst, n4)
        src, dst = dst, src

    j0 = around(place[0] - 2, 2 * n3) // 2
    k, j = iota((128, 128), 0), iota((128, 128), 1)
    unfold = (k == 16 * (j // 64) + j % 32 // 2).astype(F32)
    coarse = jnp.concatenate([src[1 + around(around(j0 - 2, n3) // 2 + m, n4)] for m in range(4)], axis=0)
    scr[0:32] = mul(coarse, unfold)
    odd = lax.rem(around(j0 - 2, n3), 2)
    js = [around(j0 - 2 + m, n3) for m in range(7)]
    v = [u2[1 + js[m]] + scr[pl.ds(pl.multiple_of(8 * ((odd + m) // 2), 8), 8), :] for m in range(7)]
    v = jnp.stack(v)

    def window(ref, first, count, by=0):
        return jnp.stack([ref[js[m] + by] for m in range(first, first + count)])

    def args(first, count):
        return window(c1, first, count), window(c1, first, count, 1), window(c2, first, count), window(c3, first, count)

    f, g = window(f3, 1, 5), window(g3, 1, 5)
    near = packed_sum(v[0:5], v[1:6], v[2:7], *args(1, 5), *THREE)
    w = v[1:6] + (1.0 / THETA) * (g * (f + near) - v[1:6])
    near = packed_sum(w[0:3], w[1:4], w[2:5], *args(2, 3), *THREE)
    x = w[1:4] + KEEP * (w[1:4] - v[2:5]) + GAIN * (g[1:4] * (f[1:4] + near) - w[1:4])
    x = x.reshape(24, 128)
    for q in range(4):
        fine = mul(x, (k == 32 * q + j % 64 // 2).astype(F32))
        scr[pl.ds(2 * q, 24, stride=8), :] = fine
        scr[pl.ds(2 * q + 1, 24, stride=8), :] = fine

    odd = lax.rem(around(place[0] - 2, 2 * n3), 2)
    base = (u2low[...], u2w[0], u2w[1], u2w[2], u2high[...])
    v = [base[m] + scr[pl.ds(pl.multiple_of(64 * ((odd + m) // 2), 64), 64), :] for m in range(5)]
    f = (low[0:64], own[0], high[0:64])
    g = (low[64:128], own[1], high[64:128])
    h1 = (c2w[1], c2w[2], high[128:192])
    w = [first_post(v[m + 1], v[m], v[m + 2], f[m], g[m], c2w[m], h1[m], c2w[3 + m], c2w[6 + m]) for m in range(3)]
    out[...] = second_post(w[1], v[2], w[0], w[2], f[1], g[1], c2w[1], h1[1], c2w[4], c2w[7])


def middle_post_kernel(place, e2low, e2, e2high, msg, low, high, u2, f, g1, w1, out, up, down, v, w):
    n = place[1]
    row, col = iota((40, 64), 0), iota((40, 64), 1)
    pick = (col == lax.rem(16 * n + (row + 4) // 2 + 60, 64)).astype(F32)
    lanes = copies_of_lanes(128, 128)
    fine = [mul(mul(pick, e[...]), lanes) for e in (e2low, e2, e2high)]
    for p in range(6):
        if p < 2:
            base = low[192 + 40 * p : 232 + 40 * p]
        elif p < 4:
            base = msg[192 + 40 * (p - 2) : 232 + 40 * (p - 2)]
        else:
            base = high[192 + 40 * (p - 4) : 232 + 40 * (p - 4)]
        v[p] = base + fine[p // 2]
    for p in range(1, 5):
        w[p] = first_post(v[p], v[p - 1], v[p + 1], f[p - 1], g1[p - 1], w1[p], w1[p + 1], w1[6 + p], w1[12 + p])
    for p in (2, 3):
        out[p - 2] = second_post(w[p], v[p], w[p - 1], w[p + 1], f[p - 1], g1[p - 1], w1[p], w1[p + 1], w1[6 + p], w1[12 + p])
    up[...] = out[1]
    down[...] = out[0]


def fine_post_kernel(e1, e1low, e1high, low, high, f, c1, c2, c3, g, u2, out, v, w, scr):
    lanes = copies_of_lanes(128, 256)
    rows = twice_rows(jnp.concatenate([e1low[...], e1[0], e1[1], e1high[...]], axis=0), scr)
    fine = mul(rows, lanes)
    for k, ref in ((0, low), (7, high)):
        part = fine[80 * (k // 2) : 80 * (k // 2) + 80]
        v[k, 0:40, 0:128] = ref[4] + part[0:40, 0:128]
        v[k, 0:40, 128:256] = ref[5] + part[0:40, 128:256]
        v[k, 40:80, 0:128] = ref[6] + part[40:80, 0:128]
        v[k, 40:80, 128:256] = ref[7] + part[40:80, 128:256]
    for k in range(1, 7):
        v[k] = u2[k] + fine[80 * (k // 2) : 80 * (k // 2) + 80]

    def post1(q, carry):
        def chunk(r0, n):
            here = pl.ds(r0, CHUNK)
            x, near = near_chunk(v, q + 1, c1, c2, c3, q, r0, n)
            w[q + 1, here, :] = x + (1.0 / THETA) * (g[q, here, :] * (f[q, here, :] + near) - x)

        chunked(80, chunk)
        return carry

    lax.fori_loop(0, 6, post1, 0)

    def post2(q, carry):
        for r0 in range(8, 72, CHUNK):
            here = pl.ds(r0, CHUNK)
            x, near = near_chunk(w, q + 1, c1, c2, c3, q, r0, 80)
            step = KEEP * (x - v[q + 1, here, :]) + GAIN * (g[q, here, :] * (f[q, here, :] + near) - x)
            out[q - 1, pl.ds(r0 - 8, CHUNK), :] = x + step
        return carry

    lax.fori_loop(1, 5, post2, 0)


def shift(x, axis, by):
    count = lax.axis_size(axis)
    return lax.ppermute(x, axis, [(i, (i + by) % count) for i in range(count)])


def body(source, coef_first, coef_second, coef_third):
    wide = lax.axis_size("wide")
    n3, n4 = wide // 2, wide // 4
    place = jnp.stack([lax.axis_index("wide"), lax.axis_index("narrow")]).astype(jnp.int32)
    big = (80, 256)

    own, up, down, mine = call(
        start_kernel,
        [(16,) + big, (18, 8, 256), (18, 8, 256), (2, 8, 256)],
        [(128, 128), pltpu.SemaphoreType.DMA((4,))],
        {k: pl.ANY for k in range(4)},
    )(source, coef_first, coef_second, coef_third)
    low, high, far = shift(up, "narrow", 1), shift(down, "narrow", -1), shift(mine, "narrow", 2)

    own, coef1, coef2, coef3, up, down = call(
        pad_kernel,
        [(16,) + big, (6, 40, 128), (3, 64, 128), (32, 128), (568, 256), (648, 256)],
        [(160, 128)],
        SCALARS,
    )(place, own, low, high, mine, far)
    low, high = shift(up, "wide", 1), shift(down, "wide", -1)
    coef3 = lax.all_gather(coef3, "wide", tiled=True).reshape(n3, 2, 4, 8, 128)

    f, c1, c2, c3, g, u2, w1, g1, up, down, c2w, f1 = call(
        fine_pre_kernel,
        [(6,) + big, (7,) + big, (6,) + big, (6,) + big, (6,) + big, (8,) + big]
        + [(18, 40, 128), (4, 40, 128), (8, 40, 128), (8, 40, 128), (9, 64, 128), (2, 40, 128)],
        [(8,) + big, (4,) + big, (160, 128)],
    )(own, coef1, coef2, low, high)
    low1, high1 = shift(up, "wide", 1), shift(down, "wide", -1)

    f1w, u2m, f2, up, down = call(
        middle_pre_kernel,
        [(4, 40, 128), (6, 40, 128), (16, 128), (32, 128), (32, 128)],
        [(6, 40, 128), (40, 128)],
    )(up, low1, high1, w1, g1)
    low, high, far = shift(up, "narrow", 1), shift(down, "narrow", -1), shift(f2, "narrow", 2)

    own2, msg, far_msg = call(
        coarse_start_kernel, [(3, 64, 128), (272, 128), (64, 128)], (), SCALARS
    )(place, f2, low, high, far, c2w, u2m)
    low2, high2 = shift(msg, "wide", 1), shift(msg, "wide", -1)
    low2f, high2f = shift(far_msg, "wide", 2), shift(far_msg, "wide", -2)

    u2w, mine, send = call(
        coarse_pre_kernel, [(3, 64, 128), (64, 128), (wide, 8, 128)], [(64, 128)]
    )(own2, c2w, low2, high2, low2f, high2f)
    u2low, u2high = shift(mine, "wide", 2), shift(mine, "wide", -2)
    parts = lax.all_to_all(send, "wide", split_axis=0, concat_axis=0, tiled=True).reshape(n3, 2, 8, 128)

    three, four = (n3, 8, 128), (n4, 8, 128)
    (e2,) = call(
        bottom_kernel,
        [(64, 128)],
        [three, (n3 + 1, 8, 128), three, three, three, three, (n3 + 2, 8, 128), (n3 + 2, 8, 128), four, four]
        + [(n4 + 1, 8, 128), four, four, four, (n4 + 2, 8, 128), (n4 + 2, 8, 128), four, (192, 128)],
        SCALARS,
    )(place, parts, coef3, own2, c2w, low2, high2, u2w, u2low, u2high)
    e2low, e2high = shift(e2, "wide", 1), shift(e2, "wide", -1)

    e1, up, down = call(
        middle_post_kernel,
        [(2, 40, 128), (40, 128), (40, 128)],
        [(6, 40, 128), (6, 40, 128)],
        SCALARS,
    )(place, e2low, e2, e2high, msg, low2, high2, u2m, f1w, g1, w1)
    e1low, e1high = shift(up, "wide", 1), shift(down, "wide", -1)

    (out,) = call(
        fine_post_kernel, [(4, 64, 256)], [(8,) + big, (8,) + big, (320, 128)]
    )(e1, e1low, e1high, low1, high1, f, c1, c2, c3, g, u2)
    return out


def solution(mesh):
    spec = P("wide", "narrow", None)
    return jax.shard_map(body, mesh=mesh, in_specs=(spec,) * 4, out_specs=spec, check_vma=False)
```

```python
import functools

import jax
import jax.numpy as jnp
from jax import lax
from jax.experimental import pallas as pl
from jax.experimental.pallas import tpu as pltpu
from jax.sharding import PartitionSpec as P

THETA = 1.125
DELTA = 0.875
RATIO = THETA / DELTA
SIG = [0.0002 * 4.0**level for level in range(5)]
F32 = jnp.float32
HIGHEST = lax.Precision.HIGHEST


def factors(degree):
    rho, out = 1.0 / RATIO, []
    for _ in range(degree - 1):
        new = 1.0 / (2.0 * RATIO - rho)
        out.append((new * rho, 2.0 * new / DELTA))
        rho = new
    return out


(KEEP, GAIN), = factors(2)


def roll(x, by, axis):
    return pltpu.roll(x, by % x.shape[axis], axis)


def gather_sum(below, here, above, c1, h1, c2, c3):
    first = c1 * below + h1 * above
    second = c2 * roll(here, 1, 0) + roll(c2 * here, -1, 0)
    third = c3 * roll(here, 1, 1) + roll(c3 * here, -1, 1)
    return first + second + third


def diagonal(sig, c1, h1, c2, c3):
    return sig + c1 + h1 + c2 + roll(c2, -1, 0) + c3 + roll(c3, -1, 1)


def iota(shape, dim):
    return lax.broadcasted_iota(jnp.int32, shape, dim)


def pairs_of_lanes(lanes, period, even=False):
    row, col = iota((lanes, 128), 0), iota((lanes, 128), 1) % period
    hit = row == 2 * col if even else row // 2 == col
    return hit.astype(F32)


def copies_of_lanes(lanes_in, lanes_out):
    row, col = iota((lanes_in, lanes_out), 0), iota((lanes_in, lanes_out), 1)
    return (row == col // 2).astype(F32)


def mul(a, b):
    return jnp.dot(a, b, precision=HIGHEST, preferred_element_type=F32)


def pair_rows(x, scratch, start=0, count=None, even=False):
    rows = x.shape[0]
    count = rows // 2 if count is None else count
    scratch[0:rows, :] = x
    first = scratch[pl.ds(start, count, stride=2), :]
    if even:
        return first
    return first + scratch[pl.ds(start + 1, count, stride=2), :]


def twice_rows(x, scratch):
    rows = x.shape[0]
    scratch[pl.ds(0, rows, stride=2), :] = x
    scratch[pl.ds(1, rows, stride=2), :] = x
    return scratch[0 : 2 * rows, :]


def coarse_coefs(planes, scratch, lanes, period, start=0, count=None):
    both = pairs_of_lanes(lanes, period)
    alone = pairs_of_lanes(lanes, period, even=True)
    return (
        0.25 * pair_rows(mul(planes[0], both), scratch, start, count),
        0.25 * pair_rows(mul(planes[1], both), scratch, start, count, even=True),
        0.25 * pair_rows(mul(planes[2], alone), scratch, start, count),
    )


def spread_block(x, block, width):
    lane = iota(x.shape, 1)
    x = jnp.where(lane // width == block, x, 0.0)
    while width < 128:
        x = x + pltpu.roll(x, width, 1)
        width *= 2
    return x


def smooth_two(u1, below, above, f, g, c1, h1, c2, c3):
    near = gather_sum(below, u1, above, c1, h1, c2, c3)
    return (1.0 + KEEP) * u1 + GAIN * (g * (f + near) - u1)


def first_post(v, below, above, f, g, c1, h1, c2, c3):
    near = gather_sum(below, v, above, c1, h1, c2, c3)
    return v + (1.0 / THETA) * (g * (f + near) - v)


def second_post(u, v, below, above, f, g, c1, h1, c2, c3):
    near = gather_sum(below, u, above, c1, h1, c2, c3)
    return u + KEEP * (u - v) + GAIN * (g * (f + near) - u)


def call(kernel, outs, scratch=(), places=(), out_places=(), limit=8):
    places, out_places = dict(places), dict(out_places)

    def run(*args):
        in_specs = [pl.BlockSpec(memory_space=places.get(i, pltpu.VMEM)) for i in range(len(args))]
        return pl.pallas_call(
            kernel,
            out_shape=[jax.ShapeDtypeStruct(s, F32) for s in outs],
            in_specs=in_specs,
            out_specs=[pl.BlockSpec(memory_space=out_places.get(i, pltpu.VMEM)) for i in range(len(outs))],
            scratch_shapes=[pltpu.VMEM(s, F32) if isinstance(s, tuple) else s for s in scratch],
            compiler_params=pltpu.CompilerParams(vmem_limit_bytes=limit * 2**20),
        )(*args)

    return run


SCALARS = {0: pltpu.SMEM}


def two_blocks(x):
    half = x.shape[0] // 2
    return jnp.where(iota((half, 128), 1) < 64, x[:half], x[half:])


def start_kernel(f, c1, c2, c3, own, up, down, far, scr, sems):
    copies = []
    for a, ref in enumerate((f, c1, c2, c3)):
        copy = pltpu.make_async_copy(ref, own.at[pl.ds(4 * a, 4), pl.ds(8, 64), :], sems.at[a])
        copy.start()
        copies.append(copy)
    for copy in copies:
        copy.wait()
    inner = pl.ds(8, 64)
    for a in range(16):
        up[a] = own[a, 64:72, :]
        down[a] = own[a, 8:16, :]
    k1 = jnp.concatenate([own[4, inner], own[6, inner]], axis=0)
    k2 = jnp.concatenate([own[8, inner] + own[9, inner], own[10, inner] + own[11, inner]], axis=0)
    k3 = jnp.concatenate([own[12, inner] + own[13, inner], own[14, inner] + own[15, inner]], axis=0)
    k1, k2, k3 = coarse_coefs((k1, k2, k3), scr, 256, 128)
    k1, k2, k3 = k1[:32], k2[:32] + k2[32:], k3[:32] + k3[32:]
    k1, k2, k3 = coarse_coefs((k1, k2, k3), scr, 128, 64)
    far[0, :, 0:128] = two_blocks(k1)
    far[0, :, 128:256] = two_blocks(k2)
    far[1, :, 0:128] = two_blocks(k3)
    far[1, :, 128:256] = jnp.zeros((8, 128), F32)
    up[16:18] = far[...]
    down[16:18] = far[...]


def pad_kernel(place, old, low, high, mine, far, own, coef1, coef2, up, down, scr):
    n = place[1]
    for a in range(16):
        own[a, 0:8] = low[a]
        own[a, 8:72] = old[a, 8:72]
        own[a, 72:80] = high[a]
    for ref, at, by in ((mine, 0, 0), (high, 16, 1), (far, 0, 2), (low, 16, 3)):
        m = lax.rem(n + by, 4)
        for a in range(3):
            tile = ref[at + a // 2, :, 128 * (a % 2) : 128 * (a % 2) + 128]
            here = pl.multiple_of(16 * m, 16)
            coef2[a, pl.ds(here, 8), :] = spread_block(tile, 0, 64)
            coef2[a, pl.ds(here + 8, 8), :] = spread_block(tile, 1, 64)
    for p, out, slot in ((1, down, 5), (2, up, 4)):
        diag = diagonal(SIG[0], own[4 + p], own[5 + p], own[8 + p], own[12 + p])
        out[80 * slot : 80 * slot + 80] = own[p] / diag / THETA
    for a in range(4):
        up[80 * a : 80 * a + 80] = own[4 * a + 3]
        down[80 * a : 80 * a + 80] = own[4 * a]
    down[320:400] = own[5]
    k1 = jnp.concatenate([own[4], own[6]], axis=0)
    k2 = jnp.concatenate([own[8] + own[9], own[10] + own[11]], axis=0)
    k3 = jnp.concatenate([own[12] + own[13], own[14] + own[15]], axis=0)
    coarse = coarse_coefs((k1, k2, k3), scr, 256, 128)
    for a in range(3):
        for p in range(2):
            coef1[2 * a + p] = coarse[a][40 * p : 40 * p + 40]
    for out, at in ((up, 400), (down, 480)):
        for k in range(6):
            row, lane = at + 40 * (k // 2), 128 * (k % 2)
            out[row : row + 40, lane : lane + 128] = coef1[k]
        for a in range(3):
            both = two_blocks(coef2[a])
            row = at + 120 + 16 * a
            out[row : row + 16, 0:128] = both[:16]
            out[row : row + 16, 128:256] = both[16:]


def unpack(ref, at, index):
    row, lane = at + 40 * (index // 2), 128 * (index % 2)
    return ref[row : row + 40, lane : lane + 128]


CHUNK = 16


def chunked(rows, body):
    for r0 in range(0, rows, CHUNK):
        body(r0, rows)


def near_chunk(u, p, c1, c2, c3, q, r0, rows):
    here = pl.ds(r0, CHUNK)
    x = u[p, here, :]
    if r0 > 0:
        lower = u[p, pl.ds(r0 - 1, CHUNK), :]
    else:
        lower = roll(x, 1, 0)
    if r0 + CHUNK < rows:
        after = pl.ds(r0 + 1, CHUNK)
        upper = c2[q, after, :] * u[p, after, :]
    else:
        upper = roll(c2[q, here, :] * x, -1, 0)
    k3 = c3[q, here, :]
    first = c1[q, here, :] * u[p - 1, here, :] + c1[q + 1, here, :] * u[p + 1, here, :]
    second = c2[q, here, :] * lower + upper
    third = k3 * roll(x, 1, 1) + roll(k3 * x, -1, 1)
    return x, first + second + third


def diag_chunk(c1, c2, c3, q, r0, rows):
    here = pl.ds(r0, CHUNK)
    k2, k3 = c2[q, here, :], c3[q, here, :]
    if r0 + CHUNK < rows:
        h2 = c2[q, pl.ds(r0 + 1, CHUNK), :]
    else:
        h2 = roll(k2, -1, 0)
    return SIG[0] + c1[q, here, :] + c1[q + 1, here, :] + k2 + h2 + k3 + roll(k3, -1, 1)


def fine_pre_kernel(own, coef1, coef2, low, high, f_out, c1_out, c2_out, c3_out, g_out, u2_out, w1, g1, msg_up, msg_down, c2w, f1,
                    f, c1, c2, c3, g, u2, u1, res, scr, sems):
    for a, ref in enumerate((f, c1, c2, c3)):
        ref[0] = low[80 * a : 80 * a + 80]
        ref[1:5] = own[4 * a : 4 * a + 4]
        ref[5] = high[80 * a : 80 * a + 80]
    c1[6] = high[320:400]
    u1[0] = low[320:400]
    u1[7] = high[400:480]
    copies = []

    def leave(*pairs):
        for src, dst in pairs:
            copy = pltpu.make_async_copy(src, dst, sems.at[len(copies)])
            copy.start()
            copies.append(copy)

    leave((f, f_out), (c1, c1_out), (c2, c2_out), (c3, c3_out))

    def smooth_first(q, carry):
        def rows(r0, n):
            here = pl.ds(r0, CHUNK)
            inverse = 1.0 / diag_chunk(c1, c2, c3, q, r0, n)
            g[q, here, :] = inverse
            u1[q + 1, here, :] = f[q, here, :] * inverse * (1.0 / THETA)

        chunked(80, rows)
        return carry

    lax.fori_loop(0, 6, smooth_first, 0)
    leave((g, g_out))

    def smooth_second(q, carry):
        def rows(r0, n):
            here = pl.ds(r0, CHUNK)
            x, near = near_chunk(u1, q + 1, c1, c2, c3, q, r0, n)
            u2[q + 1, here, :] = (1.0 + KEEP) * x + GAIN * (g[q, here, :] * (f[q, here, :] + near) - x)

        chunked(80, rows)
        return carry

    u2[0] = u1[0]
    u2[7] = u1[7]
    lax.fori_loop(0, 6, smooth_second, 0)
    leave((u2, u2_out))

    def residual(q, carry):
        def rows(r0, n):
            here = pl.ds(r0, CHUNK)
            x, near = near_chunk(u2, q + 1, c1, c2, c3, q, r0, n)
            res[q - 1, here, :] = f[q, here, :] + near - diag_chunk(c1, c2, c3, q, r0, n) * x

        chunked(80, rows)
        return carry

    lax.fori_loop(1, 5, residual, 0)

    both = pairs_of_lanes(256, 128)
    sums = jnp.concatenate([res[0] + res[1], res[2] + res[3]], axis=0)
    coarse = 0.5 * pair_rows(mul(sums, both), scr)
    f1[0] = coarse[:40]
    f1[1] = coarse[40:]
    for a in range(3):
        for p in range(2):
            w1[6 * a + p] = unpack(low, 400, 2 * a + p)
            w1[6 * a + 2 + p] = coef1[2 * a + p]
            w1[6 * a + 4 + p] = unpack(high, 480, 2 * a + p)
    for k in range(4):
        p = k + 1
        g1[k] = 1.0 / diagonal(SIG[1], w1[p], w1[p + 1], w1[6 + p], w1[12 + p])
    for p in range(2):
        start = f1[p] * g1[1 + p] * (1.0 / THETA)
        for out in (msg_up, msg_down):
            out[p] = f1[p]
            out[2 + p] = start
    for out, plane in ((msg_up, 4), (msg_down, 3)):
        out[4] = u2[plane, 0:40, 0:128]
        out[5] = u2[plane, 0:40, 128:256]
        out[6] = u2[plane, 40:80, 0:128]
        out[7] = u2[plane, 40:80, 128:256]
    for a in range(3):
        c2w[3 * a + 1] = coef2[a]
        for k, ref, at in ((0, low, 520), (2, high, 600)):
            row = at + 16 * a
            for half in range(2):
                part = ref[row : row + 16, 128 * half : 128 * half + 128]
                c2w[3 * a + k, 16 * half : 16 * half + 16] = spread_block(part, 0, 64)
                c2w[3 * a + k, 32 + 16 * half : 48 + 16 * half] = spread_block(part, 1, 64)
    for copy in copies:
        copy.wait()


def middle_pre_kernel(own, low, high, w1, g1, f, u2, f2, up, down, u1, scr):
    f[0] = low[1]
    f[1:3] = own[0:2]
    f[3] = high[0]
    u1[0:2] = low[2:4]
    u1[2:4] = own[2:4]
    u1[4:6] = high[2:4]
    u2[0] = jnp.zeros((40, 128), F32)
    u2[5] = jnp.zeros((40, 128), F32)
    for p in range(1, 5):
        u2[p] = smooth_two(u1[p], u1[p - 1], u1[p + 1], f[p - 1], g1[p - 1], w1[p], w1[p + 1], w1[6 + p], w1[12 + p])
    total = 0.0
    for p in (2, 3):
        k1, h1, k2, k3 = w1[p], w1[p + 1], w1[6 + p], w1[12 + p]
        near = gather_sum(u2[p - 1], u2[p], u2[p + 1], k1, h1, k2, k3)
        total = total + (f[p - 1] + near - diagonal(SIG[1], k1, h1, k2, k3) * u2[p])
    coarse = 0.5 * pair_rows(mul(total, pairs_of_lanes(128, 64)), scr, 4, 16)
    f2[...] = coarse
    up[0:16] = coarse
    down[0:16] = coarse
    for p in range(2):
        up[16 + 8 * p : 24 + 8 * p] = u2[2 + p, 28:36]
        down[16 + 8 * p : 24 + 8 * p] = u2[2 + p, 4:12]


def both_halves(x):
    return jnp.concatenate([spread_block(x, 0, 64), spread_block(x, 1, 64)], axis=0)


def coarse_start_kernel(place, f2, low, high, far, c2w, u2fine, own, msg):
    n = place[1]
    for piece, by in ((f2, 0), (high, 1), (far, 2), (low, 3)):
        at = pl.multiple_of(16 * lax.rem(n + by, 4), 16)
        own[0, pl.ds(at, 16), :] = piece[0:16, :]
    own[1] = 1.0 / diagonal(SIG[2], c2w[1], c2w[2], c2w[4], c2w[7])
    msg[0:32] = two_blocks(own[0])
    msg[32:64] = two_blocks(own[1])
    for p in range(2):
        at = 64 + 40 * p
        msg[at : at + 40] = u2fine[2 + p]
        msg[at : at + 4] = low[20 + 8 * p : 24 + 8 * p]
        msg[at + 36 : at + 40] = high[16 + 8 * p : 20 + 8 * p]


def coarse_tiles_kernel(place, c2w, tiles, scr):
    par = lax.rem(place[0], 2)
    for a in range(3):
        x = c2w[3 * a + 1 - par]
        if a > 0:
            x = x + c2w[3 * a + 2 - par]
        scr[...] = 0.25 * mul(x, pairs_of_lanes(128, 32, even=a == 2))
        tiles[a] = tile_of(scr, a == 1)


def tile_of(scr, even=False):
    block = iota((8, 128), 1) // 32
    packed = 0.0
    for q in range(4):
        part = scr[pl.ds(2 * q, 8, stride=8), :]
        if not even:
            part = part + scr[pl.ds(2 * q + 1, 8, stride=8), :]
        packed = jnp.where(block == q, part, packed)
    return packed


def coarse_swap_kernel(own, msg, sib, c2w, out):
    out[0:64] = msg[0:64]
    for a in range(3):
        out[64 + 32 * a : 96 + 32 * a] = two_blocks(c2w[3 * a + 1])
    out[160:192] = sib[0:32] * sib[32:64] * (1.0 / THETA)
    out[192:224] = two_blocks(c2w[2])
    out[224:304] = msg[64:144]


def coarse_pre_kernel(place, own, c2w, sib, near, other, w, u2, late, u1):
    par = lax.rem(place[0], 2)
    odd = par == 1

    def below(k):
        here = slice(32 * k, 32 * k + 32)
        return both_halves(jnp.where(odd, other[here], near[here]))

    def above(k):
        here = slice(32 * k, 32 * k + 32)
        return both_halves(jnp.where(odd, near[here], other[here]))

    for a in range(2):
        mine, theirs = own[a], both_halves(sib[32 * a : 32 * a + 32])
        w[4 * a] = below(a)
        w[4 * a + 1] = jnp.where(odd, theirs, mine)
        w[4 * a + 2] = jnp.where(odd, mine, theirs)
        w[4 * a + 3] = above(a)
    for a, base in ((0, 8), (1, 13), (2, 17)):
        w[base] = below(2 + a)
        w[base + 1] = c2w[3 * a + 1 - par]
        w[base + 2] = c2w[3 * a + 2 - par]
        w[base + 3] = above(2 + a)
    w[12] = above(6)
    u1[0] = below(5)
    u1[5] = above(5)
    for k in range(4):
        u1[k + 1] = w[k] * w[4 + k] * (1.0 / THETA)
    for k in range(4):
        u2[k] = smooth_two(u1[k + 1], u1[k], u1[k + 2], w[k], w[4 + k], w[8 + k], w[9 + k], w[13 + k], w[17 + k])
    late[...] = two_blocks(jnp.where(odd, u2[1], u2[2]))


def coarse_send_kernel(place, w, u2, tiles, send, scr):
    odd = lax.rem(place[0], 2) == 1
    total = 0.0
    for k in (1, 2):
        args = (w[8 + k], w[9 + k], w[13 + k], w[17 + k])
        near = gather_sum(u2[k - 1], u2[k], u2[k + 1], *args)
        total = total + (w[k] + near - diagonal(SIG[2], *args) * u2[k])
    scr[...] = 0.5 * mul(total, pairs_of_lanes(128, 32))
    first = jnp.where(odd, tiles[1], tile_of(scr))
    second = jnp.where(odd, tiles[2], tiles[0])
    for k in range(send.shape[0]):
        send[k, 0] = first
        send[k, 1] = second


def packed_sum(below, x, above, c1, h1, c2, c3, width, blocks):
    lane = iota(x.shape, 2)
    block, inner = lane // width % blocks, lane % width

    def second_down(x):
        x = pltpu.roll(x, width, 2)
        return jnp.where(block == 0, pltpu.roll(x, 1, 1), x)

    def second_up(x):
        x = pltpu.roll(x, 128 - width, 2)
        return jnp.where(block == blocks - 1, pltpu.roll(x, 7, 1), x)

    def third_down(x):
        return jnp.where(inner == 0, pltpu.roll(x, 129 - width, 2), pltpu.roll(x, 1, 2))

    def third_up(x):
        return jnp.where(inner == width - 1, pltpu.roll(x, width - 1, 2), pltpu.roll(x, 127, 2))

    first = c1 * below + h1 * above
    second = c2 * second_down(x) + second_up(c2 * x)
    third = c3 * third_down(x) + third_up(c3 * x)
    return first + second + third


def packed_diagonal(sig, c1, h1, c2, c3, width, blocks):
    lane = iota(c1.shape, 2)
    block, inner = lane // width % blocks, lane % width
    h2 = pltpu.roll(c2, 128 - width, 2)
    h2 = jnp.where(block == blocks - 1, pltpu.roll(h2, 7, 1), h2)
    h3 = jnp.where(inner == width - 1, pltpu.roll(c3, width - 1, 2), pltpu.roll(c3, 127, 2))
    return sig + c1 + h1 + c2 + h2 + c3 + h3


def fold_matrix(even2=False, even3=False):
    k, j = iota((128, 128), 0), iota((128, 128), 1)
    k2, k3, j2, j3 = k // 32, k % 32, j // 16 % 2, j % 16
    hit2 = k2 == 2 * j2 if even2 else k2 // 2 == j2
    hit3 = k3 == 2 * j3 if even3 else k3 // 2 == j3
    return (hit2 & hit3).astype(F32)


def wrap(ref, count):
    ref[0] = ref[count]
    ref[count + 1] = ref[1]


def around(j, n):
    return lax.rem(j + n, n)


STEP = 8
THREE, FOUR = (32, 4), (16, 2)


def bottom_kernel(place, mine, theirs, win, u2w, late, late_other, out, msg,
                  f3, c1, c2, c3, d3, g3, u1, u2, res, f4, d1, d2, e3, g4, ua, ub, st, scr):
    n3, n4 = f3.shape[0], f4.shape[0]

    def loop(body):
        def step(c, carry):
            body(pl.multiple_of(c * STEP, STEP))
            return carry

        lax.fori_loop(0, n3 // STEP, step, 0)

    odd = lax.rem(place[0], 2) == 1

    def load(j):
        here = pl.ds(j, STEP)
        a, b, c, d = mine[here, 0], mine[here, 1], theirs[here, 0], theirs[here, 1]
        f3[here] = jnp.where(odd, c, a)
        c1[here] = jnp.where(odd, d, b)
        c2[here] = jnp.where(odd, a, c)
        c3[here] = jnp.where(odd, b, d)

    loop(load)
    c1[n3] = c1[0]

    def start(j):
        here = pl.ds(j, STEP)
        diag = packed_diagonal(SIG[3], c1[here], c1[pl.ds(j + 1, STEP)], c2[here], c3[here], *THREE)
        inverse = 1.0 / diag
        d3[here] = diag
        g3[here] = inverse
        u1[pl.ds(j + 1, STEP)] = f3[here] * inverse * (1.0 / THETA)

    loop(start)
    wrap(u1, n3)

    def near3(u, j):
        here = pl.ds(j, STEP)
        x = u[pl.ds(j + 1, STEP)]
        args = (c1[here], c1[pl.ds(j + 1, STEP)], c2[here], c3[here])
        return here, x, packed_sum(u[here], x, u[pl.ds(j + 2, STEP)], *args, *THREE)

    def pre(j):
        here, x, near = near3(u1, j)
        u2[pl.ds(j + 1, STEP)] = (1.0 + KEEP) * x + GAIN * (g3[here] * (f3[here] + near) - x)

    loop(pre)
    wrap(u2, n3)

    def residual(j):
        here, x, near = near3(u2, j)
        left = (f3[here] + near - d3[here] * x).reshape(STEP // 2, 2, 8, 128)
        res[pl.ds(j // 2, STEP // 2)] = left[:, 0] + left[:, 1]

    loop(residual)

    def fold(x, *even):
        return mul(x.reshape(8 * n4, 128), fold_matrix(*even)).reshape(n4, 8, 128)

    def halves(ref):
        x = ref[0:n3].reshape(n4, 2, 8, 128)
        return x[:, 0], x[:, 1]

    f4[...] = 0.5 * fold(res[...])
    d1[0:n4] = 0.25 * fold(halves(c1)[0])
    d1[n4] = d1[0]
    d2[...] = 0.25 * fold(sum(halves(c2)), True, False)
    e3[...] = 0.25 * fold(sum(halves(c3)), False, True)
    coefs4 = (d1[0:n4], d1[1 : n4 + 1], d2[...], e3[...])
    g4[...] = 1.0 / packed_diagonal(SIG[4], *coefs4, *FOUR)
    x = f4[...] * g4[...] * (1.0 / THETA)
    ua[1 : n4 + 1] = x
    wrap(ua, n4)
    st[...] = x
    src, dst = ua, ub
    for keep, gain in factors(4):
        x = src[1 : n4 + 1]
        near = packed_sum(src[0:n4], x, src[2 : n4 + 2], d1[0:n4], d1[1 : n4 + 1], d2[...], e3[...], *FOUR)
        step = keep * st[...] + gain * (g4[...] * (f4[...] + near) - x)
        st[...] = step
        dst[1 : n4 + 1] = x + step
        wrap(dst, n4)
        src, dst = dst, src

    j0 = around(place[0] // 2 - 1, n3)
    k, j = iota((128, 128), 0), iota((128, 128), 1)
    unfold = (k == 16 * (j // 64) + j % 32 // 2).astype(F32)
    coarse = jnp.concatenate([src[1 + around(around(j0 - 2, n3) // 2 + m, n4)] for m in range(4)], axis=0)
    scr[0:32] = mul(coarse, unfold)
    shifted = lax.rem(around(j0 - 2, n3), 2)
    js = [around(j0 - 2 + m, n3) for m in range(7)]
    v = [u2[1 + js[m]] + scr[pl.ds(pl.multiple_of(8 * ((shifted + m) // 2), 8), 8), :] for m in range(7)]
    v = jnp.stack(v)

    def window(ref, first, count, by=0):
        return jnp.stack([ref[js[m] + by] for m in range(first, first + count)])

    def args(first, count):
        return window(c1, first, count), window(c1, first, count, 1), window(c2, first, count), window(c3, first, count)

    f, g = window(f3, 1, 5), window(g3, 1, 5)
    near = packed_sum(v[0:5], v[1:6], v[2:7], *args(1, 5), *THREE)
    w = v[1:6] + (1.0 / THETA) * (g * (f + near) - v[1:6])
    near = packed_sum(w[0:3], w[1:4], w[2:5], *args(2, 3), *THREE)
    x = w[1:4] + KEEP * (w[1:4] - v[2:5]) + GAIN * (g[1:4] * (f[1:4] + near) - w[1:4])
    x = x.reshape(24, 128)
    for q in range(4):
        fine = mul(x, (k == 32 * q + j % 64 // 2).astype(F32))
        scr[pl.ds(2 * q, 24, stride=8), :] = fine
        scr[pl.ds(2 * q + 1, 24, stride=8), :] = fine

    lower = both_halves(jnp.where(odd, late_other[...], late[...]))
    upper = both_halves(jnp.where(odd, late[...], late_other[...]))
    base = (lower, u2w[0], u2w[1], u2w[2], u2w[3], upper)
    v = [base[m] + scr[64 * (m // 2) : 64 * (m // 2) + 64, :] for m in range(6)]

    def args2(m):
        return win[m], win[4 + m], win[8 + m], win[9 + m], win[13 + m], win[17 + m]

    w = [first_post(v[m + 1], v[m], v[m + 2], *args2(m)) for m in range(4)]
    for p in range(2):
        out[p] = second_post(w[p + 1], v[p + 2], w[p], w[p + 2], *args2(p + 1))
    msg[...] = jnp.where(odd, out[1], out[0])


def middle_post_kernel(place, e2, far, msg, sib, near, f, g1, w1, out, up, down, v, w):
    n = place[1]
    odd = lax.rem(place[0], 2) == 1
    planes = (jnp.where(odd, e2[0], far[...]), jnp.where(odd, e2[1], e2[0]), jnp.where(odd, far[...], e2[1]))
    row, col = iota((40, 64), 0), iota((40, 64), 1)
    pick = (col == lax.rem(16 * n + (row + 4) // 2 + 60, 64)).astype(F32)
    lanes = copies_of_lanes(128, 128)
    fine = [mul(mul(pick, e), lanes) for e in planes]
    for p in range(6):
        ours, next_chip = 64 + 40 * (p % 2), 224 + 40 * (p % 2)
        if p < 2:
            base = jnp.where(odd, sib[ours : ours + 40], near[next_chip : next_chip + 40])
        elif p < 4:
            base = msg[ours : ours + 40]
        else:
            base = jnp.where(odd, near[next_chip : next_chip + 40], sib[ours : ours + 40])
        v[p] = base + fine[p // 2]
    for p in range(1, 5):
        w[p] = first_post(v[p], v[p - 1], v[p + 1], f[p - 1], g1[p - 1], w1[p], w1[p + 1], w1[6 + p], w1[12 + p])
    for p in (2, 3):
        out[p - 2] = second_post(w[p], v[p], w[p - 1], w[p + 1], f[p - 1], g1[p - 1], w1[p], w1[p + 1], w1[6 + p], w1[12 + p])
    up[...] = out[1]
    down[...] = out[0]


def fine_post_kernel(e1, e1low, e1high, low, high, f, c1, c2, c3, g, u2, out, v, w, scr):
    lanes = copies_of_lanes(128, 256)
    rows = twice_rows(jnp.concatenate([e1low[...], e1[0], e1[1], e1high[...]], axis=0), scr)
    fine = mul(rows, lanes)
    for k, ref in ((0, low), (7, high)):
        part = fine[80 * (k // 2) : 80 * (k // 2) + 80]
        v[k, 0:40, 0:128] = ref[4] + part[0:40, 0:128]
        v[k, 0:40, 128:256] = ref[5] + part[0:40, 128:256]
        v[k, 40:80, 0:128] = ref[6] + part[40:80, 0:128]
        v[k, 40:80, 128:256] = ref[7] + part[40:80, 128:256]
    for k in range(1, 7):
        v[k] = u2[k] + fine[80 * (k // 2) : 80 * (k // 2) + 80]

    def post1(q, carry):
        def chunk(r0, n):
            here = pl.ds(r0, CHUNK)
            x, near = near_chunk(v, q + 1, c1, c2, c3, q, r0, n)
            w[q + 1, here, :] = x + (1.0 / THETA) * (g[q, here, :] * (f[q, here, :] + near) - x)

        chunked(80, chunk)
        return carry

    lax.fori_loop(0, 6, post1, 0)

    def post2(q, carry):
        for r0 in range(8, 72, CHUNK):
            here = pl.ds(r0, CHUNK)
            x, near = near_chunk(w, q + 1, c1, c2, c3, q, r0, 80)
            step = KEEP * (x - v[q + 1, here, :]) + GAIN * (g[q, here, :] * (f[q, here, :] + near) - x)
            out[q - 1, pl.ds(r0 - 8, CHUNK), :] = x + step
        return carry

    lax.fori_loop(1, 5, post2, 0)


def shift(x, axis, by):
    count = lax.axis_size(axis)
    return lax.ppermute(x, axis, [(i, (i + by) % count) for i in range(count)])


def sibling(x):
    return lax.ppermute(x, "wide", [(i, i ^ 1) for i in range(lax.axis_size("wide"))])


def across(x):
    count = lax.axis_size("wide")
    return lax.ppermute(x, "wide", [(i, (i + 1 if i % 2 else i - 1) % count) for i in range(count)])


def body(source, coef_first, coef_second, coef_third):
    wide = lax.axis_size("wide")
    n3, n4 = wide // 2, wide // 4
    place = jnp.stack([lax.axis_index("wide"), lax.axis_index("narrow")]).astype(jnp.int32)
    big = (80, 256)

    own, up, down, mine = call(
        start_kernel,
        [(16,) + big, (18, 8, 256), (18, 8, 256), (2, 8, 256)],
        [(128, 128), pltpu.SemaphoreType.DMA((4,))],
        {k: pltpu.HBM for k in range(4)},
    )(source, coef_first, coef_second, coef_third)
    low, high, far = shift(up, "narrow", 1), shift(down, "narrow", -1), shift(mine, "narrow", 2)

    own, coef1, coef2, up, down = call(
        pad_kernel,
        [(16,) + big, (6, 40, 128), (3, 64, 128), (568, 256), (648, 256)],
        [(160, 128)],
        SCALARS,
    )(place, own, low, high, mine, far)
    low, high = shift(up, "wide", 1), shift(down, "wide", -1)

    windows = [(6,) + big, (7,) + big, (6,) + big, (6,) + big, (6,) + big, (8,) + big]
    f, c1, c2, c3, g, u2, w1, g1, up, down, c2w, f1 = call(
        fine_pre_kernel,
        windows + [(18, 40, 128), (4, 40, 128), (8, 40, 128), (8, 40, 128), (9, 64, 128), (2, 40, 128)],
        windows + [(8,) + big, (4,) + big, (160, 128), pltpu.SemaphoreType.DMA((6,))],
        out_places={k: pltpu.HBM for k in range(6)},
    )(own, coef1, coef2, low, high)
    low1, high1 = shift(up, "wide", 1), shift(down, "wide", -1)
    (tiles,) = call(coarse_tiles_kernel, [(3, 8, 128)], [(64, 128)], SCALARS)(place, c2w)

    f1w, u2m, f2, up, down = call(
        middle_pre_kernel,
        [(4, 40, 128), (6, 40, 128), (16, 128), (32, 128), (32, 128)],
        [(6, 40, 128), (40, 128)],
    )(up, low1, high1, w1, g1)
    low, high, far = shift(up, "narrow", 1), shift(down, "narrow", -1), shift(f2, "narrow", 2)

    own2, msg = call(coarse_start_kernel, [(2, 64, 128), (144, 128)], (), SCALARS)(place, f2, low, high, far, c2w, u2m)
    sib = sibling(msg)
    (swap,) = call(coarse_swap_kernel, [(304, 128)])(own2, msg, sib, c2w)
    near = across(swap)
    other = sibling(near)
    w2, u2w, late = call(
        coarse_pre_kernel, [(21, 64, 128), (4, 64, 128), (32, 128)], [(6, 64, 128)], SCALARS
    )(place, own2, c2w, sib, near, other)
    late = across(late)
    (send,) = call(coarse_send_kernel, [(n3, 2, 8, 128)], [(64, 128)], SCALARS)(place, w2, u2w, tiles)
    cores = [[k for k in range(wide) if k % 2 == c] for c in range(2)]
    parts = lax.all_to_all(send, "wide", split_axis=0, concat_axis=0, tiled=True, axis_index_groups=cores)
    theirs, late_other = sibling(parts), sibling(late)

    three, four = (n3, 8, 128), (n4, 8, 128)
    e2, msg2 = call(
        bottom_kernel,
        [(2, 64, 128), (64, 128)],
        [three, (n3 + 1, 8, 128), three, three, three, three, (n3 + 2, 8, 128), (n3 + 2, 8, 128), four, four]
        + [(n4 + 1, 8, 128), four, four, four, (n4 + 2, 8, 128), (n4 + 2, 8, 128), four, (192, 128)],
        SCALARS,
    )(place, parts, theirs, w2, u2w, late, late_other)
    far = across(msg2)

    e1, up, down = call(
        middle_post_kernel,
        [(2, 40, 128), (40, 128), (40, 128)],
        [(6, 40, 128), (6, 40, 128)],
        SCALARS,
    )(place, e2, far, msg, sib, near, f1w, g1, w1)
    e1low, e1high = shift(up, "wide", 1), shift(down, "wide", -1)

    (out,) = call(
        fine_post_kernel, [(4, 64, 256)], [(8,) + big, (8,) + big, (320, 128)]
    )(e1, e1low, e1high, low1, high1, f, c1, c2, c3, g, u2)
    return out


def solution(mesh):
    spec = P("wide", "narrow", None)
    return jax.shard_map(body, mesh=mesh, in_specs=(spec,) * 4, out_specs=spec, check_vma=False)
```

```python
import functools

import jax
import jax.numpy as jnp
from jax import lax
from jax.experimental import pallas as pl
from jax.experimental.pallas import tpu as pltpu
from jax.sharding import PartitionSpec as P

THETA = 1.125
DELTA = 0.875
RATIO = THETA / DELTA
SIG = [0.0002 * 4.0**level for level in range(5)]
F32 = jnp.float32


def factors(degree):
    rho, out = 1.0 / RATIO, []
    for _ in range(degree - 1):
        new = 1.0 / (2.0 * RATIO - rho)
        out.append((new * rho, 2.0 * new / DELTA))
        rho = new
    return out


(KEEP, GAIN), = factors(2)


def roll(x, by, axis):
    return pltpu.roll(x, by % x.shape[axis], axis)


def gather_sum(below, here, above, c1, h1, c2, c3):
    first = c1 * below + h1 * above
    second = c2 * roll(here, 1, 0) + roll(c2 * here, -1, 0)
    third = c3 * roll(here, 1, 1) + roll(c3 * here, -1, 1)
    return first + second + third


def diagonal(sig, c1, h1, c2, c3):
    return sig + c1 + h1 + c2 + roll(c2, -1, 0) + c3 + roll(c3, -1, 1)


def iota(shape, dim):
    return lax.broadcasted_iota(jnp.int32, shape, dim)


def pairs_of_lanes(lanes, period, even=False):
    row, col = iota((lanes, 128), 0), iota((lanes, 128), 1) % period
    hit = row == 2 * col if even else row // 2 == col
    return hit.astype(F32)


def copies_of_lanes(lanes_in, lanes_out):
    row, col = iota((lanes_in, lanes_out), 0), iota((lanes_in, lanes_out), 1)
    return (row == col // 2).astype(F32)


def pieces(x):
    out = []
    for _ in range(3):
        part = x.astype(jnp.bfloat16)
        out.append(part)
        x = x - part.astype(F32)
    return out


def mul(x, ones):
    ones = ones.astype(jnp.bfloat16)
    high, mid, low = [jnp.dot(part, ones, preferred_element_type=F32) for part in pieces(x)]
    return high + (mid + low)


def mul_left(ones, x):
    ones = ones.astype(jnp.bfloat16)
    high, mid, low = [jnp.dot(ones, part, preferred_element_type=F32) for part in pieces(x)]
    return high + (mid + low)


def pair_rows(x, scratch, start=0, count=None, even=False):
    rows = x.shape[0]
    count = rows // 2 if count is None else count
    scratch[0:rows, :] = x
    first = scratch[pl.ds(start, count, stride=2), :]
    if even:
        return first
    return first + scratch[pl.ds(start + 1, count, stride=2), :]


def twice_rows(x, scratch):
    rows = x.shape[0]
    scratch[pl.ds(0, rows, stride=2), :] = x
    scratch[pl.ds(1, rows, stride=2), :] = x
    return scratch[0 : 2 * rows, :]


def coarse_coefs(planes, scratch, lanes, period, start=0, count=None):
    both = pairs_of_lanes(lanes, period)
    alone = pairs_of_lanes(lanes, period, even=True)
    return (
        0.25 * pair_rows(mul(planes[0], both), scratch, start, count),
        0.25 * pair_rows(mul(planes[1], both), scratch, start, count, even=True),
        0.25 * pair_rows(mul(planes[2], alone), scratch, start, count),
    )


def spread_block(x, block, width):
    lane = iota(x.shape, 1)
    x = jnp.where(lane // width == block, x, 0.0)
    while width < 128:
        x = x + pltpu.roll(x, width, 1)
        width *= 2
    return x


def smooth_two(u1, below, above, f, g, c1, h1, c2, c3):
    near = gather_sum(below, u1, above, c1, h1, c2, c3)
    return (1.0 + KEEP) * u1 + GAIN * (g * (f + near) - u1)


def first_post(v, below, above, f, g, c1, h1, c2, c3):
    near = gather_sum(below, v, above, c1, h1, c2, c3)
    return v + (1.0 / THETA) * (g * (f + near) - v)


def second_post(u, v, below, above, f, g, c1, h1, c2, c3):
    near = gather_sum(below, u, above, c1, h1, c2, c3)
    return u + KEEP * (u - v) + GAIN * (g * (f + near) - u)


def call(kernel, outs, scratch=(), places=(), out_places=(), limit=8):
    places, out_places = dict(places), dict(out_places)

    def run(*args):
        in_specs = [pl.BlockSpec(memory_space=places.get(i, pltpu.VMEM)) for i in range(len(args))]
        return pl.pallas_call(
            kernel,
            out_shape=[jax.ShapeDtypeStruct(s, F32) for s in outs],
            in_specs=in_specs,
            out_specs=[pl.BlockSpec(memory_space=out_places.get(i, pltpu.VMEM)) for i in range(len(outs))],
            scratch_shapes=[pltpu.VMEM(s, F32) if isinstance(s, tuple) else s for s in scratch],
            compiler_params=pltpu.CompilerParams(vmem_limit_bytes=limit * 2**20),
        )(*args)

    return run


SCALARS = {0: pltpu.SMEM}


def two_blocks(x):
    half = x.shape[0] // 2
    return jnp.where(iota((half, 128), 1) < 64, x[:half], x[half:])


def start_kernel(f, c1, c2, c3, up, down, sems):
    copies = []
    for a, ref in enumerate((f, c1, c2, c3)):
        for k, (out, row) in enumerate(((up, 56), (down, 0))):
            copy = pltpu.make_async_copy(ref.at[:, pl.ds(row, 8), :], out.at[pl.ds(4 * a, 4)], sems.at[2 * a + k])
            copy.start()
            copies.append(copy)
    for copy in copies:
        copy.wait()


def pad_kernel(inner, low, high, own, coef1, up, down, scr):
    for a in range(16):
        own[a, 0:8] = low[a]
        own[a, 8:72] = inner[a]
        own[a, 72:80] = high[a]
    for p, out, slot in ((1, down, 5), (2, up, 4)):
        diag = diagonal(SIG[0], own[4 + p], own[5 + p], own[8 + p], own[12 + p])
        out[80 * slot : 80 * slot + 80] = own[p] / diag / THETA
    for a in range(4):
        up[80 * a : 80 * a + 80] = own[4 * a + 3]
        down[80 * a : 80 * a + 80] = own[4 * a]
    down[320:400] = own[5]
    k1 = jnp.concatenate([own[4], own[6]], axis=0)
    k2 = jnp.concatenate([own[8] + own[9], own[10] + own[11]], axis=0)
    k3 = jnp.concatenate([own[12] + own[13], own[14] + own[15]], axis=0)
    coarse = coarse_coefs((k1, k2, k3), scr, 256, 128)
    for a in range(3):
        for p in range(2):
            coef1[2 * a + p] = coarse[a][40 * p : 40 * p + 40]
    for out, at in ((up, 400), (down, 480)):
        for k in range(6):
            row, lane = at + 40 * (k // 2), 128 * (k % 2)
            out[row : row + 40, lane : lane + 128] = coef1[k]


def unpack(ref, at, index):
    row, lane = at + 40 * (index // 2), 128 * (index % 2)
    return ref[row : row + 40, lane : lane + 128]


CHUNK = 16


def chunked(rows, body):
    for r0 in range(0, rows, CHUNK):
        body(r0, rows)


def near_chunk(u, p, c1, c2, c3, q, r0, rows):
    here = pl.ds(r0, CHUNK)
    x = u[p, here, :]
    if r0 > 0:
        lower = u[p, pl.ds(r0 - 1, CHUNK), :]
    else:
        lower = roll(x, 1, 0)
    if r0 + CHUNK < rows:
        after = pl.ds(r0 + 1, CHUNK)
        upper = c2[q, after, :] * u[p, after, :]
    else:
        upper = roll(c2[q, here, :] * x, -1, 0)
    k3 = c3[q, here, :]
    first = c1[q, here, :] * u[p - 1, here, :] + c1[q + 1, here, :] * u[p + 1, here, :]
    second = c2[q, here, :] * lower + upper
    third = k3 * roll(x, 1, 1) + roll(k3 * x, -1, 1)
    return x, first + second + third


def diag_chunk(c1, c2, c3, q, r0, rows):
    here = pl.ds(r0, CHUNK)
    k2, k3 = c2[q, here, :], c3[q, here, :]
    if r0 + CHUNK < rows:
        h2 = c2[q, pl.ds(r0 + 1, CHUNK), :]
    else:
        h2 = roll(k2, -1, 0)
    return SIG[0] + c1[q, here, :] + c1[q + 1, here, :] + k2 + h2 + k3 + roll(k3, -1, 1)


def fine_pre_kernel(own, coef1, low, high, f, c1, c2, c3, g, u2, w1, g1, msg_up, msg_down, f1, u1, res, scr):
    for a, ref in enumerate((f, c1, c2, c3)):
        ref[0] = low[80 * a : 80 * a + 80]
        ref[1:5] = own[4 * a : 4 * a + 4]
        ref[5] = high[80 * a : 80 * a + 80]
    c1[6] = high[320:400]
    u1[0] = low[320:400]
    u1[7] = high[400:480]

    def smooth_first(q, carry):
        def rows(r0, n):
            here = pl.ds(r0, CHUNK)
            inverse = 1.0 / diag_chunk(c1, c2, c3, q, r0, n)
            g[q, here, :] = inverse
            u1[q + 1, here, :] = f[q, here, :] * inverse * (1.0 / THETA)

        chunked(80, rows)
        return carry

    lax.fori_loop(0, 6, smooth_first, 0)

    def smooth_second(q, carry):
        def rows(r0, n):
            here = pl.ds(r0, CHUNK)
            x, near = near_chunk(u1, q + 1, c1, c2, c3, q, r0, n)
            u2[q + 1, here, :] = (1.0 + KEEP) * x + GAIN * (g[q, here, :] * (f[q, here, :] + near) - x)

        chunked(80, rows)
        return carry

    u2[0] = u1[0]
    u2[7] = u1[7]
    lax.fori_loop(0, 6, smooth_second, 0)

    def residual(q, carry):
        def rows(r0, n):
            here = pl.ds(r0, CHUNK)
            x, near = near_chunk(u2, q + 1, c1, c2, c3, q, r0, n)
            res[q - 1, here, :] = f[q, here, :] + near - diag_chunk(c1, c2, c3, q, r0, n) * x

        chunked(80, rows)
        return carry

    lax.fori_loop(1, 5, residual, 0)

    both = pairs_of_lanes(256, 128)
    sums = jnp.concatenate([res[0] + res[1], res[2] + res[3]], axis=0)
    coarse = 0.5 * pair_rows(mul(sums, both), scr)
    f1[0] = coarse[:40]
    f1[1] = coarse[40:]
    for a in range(3):
        for p in range(2):
            w1[6 * a + p] = unpack(low, 400, 2 * a + p)
            w1[6 * a + 2 + p] = coef1[2 * a + p]
            w1[6 * a + 4 + p] = unpack(high, 480, 2 * a + p)
    for k in range(4):
        p = k + 1
        g1[k] = 1.0 / diagonal(SIG[1], w1[p], w1[p + 1], w1[6 + p], w1[12 + p])
    for p in range(2):
        start = f1[p] * g1[1 + p] * (1.0 / THETA)
        for out in (msg_up, msg_down):
            out[p] = f1[p]
            out[2 + p] = start
    for out, plane in ((msg_up, 4), (msg_down, 3)):
        out[4] = u2[plane, 0:40, 0:128]
        out[5] = u2[plane, 0:40, 128:256]
        out[6] = u2[plane, 40:80, 0:128]
        out[7] = u2[plane, 40:80, 128:256]


def coarse_coef_kernel(w1, out, scr):
    k1 = jnp.concatenate([w1[2], w1[4]], axis=0)
    k2, k3 = w1[8] + w1[9], w1[14] + w1[15]
    both, alone = pairs_of_lanes(128, 64), pairs_of_lanes(128, 64, even=True)
    k1 = 0.25 * pair_rows(mul(k1, both), scr)
    k2 = 0.25 * pair_rows(mul(k2, both), scr, even=True)
    k3 = 0.25 * pair_rows(mul(k3, alone), scr)
    for k, x in enumerate((k1[2:18], k1[22:38], k2[2:18], k3[2:18])):
        out[8 * k : 8 * k + 8] = two_blocks(x)


def middle_pre_kernel(own, low, high, w1, g1, coefs, f, u2, f2, up, down, u1, scr):
    f[0] = low[1]
    f[1:3] = own[0:2]
    f[3] = high[0]
    u1[0:2] = low[2:4]
    u1[2:4] = own[2:4]
    u1[4:6] = high[2:4]
    u2[0] = jnp.zeros((40, 128), F32)
    u2[5] = jnp.zeros((40, 128), F32)
    for p in range(1, 5):
        u2[p] = smooth_two(u1[p], u1[p - 1], u1[p + 1], f[p - 1], g1[p - 1], w1[p], w1[p + 1], w1[6 + p], w1[12 + p])
    total = 0.0
    for p in (2, 3):
        k1, h1, k2, k3 = w1[p], w1[p + 1], w1[6 + p], w1[12 + p]
        near = gather_sum(u2[p - 1], u2[p], u2[p + 1], k1, h1, k2, k3)
        total = total + (f[p - 1] + near - diagonal(SIG[1], k1, h1, k2, k3) * u2[p])
    coarse = 0.5 * pair_rows(mul(total, pairs_of_lanes(128, 64)), scr, 4, 16)
    f2[0:8] = two_blocks(coarse)
    f2[8:40] = coefs[...]
    for p in range(2):
        up[40 + 8 * p : 48 + 8 * p] = u2[2 + p, 28:36]
        down[40 + 8 * p : 48 + 8 * p] = u2[2 + p, 4:12]
    up[0:40] = f2[...]
    down[0:40] = f2[...]


def both_halves(x):
    return jnp.concatenate([spread_block(x, 0, 64), spread_block(x, 1, 64)], axis=0)


def coarse_start_kernel(place, f2, low, high, far, u2fine, own, msg):
    n = place[1]
    for piece, by in ((f2, 0), (high, 1), (far, 2), (low, 3)):
        at = pl.multiple_of(16 * lax.rem(n + by, 4), 16)
        for k in range(5):
            own[k, pl.ds(at, 16), :] = both_halves(piece[8 * k : 8 * k + 8])
    own[5] = 1.0 / diagonal(SIG[2], own[1], own[2], own[3], own[4])
    for k, plane in enumerate((0, 5, 1, 3, 4)):
        msg[32 * k : 32 * k + 32] = two_blocks(own[plane])
    for p in range(2):
        at = 160 + 40 * p
        msg[at : at + 40] = u2fine[2 + p]
        msg[at : at + 4] = low[44 + 8 * p : 48 + 8 * p]
        msg[at + 36 : at + 40] = high[40 + 8 * p : 44 + 8 * p]


def coarse_tiles_kernel(place, msg, sib, tiles, scr):
    odd = lax.rem(place[0], 2) == 1
    for a in range(3):
        here = slice(64 + 32 * a, 96 + 32 * a)
        x = jnp.where(odd, sib[here], msg[here]) if a == 0 else msg[here] + sib[here]
        scr[...] = 0.25 * mul(both_halves(x), pairs_of_lanes(128, 32, even=a == 2))
        tiles[a] = tile_of(scr, a == 1)


def tile_of(scr, even=False):
    block = iota((8, 128), 1) // 32
    packed = 0.0
    for q in range(4):
        part = scr[pl.ds(2 * q, 8, stride=8), :]
        if not even:
            part = part + scr[pl.ds(2 * q + 1, 8, stride=8), :]
        packed = jnp.where(block == q, part, packed)
    return packed


def coarse_swap_kernel(own, msg, sib, out):
    out[0:160] = msg[0:160]
    out[160:192] = sib[0:32] * sib[32:64] * (1.0 / THETA)
    out[192:224] = two_blocks(own[2])
    out[224:304] = msg[160:240]


def coarse_pre_kernel(place, own, sib, near, other, w, u2, late, u1):
    odd = lax.rem(place[0], 2) == 1

    def below(k):
        here = slice(32 * k, 32 * k + 32)
        return both_halves(jnp.where(odd, other[here], near[here]))

    def above(k):
        here = slice(32 * k, 32 * k + 32)
        return both_halves(jnp.where(odd, near[here], other[here]))

    for a, (base, plane) in enumerate(((0, 0), (4, 5), (8, 1), (13, 3), (17, 4))):
        mine, theirs = own[plane], both_halves(sib[32 * a : 32 * a + 32])
        w[base] = below(a)
        w[base + 1] = jnp.where(odd, theirs, mine)
        w[base + 2] = jnp.where(odd, mine, theirs)
        w[base + 3] = above(a)
    w[12] = above(6)
    u1[0] = below(5)
    u1[5] = above(5)
    for k in range(4):
        u1[k + 1] = w[k] * w[4 + k] * (1.0 / THETA)
    for k in range(4):
        u2[k] = smooth_two(u1[k + 1], u1[k], u1[k + 2], w[k], w[4 + k], w[8 + k], w[9 + k], w[13 + k], w[17 + k])
    late[...] = two_blocks(jnp.where(odd, u2[1], u2[2]))


def coarse_send_kernel(place, w, u2, tiles, send, scr):
    odd = lax.rem(place[0], 2) == 1
    total = 0.0
    for k in (1, 2):
        args = (w[8 + k], w[9 + k], w[13 + k], w[17 + k])
        near = gather_sum(u2[k - 1], u2[k], u2[k + 1], *args)
        total = total + (w[k] + near - diagonal(SIG[2], *args) * u2[k])
    scr[...] = 0.5 * mul(total, pairs_of_lanes(128, 32))
    first = jnp.where(odd, tiles[1], tile_of(scr))
    second = jnp.where(odd, tiles[2], tiles[0])
    for k in range(send.shape[0]):
        send[k, 0] = first
        send[k, 1] = second


def packed_sum(below, x, above, c1, h1, c2, c3, width, blocks):
    lane = iota(x.shape, 2)
    block, inner = lane // width % blocks, lane % width

    def second_down(x):
        x = pltpu.roll(x, width, 2)
        return jnp.where(block == 0, pltpu.roll(x, 1, 1), x)

    def second_up(x):
        x = pltpu.roll(x, 128 - width, 2)
        return jnp.where(block == blocks - 1, pltpu.roll(x, 7, 1), x)

    def third_down(x):
        return jnp.where(inner == 0, pltpu.roll(x, 129 - width, 2), pltpu.roll(x, 1, 2))

    def third_up(x):
        return jnp.where(inner == width - 1, pltpu.roll(x, width - 1, 2), pltpu.roll(x, 127, 2))

    first = c1 * below + h1 * above
    second = c2 * second_down(x) + second_up(c2 * x)
    third = c3 * third_down(x) + third_up(c3 * x)
    return first + second + third


def packed_diagonal(sig, c1, h1, c2, c3, width, blocks):
    lane = iota(c1.shape, 2)
    block, inner = lane // width % blocks, lane % width
    h2 = pltpu.roll(c2, 128 - width, 2)
    h2 = jnp.where(block == blocks - 1, pltpu.roll(h2, 7, 1), h2)
    h3 = jnp.where(inner == width - 1, pltpu.roll(c3, width - 1, 2), pltpu.roll(c3, 127, 2))
    return sig + c1 + h1 + c2 + h2 + c3 + h3


def fold_matrix(even2=False, even3=False):
    k, j = iota((128, 128), 0), iota((128, 128), 1)
    k2, k3, j2, j3 = k // 32, k % 32, j // 16 % 2, j % 16
    hit2 = k2 == 2 * j2 if even2 else k2 // 2 == j2
    hit3 = k3 == 2 * j3 if even3 else k3 // 2 == j3
    return (hit2 & hit3).astype(F32)


def wrap(ref, count):
    ref[0] = ref[count]
    ref[count + 1] = ref[1]


def around(j, n):
    return lax.rem(j + n, n)


STEP = 8
THREE, FOUR = (32, 4), (16, 2)


def bottom_kernel(place, mine, theirs, e2,
                  f3, c1, c2, c3, d3, g3, u1, u2, res, f4, d1, d2, e3, g4, ua, ub, st, scr):
    n3, n4 = f3.shape[0], f4.shape[0]

    def loop(body):
        def step(c, carry):
            body(pl.multiple_of(c * STEP, STEP))
            return carry

        lax.fori_loop(0, n3 // STEP, step, 0)

    odd = lax.rem(place[0], 2) == 1

    def load(j):
        here = pl.ds(j, STEP)
        a, b, c, d = mine[here, 0], mine[here, 1], theirs[here, 0], theirs[here, 1]
        f3[here] = jnp.where(odd, c, a)
        c1[here] = jnp.where(odd, d, b)
        c2[here] = jnp.where(odd, a, c)
        c3[here] = jnp.where(odd, b, d)

    loop(load)
    c1[n3] = c1[0]

    def start(j):
        here = pl.ds(j, STEP)
        diag = packed_diagonal(SIG[3], c1[here], c1[pl.ds(j + 1, STEP)], c2[here], c3[here], *THREE)
        inverse = 1.0 / diag
        d3[here] = diag
        g3[here] = inverse
        u1[pl.ds(j + 1, STEP)] = f3[here] * inverse * (1.0 / THETA)

    loop(start)
    wrap(u1, n3)

    def near3(u, j):
        here = pl.ds(j, STEP)
        x = u[pl.ds(j + 1, STEP)]
        args = (c1[here], c1[pl.ds(j + 1, STEP)], c2[here], c3[here])
        return here, x, packed_sum(u[here], x, u[pl.ds(j + 2, STEP)], *args, *THREE)

    def pre(j):
        here, x, near = near3(u1, j)
        u2[pl.ds(j + 1, STEP)] = (1.0 + KEEP) * x + GAIN * (g3[here] * (f3[here] + near) - x)

    loop(pre)
    wrap(u2, n3)

    def residual(j):
        here, x, near = near3(u2, j)
        left = (f3[here] + near - d3[here] * x).reshape(STEP // 2, 2, 8, 128)
        res[pl.ds(j // 2, STEP // 2)] = left[:, 0] + left[:, 1]

    loop(residual)

    def fold(x, *even):
        return mul(x.reshape(8 * n4, 128), fold_matrix(*even)).reshape(n4, 8, 128)

    def halves(ref):
        x = ref[0:n3].reshape(n4, 2, 8, 128)
        return x[:, 0], x[:, 1]

    f4[...] = 0.5 * fold(res[...])
    d1[0:n4] = 0.25 * fold(halves(c1)[0])
    d1[n4] = d1[0]
    d2[...] = 0.25 * fold(sum(halves(c2)), True, False)
    e3[...] = 0.25 * fold(sum(halves(c3)), False, True)
    coefs4 = (d1[0:n4], d1[1 : n4 + 1], d2[...], e3[...])
    g4[...] = 1.0 / packed_diagonal(SIG[4], *coefs4, *FOUR)
    x = f4[...] * g4[...] * (1.0 / THETA)
    ua[1 : n4 + 1] = x
    wrap(ua, n4)
    st[...] = x
    src, dst = ua, ub
    for keep, gain in factors(4):
        x = src[1 : n4 + 1]
        near = packed_sum(src[0:n4], x, src[2 : n4 + 2], d1[0:n4], d1[1 : n4 + 1], d2[...], e3[...], *FOUR)
        step = keep * st[...] + gain * (g4[...] * (f4[...] + near) - x)
        st[...] = step
        dst[1 : n4 + 1] = x + step
        wrap(dst, n4)
        src, dst = dst, src

    j0 = around(place[0] // 2 - 1, n3)
    k, j = iota((128, 128), 0), iota((128, 128), 1)
    unfold = (k == 16 * (j // 64) + j % 32 // 2).astype(F32)
    coarse = jnp.concatenate([src[1 + around(around(j0 - 2, n3) // 2 + m, n4)] for m in range(4)], axis=0)
    scr[0:32] = mul(coarse, unfold)
    shifted = lax.rem(around(j0 - 2, n3), 2)
    js = [around(j0 - 2 + m, n3) for m in range(7)]
    v = [u2[1 + js[m]] + scr[pl.ds(pl.multiple_of(8 * ((shifted + m) // 2), 8), 8), :] for m in range(7)]
    v = jnp.stack(v)

    def window(ref, first, count, by=0):
        return jnp.stack([ref[js[m] + by] for m in range(first, first + count)])

    def args(first, count):
        return window(c1, first, count), window(c1, first, count, 1), window(c2, first, count), window(c3, first, count)

    f, g = window(f3, 1, 5), window(g3, 1, 5)
    near = packed_sum(v[0:5], v[1:6], v[2:7], *args(1, 5), *THREE)
    w = v[1:6] + (1.0 / THETA) * (g * (f + near) - v[1:6])
    near = packed_sum(w[0:3], w[1:4], w[2:5], *args(2, 3), *THREE)
    x = w[1:4] + KEEP * (w[1:4] - v[2:5]) + GAIN * (g[1:4] * (f[1:4] + near) - w[1:4])
    x = x.reshape(24, 128)
    for q in range(4):
        fine = mul(x, (k == 32 * q + j % 64 // 2).astype(F32))
        e2[pl.ds(2 * q, 24, stride=8), :] = fine
        e2[pl.ds(2 * q + 1, 24, stride=8), :] = fine


def coarse_post_kernel(place, e2, win, u2, late, out):
    par = lax.rem(place[0], 2)
    odd = par == 1
    late = both_halves(late[...])
    v = [jnp.where(odd, u2[0], late), u2[par], u2[1 + par], u2[2 + par], jnp.where(odd, late, u2[3])]
    v = [v[m] + e2[pl.ds(pl.multiple_of(64 * ((m + par) // 2), 64), 64), :] for m in range(5)]

    def args(m):
        k = m + par
        return win[k], win[4 + k], win[8 + k], win[9 + k], win[13 + k], win[17 + k]

    w = [first_post(v[m + 1], v[m], v[m + 2], *args(m)) for m in range(3)]
    out[...] = second_post(w[1], v[2], w[0], w[2], *args(1))


def middle_post_kernel(place, e2, e2sib, far, msg, sib, near, f, g1, w1, out, up, down, v, w):
    n = place[1]
    odd = lax.rem(place[0], 2) == 1
    planes = (jnp.where(odd, e2sib[...], far[...]), e2[...], jnp.where(odd, far[...], e2sib[...]))
    row, col = iota((40, 64), 0), iota((40, 64), 1)
    pick = (col == lax.rem(16 * n + (row + 4) // 2 + 60, 64)).astype(F32)
    lanes = copies_of_lanes(128, 128)
    fine = [mul(mul_left(pick, e), lanes) for e in planes]
    for p in range(6):
        ours, next_chip = 160 + 40 * (p % 2), 224 + 40 * (p % 2)
        if p < 2:
            base = jnp.where(odd, sib[ours : ours + 40], near[next_chip : next_chip + 40])
        elif p < 4:
            base = msg[ours : ours + 40]
        else:
            base = jnp.where(odd, near[next_chip : next_chip + 40], sib[ours : ours + 40])
        v[p] = base + fine[p // 2]
    for p in range(1, 5):
        w[p] = first_post(v[p], v[p - 1], v[p + 1], f[p - 1], g1[p - 1], w1[p], w1[p + 1], w1[6 + p], w1[12 + p])
    for p in (2, 3):
        out[p - 2] = second_post(w[p], v[p], w[p - 1], w[p + 1], f[p - 1], g1[p - 1], w1[p], w1[p + 1], w1[6 + p], w1[12 + p])
    up[...] = out[1]
    down[...] = out[0]


def fine_post_kernel(e1, e1low, e1high, low, high, f, c1, c2, c3, g, u2, out, v, w, scr):
    x = jnp.concatenate([e1low[...], e1[0], e1[1], e1high[...]], axis=0)
    for half in range(2):
        here = slice(128 * half, 128 * half + 128)
        row, col = iota((128, 128), 0), iota((128, 128), 1)
        fine = mul(x, (row == 64 * half + col // 2).astype(F32))
        scr[pl.ds(0, 160, stride=2), :] = fine
        scr[pl.ds(1, 160, stride=2), :] = fine
        for k, ref in ((0, low), (7, high)):
            at = 80 * (k // 2)
            v[k, 0:40, here] = ref[4 + half] + scr[at : at + 40, :]
            v[k, 40:80, here] = ref[6 + half] + scr[at + 40 : at + 80, :]
        for k in range(1, 7):
            at = 80 * (k // 2)
            v[k, :, here] = u2[k, :, here] + scr[at : at + 80, :]

    def post1(q, carry):
        def chunk(r0, n):
            here = pl.ds(r0, CHUNK)
            x, near = near_chunk(v, q + 1, c1, c2, c3, q, r0, n)
            w[q + 1, here, :] = x + (1.0 / THETA) * (g[q, here, :] * (f[q, here, :] + near) - x)

        chunked(80, chunk)
        return carry

    lax.fori_loop(0, 6, post1, 0)

    def post2(q, carry):
        for r0 in range(8, 72, CHUNK):
            here = pl.ds(r0, CHUNK)
            x, near = near_chunk(w, q + 1, c1, c2, c3, q, r0, 80)
            step = KEEP * (x - v[q + 1, here, :]) + GAIN * (g[q, here, :] * (f[q, here, :] + near) - x)
            out[q - 1, pl.ds(r0 - 8, CHUNK), :] = x + step
        return carry

    lax.fori_loop(1, 5, post2, 0)


def shift(x, axis, by):
    count = lax.axis_size(axis)
    return lax.ppermute(x, axis, [(i, (i + by) % count) for i in range(count)])


def sibling(x):
    return lax.ppermute(x, "wide", [(i, i ^ 1) for i in range(lax.axis_size("wide"))])


def across(x):
    count = lax.axis_size("wide")
    return lax.ppermute(x, "wide", [(i, (i + 1 if i % 2 else i - 1) % count) for i in range(count)])


def body(source, coef_first, coef_second, coef_third):
    wide = lax.axis_size("wide")
    n3, n4 = wide // 2, wide // 4
    place = jnp.stack([lax.axis_index("wide"), lax.axis_index("narrow")]).astype(jnp.int32)
    big = (80, 256)
    inputs = (source, coef_first, coef_second, coef_third)

    up, down = call(
        start_kernel,
        [(16, 8, 256), (16, 8, 256)],
        [pltpu.SemaphoreType.DMA((8,))],
        {k: pltpu.HBM for k in range(4)},
        {k: pltpu.HBM for k in range(2)},
        limit=60,
    )(*inputs)
    low, high = shift(up, "narrow", 1), shift(down, "narrow", -1)

    own, coef1, up, down = call(
        pad_kernel, [(16,) + big, (6, 40, 128), (520, 256), (600, 256)], [(160, 128)]
    )(jnp.concatenate(inputs, axis=0), low, high)
    low, high = shift(up, "wide", 1), shift(down, "wide", -1)

    f, c1, c2, c3, g, u2, w1, g1, up, down, f1 = call(
        fine_pre_kernel,
        [(6,) + big, (7,) + big, (6,) + big, (6,) + big, (6,) + big, (8,) + big]
        + [(18, 40, 128), (4, 40, 128), (8, 40, 128), (8, 40, 128), (2, 40, 128)],
        [(8,) + big, (4,) + big, (160, 128)],
    )(own, coef1, low, high)
    low1, high1 = shift(up, "wide", 1), shift(down, "wide", -1)
    (coefs,) = call(coarse_coef_kernel, [(32, 128)], [(80, 128)])(w1)

    f1w, u2m, f2, up, down = call(
        middle_pre_kernel,
        [(4, 40, 128), (6, 40, 128), (40, 128), (56, 128), (56, 128)],
        [(6, 40, 128), (40, 128)],
    )(up, low1, high1, w1, g1, coefs)
    low, high, far = shift(up, "narrow", 1), shift(down, "narrow", -1), shift(f2, "narrow", 2)

    own2, msg = call(coarse_start_kernel, [(6, 64, 128), (240, 128)], (), SCALARS)(place, f2, low, high, far, u2m)
    sib = sibling(msg)
    (swap,) = call(coarse_swap_kernel, [(304, 128)])(own2, msg, sib)
    near = across(swap)
    (tiles,) = call(coarse_tiles_kernel, [(3, 8, 128)], [(64, 128)], SCALARS)(place, msg, sib)
    other = sibling(near)
    w2, u2w, late = call(
        coarse_pre_kernel, [(21, 64, 128), (4, 64, 128), (32, 128)], [(6, 64, 128)], SCALARS
    )(place, own2, sib, near, other)
    (send,) = call(coarse_send_kernel, [(n3, 2, 8, 128)], [(64, 128)], SCALARS)(place, w2, u2w, tiles)
    cores = [[k for k in range(wide) if k % 2 == c] for c in range(2)]
    parts = lax.all_to_all(send, "wide", split_axis=0, concat_axis=0, tiled=True, axis_index_groups=cores)
    theirs, late = sibling(parts), across(late)

    three, four = (n3, 8, 128), (n4, 8, 128)
    (fine2,) = call(
        bottom_kernel,
        [(192, 128)],
        [three, (n3 + 1, 8, 128), three, three, three, three, (n3 + 2, 8, 128), (n3 + 2, 8, 128), four, four]
        + [(n4 + 1, 8, 128), four, four, four, (n4 + 2, 8, 128), (n4 + 2, 8, 128), four, (32, 128)],
        SCALARS,
    )(place, parts, theirs)
    (e2,) = call(coarse_post_kernel, [(64, 128)], (), SCALARS)(place, fine2, w2, u2w, late)
    e2sib, far = sibling(e2), across(e2)

    e1, up, down = call(
        middle_post_kernel,
        [(2, 40, 128), (40, 128), (40, 128)],
        [(6, 40, 128), (6, 40, 128)],
        SCALARS,
    )(place, e2, e2sib, far, msg, sib, near, f1w, g1, w1)
    e1low, e1high = shift(up, "wide", 1), shift(down, "wide", -1)

    (out,) = call(
        fine_post_kernel, [(4, 64, 256)], [(8,) + big, (8,) + big, (320, 128)]
    )(e1, e1low, e1high, low1, high1, f, c1, c2, c3, g, u2)
    return out


def solution(mesh):
    spec = P("wide", "narrow", None)
    return jax.shard_map(body, mesh=mesh, in_specs=(spec,) * 4, out_specs=spec, check_vma=False)
```

```python
import functools

import jax
import jax.numpy as jnp
from jax import lax
from jax.experimental import pallas as pl
from jax.experimental.pallas import tpu as pltpu
from jax.sharding import PartitionSpec as P

THETA = 1.125
DELTA = 0.875
RATIO = THETA / DELTA
SIG = [0.0002 * 4.0**level for level in range(5)]
F32 = jnp.float32


def factors(degree):
    rho, out = 1.0 / RATIO, []
    for _ in range(degree - 1):
        new = 1.0 / (2.0 * RATIO - rho)
        out.append((new * rho, 2.0 * new / DELTA))
        rho = new
    return out


(KEEP, GAIN), = factors(2)


def roll(x, by, axis):
    return pltpu.roll(x, by % x.shape[axis], axis)


def gather_sum(below, here, above, c1, h1, c2, c3):
    first = c1 * below + h1 * above
    second = c2 * roll(here, 1, 0) + roll(c2 * here, -1, 0)
    third = c3 * roll(here, 1, 1) + roll(c3 * here, -1, 1)
    return first + second + third


def diagonal(sig, c1, h1, c2, c3):
    return sig + c1 + h1 + c2 + roll(c2, -1, 0) + c3 + roll(c3, -1, 1)


def iota(shape, dim):
    return lax.broadcasted_iota(jnp.int32, shape, dim)


def pairs_of_lanes(lanes, period, even=False):
    row, col = iota((lanes, 128), 0), iota((lanes, 128), 1) % period
    hit = row == 2 * col if even else row // 2 == col
    return hit.astype(F32)


def copies_of_lanes(lanes_in, lanes_out):
    row, col = iota((lanes_in, lanes_out), 0), iota((lanes_in, lanes_out), 1)
    return (row == col // 2).astype(F32)


def pieces(x):
    out = []
    for _ in range(3):
        part = x.astype(jnp.bfloat16)
        out.append(part)
        x = x - part.astype(F32)
    return out


def mul(x, ones):
    ones = ones.astype(jnp.bfloat16)
    high, mid, low = [jnp.dot(part, ones, preferred_element_type=F32) for part in pieces(x)]
    return high + (mid + low)


def mul_left(ones, x):
    ones = ones.astype(jnp.bfloat16)
    high, mid, low = [jnp.dot(ones, part, preferred_element_type=F32) for part in pieces(x)]
    return high + (mid + low)


def pair_rows(x, scratch, start=0, count=None, even=False):
    rows = x.shape[0]
    count = rows // 2 if count is None else count
    scratch[0:rows, :] = x
    first = scratch[pl.ds(start, count, stride=2), :]
    if even:
        return first
    return first + scratch[pl.ds(start + 1, count, stride=2), :]


def twice_rows(x, scratch):
    rows = x.shape[0]
    scratch[pl.ds(0, rows, stride=2), :] = x
    scratch[pl.ds(1, rows, stride=2), :] = x
    return scratch[0 : 2 * rows, :]


def coarse_coefs(planes, scratch, lanes, period, start=0, count=None):
    both = pairs_of_lanes(lanes, period)
    alone = pairs_of_lanes(lanes, period, even=True)
    return (
        0.25 * pair_rows(mul(planes[0], both), scratch, start, count),
        0.25 * pair_rows(mul(planes[1], both), scratch, start, count, even=True),
        0.25 * pair_rows(mul(planes[2], alone), scratch, start, count),
    )


def spread_block(x, block, width):
    lane = iota(x.shape, 1)
    x = jnp.where(lane // width == block, x, 0.0)
    while width < 128:
        x = x + pltpu.roll(x, width, 1)
        width *= 2
    return x


def smooth_two(u1, below, above, f, g, c1, h1, c2, c3):
    near = gather_sum(below, u1, above, c1, h1, c2, c3)
    return (1.0 + KEEP) * u1 + GAIN * (g * (f + near) - u1)


def first_post(v, below, above, f, g, c1, h1, c2, c3):
    near = gather_sum(below, v, above, c1, h1, c2, c3)
    return v + (1.0 / THETA) * (g * (f + near) - v)


def second_post(u, v, below, above, f, g, c1, h1, c2, c3):
    near = gather_sum(below, u, above, c1, h1, c2, c3)
    return u + KEEP * (u - v) + GAIN * (g * (f + near) - u)


def call(kernel, outs, scratch=(), places=(), out_places=(), limit=4):
    places, out_places = dict(places), dict(out_places)

    def run(*args):
        in_specs = [pl.BlockSpec(memory_space=places.get(i, pltpu.VMEM)) for i in range(len(args))]
        return pl.pallas_call(
            kernel,
            out_shape=[jax.ShapeDtypeStruct(s, F32) for s in outs],
            in_specs=in_specs,
            out_specs=[pl.BlockSpec(memory_space=out_places.get(i, pltpu.VMEM)) for i in range(len(outs))],
            scratch_shapes=[pltpu.VMEM(s, F32) if isinstance(s, tuple) else s for s in scratch],
            compiler_params=pltpu.CompilerParams(vmem_limit_bytes=limit * 2**20),
        )(*args)

    return run


SCALARS = {0: pltpu.SMEM}


def two_blocks(x):
    half = x.shape[0] // 2
    return jnp.where(iota((half, 128), 1) < 64, x[:half], x[half:])


def start_kernel(f, c1, c2, c3, up, down, sems):
    copies = []
    for a, ref in enumerate((f, c1, c2, c3)):
        for k, (out, row) in enumerate(((up, 56), (down, 0))):
            copy = pltpu.make_async_copy(ref.at[:, pl.ds(row, 8), :], out.at[pl.ds(4 * a, 4)], sems.at[2 * a + k])
            copy.start()
            copies.append(copy)
    for copy in copies:
        copy.wait()


def pad_kernel(inner, low, high, own, coef1, up, down, scr):
    for a in range(16):
        own[a, 0:8] = low[a]
        own[a, 8:72] = inner[a]
        own[a, 72:80] = high[a]
    for p, out, slot in ((1, down, 5), (2, up, 4)):
        diag = diagonal(SIG[0], own[4 + p], own[5 + p], own[8 + p], own[12 + p])
        out[80 * slot : 80 * slot + 80] = own[p] / diag / THETA
    for a in range(4):
        up[80 * a : 80 * a + 80] = own[4 * a + 3]
        down[80 * a : 80 * a + 80] = own[4 * a]
    down[320:400] = own[5]
    k1 = jnp.concatenate([own[4], own[6]], axis=0)
    k2 = jnp.concatenate([own[8] + own[9], own[10] + own[11]], axis=0)
    k3 = jnp.concatenate([own[12] + own[13], own[14] + own[15]], axis=0)
    coarse = coarse_coefs((k1, k2, k3), scr, 256, 128)
    for a in range(3):
        for p in range(2):
            coef1[2 * a + p] = coarse[a][40 * p : 40 * p + 40]
    for out, at in ((up, 400), (down, 480)):
        for k in range(6):
            row, lane = at + 40 * (k // 2), 128 * (k % 2)
            out[row : row + 40, lane : lane + 128] = coef1[k]


def unpack(ref, at, index):
    row, lane = at + 40 * (index // 2), 128 * (index % 2)
    return ref[row : row + 40, lane : lane + 128]


CHUNK = 16


def chunked(rows, body):
    for r0 in range(0, rows, CHUNK):
        body(r0, rows)


def near_chunk(u, p, c1, c2, c3, q, r0, rows):
    here = pl.ds(r0, CHUNK)
    x = u[p, here, :]
    if r0 > 0:
        lower = u[p, pl.ds(r0 - 1, CHUNK), :]
    else:
        lower = roll(x, 1, 0)
    if r0 + CHUNK < rows:
        after = pl.ds(r0 + 1, CHUNK)
        upper = c2[q, after, :] * u[p, after, :]
    else:
        upper = roll(c2[q, here, :] * x, -1, 0)
    k3 = c3[q, here, :]
    first = c1[q, here, :] * u[p - 1, here, :] + c1[q + 1, here, :] * u[p + 1, here, :]
    second = c2[q, here, :] * lower + upper
    third = k3 * roll(x, 1, 1) + roll(k3 * x, -1, 1)
    return x, first + second + third


def diag_chunk(c1, c2, c3, q, r0, rows):
    here = pl.ds(r0, CHUNK)
    k2, k3 = c2[q, here, :], c3[q, here, :]
    if r0 + CHUNK < rows:
        h2 = c2[q, pl.ds(r0 + 1, CHUNK), :]
    else:
        h2 = roll(k2, -1, 0)
    return SIG[0] + c1[q, here, :] + c1[q + 1, here, :] + k2 + h2 + k3 + roll(k3, -1, 1)


def fine_pre_kernel(own, coef1, low, high, f, c1, c2, c3, g, u2, w1, msg_up, msg_down, f1, u1, res, scr):
    for a, ref in enumerate((f, c1, c2, c3)):
        ref[0] = low[80 * a : 80 * a + 80]
        ref[1:5] = own[4 * a : 4 * a + 4]
        ref[5] = high[80 * a : 80 * a + 80]
    c1[6] = high[320:400]
    u1[0] = low[320:400]
    u1[7] = high[400:480]

    def smooth_first(q, carry):
        def rows(r0, n):
            here = pl.ds(r0, CHUNK)
            inverse = 1.0 / diag_chunk(c1, c2, c3, q, r0, n)
            g[q, here, :] = inverse
            u1[q + 1, here, :] = f[q, here, :] * inverse * (1.0 / THETA)

        chunked(80, rows)
        return carry

    lax.fori_loop(0, 6, smooth_first, 0)

    def smooth_second(q, carry):
        def rows(r0, n):
            here = pl.ds(r0, CHUNK)
            x, near = near_chunk(u1, q + 1, c1, c2, c3, q, r0, n)
            u2[q + 1, here, :] = (1.0 + KEEP) * x + GAIN * (g[q, here, :] * (f[q, here, :] + near) - x)

        chunked(80, rows)
        return carry

    u2[0] = u1[0]
    u2[7] = u1[7]
    lax.fori_loop(0, 6, smooth_second, 0)

    def residual(q, carry):
        def rows(r0, n):
            here = pl.ds(r0, CHUNK)
            x, near = near_chunk(u2, q + 1, c1, c2, c3, q, r0, n)
            res[q - 1, here, :] = f[q, here, :] + near - diag_chunk(c1, c2, c3, q, r0, n) * x

        chunked(80, rows)
        return carry

    lax.fori_loop(1, 5, residual, 0)

    both = pairs_of_lanes(256, 128)
    sums = jnp.concatenate([res[0] + res[1], res[2] + res[3]], axis=0)
    coarse = 0.5 * pair_rows(mul(sums, both), scr)
    f1[0] = coarse[:40]
    f1[1] = coarse[40:]
    for a in range(3):
        for p in range(2):
            w1[6 * a + p] = unpack(low, 400, 2 * a + p)
            w1[6 * a + 2 + p] = coef1[2 * a + p]
            w1[6 * a + 4 + p] = unpack(high, 480, 2 * a + p)
    for p in range(2):
        k = p + 2
        inverse = 1.0 / diagonal(SIG[1], w1[k], w1[k + 1], w1[6 + k], w1[12 + k])
        for out in (msg_up, msg_down):
            out[p] = f1[p]
            out[2 + p] = inverse
    for out, plane in ((msg_up, 4), (msg_down, 3)):
        out[4] = u2[plane, 0:40, 0:128]
        out[5] = u2[plane, 0:40, 128:256]
        out[6] = u2[plane, 40:80, 0:128]
        out[7] = u2[plane, 40:80, 128:256]


def coarse_coef_kernel(w1, out, scr):
    k1 = jnp.concatenate([w1[2], w1[4]], axis=0)
    k2, k3 = w1[8] + w1[9], w1[14] + w1[15]
    both, alone = pairs_of_lanes(128, 64), pairs_of_lanes(128, 64, even=True)
    k1 = 0.25 * pair_rows(mul(k1, both), scr)
    k2 = 0.25 * pair_rows(mul(k2, both), scr, even=True)
    k3 = 0.25 * pair_rows(mul(k3, alone), scr)
    for k, x in enumerate((k1[2:18], k1[22:38], k2[2:18], k3[2:18])):
        out[8 * k : 8 * k + 8] = two_blocks(x)


def middle_pre_kernel(own, low, high, w1, coefs, f, g, u2, f2, up, down, u1, scr):
    for k, ref in enumerate((low, own, high)):
        f[2 * k : 2 * k + 2] = ref[0:2]
        g[2 * k : 2 * k + 2] = ref[2:4]
    for p in range(6):
        u1[p] = f[p] * g[p] * (1.0 / THETA)
    u2[0] = u1[0]
    u2[5] = u1[5]
    for p in range(1, 5):
        u2[p] = smooth_two(u1[p], u1[p - 1], u1[p + 1], f[p], g[p], w1[p], w1[p + 1], w1[6 + p], w1[12 + p])
    total = 0.0
    for p in (2, 3):
        k1, h1, k2, k3 = w1[p], w1[p + 1], w1[6 + p], w1[12 + p]
        near = gather_sum(u2[p - 1], u2[p], u2[p + 1], k1, h1, k2, k3)
        total = total + (f[p] + near - diagonal(SIG[1], k1, h1, k2, k3) * u2[p])
    coarse = 0.5 * pair_rows(mul(total, pairs_of_lanes(128, 64)), scr, 4, 16)
    f2[0:8] = two_blocks(coarse)
    f2[8:40] = coefs[...]
    for p in range(2):
        up[40 + 8 * p : 48 + 8 * p] = u2[2 + p, 28:36]
        down[40 + 8 * p : 48 + 8 * p] = u2[2 + p, 4:12]
    up[0:40] = f2[...]
    down[0:40] = f2[...]


def both_halves(x):
    return jnp.concatenate([spread_block(x, 0, 64), spread_block(x, 1, 64)], axis=0)


def coarse_start_kernel(place, f2, low, high, far, u2fine, own, msg):
    n = place[1]
    for piece, by in ((f2, 0), (high, 1), (far, 2), (low, 3)):
        at = pl.multiple_of(16 * lax.rem(n + by, 4), 16)
        for k in range(5):
            own[k, pl.ds(at, 16), :] = both_halves(piece[8 * k : 8 * k + 8])
    own[5] = 1.0 / diagonal(SIG[2], own[1], own[2], own[3], own[4])
    for k, plane in enumerate((0, 5, 1, 3, 4)):
        msg[32 * k : 32 * k + 32] = two_blocks(own[plane])
    for p in range(2):
        at = 160 + 40 * p
        msg[at : at + 40] = u2fine[2 + p]
        msg[at : at + 4] = low[44 + 8 * p : 48 + 8 * p]
        msg[at + 36 : at + 40] = high[40 + 8 * p : 44 + 8 * p]


def coarse_tiles_kernel(place, msg, sib, tiles, scr):
    odd = lax.rem(place[0], 2) == 1
    for a in range(3):
        here = slice(64 + 32 * a, 96 + 32 * a)
        x = jnp.where(odd, sib[here], msg[here]) if a == 0 else msg[here] + sib[here]
        scr[...] = 0.25 * mul(both_halves(x), pairs_of_lanes(128, 32, even=a == 2))
        tiles[a] = tile_of(scr, a == 1)


def tile_of(scr, even=False):
    block = iota((8, 128), 1) // 32
    packed = 0.0
    for q in range(4):
        part = scr[pl.ds(2 * q, 8, stride=8), :]
        if not even:
            part = part + scr[pl.ds(2 * q + 1, 8, stride=8), :]
        packed = jnp.where(block == q, part, packed)
    return packed


def coarse_swap_kernel(place, own, msg, sib, w1, out):
    out[0:160] = msg[0:160]
    out[160:192] = sib[0:32] * sib[32:64] * (1.0 / THETA)
    out[192:224] = two_blocks(own[2])
    out[224:304] = msg[160:240]
    par = lax.rem(place[0], 2)
    out[304:344] = sib[pl.ds(pl.multiple_of(160 + 40 * par, 8), 40), :]
    out[344:384] = w1[4]


def coarse_pre_kernel(place, own, sib, near, other, w, u2, late, u1):
    odd = lax.rem(place[0], 2) == 1

    def below(k):
        here = slice(32 * k, 32 * k + 32)
        return both_halves(jnp.where(odd, other[here], near[here]))

    def above(k):
        here = slice(32 * k, 32 * k + 32)
        return both_halves(jnp.where(odd, near[here], other[here]))

    for a, (base, plane) in enumerate(((0, 0), (4, 5), (8, 1), (13, 3), (17, 4))):
        mine, theirs = own[plane], both_halves(sib[32 * a : 32 * a + 32])
        w[base] = below(a)
        w[base + 1] = jnp.where(odd, theirs, mine)
        w[base + 2] = jnp.where(odd, mine, theirs)
        w[base + 3] = above(a)
    w[12] = above(6)
    u1[0] = below(5)
    u1[5] = above(5)
    for k in range(4):
        u1[k + 1] = w[k] * w[4 + k] * (1.0 / THETA)
    for k in range(4):
        u2[k] = smooth_two(u1[k + 1], u1[k], u1[k + 2], w[k], w[4 + k], w[8 + k], w[9 + k], w[13 + k], w[17 + k])
    late[...] = two_blocks(jnp.where(odd, u2[1], u2[2]))


def coarse_send_kernel(place, w, u2, tiles, send, scr):
    odd = lax.rem(place[0], 2) == 1
    total = 0.0
    for k in (1, 2):
        args = (w[8 + k], w[9 + k], w[13 + k], w[17 + k])
        near = gather_sum(u2[k - 1], u2[k], u2[k + 1], *args)
        total = total + (w[k] + near - diagonal(SIG[2], *args) * u2[k])
    scr[...] = 0.5 * mul(total, pairs_of_lanes(128, 32))
    first = jnp.where(odd, tiles[1], tile_of(scr))
    second = jnp.where(odd, tiles[2], tiles[0])
    for k in range(send.shape[0]):
        send[k, 0] = first
        send[k, 1] = second


def packed_sum(below, x, above, c1, h1, c2, c3, width, blocks):
    lane = iota(x.shape, 2)
    block, inner = lane // width % blocks, lane % width

    def second_down(x):
        x = pltpu.roll(x, width, 2)
        return jnp.where(block == 0, pltpu.roll(x, 1, 1), x)

    def second_up(x):
        x = pltpu.roll(x, 128 - width, 2)
        return jnp.where(block == blocks - 1, pltpu.roll(x, 7, 1), x)

    def third_down(x):
        return jnp.where(inner == 0, pltpu.roll(x, 129 - width, 2), pltpu.roll(x, 1, 2))

    def third_up(x):
        return jnp.where(inner == width - 1, pltpu.roll(x, width - 1, 2), pltpu.roll(x, 127, 2))

    first = c1 * below + h1 * above
    second = c2 * second_down(x) + second_up(c2 * x)
    third = c3 * third_down(x) + third_up(c3 * x)
    return first + second + third


def packed_diagonal(sig, c1, h1, c2, c3, width, blocks):
    lane = iota(c1.shape, 2)
    block, inner = lane // width % blocks, lane % width
    h2 = pltpu.roll(c2, 128 - width, 2)
    h2 = jnp.where(block == blocks - 1, pltpu.roll(h2, 7, 1), h2)
    h3 = jnp.where(inner == width - 1, pltpu.roll(c3, width - 1, 2), pltpu.roll(c3, 127, 2))
    return sig + c1 + h1 + c2 + h2 + c3 + h3


def fold_matrix(even2=False, even3=False):
    k, j = iota((128, 128), 0), iota((128, 128), 1)
    k2, k3, j2, j3 = k // 32, k % 32, j // 16 % 2, j % 16
    hit2 = k2 == 2 * j2 if even2 else k2 // 2 == j2
    hit3 = k3 == 2 * j3 if even3 else k3 // 2 == j3
    return (hit2 & hit3).astype(F32)


def wrap(ref, count):
    ref[0] = ref[count]
    ref[count + 1] = ref[1]


def around(j, n):
    return lax.rem(j + n, n)


STEP = 8
THREE, FOUR = (32, 4), (16, 2)


def bottom_kernel(place, mine, theirs, e2,
                  f3, c1, c2, c3, d3, g3, u1, u2, res, f4, d1, d2, e3, g4, ua, ub, st, scr):
    n3, n4 = f3.shape[0], f4.shape[0]

    def loop(body):
        def step(c, carry):
            body(pl.multiple_of(c * STEP, STEP))
            return carry

        lax.fori_loop(0, n3 // STEP, step, 0)

    odd = lax.rem(place[0], 2) == 1

    def load(j):
        here = pl.ds(j, STEP)
        a, b, c, d = mine[here, 0], mine[here, 1], theirs[here, 0], theirs[here, 1]
        f3[here] = jnp.where(odd, c, a)
        c1[here] = jnp.where(odd, d, b)
        c2[here] = jnp.where(odd, a, c)
        c3[here] = jnp.where(odd, b, d)

    loop(load)
    c1[n3] = c1[0]

    def start(j):
        here = pl.ds(j, STEP)
        diag = packed_diagonal(SIG[3], c1[here], c1[pl.ds(j + 1, STEP)], c2[here], c3[here], *THREE)
        inverse = 1.0 / diag
        d3[here] = diag
        g3[here] = inverse
        u1[pl.ds(j + 1, STEP)] = f3[here] * inverse * (1.0 / THETA)

    loop(start)
    wrap(u1, n3)

    def near3(u, j):
        here = pl.ds(j, STEP)
        x = u[pl.ds(j + 1, STEP)]
        args = (c1[here], c1[pl.ds(j + 1, STEP)], c2[here], c3[here])
        return here, x, packed_sum(u[here], x, u[pl.ds(j + 2, STEP)], *args, *THREE)

    def pre(j):
        here, x, near = near3(u1, j)
        u2[pl.ds(j + 1, STEP)] = (1.0 + KEEP) * x + GAIN * (g3[here] * (f3[here] + near) - x)

    loop(pre)
    wrap(u2, n3)

    def residual(j):
        here, x, near = near3(u2, j)
        left = (f3[here] + near - d3[here] * x).reshape(STEP // 2, 2, 8, 128)
        res[pl.ds(j // 2, STEP // 2)] = left[:, 0] + left[:, 1]

    loop(residual)

    def fold(x, *even):
        return mul(x.reshape(8 * n4, 128), fold_matrix(*even)).reshape(n4, 8, 128)

    def halves(ref):
        x = ref[0:n3].reshape(n4, 2, 8, 128)
        return x[:, 0], x[:, 1]

    f4[...] = 0.5 * fold(res[...])
    d1[0:n4] = 0.25 * fold(halves(c1)[0])
    d1[n4] = d1[0]
    d2[...] = 0.25 * fold(sum(halves(c2)), True, False)
    e3[...] = 0.25 * fold(sum(halves(c3)), False, True)
    coefs4 = (d1[0:n4], d1[1 : n4 + 1], d2[...], e3[...])
    g4[...] = 1.0 / packed_diagonal(SIG[4], *coefs4, *FOUR)
    x = f4[...] * g4[...] * (1.0 / THETA)
    ua[1 : n4 + 1] = x
    wrap(ua, n4)
    st[...] = x
    src, dst = ua, ub
    for keep, gain in factors(4):
        x = src[1 : n4 + 1]
        near = packed_sum(src[0:n4], x, src[2 : n4 + 2], d1[0:n4], d1[1 : n4 + 1], d2[...], e3[...], *FOUR)
        step = keep * st[...] + gain * (g4[...] * (f4[...] + near) - x)
        st[...] = step
        dst[1 : n4 + 1] = x + step
        wrap(dst, n4)
        src, dst = dst, src

    j0 = around(place[0] // 2 - 1, n3)
    k, j = iota((128, 128), 0), iota((128, 128), 1)
    unfold = (k == 16 * (j // 64) + j % 32 // 2).astype(F32)
    coarse = jnp.concatenate([src[1 + around(around(j0 - 2, n3) // 2 + m, n4)] for m in range(4)], axis=0)
    scr[0:32] = mul(coarse, unfold)
    shifted = lax.rem(around(j0 - 2, n3), 2)
    js = [around(j0 - 2 + m, n3) for m in range(7)]
    v = [u2[1 + js[m]] + scr[pl.ds(pl.multiple_of(8 * ((shifted + m) // 2), 8), 8), :] for m in range(7)]
    v = jnp.stack(v)

    def window(ref, first, count, by=0):
        return jnp.stack([ref[js[m] + by] for m in range(first, first + count)])

    def args(first, count):
        return window(c1, first, count), window(c1, first, count, 1), window(c2, first, count), window(c3, first, count)

    f, g = window(f3, 1, 5), window(g3, 1, 5)
    near = packed_sum(v[0:5], v[1:6], v[2:7], *args(1, 5), *THREE)
    w = v[1:6] + (1.0 / THETA) * (g * (f + near) - v[1:6])
    near = packed_sum(w[0:3], w[1:4], w[2:5], *args(2, 3), *THREE)
    x = w[1:4] + KEEP * (w[1:4] - v[2:5]) + GAIN * (g[1:4] * (f[1:4] + near) - w[1:4])
    x = x.reshape(24, 128)
    for q in range(4):
        fine = mul(x, (k == 32 * q + j % 64 // 2).astype(F32))
        e2[pl.ds(2 * q, 24, stride=8), :] = fine
        e2[pl.ds(2 * q + 1, 24, stride=8), :] = fine


def coarse_post_kernel(place, e2, win, u2, late, out):
    par = lax.rem(place[0], 2)
    odd = par == 1
    late = both_halves(late[...])
    v = [jnp.where(odd, u2[0], late), u2[par], u2[1 + par], u2[2 + par], jnp.where(odd, late, u2[3])]
    v = [v[m] + e2[pl.ds(pl.multiple_of(64 * ((m + par) // 2), 64), 64), :] for m in range(5)]

    def args(m):
        k = m + par
        return win[k], win[4 + k], win[8 + k], win[9 + k], win[13 + k], win[17 + k]

    w = [first_post(v[m + 1], v[m], v[m + 2], *args(m)) for m in range(3)]
    out[...] = second_post(w[1], v[2], w[0], w[2], *args(1))


def middle_post_kernel(place, e2, e2sib, near0, near1, msg, sib, near, f, g, w1, own, edge, send, fine, c1, v, w):
    n, par = place[1], lax.rem(place[0], 2)
    odd = par == 1
    row, col = iota((40, 64), 0), iota((40, 64), 1)
    pick = (col == lax.rem(16 * n + (row + 4) // 2 + 60, 64)).astype(F32)
    lanes = copies_of_lanes(128, 128)
    e2, e2sib, near0, near1 = e2[...], e2sib[...], near0[...], near1[...]
    for k, (upper, lower) in enumerate(((e2sib, near1), (e2, near0), (near0, e2), (near1, e2sib))):
        fine[k] = mul(mul_left(pick, jnp.where(odd, upper, lower)), lanes)
    c1[0:6] = w1[0:6]
    c1[6] = near[344:384]
    ours = [msg[160 + 40 * p : 200 + 40 * p] for p in range(2)]
    sibs = [sib[160 + 40 * p : 200 + 40 * p] for p in range(2)]
    next_chip = [near[224 + 40 * p : 264 + 40 * p] for p in range(3)]
    upper = sibs + ours + next_chip
    lower = [next_chip[2]] + next_chip[:2] + ours + sibs
    for i in range(7):
        v[i] = jnp.where(odd, upper[i], lower[i]) + fine[(i + 1 - par) // 2]

    def args(i):
        k = i - 1 + par
        return f[k], g[k], c1[k], c1[k + 1], w1[6 + k], w1[12 + k]

    for i in range(1, 6):
        w[i] = first_post(v[i], v[i - 1], v[i + 1], *args(i))
    out = [second_post(w[i], v[i], w[i - 1], w[i + 1], *args(i)) for i in (2, 3, 4)]
    own[0] = jnp.where(odd, out[0], out[1])
    own[1] = jnp.where(odd, out[1], out[2])
    edge[...] = jnp.where(odd, out[2], out[0])
    send[...] = jnp.where(odd, out[0], out[2])


def fine_post_kernel(place, e1, edge, other, low, high, f, c1, c2, c3, g, u2, out, v, w, scr):
    odd = lax.rem(place[0], 2) == 1
    below, above = jnp.where(odd, other[...], edge[...]), jnp.where(odd, edge[...], other[...])
    x = jnp.concatenate([below, e1[0], e1[1], above], axis=0)
    for half in range(2):
        here = slice(128 * half, 128 * half + 128)
        row, col = iota((128, 128), 0), iota((128, 128), 1)
        fine = mul(x, (row == 64 * half + col // 2).astype(F32))
        scr[pl.ds(0, 160, stride=2), :] = fine
        scr[pl.ds(1, 160, stride=2), :] = fine
        for k, ref in ((0, low), (7, high)):
            at = 80 * (k // 2)
            v[k, 0:40, here] = ref[4 + half] + scr[at : at + 40, :]
            v[k, 40:80, here] = ref[6 + half] + scr[at + 40 : at + 80, :]
        for k in range(1, 7):
            at = 80 * (k // 2)
            v[k, :, here] = u2[k, :, here] + scr[at : at + 80, :]

    def post1(q, carry):
        def chunk(r0, n):
            here = pl.ds(r0, CHUNK)
            x, near = near_chunk(v, q + 1, c1, c2, c3, q, r0, n)
            w[q + 1, here, :] = x + (1.0 / THETA) * (g[q, here, :] * (f[q, here, :] + near) - x)

        chunked(80, chunk)
        return carry

    lax.fori_loop(0, 6, post1, 0)

    def post2(q, carry):
        for r0 in range(8, 72, CHUNK):
            here = pl.ds(r0, CHUNK)
            x, near = near_chunk(w, q + 1, c1, c2, c3, q, r0, 80)
            step = KEEP * (x - v[q + 1, here, :]) + GAIN * (g[q, here, :] * (f[q, here, :] + near) - x)
            out[q - 1, pl.ds(r0 - 8, CHUNK), :] = x + step
        return carry

    lax.fori_loop(1, 5, post2, 0)


def shift(x, axis, by):
    count = lax.axis_size(axis)
    return lax.ppermute(x, axis, [(i, (i + by) % count) for i in range(count)])


def sibling(x):
    return lax.ppermute(x, "wide", [(i, i ^ 1) for i in range(lax.axis_size("wide"))])


def across(x):
    count = lax.axis_size("wide")
    return lax.ppermute(x, "wide", [(i, (i + 1 if i % 2 else i - 1) % count) for i in range(count)])


def body(source, coef_first, coef_second, coef_third):
    wide = lax.axis_size("wide")
    n3, n4 = wide // 2, wide // 4
    place = jnp.stack([lax.axis_index("wide"), lax.axis_index("narrow")]).astype(jnp.int32)
    big = (80, 256)
    inputs = (source, coef_first, coef_second, coef_third)

    up, down = call(
        start_kernel,
        [(16, 8, 256), (16, 8, 256)],
        [pltpu.SemaphoreType.DMA((8,))],
        {k: pltpu.HBM for k in range(4)},
        limit=60,
    )(*inputs)
    low, high = shift(up, "narrow", 1), shift(down, "narrow", -1)

    own, coef1, up, down = call(
        pad_kernel, [(16,) + big, (6, 40, 128), (520, 256), (600, 256)], [(160, 128)]
    )(jnp.concatenate(inputs, axis=0), low, high)
    low, high = shift(up, "wide", 1), shift(down, "wide", -1)

    f, c1, c2, c3, g, u2, w1, up, down, f1 = call(
        fine_pre_kernel,
        [(6,) + big, (7,) + big, (6,) + big, (6,) + big, (6,) + big, (8,) + big]
        + [(18, 40, 128), (8, 40, 128), (8, 40, 128), (2, 40, 128)],
        [(8,) + big, (4,) + big, (160, 128)],
    )(own, coef1, low, high)
    low1, high1 = shift(up, "wide", 1), shift(down, "wide", -1)
    (coefs,) = call(coarse_coef_kernel, [(32, 128)], [(80, 128)])(w1)

    six = (6, 40, 128)
    f1w, g1w, u2m, f2, up, down = call(
        middle_pre_kernel, [six, six, six, (40, 128), (56, 128), (56, 128)], [six, (40, 128)]
    )(up, low1, high1, w1, coefs)
    low, high, far = shift(up, "narrow", 1), shift(down, "narrow", -1), shift(f2, "narrow", 2)

    own2, msg = call(coarse_start_kernel, [(6, 64, 128), (240, 128)], (), SCALARS)(place, f2, low, high, far, u2m)
    sib = sibling(msg)
    (swap,) = call(coarse_swap_kernel, [(384, 128)], (), SCALARS)(place, own2, msg, sib, w1)
    near = across(swap)
    (tiles,) = call(coarse_tiles_kernel, [(3, 8, 128)], [(64, 128)], SCALARS)(place, msg, sib)
    other = sibling(near)
    w2, u2w, late = call(
        coarse_pre_kernel, [(21, 64, 128), (4, 64, 128), (32, 128)], [(6, 64, 128)], SCALARS
    )(place, own2, sib, near, other)
    (send,) = call(coarse_send_kernel, [(n3, 2, 8, 128)], [(64, 128)], SCALARS)(place, w2, u2w, tiles)
    cores = [[k for k in range(wide) if k % 2 == c] for c in range(2)]
    parts = lax.all_to_all(send, "wide", split_axis=0, concat_axis=0, tiled=True, axis_index_groups=cores)
    theirs, late = sibling(parts), across(late)

    three, four = (n3, 8, 128), (n4, 8, 128)
    (fine2,) = call(
        bottom_kernel,
        [(192, 128)],
        [three, (n3 + 1, 8, 128), three, three, three, three, (n3 + 2, 8, 128), (n3 + 2, 8, 128), four, four]
        + [(n4 + 1, 8, 128), four, four, four, (n4 + 2, 8, 128), (n4 + 2, 8, 128), four, (32, 128)],
        SCALARS,
    )(place, parts, theirs)
    (e2,) = call(coarse_post_kernel, [(64, 128)], (), SCALARS)(place, fine2, w2, u2w, late)
    near0, e2sib = across(e2), sibling(e2)
    near1 = across(e2sib)

    e1, edge, send = call(
        middle_post_kernel,
        [(2, 40, 128), (40, 128), (40, 128)],
        [(4, 40, 128), (7, 40, 128), (7, 40, 128), (7, 40, 128)],
        SCALARS,
    )(place, e2, e2sib, near0, near1, msg, sib, near, f1w, g1w, w1)
    other1 = sibling(send)

    (out,) = call(
        fine_post_kernel, [(4, 64, 256)], [(8,) + big, (8,) + big, (320, 128)], SCALARS
    )(place, e1, edge, other1, low1, high1, f, c1, c2, c3, g, u2)
    return out


def solution(mesh):
    spec = P("wide", "narrow", None)
    return jax.shard_map(body, mesh=mesh, in_specs=(spec,) * 4, out_specs=spec, check_vma=False)
```

```python
import functools

import jax
import jax.numpy as jnp
from jax import lax
from jax.experimental import pallas as pl
from jax.experimental.pallas import tpu as pltpu
from jax.sharding import PartitionSpec as P

THETA = 1.125
DELTA = 0.875
RATIO = THETA / DELTA
SIG = [0.0002 * 4.0**level for level in range(5)]
F32 = jnp.float32


def factors(degree):
    rho, out = 1.0 / RATIO, []
    for _ in range(degree - 1):
        new = 1.0 / (2.0 * RATIO - rho)
        out.append((new * rho, 2.0 * new / DELTA))
        rho = new
    return out


(KEEP, GAIN), = factors(2)


def roll(x, by, axis):
    return pltpu.roll(x, by % x.shape[axis], axis)


def gather_sum(below, here, above, c1, h1, c2, c3):
    first = c1 * below + h1 * above
    second = c2 * roll(here, 1, 0) + roll(c2 * here, -1, 0)
    third = c3 * roll(here, 1, 1) + roll(c3 * here, -1, 1)
    return first + second + third


def diagonal(sig, c1, h1, c2, c3):
    return sig + c1 + h1 + c2 + roll(c2, -1, 0) + c3 + roll(c3, -1, 1)


def iota(shape, dim):
    return lax.broadcasted_iota(jnp.int32, shape, dim)


def pairs_of_lanes(lanes, period, even=False):
    row, col = iota((lanes, 128), 0), iota((lanes, 128), 1) % period
    hit = row == 2 * col if even else row // 2 == col
    return hit.astype(F32)


def copies_of_lanes(lanes_in, lanes_out):
    row, col = iota((lanes_in, lanes_out), 0), iota((lanes_in, lanes_out), 1)
    return (row == col // 2).astype(F32)


def pieces(x):
    out = []
    for _ in range(3):
        part = x.astype(jnp.bfloat16)
        out.append(part)
        x = x - part.astype(F32)
    return out


def mul(x, ones):
    ones = ones.astype(jnp.bfloat16)
    high, mid, low = [jnp.dot(part, ones, preferred_element_type=F32) for part in pieces(x)]
    return high + (mid + low)


def mul_left(ones, x):
    ones = ones.astype(jnp.bfloat16)
    high, mid, low = [jnp.dot(ones, part, preferred_element_type=F32) for part in pieces(x)]
    return high + (mid + low)


def pair_rows(x, scratch, start=0, count=None, even=False):
    rows = x.shape[0]
    count = rows // 2 if count is None else count
    scratch[0:rows, :] = x
    first = scratch[pl.ds(start, count, stride=2), :]
    if even:
        return first
    return first + scratch[pl.ds(start + 1, count, stride=2), :]


def twice_rows(x, scratch):
    rows = x.shape[0]
    scratch[pl.ds(0, rows, stride=2), :] = x
    scratch[pl.ds(1, rows, stride=2), :] = x
    return scratch[0 : 2 * rows, :]


def coarse_coefs(planes, scratch, lanes, period, start=0, count=None):
    both = pairs_of_lanes(lanes, period)
    alone = pairs_of_lanes(lanes, period, even=True)
    return (
        0.25 * pair_rows(mul(planes[0], both), scratch, start, count),
        0.25 * pair_rows(mul(planes[1], both), scratch, start, count, even=True),
        0.25 * pair_rows(mul(planes[2], alone), scratch, start, count),
    )


def spread_block(x, block, width):
    lane = iota(x.shape, 1)
    x = jnp.where(lane // width == block, x, 0.0)
    while width < 128:
        x = x + pltpu.roll(x, width, 1)
        width *= 2
    return x


def smooth_two(u1, below, above, f, g, c1, h1, c2, c3):
    near = gather_sum(below, u1, above, c1, h1, c2, c3)
    return (1.0 + KEEP) * u1 + GAIN * (g * (f + near) - u1)


def first_post(v, below, above, f, g, c1, h1, c2, c3):
    near = gather_sum(below, v, above, c1, h1, c2, c3)
    return v + (1.0 / THETA) * (g * (f + near) - v)


def second_post(u, v, below, above, f, g, c1, h1, c2, c3):
    near = gather_sum(below, u, above, c1, h1, c2, c3)
    return u + KEEP * (u - v) + GAIN * (g * (f + near) - u)


def call(kernel, outs, scratch=(), places=(), out_places=(), limit=4):
    places, out_places = dict(places), dict(out_places)

    def run(*args):
        in_specs = [pl.BlockSpec(memory_space=places.get(i, pltpu.VMEM)) for i in range(len(args))]
        return pl.pallas_call(
            kernel,
            out_shape=[jax.ShapeDtypeStruct(s, F32) for s in outs],
            in_specs=in_specs,
            out_specs=[pl.BlockSpec(memory_space=out_places.get(i, pltpu.VMEM)) for i in range(len(outs))],
            scratch_shapes=[pltpu.VMEM(s, F32) if isinstance(s, tuple) else s for s in scratch],
            compiler_params=pltpu.CompilerParams(vmem_limit_bytes=limit * 2**20),
        )(*args)

    return run


def two_blocks(x):
    half = x.shape[0] // 2
    return jnp.where(iota((half, 128), 1) < 64, x[:half], x[half:])


def start_kernel(f, c1, c2, c3, up, down, sems):
    copies = []
    for a, ref in enumerate((f, c1, c2, c3)):
        for k, (out, row) in enumerate(((up, 56), (down, 0))):
            copy = pltpu.make_async_copy(ref.at[:, pl.ds(row, 8), :], out.at[pl.ds(4 * a, 4)], sems.at[2 * a + k])
            copy.start()
            copies.append(copy)
    for copy in copies:
        copy.wait()


def pad_kernel(inner, low, high, own, coef1, up, down, scr):
    for a in range(16):
        own[a, 0:8] = low[a]
        own[a, 8:72] = inner[a]
        own[a, 72:80] = high[a]
    for p, out, slot in ((1, down, 5), (2, up, 4)):
        diag = diagonal(SIG[0], own[4 + p], own[5 + p], own[8 + p], own[12 + p])
        out[80 * slot : 80 * slot + 80] = own[p] / diag / THETA
    for a in range(4):
        up[80 * a : 80 * a + 80] = own[4 * a + 3]
        down[80 * a : 80 * a + 80] = own[4 * a]
    down[320:400] = own[5]
    k1 = jnp.concatenate([own[4], own[6]], axis=0)
    k2 = jnp.concatenate([own[8] + own[9], own[10] + own[11]], axis=0)
    k3 = jnp.concatenate([own[12] + own[13], own[14] + own[15]], axis=0)
    coarse = coarse_coefs((k1, k2, k3), scr, 256, 128)
    for a in range(3):
        for p in range(2):
            coef1[2 * a + p] = coarse[a][40 * p : 40 * p + 40]
    for out, at in ((up, 400), (down, 480)):
        for k in range(6):
            row, lane = at + 40 * (k // 2), 128 * (k % 2)
            out[row : row + 40, lane : lane + 128] = coef1[k]


def unpack(ref, at, index):
    row, lane = at + 40 * (index // 2), 128 * (index % 2)
    return ref[row : row + 40, lane : lane + 128]


CHUNK = 16


def chunked(rows, body):
    for r0 in range(0, rows, CHUNK):
        body(r0, rows)


def near_chunk(u, p, c1, c2, c3, q, r0, rows):
    here = pl.ds(r0, CHUNK)
    x = u[p, here, :]
    if r0 > 0:
        lower = u[p, pl.ds(r0 - 1, CHUNK), :]
    else:
        lower = roll(x, 1, 0)
    if r0 + CHUNK < rows:
        after = pl.ds(r0 + 1, CHUNK)
        upper = c2[q, after, :] * u[p, after, :]
    else:
        upper = roll(c2[q, here, :] * x, -1, 0)
    k3 = c3[q, here, :]
    first = c1[q, here, :] * u[p - 1, here, :] + c1[q + 1, here, :] * u[p + 1, here, :]
    second = c2[q, here, :] * lower + upper
    third = k3 * roll(x, 1, 1) + roll(k3 * x, -1, 1)
    return x, first + second + third


def diag_chunk(c1, c2, c3, q, r0, rows):
    here = pl.ds(r0, CHUNK)
    k2, k3 = c2[q, here, :], c3[q, here, :]
    if r0 + CHUNK < rows:
        h2 = c2[q, pl.ds(r0 + 1, CHUNK), :]
    else:
        h2 = roll(k2, -1, 0)
    return SIG[0] + c1[q, here, :] + c1[q + 1, here, :] + k2 + h2 + k3 + roll(k3, -1, 1)


def fine_pre_kernel(own, coef1, low, high, f, c1, c2, c3, g, u2, w1, msg_up, msg_down, f1, u1, res, scr):
    for a, ref in enumerate((f, c1, c2, c3)):
        ref[0] = low[80 * a : 80 * a + 80]
        ref[1:5] = own[4 * a : 4 * a + 4]
        ref[5] = high[80 * a : 80 * a + 80]
    c1[6] = high[320:400]
    u1[0] = low[320:400]
    u1[7] = high[400:480]

    def smooth_first(q, carry):
        def rows(r0, n):
            here = pl.ds(r0, CHUNK)
            inverse = 1.0 / diag_chunk(c1, c2, c3, q, r0, n)
            g[q, here, :] = inverse
            u1[q + 1, here, :] = f[q, here, :] * inverse * (1.0 / THETA)

        chunked(80, rows)
        return carry

    lax.fori_loop(0, 6, smooth_first, 0)

    def smooth_second(q, carry):
        def rows(r0, n):
            here = pl.ds(r0, CHUNK)
            x, near = near_chunk(u1, q + 1, c1, c2, c3, q, r0, n)
            u2[q + 1, here, :] = (1.0 + KEEP) * x + GAIN * (g[q, here, :] * (f[q, here, :] + near) - x)

        chunked(80, rows)
        return carry

    u2[0] = u1[0]
    u2[7] = u1[7]
    lax.fori_loop(0, 6, smooth_second, 0)

    def residual(q, carry):
        def rows(r0, n):
            here = pl.ds(r0, CHUNK)
            x, near = near_chunk(u2, q + 1, c1, c2, c3, q, r0, n)
            res[q - 1, here, :] = f[q, here, :] + near - diag_chunk(c1, c2, c3, q, r0, n) * x

        chunked(80, rows)
        return carry

    lax.fori_loop(1, 5, residual, 0)

    both = pairs_of_lanes(256, 128)
    sums = jnp.concatenate([res[0] + res[1], res[2] + res[3]], axis=0)
    coarse = 0.5 * pair_rows(mul(sums, both), scr)
    f1[0] = coarse[:40]
    f1[1] = coarse[40:]
    for a in range(3):
        for p in range(2):
            w1[6 * a + p] = unpack(low, 400, 2 * a + p)
            w1[6 * a + 2 + p] = coef1[2 * a + p]
            w1[6 * a + 4 + p] = unpack(high, 480, 2 * a + p)
    for p in range(2):
        k = p + 2
        inverse = 1.0 / diagonal(SIG[1], w1[k], w1[k + 1], w1[6 + k], w1[12 + k])
        for out in (msg_up, msg_down):
            out[p] = f1[p]
            out[2 + p] = inverse
    for out, plane in ((msg_up, 4), (msg_down, 3)):
        out[4] = u2[plane, 0:40, 0:128]
        out[5] = u2[plane, 0:40, 128:256]
        out[6] = u2[plane, 40:80, 0:128]
        out[7] = u2[plane, 40:80, 128:256]


def coarse_coef_kernel(w1, out, scr):
    k1 = jnp.concatenate([w1[2], w1[4]], axis=0)
    k2, k3 = w1[8] + w1[9], w1[14] + w1[15]
    both, alone = pairs_of_lanes(128, 64), pairs_of_lanes(128, 64, even=True)
    k1 = 0.25 * pair_rows(mul(k1, both), scr)
    k2 = 0.25 * pair_rows(mul(k2, both), scr, even=True)
    k3 = 0.25 * pair_rows(mul(k3, alone), scr)
    for k, x in enumerate((k1[2:18], k1[22:38], k2[2:18], k3[2:18])):
        out[8 * k : 8 * k + 8] = two_blocks(x)


def middle_pre_kernel(own, low, high, w1, coefs, f, g, u2, f2, up, down, u1, scr):
    for k, ref in enumerate((low, own, high)):
        f[2 * k : 2 * k + 2] = ref[0:2]
        g[2 * k : 2 * k + 2] = ref[2:4]
    for p in range(6):
        u1[p] = f[p] * g[p] * (1.0 / THETA)
    u2[0] = u1[0]
    u2[5] = u1[5]
    for p in range(1, 5):
        u2[p] = smooth_two(u1[p], u1[p - 1], u1[p + 1], f[p], g[p], w1[p], w1[p + 1], w1[6 + p], w1[12 + p])
    total = 0.0
    for p in (2, 3):
        k1, h1, k2, k3 = w1[p], w1[p + 1], w1[6 + p], w1[12 + p]
        near = gather_sum(u2[p - 1], u2[p], u2[p + 1], k1, h1, k2, k3)
        total = total + (f[p] + near - diagonal(SIG[1], k1, h1, k2, k3) * u2[p])
    coarse = 0.5 * pair_rows(mul(total, pairs_of_lanes(128, 64)), scr, 4, 16)
    f2[0:8] = two_blocks(coarse)
    f2[8:40] = coefs[...]
    for p in range(2):
        up[40 + 8 * p : 48 + 8 * p] = u2[2 + p, 28:36]
        down[40 + 8 * p : 48 + 8 * p] = u2[2 + p, 4:12]
    up[0:40] = f2[...]
    down[0:40] = f2[...]


def both_halves(x):
    return jnp.concatenate([spread_block(x, 0, 64), spread_block(x, 1, 64)], axis=0)


def coarse_start_kernel(f2, low, high, far, u2fine, own, msg):
    n = lax.axis_index("narrow")
    for piece, by in ((f2, 0), (high, 1), (far, 2), (low, 3)):
        at = pl.multiple_of(16 * lax.rem(n + by, 4), 16)
        for k in range(5):
            own[k, pl.ds(at, 16), :] = both_halves(piece[8 * k : 8 * k + 8])
    own[5] = 1.0 / diagonal(SIG[2], own[1], own[2], own[3], own[4])
    for k, plane in enumerate((0, 5, 1, 3, 4)):
        msg[32 * k : 32 * k + 32] = two_blocks(own[plane])
    for p in range(2):
        at = 160 + 40 * p
        msg[at : at + 40] = u2fine[2 + p]
        msg[at : at + 4] = low[44 + 8 * p : 48 + 8 * p]
        msg[at + 36 : at + 40] = high[40 + 8 * p : 44 + 8 * p]


def coarse_tiles_kernel(msg, sib, tiles, scr):
    odd = lax.rem(lax.axis_index("wide"), 2) == 1
    for a in range(3):
        here = slice(64 + 32 * a, 96 + 32 * a)
        x = jnp.where(odd, sib[here], msg[here]) if a == 0 else msg[here] + sib[here]
        scr[...] = 0.25 * mul(both_halves(x), pairs_of_lanes(128, 32, even=a == 2))
        tiles[a] = tile_of(scr, a == 1)


def tile_of(scr, even=False):
    block = iota((8, 128), 1) // 32
    packed = 0.0
    for q in range(4):
        part = scr[pl.ds(2 * q, 8, stride=8), :]
        if not even:
            part = part + scr[pl.ds(2 * q + 1, 8, stride=8), :]
        packed = jnp.where(block == q, part, packed)
    return packed


def coarse_swap_kernel(own, msg, sib, w1, out):
    out[0:160] = msg[0:160]
    out[160:192] = sib[0:32] * sib[32:64] * (1.0 / THETA)
    out[192:224] = two_blocks(own[2])
    out[224:304] = msg[160:240]
    par = lax.rem(lax.axis_index("wide"), 2)
    out[304:344] = sib[pl.ds(pl.multiple_of(160 + 40 * par, 8), 40), :]
    out[344:384] = w1[4]


def coarse_pre_kernel(own, sib, near, other, w, u2, late, u1):
    odd = lax.rem(lax.axis_index("wide"), 2) == 1

    def below(k):
        here = slice(32 * k, 32 * k + 32)
        return both_halves(jnp.where(odd, other[here], near[here]))

    def above(k):
        here = slice(32 * k, 32 * k + 32)
        return both_halves(jnp.where(odd, near[here], other[here]))

    for a, (base, plane) in enumerate(((0, 0), (4, 5), (8, 1), (13, 3), (17, 4))):
        mine, theirs = own[plane], both_halves(sib[32 * a : 32 * a + 32])
        w[base] = below(a)
        w[base + 1] = jnp.where(odd, theirs, mine)
        w[base + 2] = jnp.where(odd, mine, theirs)
        w[base + 3] = above(a)
    w[12] = above(6)
    u1[0] = below(5)
    u1[5] = above(5)
    for k in range(4):
        u1[k + 1] = w[k] * w[4 + k] * (1.0 / THETA)
    for k in range(4):
        u2[k] = smooth_two(u1[k + 1], u1[k], u1[k + 2], w[k], w[4 + k], w[8 + k], w[9 + k], w[13 + k], w[17 + k])
    late[...] = two_blocks(jnp.where(odd, u2[1], u2[2]))


def coarse_send_kernel(w, u2, tiles, send, scr):
    odd = lax.rem(lax.axis_index("wide"), 2) == 1
    total = 0.0
    for k in (1, 2):
        args = (w[8 + k], w[9 + k], w[13 + k], w[17 + k])
        near = gather_sum(u2[k - 1], u2[k], u2[k + 1], *args)
        total = total + (w[k] + near - diagonal(SIG[2], *args) * u2[k])
    scr[...] = 0.5 * mul(total, pairs_of_lanes(128, 32))
    first = jnp.where(odd, tiles[1], tile_of(scr))
    second = jnp.where(odd, tiles[2], tiles[0])
    for k in range(send.shape[0]):
        send[k, 0] = first
        send[k, 1] = second


def packed_sum(below, x, above, c1, h1, c2, c3, width, blocks):
    lane = iota(x.shape, 2)
    block, inner = lane // width % blocks, lane % width

    def second_down(x):
        x = pltpu.roll(x, width, 2)
        return jnp.where(block == 0, pltpu.roll(x, 1, 1), x)

    def second_up(x):
        x = pltpu.roll(x, 128 - width, 2)
        return jnp.where(block == blocks - 1, pltpu.roll(x, 7, 1), x)

    def third_down(x):
        return jnp.where(inner == 0, pltpu.roll(x, 129 - width, 2), pltpu.roll(x, 1, 2))

    def third_up(x):
        return jnp.where(inner == width - 1, pltpu.roll(x, width - 1, 2), pltpu.roll(x, 127, 2))

    first = c1 * below + h1 * above
    second = c2 * second_down(x) + second_up(c2 * x)
    third = c3 * third_down(x) + third_up(c3 * x)
    return first + second + third


def packed_diagonal(sig, c1, h1, c2, c3, width, blocks):
    lane = iota(c1.shape, 2)
    block, inner = lane // width % blocks, lane % width
    h2 = pltpu.roll(c2, 128 - width, 2)
    h2 = jnp.where(block == blocks - 1, pltpu.roll(h2, 7, 1), h2)
    h3 = jnp.where(inner == width - 1, pltpu.roll(c3, width - 1, 2), pltpu.roll(c3, 127, 2))
    return sig + c1 + h1 + c2 + h2 + c3 + h3


def fold_matrix(even2=False, even3=False):
    k, j = iota((128, 128), 0), iota((128, 128), 1)
    k2, k3, j2, j3 = k // 32, k % 32, j // 16 % 2, j % 16
    hit2 = k2 == 2 * j2 if even2 else k2 // 2 == j2
    hit3 = k3 == 2 * j3 if even3 else k3 // 2 == j3
    return (hit2 & hit3).astype(F32)


def wrap(ref, count):
    ref[0] = ref[count]
    ref[count + 1] = ref[1]


def around(j, n):
    return lax.rem(j + n, n)


STEP = 8
THREE, FOUR = (32, 4), (16, 2)


def bottom_kernel(mine, theirs, e2,
                  f3, c1, c2, c3, d3, g3, u1, u2, res, f4, d1, d2, e3, g4, ua, ub, st, scr):
    n3, n4 = f3.shape[0], f4.shape[0]

    def loop(body):
        def step(c, carry):
            body(pl.multiple_of(c * STEP, STEP))
            return carry

        lax.fori_loop(0, n3 // STEP, step, 0)

    odd = lax.rem(lax.axis_index("wide"), 2) == 1

    def load(j):
        here = pl.ds(j, STEP)
        a, b, c, d = mine[here, 0], mine[here, 1], theirs[here, 0], theirs[here, 1]
        f3[here] = jnp.where(odd, c, a)
        c1[here] = jnp.where(odd, d, b)
        c2[here] = jnp.where(odd, a, c)
        c3[here] = jnp.where(odd, b, d)

    loop(load)
    c1[n3] = c1[0]

    def start(j):
        here = pl.ds(j, STEP)
        diag = packed_diagonal(SIG[3], c1[here], c1[pl.ds(j + 1, STEP)], c2[here], c3[here], *THREE)
        inverse = 1.0 / diag
        d3[here] = diag
        g3[here] = inverse
        u1[pl.ds(j + 1, STEP)] = f3[here] * inverse * (1.0 / THETA)

    loop(start)
    wrap(u1, n3)

    def near3(u, j):
        here = pl.ds(j, STEP)
        x = u[pl.ds(j + 1, STEP)]
        args = (c1[here], c1[pl.ds(j + 1, STEP)], c2[here], c3[here])
        return here, x, packed_sum(u[here], x, u[pl.ds(j + 2, STEP)], *args, *THREE)

    def pre(j):
        here, x, near = near3(u1, j)
        u2[pl.ds(j + 1, STEP)] = (1.0 + KEEP) * x + GAIN * (g3[here] * (f3[here] + near) - x)

    loop(pre)
    wrap(u2, n3)

    def residual(j):
        here, x, near = near3(u2, j)
        left = (f3[here] + near - d3[here] * x).reshape(STEP // 2, 2, 8, 128)
        res[pl.ds(j // 2, STEP // 2)] = left[:, 0] + left[:, 1]

    loop(residual)

    def fold(x, *even):
        return mul(x.reshape(8 * n4, 128), fold_matrix(*even)).reshape(n4, 8, 128)

    def halves(ref):
        x = ref[0:n3].reshape(n4, 2, 8, 128)
        return x[:, 0], x[:, 1]

    f4[...] = 0.5 * fold(res[...])
    d1[0:n4] = 0.25 * fold(halves(c1)[0])
    d1[n4] = d1[0]
    d2[...] = 0.25 * fold(sum(halves(c2)), True, False)
    e3[...] = 0.25 * fold(sum(halves(c3)), False, True)
    coefs4 = (d1[0:n4], d1[1 : n4 + 1], d2[...], e3[...])
    g4[...] = 1.0 / packed_diagonal(SIG[4], *coefs4, *FOUR)
    x = f4[...] * g4[...] * (1.0 / THETA)
    ua[1 : n4 + 1] = x
    wrap(ua, n4)
    st[...] = x
    src, dst = ua, ub
    for keep, gain in factors(4):
        x = src[1 : n4 + 1]
        near = packed_sum(src[0:n4], x, src[2 : n4 + 2], d1[0:n4], d1[1 : n4 + 1], d2[...], e3[...], *FOUR)
        step = keep * st[...] + gain * (g4[...] * (f4[...] + near) - x)
        st[...] = step
        dst[1 : n4 + 1] = x + step
        wrap(dst, n4)
        src, dst = dst, src

    j0 = around(lax.axis_index("wide") // 2 - 1, n3)
    k, j = iota((128, 128), 0), iota((128, 128), 1)
    unfold = (k == 16 * (j // 64) + j % 32 // 2).astype(F32)
    coarse = jnp.concatenate([src[1 + around(around(j0 - 2, n3) // 2 + m, n4)] for m in range(4)], axis=0)
    scr[0:32] = mul(coarse, unfold)
    shifted = lax.rem(around(j0 - 2, n3), 2)
    js = [around(j0 - 2 + m, n3) for m in range(7)]
    v = [u2[1 + js[m]] + scr[pl.ds(pl.multiple_of(8 * ((shifted + m) // 2), 8), 8), :] for m in range(7)]
    v = jnp.stack(v)

    def window(ref, first, count, by=0):
        return jnp.stack([ref[js[m] + by] for m in range(first, first + count)])

    def args(first, count):
        return window(c1, first, count), window(c1, first, count, 1), window(c2, first, count), window(c3, first, count)

    f, g = window(f3, 1, 5), window(g3, 1, 5)
    near = packed_sum(v[0:5], v[1:6], v[2:7], *args(1, 5), *THREE)
    w = v[1:6] + (1.0 / THETA) * (g * (f + near) - v[1:6])
    near = packed_sum(w[0:3], w[1:4], w[2:5], *args(2, 3), *THREE)
    x = w[1:4] + KEEP * (w[1:4] - v[2:5]) + GAIN * (g[1:4] * (f[1:4] + near) - w[1:4])
    x = x.reshape(24, 128)
    for q in range(4):
        fine = mul(x, (k == 32 * q + j % 64 // 2).astype(F32))
        e2[pl.ds(2 * q, 24, stride=8), :] = fine
        e2[pl.ds(2 * q + 1, 24, stride=8), :] = fine


def coarse_post_kernel(e2, win, u2, late, out):
    par = lax.rem(lax.axis_index("wide"), 2)
    odd = par == 1
    late = both_halves(late[...])
    v = [jnp.where(odd, u2[0], late), u2[par], u2[1 + par], u2[2 + par], jnp.where(odd, late, u2[3])]
    v = [v[m] + e2[pl.ds(pl.multiple_of(64 * ((m + par) // 2), 64), 64), :] for m in range(5)]

    def args(m):
        k = m + par
        return win[k], win[4 + k], win[8 + k], win[9 + k], win[13 + k], win[17 + k]

    w = [first_post(v[m + 1], v[m], v[m + 2], *args(m)) for m in range(3)]
    out[...] = second_post(w[1], v[2], w[0], w[2], *args(1))


def pair_kernel(a, b, out):
    out[0] = a[...]
    out[1] = b[...]


def middle_post_kernel(e2, e2sib, far, msg, sib, near, f, g, w1, own, edge, send, fine, c1, v, w):
    n, par = lax.axis_index("narrow"), lax.rem(lax.axis_index("wide"), 2)
    odd = par == 1
    row, col = iota((40, 64), 0), iota((40, 64), 1)
    pick = (col == lax.rem(16 * n + (row + 4) // 2 + 60, 64)).astype(F32)
    lanes = copies_of_lanes(128, 128)
    e2, e2sib, near0, near1 = e2[...], e2sib[...], far[0], far[1]
    for k, (upper, lower) in enumerate(((e2sib, near1), (e2, near0), (near0, e2), (near1, e2sib))):
        fine[k] = mul(mul_left(pick, jnp.where(odd, upper, lower)), lanes)
    c1[0:6] = w1[0:6]
    c1[6] = near[344:384]
    ours = [msg[160 + 40 * p : 200 + 40 * p] for p in range(2)]
    sibs = [sib[160 + 40 * p : 200 + 40 * p] for p in range(2)]
    next_chip = [near[224 + 40 * p : 264 + 40 * p] for p in range(3)]
    upper = sibs + ours + next_chip
    lower = [next_chip[2]] + next_chip[:2] + ours + sibs
    for i in range(7):
        v[i] = jnp.where(odd, upper[i], lower[i]) + fine[(i + 1 - par) // 2]

    def args(i):
        k = i - 1 + par
        return f[k], g[k], c1[k], c1[k + 1], w1[6 + k], w1[12 + k]

    for i in range(1, 6):
        w[i] = first_post(v[i], v[i - 1], v[i + 1], *args(i))
    out = [second_post(w[i], v[i], w[i - 1], w[i + 1], *args(i)) for i in (2, 3, 4)]
    own[0] = jnp.where(odd, out[0], out[1])
    own[1] = jnp.where(odd, out[1], out[2])
    edge[...] = jnp.where(odd, out[2], out[0])
    send[...] = jnp.where(odd, out[0], out[2])


def fine_post_kernel(e1, edge, other, low, high, f, c1, c2, c3, g, u2, out, v, w, scr):
    odd = lax.rem(lax.axis_index("wide"), 2) == 1
    below, above = jnp.where(odd, other[...], edge[...]), jnp.where(odd, edge[...], other[...])
    x = jnp.concatenate([below, e1[0], e1[1], above], axis=0)
    for half in range(2):
        here = slice(128 * half, 128 * half + 128)
        row, col = iota((128, 128), 0), iota((128, 128), 1)
        fine = mul(x, (row == 64 * half + col // 2).astype(F32))
        scr[pl.ds(0, 160, stride=2), :] = fine
        scr[pl.ds(1, 160, stride=2), :] = fine
        for k, ref in ((0, low), (7, high)):
            at = 80 * (k // 2)
            v[k, 0:40, here] = ref[4 + half] + scr[at : at + 40, :]
            v[k, 40:80, here] = ref[6 + half] + scr[at + 40 : at + 80, :]
        for k in range(1, 7):
            at = 80 * (k // 2)
            v[k, :, here] = u2[k, :, here] + scr[at : at + 80, :]

    def post1(q, carry):
        def chunk(r0, n):
            here = pl.ds(r0, CHUNK)
            x, near = near_chunk(v, q + 1, c1, c2, c3, q, r0, n)
            w[q + 1, here, :] = x + (1.0 / THETA) * (g[q, here, :] * (f[q, here, :] + near) - x)

        chunked(80, chunk)
        return carry

    lax.fori_loop(0, 6, post1, 0)

    def post2(q, carry):
        for r0 in range(8, 72, CHUNK):
            here = pl.ds(r0, CHUNK)
            x, near = near_chunk(w, q + 1, c1, c2, c3, q, r0, 80)
            step = KEEP * (x - v[q + 1, here, :]) + GAIN * (g[q, here, :] * (f[q, here, :] + near) - x)
            out[q - 1, pl.ds(r0 - 8, CHUNK), :] = x + step
        return carry

    lax.fori_loop(1, 5, post2, 0)


def shift(x, axis, by):
    count = lax.axis_size(axis)
    return lax.ppermute(x, axis, [(i, (i + by) % count) for i in range(count)])


def sibling(x):
    return lax.ppermute(x, "wide", [(i, i ^ 1) for i in range(lax.axis_size("wide"))])


def across(x):
    count = lax.axis_size("wide")
    return lax.ppermute(x, "wide", [(i, (i + 1 if i % 2 else i - 1) % count) for i in range(count)])


def body(source, coef_first, coef_second, coef_third):
    wide = lax.axis_size("wide")
    n3, n4 = wide // 2, wide // 4
    big = (80, 256)
    inputs = (source, coef_first, coef_second, coef_third)

    up, down = call(
        start_kernel,
        [(16, 8, 256), (16, 8, 256)],
        [pltpu.SemaphoreType.DMA((8,))],
        {k: pltpu.HBM for k in range(4)},
        limit=60,
    )(*inputs)
    low, high = shift(up, "narrow", 1), shift(down, "narrow", -1)

    own, coef1, up, down = call(
        pad_kernel, [(16,) + big, (6, 40, 128), (520, 256), (600, 256)], [(160, 128)]
    )(jnp.concatenate(inputs, axis=0), low, high)
    low, high = shift(up, "wide", 1), shift(down, "wide", -1)

    f, c1, c2, c3, g, u2, w1, up, down, f1 = call(
        fine_pre_kernel,
        [(6,) + big, (7,) + big, (6,) + big, (6,) + big, (6,) + big, (8,) + big]
        + [(18, 40, 128), (8, 40, 128), (8, 40, 128), (2, 40, 128)],
        [(8,) + big, (4,) + big, (160, 128)],
    )(own, coef1, low, high)
    low1, high1 = shift(up, "wide", 1), shift(down, "wide", -1)
    (coefs,) = call(coarse_coef_kernel, [(32, 128)], [(80, 128)])(w1)

    six = (6, 40, 128)
    f1w, g1w, u2m, f2, up, down = call(
        middle_pre_kernel, [six, six, six, (40, 128), (56, 128), (56, 128)], [six, (40, 128)]
    )(up, low1, high1, w1, coefs)
    low, high, far = shift(up, "narrow", 1), shift(down, "narrow", -1), shift(f2, "narrow", 2)

    own2, msg = call(coarse_start_kernel, [(6, 64, 128), (240, 128)])(f2, low, high, far, u2m)
    sib = sibling(msg)
    (swap,) = call(coarse_swap_kernel, [(384, 128)])(own2, msg, sib, w1)
    near = across(swap)
    (tiles,) = call(coarse_tiles_kernel, [(3, 8, 128)], [(64, 128)])(msg, sib)
    near, tiles = lax.optimization_barrier((near, tiles))
    other = sibling(near)
    w2, u2w, late = call(
        coarse_pre_kernel, [(21, 64, 128), (4, 64, 128), (32, 128)], [(6, 64, 128)]
    )(own2, sib, near, other)
    (send,) = call(coarse_send_kernel, [(n3, 2, 8, 128)], [(64, 128)])(w2, u2w, tiles)
    cores = [[k for k in range(wide) if k % 2 == c] for c in range(2)]
    parts = lax.all_to_all(send, "wide", split_axis=0, concat_axis=0, tiled=True, axis_index_groups=cores)
    theirs, late = sibling(parts), across(late)

    three, four = (n3, 8, 128), (n4, 8, 128)
    (fine2,) = call(
        bottom_kernel,
        [(192, 128)],
        [three, (n3 + 1, 8, 128), three, three, three, three, (n3 + 2, 8, 128), (n3 + 2, 8, 128), four, four]
        + [(n4 + 1, 8, 128), four, four, four, (n4 + 2, 8, 128), (n4 + 2, 8, 128), four, (32, 128)],
    )(parts, theirs)
    (e2,) = call(coarse_post_kernel, [(64, 128)])(fine2, w2, u2w, late)
    e2sib = sibling(e2)
    (both,) = call(pair_kernel, [(2, 64, 128)])(e2, e2sib)
    far = across(both)

    e1, edge, send = call(
        middle_post_kernel,
        [(2, 40, 128), (40, 128), (40, 128)],
        [(4, 40, 128), (7, 40, 128), (7, 40, 128), (7, 40, 128)],
    )(e2, e2sib, far, msg, sib, near, f1w, g1w, w1)
    other1 = sibling(send)

    (out,) = call(
        fine_post_kernel, [(4, 64, 256)], [(8,) + big, (8,) + big, (320, 128)]
    )(e1, edge, other1, low1, high1, f, c1, c2, c3, g, u2)
    return out


def solution(mesh):
    spec = P("wide", "narrow", None)
    return jax.shard_map(body, mesh=mesh, in_specs=(spec,) * 4, out_specs=spec, check_vma=False)
```

```python
import functools

import jax
import jax.numpy as jnp
from jax import lax
from jax.experimental import pallas as pl
from jax.experimental.pallas import tpu as pltpu
from jax.sharding import PartitionSpec as P

THETA = 1.125
DELTA = 0.875
RATIO = THETA / DELTA
SIG = [0.0002 * 4.0**level for level in range(5)]
F32 = jnp.float32


def factors(degree):
    rho, out = 1.0 / RATIO, []
    for _ in range(degree - 1):
        new = 1.0 / (2.0 * RATIO - rho)
        out.append((new * rho, 2.0 * new / DELTA))
        rho = new
    return out


(KEEP, GAIN), = factors(2)


def roll(x, by, axis):
    return pltpu.roll(x, by % x.shape[axis], axis)


def gather_sum(below, here, above, c1, h1, c2, c3):
    first = c1 * below + h1 * above
    second = c2 * roll(here, 1, 0) + roll(c2 * here, -1, 0)
    third = c3 * roll(here, 1, 1) + roll(c3 * here, -1, 1)
    return first + second + third


def diagonal(sig, c1, h1, c2, c3):
    return sig + c1 + h1 + c2 + roll(c2, -1, 0) + c3 + roll(c3, -1, 1)


def iota(shape, dim):
    return lax.broadcasted_iota(jnp.int32, shape, dim)


def pairs_of_lanes(lanes, period, even=False):
    row, col = iota((lanes, 128), 0), iota((lanes, 128), 1) % period
    hit = row == 2 * col if even else row // 2 == col
    return hit.astype(F32)


def copies_of_lanes(lanes_in, lanes_out):
    row, col = iota((lanes_in, lanes_out), 0), iota((lanes_in, lanes_out), 1)
    return (row == col // 2).astype(F32)


def pieces(x):
    out = []
    for _ in range(3):
        part = x.astype(jnp.bfloat16)
        out.append(part)
        x = x - part.astype(F32)
    return out


def mul(x, ones):
    ones = ones.astype(jnp.bfloat16)
    high, mid, low = [jnp.dot(part, ones, preferred_element_type=F32) for part in pieces(x)]
    return high + (mid + low)


def mul_left(ones, x):
    ones = ones.astype(jnp.bfloat16)
    high, mid, low = [jnp.dot(ones, part, preferred_element_type=F32) for part in pieces(x)]
    return high + (mid + low)


def pair_rows(x, scratch, start=0, count=None, even=False):
    rows = x.shape[0]
    count = rows // 2 if count is None else count
    scratch[0:rows, :] = x
    first = scratch[pl.ds(start, count, stride=2), :]
    if even:
        return first
    return first + scratch[pl.ds(start + 1, count, stride=2), :]


def twice_rows(x, scratch):
    rows = x.shape[0]
    scratch[pl.ds(0, rows, stride=2), :] = x
    scratch[pl.ds(1, rows, stride=2), :] = x
    return scratch[0 : 2 * rows, :]


def coarse_coefs(planes, scratch, lanes, period, start=0, count=None):
    both = pairs_of_lanes(lanes, period)
    alone = pairs_of_lanes(lanes, period, even=True)
    return (
        0.25 * pair_rows(mul(planes[0], both), scratch, start, count),
        0.25 * pair_rows(mul(planes[1], both), scratch, start, count, even=True),
        0.25 * pair_rows(mul(planes[2], alone), scratch, start, count),
    )


def spread_block(x, block, width):
    lane = iota(x.shape, 1)
    x = jnp.where(lane // width == block, x, 0.0)
    while width < 128:
        x = x + pltpu.roll(x, width, 1)
        width *= 2
    return x


def smooth_two(u1, below, above, f, g, c1, h1, c2, c3):
    near = gather_sum(below, u1, above, c1, h1, c2, c3)
    return (1.0 + KEEP) * u1 + GAIN * (g * (f + near) - u1)


def first_post(v, below, above, f, g, c1, h1, c2, c3):
    near = gather_sum(below, v, above, c1, h1, c2, c3)
    return v + (1.0 / THETA) * (g * (f + near) - v)


def second_post(u, v, below, above, f, g, c1, h1, c2, c3):
    near = gather_sum(below, u, above, c1, h1, c2, c3)
    return u + KEEP * (u - v) + GAIN * (g * (f + near) - u)


def call(kernel, outs, scratch=(), places=(), out_places=(), limit=4):
    places, out_places = dict(places), dict(out_places)

    def run(*args):
        in_specs = [pl.BlockSpec(memory_space=places.get(i, pltpu.VMEM)) for i in range(len(args))]
        return pl.pallas_call(
            kernel,
            out_shape=[jax.ShapeDtypeStruct(s, F32) for s in outs],
            in_specs=in_specs,
            out_specs=[pl.BlockSpec(memory_space=out_places.get(i, pltpu.VMEM)) for i in range(len(outs))],
            scratch_shapes=[pltpu.VMEM(s, F32) if isinstance(s, tuple) else s for s in scratch],
            compiler_params=pltpu.CompilerParams(vmem_limit_bytes=limit * 2**20),
        )(*args)

    return run


def two_blocks(x):
    half = x.shape[0] // 2
    return jnp.where(iota((half, 128), 1) < 64, x[:half], x[half:])


def start_kernel(f, c1, c2, c3, up, down, sems):
    copies = []
    for a, ref in enumerate((f, c1, c2, c3)):
        for k, (out, row) in enumerate(((up, 56), (down, 0))):
            copy = pltpu.make_async_copy(ref.at[:, pl.ds(row, 8), :], out.at[pl.ds(4 * a, 4)], sems.at[2 * a + k])
            copy.start()
            copies.append(copy)
    for copy in copies:
        copy.wait()


def pad_kernel(inner, low, high, own, coef1, out_far, out_sib, first, scr):
    for a in range(16):
        own[a, 0:8] = low[a]
        own[a, 8:72] = inner[a]
        own[a, 72:80] = high[a]
    par = lax.rem(lax.axis_index("wide"), 2)
    for k in range(2):
        diag = diagonal(SIG[0], own[5 + k], own[6 + k], own[9 + k], own[13 + k])
        first[k] = own[1 + k] / diag / THETA
    for out, up in ((out_far, par), (out_sib, 1 - par)):
        for a in range(4):
            out[80 * a : 80 * a + 80] = own[4 * a + 3 * up]
        out[320:400] = own[5]
        out[400:480] = first[up]
    k1 = jnp.concatenate([own[4], own[6]], axis=0)
    k2 = jnp.concatenate([own[8] + own[9], own[10] + own[11]], axis=0)
    k3 = jnp.concatenate([own[12] + own[13], own[14] + own[15]], axis=0)
    coarse = coarse_coefs((k1, k2, k3), scr, 256, 128)
    for a in range(3):
        for p in range(2):
            coef1[2 * a + p] = coarse[a][40 * p : 40 * p + 40]
    for out in (out_far, out_sib):
        for k in range(6):
            row, lane = 480 + 40 * (k // 2), 128 * (k % 2)
            out[row : row + 40, lane : lane + 128] = coef1[k]


def block(index):
    row, lane = 480 + 40 * (index // 2), 128 * (index % 2)
    return slice(row, row + 40), slice(lane, lane + 128)


def sides(far, sib):
    odd = lax.rem(lax.axis_index("wide"), 2) == 1

    def below(*at):
        return jnp.where(odd, sib[at], far[at])

    def above(*at):
        return jnp.where(odd, far[at], sib[at])

    return below, above


CHUNK = 16


def chunked(rows, body):
    for r0 in range(0, rows, CHUNK):
        body(r0, rows)


def near_chunk(u, p, c1, c2, c3, q, r0, rows):
    here = pl.ds(r0, CHUNK)
    x = u[p, here, :]
    if r0 > 0:
        lower = u[p, pl.ds(r0 - 1, CHUNK), :]
    else:
        lower = roll(x, 1, 0)
    if r0 + CHUNK < rows:
        after = pl.ds(r0 + 1, CHUNK)
        upper = c2[q, after, :] * u[p, after, :]
    else:
        upper = roll(c2[q, here, :] * x, -1, 0)
    k3 = c3[q, here, :]
    first = c1[q, here, :] * u[p - 1, here, :] + c1[q + 1, here, :] * u[p + 1, here, :]
    second = c2[q, here, :] * lower + upper
    third = k3 * roll(x, 1, 1) + roll(k3 * x, -1, 1)
    return x, first + second + third


def diag_chunk(c1, c2, c3, q, r0, rows):
    here = pl.ds(r0, CHUNK)
    k2, k3 = c2[q, here, :], c3[q, here, :]
    if r0 + CHUNK < rows:
        h2 = c2[q, pl.ds(r0 + 1, CHUNK), :]
    else:
        h2 = roll(k2, -1, 0)
    return SIG[0] + c1[q, here, :] + c1[q + 1, here, :] + k2 + h2 + k3 + roll(k3, -1, 1)


def fine_pre_kernel(own, coef1, far, sib, f, c1, c2, c3, g, u2, w1, out_far, out_sib, f1, u1, res, scr):
    below, above = sides(far, sib)
    for a, ref in enumerate((f, c1, c2, c3)):
        here = slice(80 * a, 80 * a + 80)
        ref[0] = below(here)
        ref[1:5] = own[4 * a : 4 * a + 4]
        ref[5] = above(here)
    c1[6] = above(slice(320, 400))
    u1[0] = below(slice(400, 480))
    u1[7] = above(slice(400, 480))

    def smooth_first(q, carry):
        def rows(r0, n):
            here = pl.ds(r0, CHUNK)
            inverse = 1.0 / diag_chunk(c1, c2, c3, q, r0, n)
            g[q, here, :] = inverse
            u1[q + 1, here, :] = f[q, here, :] * inverse * (1.0 / THETA)

        chunked(80, rows)
        return carry

    lax.fori_loop(0, 6, smooth_first, 0)

    def smooth_second(q, carry):
        def rows(r0, n):
            here = pl.ds(r0, CHUNK)
            x, near = near_chunk(u1, q + 1, c1, c2, c3, q, r0, n)
            u2[q + 1, here, :] = (1.0 + KEEP) * x + GAIN * (g[q, here, :] * (f[q, here, :] + near) - x)

        chunked(80, rows)
        return carry

    u2[0] = u1[0]
    u2[7] = u1[7]
    lax.fori_loop(0, 6, smooth_second, 0)

    def residual(q, carry):
        def rows(r0, n):
            here = pl.ds(r0, CHUNK)
            x, near = near_chunk(u2, q + 1, c1, c2, c3, q, r0, n)
            res[q - 1, here, :] = f[q, here, :] + near - diag_chunk(c1, c2, c3, q, r0, n) * x

        chunked(80, rows)
        return carry

    lax.fori_loop(1, 5, residual, 0)

    both = pairs_of_lanes(256, 128)
    sums = jnp.concatenate([res[0] + res[1], res[2] + res[3]], axis=0)
    coarse = 0.5 * pair_rows(mul(sums, both), scr)
    f1[0] = coarse[:40]
    f1[1] = coarse[40:]
    for a in range(3):
        for p in range(2):
            w1[6 * a + p] = below(*block(2 * a + p))
            w1[6 * a + 2 + p] = coef1[2 * a + p]
            w1[6 * a + 4 + p] = above(*block(2 * a + p))
    for p in range(2):
        k = p + 2
        inverse = 1.0 / diagonal(SIG[1], w1[k], w1[k + 1], w1[6 + k], w1[12 + k])
        for out in (out_far, out_sib):
            out[p] = f1[p]
            out[2 + p] = inverse
    par = lax.rem(lax.axis_index("wide"), 2)
    for out, plane in ((out_far, 3 + par), (out_sib, 4 - par)):
        out[4] = u2[plane, 0:40, 0:128]
        out[5] = u2[plane, 0:40, 128:256]
        out[6] = u2[plane, 40:80, 0:128]
        out[7] = u2[plane, 40:80, 128:256]


def coarse_coef_kernel(w1, out, scr):
    k1 = jnp.concatenate([w1[2], w1[4]], axis=0)
    k2, k3 = w1[8] + w1[9], w1[14] + w1[15]
    both, alone = pairs_of_lanes(128, 64), pairs_of_lanes(128, 64, even=True)
    k1 = 0.25 * pair_rows(mul(k1, both), scr)
    k2 = 0.25 * pair_rows(mul(k2, both), scr, even=True)
    k3 = 0.25 * pair_rows(mul(k3, alone), scr)
    for k, x in enumerate((k1[2:18], k1[22:38], k2[2:18], k3[2:18])):
        out[8 * k : 8 * k + 8] = two_blocks(x)


def middle_pre_kernel(own, far, sib, w1, coefs, f, g, u2, f2, up, down, u1, scr):
    below, above = sides(far, sib)
    for k, read in enumerate((below, own.__getitem__, above)):
        for p in range(2):
            f[2 * k + p] = read(p)
            g[2 * k + p] = read(2 + p)
    for p in range(6):
        u1[p] = f[p] * g[p] * (1.0 / THETA)
    u2[0] = u1[0]
    u2[5] = u1[5]
    for p in range(1, 5):
        u2[p] = smooth_two(u1[p], u1[p - 1], u1[p + 1], f[p], g[p], w1[p], w1[p + 1], w1[6 + p], w1[12 + p])
    total = 0.0
    for p in (2, 3):
        k1, h1, k2, k3 = w1[p], w1[p + 1], w1[6 + p], w1[12 + p]
        near = gather_sum(u2[p - 1], u2[p], u2[p + 1], k1, h1, k2, k3)
        total = total + (f[p] + near - diagonal(SIG[1], k1, h1, k2, k3) * u2[p])
    coarse = 0.5 * pair_rows(mul(total, pairs_of_lanes(128, 64)), scr, 4, 16)
    f2[0:8] = two_blocks(coarse)
    f2[8:40] = coefs[...]
    for p in range(2):
        up[40 + 8 * p : 48 + 8 * p] = u2[2 + p, 28:36]
        down[40 + 8 * p : 48 + 8 * p] = u2[2 + p, 4:12]
    up[0:40] = f2[...]
    down[0:40] = f2[...]


def both_halves(x):
    return jnp.concatenate([spread_block(x, 0, 64), spread_block(x, 1, 64)], axis=0)


def coarse_start_kernel(f2, low, high, far, u2fine, own, msg):
    n = lax.axis_index("narrow")
    for piece, by in ((f2, 0), (high, 1), (far, 2), (low, 3)):
        at = pl.multiple_of(16 * lax.rem(n + by, 4), 16)
        for k in range(5):
            own[k, pl.ds(at, 16), :] = both_halves(piece[8 * k : 8 * k + 8])
    own[5] = 1.0 / diagonal(SIG[2], own[1], own[2], own[3], own[4])
    for k, plane in enumerate((0, 5, 1, 3, 4)):
        msg[32 * k : 32 * k + 32] = two_blocks(own[plane])
    for p in range(2):
        at = 160 + 40 * p
        msg[at : at + 40] = u2fine[2 + p]
        msg[at : at + 4] = low[44 + 8 * p : 48 + 8 * p]
        msg[at + 36 : at + 40] = high[40 + 8 * p : 44 + 8 * p]


def coarse_tiles_kernel(msg, sib, tiles, scr):
    odd = lax.rem(lax.axis_index("wide"), 2) == 1
    for a in range(3):
        here = slice(64 + 32 * a, 96 + 32 * a)
        x = jnp.where(odd, sib[here], msg[here]) if a == 0 else msg[here] + sib[here]
        scr[...] = 0.25 * mul(both_halves(x), pairs_of_lanes(128, 32, even=a == 2))
        tiles[a] = tile_of(scr, a == 1)


def tile_of(scr, even=False):
    block = iota((8, 128), 1) // 32
    packed = 0.0
    for q in range(4):
        part = scr[pl.ds(2 * q, 8, stride=8), :]
        if not even:
            part = part + scr[pl.ds(2 * q + 1, 8, stride=8), :]
        packed = jnp.where(block == q, part, packed)
    return packed


def coarse_swap_kernel(own, msg, sib, w1, out):
    out[0:160] = msg[0:160]
    out[160:192] = sib[0:32] * sib[32:64] * (1.0 / THETA)
    out[192:224] = two_blocks(own[2])
    out[224:304] = msg[160:240]
    par = lax.rem(lax.axis_index("wide"), 2)
    out[304:344] = sib[pl.ds(pl.multiple_of(160 + 40 * par, 8), 40), :]
    out[344:384] = w1[4]


def coarse_pre_kernel(own, sib, near, other, w, u2, late, u1):
    odd = lax.rem(lax.axis_index("wide"), 2) == 1

    def below(k):
        here = slice(32 * k, 32 * k + 32)
        return both_halves(jnp.where(odd, other[here], near[here]))

    def above(k):
        here = slice(32 * k, 32 * k + 32)
        return both_halves(jnp.where(odd, near[here], other[here]))

    for a, (base, plane) in enumerate(((0, 0), (4, 5), (8, 1), (13, 3), (17, 4))):
        mine, theirs = own[plane], both_halves(sib[32 * a : 32 * a + 32])
        w[base] = below(a)
        w[base + 1] = jnp.where(odd, theirs, mine)
        w[base + 2] = jnp.where(odd, mine, theirs)
        w[base + 3] = above(a)
    w[12] = above(6)
    u1[0] = below(5)
    u1[5] = above(5)
    for k in range(4):
        u1[k + 1] = w[k] * w[4 + k] * (1.0 / THETA)
    for k in range(4):
        u2[k] = smooth_two(u1[k + 1], u1[k], u1[k + 2], w[k], w[4 + k], w[8 + k], w[9 + k], w[13 + k], w[17 + k])
    late[...] = two_blocks(jnp.where(odd, u2[1], u2[2]))


def coarse_send_kernel(w, u2, tiles, send, scr):
    odd = lax.rem(lax.axis_index("wide"), 2) == 1
    total = 0.0
    for k in (1, 2):
        args = (w[8 + k], w[9 + k], w[13 + k], w[17 + k])
        near = gather_sum(u2[k - 1], u2[k], u2[k + 1], *args)
        total = total + (w[k] + near - diagonal(SIG[2], *args) * u2[k])
    scr[...] = 0.5 * mul(total, pairs_of_lanes(128, 32))
    first = jnp.where(odd, tiles[1], tile_of(scr))
    second = jnp.where(odd, tiles[2], tiles[0])
    for k in range(send.shape[0]):
        send[k, 0] = first
        send[k, 1] = second


def packed_sum(below, x, above, c1, h1, c2, c3, width, blocks):
    lane = iota(x.shape, 2)
    block, inner = lane // width % blocks, lane % width

    def second_down(x):
        x = pltpu.roll(x, width, 2)
        return jnp.where(block == 0, pltpu.roll(x, 1, 1), x)

    def second_up(x):
        x = pltpu.roll(x, 128 - width, 2)
        return jnp.where(block == blocks - 1, pltpu.roll(x, 7, 1), x)

    def third_down(x):
        return jnp.where(inner == 0, pltpu.roll(x, 129 - width, 2), pltpu.roll(x, 1, 2))

    def third_up(x):
        return jnp.where(inner == width - 1, pltpu.roll(x, width - 1, 2), pltpu.roll(x, 127, 2))

    first = c1 * below + h1 * above
    second = c2 * second_down(x) + second_up(c2 * x)
    third = c3 * third_down(x) + third_up(c3 * x)
    return first + second + third


def packed_diagonal(sig, c1, h1, c2, c3, width, blocks):
    lane = iota(c1.shape, 2)
    block, inner = lane // width % blocks, lane % width
    h2 = pltpu.roll(c2, 128 - width, 2)
    h2 = jnp.where(block == blocks - 1, pltpu.roll(h2, 7, 1), h2)
    h3 = jnp.where(inner == width - 1, pltpu.roll(c3, width - 1, 2), pltpu.roll(c3, 127, 2))
    return sig + c1 + h1 + c2 + h2 + c3 + h3


def fold_matrix(even2=False, even3=False):
    k, j = iota((128, 128), 0), iota((128, 128), 1)
    k2, k3, j2, j3 = k // 32, k % 32, j // 16 % 2, j % 16
    hit2 = k2 == 2 * j2 if even2 else k2 // 2 == j2
    hit3 = k3 == 2 * j3 if even3 else k3 // 2 == j3
    return (hit2 & hit3).astype(F32)


def wrap(ref, count):
    ref[0] = ref[count]
    ref[count + 1] = ref[1]


def around(j, n):
    return lax.rem(j + n, n)


STEP = 8
THREE, FOUR = (32, 4), (16, 2)


def bottom_kernel(mine, theirs, e2,
                  f3, c1, c2, c3, d3, g3, u1, u2, res, f4, d1, d2, e3, g4, ua, ub, st, scr):
    n3, n4 = f3.shape[0], f4.shape[0]

    def loop(body):
        def step(c, carry):
            body(pl.multiple_of(c * STEP, STEP))
            return carry

        lax.fori_loop(0, n3 // STEP, step, 0)

    odd = lax.rem(lax.axis_index("wide"), 2) == 1

    def load(j):
        here = pl.ds(j, STEP)
        a, b, c, d = mine[here, 0], mine[here, 1], theirs[here, 0], theirs[here, 1]
        f3[here] = jnp.where(odd, c, a)
        c1[here] = jnp.where(odd, d, b)
        c2[here] = jnp.where(odd, a, c)
        c3[here] = jnp.where(odd, b, d)

    loop(load)
    c1[n3] = c1[0]

    def start(j):
        here = pl.ds(j, STEP)
        diag = packed_diagonal(SIG[3], c1[here], c1[pl.ds(j + 1, STEP)], c2[here], c3[here], *THREE)
        inverse = 1.0 / diag
        d3[here] = diag
        g3[here] = inverse
        u1[pl.ds(j + 1, STEP)] = f3[here] * inverse * (1.0 / THETA)

    loop(start)
    wrap(u1, n3)

    def near3(u, j):
        here = pl.ds(j, STEP)
        x = u[pl.ds(j + 1, STEP)]
        args = (c1[here], c1[pl.ds(j + 1, STEP)], c2[here], c3[here])
        return here, x, packed_sum(u[here], x, u[pl.ds(j + 2, STEP)], *args, *THREE)

    def pre(j):
        here, x, near = near3(u1, j)
        u2[pl.ds(j + 1, STEP)] = (1.0 + KEEP) * x + GAIN * (g3[here] * (f3[here] + near) - x)

    loop(pre)
    wrap(u2, n3)

    def residual(j):
        here, x, near = near3(u2, j)
        left = (f3[here] + near - d3[here] * x).reshape(STEP // 2, 2, 8, 128)
        res[pl.ds(j // 2, STEP // 2)] = left[:, 0] + left[:, 1]

    loop(residual)

    def fold(x, *even):
        return mul(x.reshape(8 * n4, 128), fold_matrix(*even)).reshape(n4, 8, 128)

    def halves(ref):
        x = ref[0:n3].reshape(n4, 2, 8, 128)
        return x[:, 0], x[:, 1]

    f4[...] = 0.5 * fold(res[...])
    d1[0:n4] = 0.25 * fold(halves(c1)[0])
    d1[n4] = d1[0]
    d2[...] = 0.25 * fold(sum(halves(c2)), True, False)
    e3[...] = 0.25 * fold(sum(halves(c3)), False, True)
    coefs4 = (d1[0:n4], d1[1 : n4 + 1], d2[...], e3[...])
    g4[...] = 1.0 / packed_diagonal(SIG[4], *coefs4, *FOUR)
    x = f4[...] * g4[...] * (1.0 / THETA)
    ua[1 : n4 + 1] = x
    wrap(ua, n4)
    st[...] = x
    src, dst = ua, ub
    for keep, gain in factors(4):
        x = src[1 : n4 + 1]
        near = packed_sum(src[0:n4], x, src[2 : n4 + 2], d1[0:n4], d1[1 : n4 + 1], d2[...], e3[...], *FOUR)
        step = keep * st[...] + gain * (g4[...] * (f4[...] + near) - x)
        st[...] = step
        dst[1 : n4 + 1] = x + step
        wrap(dst, n4)
        src, dst = dst, src

    j0 = around(lax.axis_index("wide") // 2 - 1, n3)
    k, j = iota((128, 128), 0), iota((128, 128), 1)
    unfold = (k == 16 * (j // 64) + j % 32 // 2).astype(F32)
    coarse = jnp.concatenate([src[1 + around(around(j0 - 2, n3) // 2 + m, n4)] for m in range(4)], axis=0)
    scr[0:32] = mul(coarse, unfold)
    shifted = lax.rem(around(j0 - 2, n3), 2)
    js = [around(j0 - 2 + m, n3) for m in range(7)]
    v = [u2[1 + js[m]] + scr[pl.ds(pl.multiple_of(8 * ((shifted + m) // 2), 8), 8), :] for m in range(7)]
    v = jnp.stack(v)

    def window(ref, first, count, by=0):
        return jnp.stack([ref[js[m] + by] for m in range(first, first + count)])

    def args(first, count):
        return window(c1, first, count), window(c1, first, count, 1), window(c2, first, count), window(c3, first, count)

    f, g = window(f3, 1, 5), window(g3, 1, 5)
    near = packed_sum(v[0:5], v[1:6], v[2:7], *args(1, 5), *THREE)
    w = v[1:6] + (1.0 / THETA) * (g * (f + near) - v[1:6])
    near = packed_sum(w[0:3], w[1:4], w[2:5], *args(2, 3), *THREE)
    x = w[1:4] + KEEP * (w[1:4] - v[2:5]) + GAIN * (g[1:4] * (f[1:4] + near) - w[1:4])
    x = x.reshape(24, 128)
    for q in range(4):
        fine = mul(x, (k == 32 * q + j % 64 // 2).astype(F32))
        e2[pl.ds(2 * q, 24, stride=8), :] = fine
        e2[pl.ds(2 * q + 1, 24, stride=8), :] = fine


def coarse_post_kernel(e2, win, u2, late, late_sib, out):
    below, above = sides(late, late_sib)
    v = [both_halves(below(...)), u2[0], u2[1], u2[2], u2[3], both_halves(above(...))]
    v = [v[m] + e2[64 * (m // 2) : 64 * (m // 2) + 64, :] for m in range(6)]

    def args(k):
        return win[k], win[4 + k], win[8 + k], win[9 + k], win[13 + k], win[17 + k]

    w = [first_post(v[m + 1], v[m], v[m + 2], *args(m)) for m in range(4)]
    for p in range(2):
        out[p] = second_post(w[p + 1], v[p + 2], w[p], w[p + 2], *args(p + 1))


def middle_post_kernel(e2, far, msg, sib, near, f, g, w1, own, edge, send, fine, c1, v, w):
    n, par = lax.axis_index("narrow"), lax.rem(lax.axis_index("wide"), 2)
    odd = par == 1
    row, col = iota((40, 64), 0), iota((40, 64), 1)
    pick = (col == lax.rem(16 * n + (row + 4) // 2 + 60, 64)).astype(F32)
    lanes = copies_of_lanes(128, 128)
    planes = (e2[0], e2[1], far[0], far[1])
    for k in range(4):
        fine[k] = mul(mul_left(pick, jnp.where(odd, planes[k], planes[(k + 2) % 4])), lanes)
    c1[0:6] = w1[0:6]
    c1[6] = near[344:384]
    ours = [msg[160 + 40 * p : 200 + 40 * p] for p in range(2)]
    sibs = [sib[160 + 40 * p : 200 + 40 * p] for p in range(2)]
    next_chip = [near[224 + 40 * p : 264 + 40 * p] for p in range(3)]
    upper = sibs + ours + next_chip
    lower = [next_chip[2]] + next_chip[:2] + ours + sibs
    for i in range(7):
        v[i] = jnp.where(odd, upper[i], lower[i]) + fine[(i + 1 - par) // 2]

    def args(i):
        k = i - 1 + par
        return f[k], g[k], c1[k], c1[k + 1], w1[6 + k], w1[12 + k]

    for i in range(1, 6):
        w[i] = first_post(v[i], v[i - 1], v[i + 1], *args(i))
    out = [second_post(w[i], v[i], w[i - 1], w[i + 1], *args(i)) for i in (2, 3, 4)]
    own[0] = jnp.where(odd, out[0], out[1])
    own[1] = jnp.where(odd, out[1], out[2])
    edge[...] = jnp.where(odd, out[2], out[0])
    send[...] = jnp.where(odd, out[0], out[2])


def fine_post_kernel(e1, edge, other, far, sib, f, c1, c2, c3, g, u2, out, v, w, scr):
    below, above = sides(edge, other)
    x = jnp.concatenate([below(...), e1[0], e1[1], above(...)], axis=0)
    below, above = sides(far, sib)
    for half in range(2):
        here = slice(128 * half, 128 * half + 128)
        row, col = iota((128, 128), 0), iota((128, 128), 1)
        fine = mul(x, (row == 64 * half + col // 2).astype(F32))
        scr[pl.ds(0, 160, stride=2), :] = fine
        scr[pl.ds(1, 160, stride=2), :] = fine
        for k, read in ((0, below), (7, above)):
            at = 80 * (k // 2)
            v[k, 0:40, here] = read(4 + half) + scr[at : at + 40, :]
            v[k, 40:80, here] = read(6 + half) + scr[at + 40 : at + 80, :]
        for k in range(1, 7):
            at = 80 * (k // 2)
            v[k, :, here] = u2[k, :, here] + scr[at : at + 80, :]

    def post1(q, carry):
        def chunk(r0, n):
            here = pl.ds(r0, CHUNK)
            x, near = near_chunk(v, q + 1, c1, c2, c3, q, r0, n)
            w[q + 1, here, :] = x + (1.0 / THETA) * (g[q, here, :] * (f[q, here, :] + near) - x)

        chunked(80, chunk)
        return carry

    lax.fori_loop(0, 6, post1, 0)

    def post2(q, carry):
        for r0 in range(8, 72, CHUNK):
            here = pl.ds(r0, CHUNK)
            x, near = near_chunk(w, q + 1, c1, c2, c3, q, r0, 80)
            step = KEEP * (x - v[q + 1, here, :]) + GAIN * (g[q, here, :] * (f[q, here, :] + near) - x)
            out[q - 1, pl.ds(r0 - 8, CHUNK), :] = x + step
        return carry

    lax.fori_loop(1, 5, post2, 0)


def shift(x, axis, by):
    count = lax.axis_size(axis)
    return lax.ppermute(x, axis, [(i, (i + by) % count) for i in range(count)])


def sibling(x):
    return lax.ppermute(x, "wide", [(i, i ^ 1) for i in range(lax.axis_size("wide"))])


def across(x):
    count = lax.axis_size("wide")
    return lax.ppermute(x, "wide", [(i, (i + 1 if i % 2 else i - 1) % count) for i in range(count)])


def body(source, coef_first, coef_second, coef_third):
    wide = lax.axis_size("wide")
    n3, n4 = wide // 2, wide // 4
    big = (80, 256)
    inputs = (source, coef_first, coef_second, coef_third)

    up, down = call(
        start_kernel,
        [(16, 8, 256), (16, 8, 256)],
        [pltpu.SemaphoreType.DMA((8,))],
        {k: pltpu.HBM for k in range(4)},
        limit=60,
    )(*inputs)
    low, high = shift(up, "narrow", 1), shift(down, "narrow", -1)

    own, coef1, far, sib = call(
        pad_kernel, [(16,) + big, (6, 40, 128), (600, 256), (600, 256)], [(2,) + big, (160, 128)]
    )(jnp.concatenate(inputs, axis=0), low, high)
    far, sib = across(far), sibling(sib)

    f, c1, c2, c3, g, u2, w1, out_far, out_sib, _ = call(
        fine_pre_kernel,
        [(6,) + big, (7,) + big, (6,) + big, (6,) + big, (6,) + big, (8,) + big]
        + [(18, 40, 128), (8, 40, 128), (8, 40, 128), (2, 40, 128)],
        [(8,) + big, (4,) + big, (160, 128)],
    )(own, coef1, far, sib)
    far1, sib1 = across(out_far), sibling(out_sib)
    (coefs,) = call(coarse_coef_kernel, [(32, 128)], [(80, 128)])(w1)

    six = (6, 40, 128)
    f1w, g1w, u2m, f2, up, down = call(
        middle_pre_kernel, [six, six, six, (40, 128), (56, 128), (56, 128)], [six, (40, 128)]
    )(out_far, far1, sib1, w1, coefs)
    low, high, far = shift(up, "narrow", 1), shift(down, "narrow", -1), shift(f2, "narrow", 2)

    own2, msg = call(coarse_start_kernel, [(6, 64, 128), (240, 128)])(f2, low, high, far, u2m)
    sib = sibling(msg)
    (swap,) = call(coarse_swap_kernel, [(384, 128)])(own2, msg, sib, w1)
    near = across(swap)
    (tiles,) = call(coarse_tiles_kernel, [(3, 8, 128)], [(64, 128)])(msg, sib)
    near, tiles = lax.optimization_barrier((near, tiles))
    other = sibling(near)
    w2, u2w, late = call(
        coarse_pre_kernel, [(21, 64, 128), (4, 64, 128), (32, 128)], [(6, 64, 128)]
    )(own2, sib, near, other)
    (send,) = call(coarse_send_kernel, [(n3, 2, 8, 128)], [(64, 128)])(w2, u2w, tiles)
    late = across(late)
    cores = [[k for k in range(wide) if k % 2 == c] for c in range(2)]
    parts = lax.all_to_all(send, "wide", split_axis=0, concat_axis=0, tiled=True, axis_index_groups=cores)
    parts, late = lax.optimization_barrier((parts, late))
    theirs, late_sib = sibling(parts), sibling(late)

    three, four = (n3, 8, 128), (n4, 8, 128)
    (fine2,) = call(
        bottom_kernel,
        [(192, 128)],
        [three, (n3 + 1, 8, 128), three, three, three, three, (n3 + 2, 8, 128), (n3 + 2, 8, 128), four, four]
        + [(n4 + 1, 8, 128), four, four, four, (n4 + 2, 8, 128), (n4 + 2, 8, 128), four, (32, 128)],
    )(parts, theirs)
    (e2,) = call(coarse_post_kernel, [(2, 64, 128)])(fine2, w2, u2w, late, late_sib)
    far = across(e2)

    e1, edge, send = call(
        middle_post_kernel,
        [(2, 40, 128), (40, 128), (40, 128)],
        [(4, 40, 128), (7, 40, 128), (7, 40, 128), (7, 40, 128)],
    )(e2, far, msg, sib, near, f1w, g1w, w1)
    other1 = sibling(send)

    (out,) = call(
        fine_post_kernel, [(4, 64, 256)], [(8,) + big, (8,) + big, (320, 128)]
    )(e1, edge, other1, far1, sib1, f, c1, c2, c3, g, u2)
    return out


def solution(mesh):
    spec = P("wide", "narrow", None)
    return jax.shard_map(body, mesh=mesh, in_specs=(spec,) * 4, out_specs=spec, check_vma=False)
```

```python
import functools

import jax
import jax.numpy as jnp
from jax import lax
from jax.experimental import pallas as pl
from jax.experimental.pallas import tpu as pltpu
from jax.sharding import PartitionSpec as P

THETA = 1.125
DELTA = 0.875
RATIO = THETA / DELTA
SIG = [0.0002 * 4.0**level for level in range(5)]
F32 = jnp.float32


def factors(degree):
    rho, out = 1.0 / RATIO, []
    for _ in range(degree - 1):
        new = 1.0 / (2.0 * RATIO - rho)
        out.append((new * rho, 2.0 * new / DELTA))
        rho = new
    return out


(KEEP, GAIN), = factors(2)


def roll(x, by, axis):
    return pltpu.roll(x, by % x.shape[axis], axis)


def gather_sum(below, here, above, c1, h1, c2, c3):
    first = c1 * below + h1 * above
    second = c2 * roll(here, 1, 0) + roll(c2 * here, -1, 0)
    third = c3 * roll(here, 1, 1) + roll(c3 * here, -1, 1)
    return first + second + third


def diagonal(sig, c1, h1, c2, c3):
    return sig + c1 + h1 + c2 + roll(c2, -1, 0) + c3 + roll(c3, -1, 1)


def iota(shape, dim):
    return lax.broadcasted_iota(jnp.int32, shape, dim)


def pairs_of_lanes(lanes, period, even=False):
    row, col = iota((lanes, 128), 0), iota((lanes, 128), 1) % period
    hit = row == 2 * col if even else row // 2 == col
    return hit.astype(F32)


def copies_of_lanes(lanes_in, lanes_out):
    row, col = iota((lanes_in, lanes_out), 0), iota((lanes_in, lanes_out), 1)
    return (row == col // 2).astype(F32)


def pieces(x):
    out = []
    for _ in range(3):
        part = x.astype(jnp.bfloat16)
        out.append(part)
        x = x - part.astype(F32)
    return out


def mul(x, ones):
    ones = ones.astype(jnp.bfloat16)
    high, mid, low = [jnp.dot(part, ones, preferred_element_type=F32) for part in pieces(x)]
    return high + (mid + low)


def mul_left(ones, x):
    ones = ones.astype(jnp.bfloat16)
    high, mid, low = [jnp.dot(ones, part, preferred_element_type=F32) for part in pieces(x)]
    return high + (mid + low)


def pair_rows(x, scratch, start=0, count=None, even=False):
    rows = x.shape[0]
    count = rows // 2 if count is None else count
    scratch[0:rows, :] = x
    first = scratch[pl.ds(start, count, stride=2), :]
    if even:
        return first
    return first + scratch[pl.ds(start + 1, count, stride=2), :]


def twice_rows(x, scratch):
    rows = x.shape[0]
    scratch[pl.ds(0, rows, stride=2), :] = x
    scratch[pl.ds(1, rows, stride=2), :] = x
    return scratch[0 : 2 * rows, :]


def coarse_coefs(planes, scratch, lanes, period, start=0, count=None):
    both = pairs_of_lanes(lanes, period)
    alone = pairs_of_lanes(lanes, period, even=True)
    return (
        0.25 * pair_rows(mul(planes[0], both), scratch, start, count),
        0.25 * pair_rows(mul(planes[1], both), scratch, start, count, even=True),
        0.25 * pair_rows(mul(planes[2], alone), scratch, start, count),
    )


def spread_block(x, block, width):
    lane = iota(x.shape, 1)
    x = jnp.where(lane // width == block, x, 0.0)
    while width < 128:
        x = x + pltpu.roll(x, width, 1)
        width *= 2
    return x


def smooth_two(u1, below, above, f, g, c1, h1, c2, c3):
    near = gather_sum(below, u1, above, c1, h1, c2, c3)
    return (1.0 + KEEP) * u1 + GAIN * (g * (f + near) - u1)


def first_post(v, below, above, f, g, c1, h1, c2, c3):
    near = gather_sum(below, v, above, c1, h1, c2, c3)
    return v + (1.0 / THETA) * (g * (f + near) - v)


def second_post(u, v, below, above, f, g, c1, h1, c2, c3):
    near = gather_sum(below, u, above, c1, h1, c2, c3)
    return u + KEEP * (u - v) + GAIN * (g * (f + near) - u)


def call(kernel, outs, scratch=(), places=(), out_places=(), limit=4):
    places, out_places = dict(places), dict(out_places)

    def run(*args):
        in_specs = [pl.BlockSpec(memory_space=places.get(i, pltpu.VMEM)) for i in range(len(args))]
        return pl.pallas_call(
            kernel,
            out_shape=[jax.ShapeDtypeStruct(s, F32) for s in outs],
            in_specs=in_specs,
            out_specs=[pl.BlockSpec(memory_space=out_places.get(i, pltpu.VMEM)) for i in range(len(outs))],
            scratch_shapes=[pltpu.VMEM(s, F32) if isinstance(s, tuple) else s for s in scratch],
            compiler_params=pltpu.CompilerParams(vmem_limit_bytes=limit * 2**20),
        )(*args)

    return run


def two_blocks(x):
    half = x.shape[0] // 2
    return jnp.where(iota((half, 128), 1) < 64, x[:half], x[half:])


def start_kernel(f, c1, c2, c3, up, down, sems):
    copies = []
    for a, ref in enumerate((f, c1, c2, c3)):
        for k, (out, row) in enumerate(((up, 56), (down, 0))):
            copy = pltpu.make_async_copy(ref.at[:, pl.ds(row, 8), :], out.at[pl.ds(4 * a, 4)], sems.at[2 * a + k])
            copy.start()
            copies.append(copy)
    for copy in copies:
        copy.wait()


def pad_kernel(inner, low, high, own, coef1, out_far, out_sib, first, scr):
    for a in range(16):
        own[a, 0:8] = low[a]
        own[a, 8:72] = inner[a]
        own[a, 72:80] = high[a]
    par = lax.rem(lax.axis_index("wide"), 2)
    for k in range(2):
        diag = diagonal(SIG[0], own[5 + k], own[6 + k], own[9 + k], own[13 + k])
        first[k] = own[1 + k] / diag / THETA
    for out, up in ((out_far, par), (out_sib, 1 - par)):
        for a in range(4):
            out[80 * a : 80 * a + 80] = own[4 * a + 3 * up]
        out[320:400] = own[5]
        out[400:480] = first[up]
    k1 = jnp.concatenate([own[4], own[6]], axis=0)
    k2 = jnp.concatenate([own[8] + own[9], own[10] + own[11]], axis=0)
    k3 = jnp.concatenate([own[12] + own[13], own[14] + own[15]], axis=0)
    coarse = coarse_coefs((k1, k2, k3), scr, 256, 128)
    for a in range(3):
        for p in range(2):
            coef1[2 * a + p] = coarse[a][40 * p : 40 * p + 40]
    for out in (out_far, out_sib):
        for k in range(6):
            row, lane = 480 + 40 * (k // 2), 128 * (k % 2)
            out[row : row + 40, lane : lane + 128] = coef1[k]


def block(index):
    row, lane = 480 + 40 * (index // 2), 128 * (index % 2)
    return slice(row, row + 40), slice(lane, lane + 128)


def sides(far, sib):
    odd = lax.rem(lax.axis_index("wide"), 2) == 1

    def below(*at):
        return jnp.where(odd, sib[at], far[at])

    def above(*at):
        return jnp.where(odd, far[at], sib[at])

    return below, above


CHUNK = 16


def chunked(rows, body):
    for r0 in range(0, rows, CHUNK):
        body(r0, rows)


def near_chunk(u, p, c1, c2, c3, q, r0, rows):
    here = pl.ds(r0, CHUNK)
    x = u[p, here, :]
    if r0 > 0:
        lower = u[p, pl.ds(r0 - 1, CHUNK), :]
    else:
        lower = roll(x, 1, 0)
    if r0 + CHUNK < rows:
        after = pl.ds(r0 + 1, CHUNK)
        upper = c2[q, after, :] * u[p, after, :]
    else:
        upper = roll(c2[q, here, :] * x, -1, 0)
    k3 = c3[q, here, :]
    first = c1[q, here, :] * u[p - 1, here, :] + c1[q + 1, here, :] * u[p + 1, here, :]
    second = c2[q, here, :] * lower + upper
    third = k3 * roll(x, 1, 1) + roll(k3 * x, -1, 1)
    return x, first + second + third


def diag_chunk(c1, c2, c3, q, r0, rows):
    here = pl.ds(r0, CHUNK)
    k2, k3 = c2[q, here, :], c3[q, here, :]
    if r0 + CHUNK < rows:
        h2 = c2[q, pl.ds(r0 + 1, CHUNK), :]
    else:
        h2 = roll(k2, -1, 0)
    return SIG[0] + c1[q, here, :] + c1[q + 1, here, :] + k2 + h2 + k3 + roll(k3, -1, 1)


def fine_pre_kernel(own, coef1, far, sib, f, c1, c2, c3, g, u2, w1, out_far, out_sib, f1, u1, res, scr):
    below, above = sides(far, sib)
    for a, ref in enumerate((f, c1, c2, c3)):
        here = slice(80 * a, 80 * a + 80)
        ref[0] = below(here)
        ref[1:5] = own[4 * a : 4 * a + 4]
        ref[5] = above(here)
    c1[6] = above(slice(320, 400))
    u1[0] = below(slice(400, 480))
    u1[7] = above(slice(400, 480))

    def smooth_first(q, carry):
        def rows(r0, n):
            here = pl.ds(r0, CHUNK)
            inverse = 1.0 / diag_chunk(c1, c2, c3, q, r0, n)
            g[q, here, :] = inverse
            u1[q + 1, here, :] = f[q, here, :] * inverse * (1.0 / THETA)

        chunked(80, rows)
        return carry

    lax.fori_loop(0, 6, smooth_first, 0)

    def smooth_second(q, carry):
        def rows(r0, n):
            here = pl.ds(r0, CHUNK)
            x, near = near_chunk(u1, q + 1, c1, c2, c3, q, r0, n)
            u2[q + 1, here, :] = (1.0 + KEEP) * x + GAIN * (g[q, here, :] * (f[q, here, :] + near) - x)

        chunked(80, rows)
        return carry

    u2[0] = u1[0]
    u2[7] = u1[7]
    lax.fori_loop(0, 6, smooth_second, 0)

    def residual(q, carry):
        def rows(r0, n):
            here = pl.ds(r0, CHUNK)
            x, near = near_chunk(u2, q + 1, c1, c2, c3, q, r0, n)
            res[q - 1, here, :] = f[q, here, :] + near - diag_chunk(c1, c2, c3, q, r0, n) * x

        chunked(80, rows)
        return carry

    lax.fori_loop(1, 5, residual, 0)

    both = pairs_of_lanes(256, 128)
    sums = jnp.concatenate([res[0] + res[1], res[2] + res[3]], axis=0)
    coarse = 0.5 * pair_rows(mul(sums, both), scr)
    f1[0] = coarse[:40]
    f1[1] = coarse[40:]
    for a in range(3):
        for p in range(2):
            w1[6 * a + p] = below(*block(2 * a + p))
            w1[6 * a + 2 + p] = coef1[2 * a + p]
            w1[6 * a + 4 + p] = above(*block(2 * a + p))
    for p in range(2):
        k = p + 2
        inverse = 1.0 / diagonal(SIG[1], w1[k], w1[k + 1], w1[6 + k], w1[12 + k])
        for out in (out_far, out_sib):
            out[p] = f1[p]
            out[2 + p] = inverse
    par = lax.rem(lax.axis_index("wide"), 2)
    for out, plane in ((out_far, 3 + par), (out_sib, 4 - par)):
        out[4] = u2[plane, 0:40, 0:128]
        out[5] = u2[plane, 0:40, 128:256]
        out[6] = u2[plane, 40:80, 0:128]
        out[7] = u2[plane, 40:80, 128:256]


def coarse_coef_kernel(w1, out, scr):
    k1 = jnp.concatenate([w1[2], w1[4]], axis=0)
    k2, k3 = w1[8] + w1[9], w1[14] + w1[15]
    both, alone = pairs_of_lanes(128, 64), pairs_of_lanes(128, 64, even=True)
    k1 = 0.25 * pair_rows(mul(k1, both), scr)
    k2 = 0.25 * pair_rows(mul(k2, both), scr, even=True)
    k3 = 0.25 * pair_rows(mul(k3, alone), scr)
    for k, x in enumerate((k1[2:18], k1[22:38], k2[2:18], k3[2:18])):
        out[8 * k : 8 * k + 8] = two_blocks(x)


def middle_pre_kernel(own, far, sib, w1, coefs, f, g, u2, f2, up, down, u1, scr):
    below, above = sides(far, sib)
    for k, read in enumerate((below, own.__getitem__, above)):
        for p in range(2):
            f[2 * k + p] = read(p)
            g[2 * k + p] = read(2 + p)
    for p in range(6):
        u1[p] = f[p] * g[p] * (1.0 / THETA)
    u2[0] = u1[0]
    u2[5] = u1[5]
    for p in range(1, 5):
        u2[p] = smooth_two(u1[p], u1[p - 1], u1[p + 1], f[p], g[p], w1[p], w1[p + 1], w1[6 + p], w1[12 + p])
    total = 0.0
    for p in (2, 3):
        k1, h1, k2, k3 = w1[p], w1[p + 1], w1[6 + p], w1[12 + p]
        near = gather_sum(u2[p - 1], u2[p], u2[p + 1], k1, h1, k2, k3)
        total = total + (f[p] + near - diagonal(SIG[1], k1, h1, k2, k3) * u2[p])
    coarse = 0.5 * pair_rows(mul(total, pairs_of_lanes(128, 64)), scr, 4, 16)
    f2[0:8] = two_blocks(coarse)
    f2[8:40] = coefs[...]
    for p in range(2):
        up[40 + 8 * p : 48 + 8 * p] = u2[2 + p, 28:36]
        down[40 + 8 * p : 48 + 8 * p] = u2[2 + p, 4:12]
    up[0:40] = f2[...]
    down[0:40] = f2[...]


def both_halves(x):
    return jnp.concatenate([spread_block(x, 0, 64), spread_block(x, 1, 64)], axis=0)


def coarse_start_kernel(f2, low, high, far, u2fine, own, msg):
    n = lax.axis_index("narrow")
    for piece, by in ((f2, 0), (high, 1), (far, 2), (low, 3)):
        at = pl.multiple_of(16 * lax.rem(n + by, 4), 16)
        for k in range(5):
            own[k, pl.ds(at, 16), :] = both_halves(piece[8 * k : 8 * k + 8])
    own[5] = 1.0 / diagonal(SIG[2], own[1], own[2], own[3], own[4])
    for k, plane in enumerate((0, 5, 1, 3, 4)):
        msg[32 * k : 32 * k + 32] = two_blocks(own[plane])
    for p in range(2):
        at = 160 + 40 * p
        msg[at : at + 40] = u2fine[2 + p]
        msg[at : at + 4] = low[44 + 8 * p : 48 + 8 * p]
        msg[at + 36 : at + 40] = high[40 + 8 * p : 44 + 8 * p]


def coarse_tiles_kernel(msg, sib, tiles, scr):
    odd = lax.rem(lax.axis_index("wide"), 2) == 1
    for a in range(3):
        here = slice(64 + 32 * a, 96 + 32 * a)
        x = jnp.where(odd, sib[here], msg[here]) if a == 0 else msg[here] + sib[here]
        scr[...] = 0.25 * mul(both_halves(x), pairs_of_lanes(128, 32, even=a == 2))
        tiles[a] = tile_of(scr, a == 1)


def tile_of(scr, even=False):
    block = iota((8, 128), 1) // 32
    packed = 0.0
    for q in range(4):
        part = scr[pl.ds(2 * q, 8, stride=8), :]
        if not even:
            part = part + scr[pl.ds(2 * q + 1, 8, stride=8), :]
        packed = jnp.where(block == q, part, packed)
    return packed


def coarse_swap_kernel(own, msg, sib, w1, out):
    out[0:160] = msg[0:160]
    out[160:192] = sib[0:32] * sib[32:64] * (1.0 / THETA)
    out[192:224] = two_blocks(own[2])
    out[224:304] = msg[160:240]
    par = lax.rem(lax.axis_index("wide"), 2)
    out[304:344] = sib[pl.ds(pl.multiple_of(160 + 40 * par, 8), 40), :]
    out[344:384] = w1[4]


def coarse_pre_kernel(own, sib, near, other, w, u2, late, u1):
    odd = lax.rem(lax.axis_index("wide"), 2) == 1

    def below(k):
        here = slice(32 * k, 32 * k + 32)
        return both_halves(jnp.where(odd, other[here], near[here]))

    def above(k):
        here = slice(32 * k, 32 * k + 32)
        return both_halves(jnp.where(odd, near[here], other[here]))

    for a, (base, plane) in enumerate(((0, 0), (4, 5), (8, 1), (13, 3), (17, 4))):
        mine, theirs = own[plane], both_halves(sib[32 * a : 32 * a + 32])
        w[base] = below(a)
        w[base + 1] = jnp.where(odd, theirs, mine)
        w[base + 2] = jnp.where(odd, mine, theirs)
        w[base + 3] = above(a)
    w[12] = above(6)
    u1[0] = below(5)
    u1[5] = above(5)
    for k in range(4):
        u1[k + 1] = w[k] * w[4 + k] * (1.0 / THETA)
    for k in range(4):
        u2[k] = smooth_two(u1[k + 1], u1[k], u1[k + 2], w[k], w[4 + k], w[8 + k], w[9 + k], w[13 + k], w[17 + k])
    late[...] = two_blocks(jnp.where(odd, u2[1], u2[2]))


def coarse_send_kernel(w, u2, tiles, send, scr):
    odd = lax.rem(lax.axis_index("wide"), 2) == 1
    total = 0.0
    for k in (1, 2):
        args = (w[8 + k], w[9 + k], w[13 + k], w[17 + k])
        near = gather_sum(u2[k - 1], u2[k], u2[k + 1], *args)
        total = total + (w[k] + near - diagonal(SIG[2], *args) * u2[k])
    scr[...] = 0.5 * mul(total, pairs_of_lanes(128, 32))
    first = jnp.where(odd, tiles[1], tile_of(scr))
    second = jnp.where(odd, tiles[2], tiles[0])
    for k in range(send.shape[0]):
        send[k, 0] = first
        send[k, 1] = second


def packed_sum(below, x, above, c1, h1, c2, c3, width, blocks):
    lane = iota(x.shape, 2)
    block, inner = lane // width % blocks, lane % width

    def second_down(x):
        x = pltpu.roll(x, width, 2)
        return jnp.where(block == 0, pltpu.roll(x, 1, 1), x)

    def second_up(x):
        x = pltpu.roll(x, 128 - width, 2)
        return jnp.where(block == blocks - 1, pltpu.roll(x, 7, 1), x)

    def third_down(x):
        return jnp.where(inner == 0, pltpu.roll(x, 129 - width, 2), pltpu.roll(x, 1, 2))

    def third_up(x):
        return jnp.where(inner == width - 1, pltpu.roll(x, width - 1, 2), pltpu.roll(x, 127, 2))

    first = c1 * below + h1 * above
    second = c2 * second_down(x) + second_up(c2 * x)
    third = c3 * third_down(x) + third_up(c3 * x)
    return first + second + third


def packed_diagonal(sig, c1, h1, c2, c3, width, blocks):
    lane = iota(c1.shape, 2)
    block, inner = lane // width % blocks, lane % width
    h2 = pltpu.roll(c2, 128 - width, 2)
    h2 = jnp.where(block == blocks - 1, pltpu.roll(h2, 7, 1), h2)
    h3 = jnp.where(inner == width - 1, pltpu.roll(c3, width - 1, 2), pltpu.roll(c3, 127, 2))
    return sig + c1 + h1 + c2 + h2 + c3 + h3


def fold_matrix(even2=False, even3=False):
    k, j = iota((128, 128), 0), iota((128, 128), 1)
    k2, k3, j2, j3 = k // 32, k % 32, j // 16 % 2, j % 16
    hit2 = k2 == 2 * j2 if even2 else k2 // 2 == j2
    hit3 = k3 == 2 * j3 if even3 else k3 // 2 == j3
    return (hit2 & hit3).astype(F32)


def wrap(ref, count):
    ref[0] = ref[count]
    ref[count + 1] = ref[1]


def around(j, n):
    return lax.rem(j + n, n)


STEP = 8
THREE, FOUR = (32, 4), (16, 2)


def bottom_kernel(mine, theirs, e2,
                  f3, c1, c2, c3, d3, g3, u1, u2, res, f4, d1, d2, e3, g4, ua, ub, st, scr):
    n3, n4 = f3.shape[0], f4.shape[0]

    def loop(body):
        def step(c, carry):
            body(pl.multiple_of(c * STEP, STEP))
            return carry

        lax.fori_loop(0, n3 // STEP, step, 0)

    odd = lax.rem(lax.axis_index("wide"), 2) == 1

    def load(j):
        here = pl.ds(j, STEP)
        a, b, c, d = mine[here, 0], mine[here, 1], theirs[here, 0], theirs[here, 1]
        f3[here] = jnp.where(odd, c, a)
        c1[here] = jnp.where(odd, d, b)
        c2[here] = jnp.where(odd, a, c)
        c3[here] = jnp.where(odd, b, d)

    loop(load)
    c1[n3] = c1[0]

    def start(j):
        here = pl.ds(j, STEP)
        diag = packed_diagonal(SIG[3], c1[here], c1[pl.ds(j + 1, STEP)], c2[here], c3[here], *THREE)
        inverse = 1.0 / diag
        d3[here] = diag
        g3[here] = inverse
        u1[pl.ds(j + 1, STEP)] = f3[here] * inverse * (1.0 / THETA)

    loop(start)
    wrap(u1, n3)

    def near3(u, j):
        here = pl.ds(j, STEP)
        x = u[pl.ds(j + 1, STEP)]
        args = (c1[here], c1[pl.ds(j + 1, STEP)], c2[here], c3[here])
        return here, x, packed_sum(u[here], x, u[pl.ds(j + 2, STEP)], *args, *THREE)

    def pre(j):
        here, x, near = near3(u1, j)
        u2[pl.ds(j + 1, STEP)] = (1.0 + KEEP) * x + GAIN * (g3[here] * (f3[here] + near) - x)

    loop(pre)
    wrap(u2, n3)

    def residual(j):
        here, x, near = near3(u2, j)
        left = (f3[here] + near - d3[here] * x).reshape(STEP // 2, 2, 8, 128)
        res[pl.ds(j // 2, STEP // 2)] = left[:, 0] + left[:, 1]

    loop(residual)

    def fold(x, *even):
        return mul(x.reshape(8 * n4, 128), fold_matrix(*even)).reshape(n4, 8, 128)

    def halves(ref):
        x = ref[0:n3].reshape(n4, 2, 8, 128)
        return x[:, 0], x[:, 1]

    f4[...] = 0.5 * fold(res[...])
    d1[0:n4] = 0.25 * fold(halves(c1)[0])
    d1[n4] = d1[0]
    d2[...] = 0.25 * fold(sum(halves(c2)), True, False)
    e3[...] = 0.25 * fold(sum(halves(c3)), False, True)
    coefs4 = (d1[0:n4], d1[1 : n4 + 1], d2[...], e3[...])
    g4[...] = 1.0 / packed_diagonal(SIG[4], *coefs4, *FOUR)
    x = f4[...] * g4[...] * (1.0 / THETA)
    ua[1 : n4 + 1] = x
    wrap(ua, n4)
    st[...] = x
    src, dst = ua, ub
    for keep, gain in factors(4):
        x = src[1 : n4 + 1]
        near = packed_sum(src[0:n4], x, src[2 : n4 + 2], d1[0:n4], d1[1 : n4 + 1], d2[...], e3[...], *FOUR)
        step = keep * st[...] + gain * (g4[...] * (f4[...] + near) - x)
        st[...] = step
        dst[1 : n4 + 1] = x + step
        wrap(dst, n4)
        src, dst = dst, src

    j0 = around(lax.axis_index("wide") // 2 - 1, n3)
    k, j = iota((128, 128), 0), iota((128, 128), 1)
    unfold = (k == 16 * (j // 64) + j % 32 // 2).astype(F32)
    coarse = jnp.concatenate([src[1 + around(around(j0 - 2, n3) // 2 + m, n4)] for m in range(4)], axis=0)
    scr[0:32] = mul(coarse, unfold)
    shifted = lax.rem(around(j0 - 2, n3), 2)
    js = [around(j0 - 2 + m, n3) for m in range(7)]
    v = [u2[1 + js[m]] + scr[pl.ds(pl.multiple_of(8 * ((shifted + m) // 2), 8), 8), :] for m in range(7)]
    v = jnp.stack(v)

    def window(ref, first, count, by=0):
        return jnp.stack([ref[js[m] + by] for m in range(first, first + count)])

    def args(first, count):
        return window(c1, first, count), window(c1, first, count, 1), window(c2, first, count), window(c3, first, count)

    f, g = window(f3, 1, 5), window(g3, 1, 5)
    near = packed_sum(v[0:5], v[1:6], v[2:7], *args(1, 5), *THREE)
    w = v[1:6] + (1.0 / THETA) * (g * (f + near) - v[1:6])
    near = packed_sum(w[0:3], w[1:4], w[2:5], *args(2, 3), *THREE)
    x = w[1:4] + KEEP * (w[1:4] - v[2:5]) + GAIN * (g[1:4] * (f[1:4] + near) - w[1:4])
    x = x.reshape(24, 128)
    for q in range(4):
        fine = mul(x, (k == 32 * q + j % 64 // 2).astype(F32))
        e2[pl.ds(2 * q, 24, stride=8), :] = fine
        e2[pl.ds(2 * q + 1, 24, stride=8), :] = fine


def coarse_post_kernel(e2, win, u2, late, late_sib, out):
    below, above = sides(late, late_sib)
    v = [both_halves(below(...)), u2[0], u2[1], u2[2], u2[3], both_halves(above(...))]
    v = [v[m] + e2[64 * (m // 2) : 64 * (m // 2) + 64, :] for m in range(6)]

    def args(k):
        return win[k], win[4 + k], win[8 + k], win[9 + k], win[13 + k], win[17 + k]

    w = [first_post(v[m + 1], v[m], v[m + 2], *args(m)) for m in range(4)]
    for p in range(2):
        out[p] = second_post(w[p + 1], v[p + 2], w[p], w[p + 2], *args(p + 1))


def middle_post_kernel(e2, far, msg, sib, near, f, g, w1, own, edge, send, fine, c1, v, w):
    n, par = lax.axis_index("narrow"), lax.rem(lax.axis_index("wide"), 2)
    odd = par == 1
    row, col = iota((40, 64), 0), iota((40, 64), 1)
    pick = (col == lax.rem(16 * n + (row + 4) // 2 + 60, 64)).astype(F32)
    lanes = copies_of_lanes(128, 128)
    planes = (e2[0], e2[1], far[0], far[1])
    for k in range(4):
        fine[k] = mul(mul_left(pick, jnp.where(odd, planes[k], planes[(k + 2) % 4])), lanes)
    c1[0:6] = w1[0:6]
    c1[6] = near[344:384]
    ours = [msg[160 + 40 * p : 200 + 40 * p] for p in range(2)]
    sibs = [sib[160 + 40 * p : 200 + 40 * p] for p in range(2)]
    next_chip = [near[224 + 40 * p : 264 + 40 * p] for p in range(3)]
    upper = sibs + ours + next_chip
    lower = [next_chip[2]] + next_chip[:2] + ours + sibs
    for i in range(7):
        v[i] = jnp.where(odd, upper[i], lower[i]) + fine[(i + 1 - par) // 2]

    def args(i):
        k = i - 1 + par
        return f[k], g[k], c1[k], c1[k + 1], w1[6 + k], w1[12 + k]

    for i in range(1, 6):
        w[i] = first_post(v[i], v[i - 1], v[i + 1], *args(i))
    out = [second_post(w[i], v[i], w[i - 1], w[i + 1], *args(i)) for i in (2, 3, 4)]
    own[0] = jnp.where(odd, out[0], out[1])
    own[1] = jnp.where(odd, out[1], out[2])
    edge[...] = jnp.where(odd, out[2], out[0])
    send[...] = jnp.where(odd, out[0], out[2])


def fine_post_kernel(e1, edge, other, far, sib, f, c1, c2, c3, g, u2, out, v, w, scr):
    below, above = sides(edge, other)
    x = jnp.concatenate([below(...), e1[0], e1[1], above(...)], axis=0)
    below, above = sides(far, sib)
    for half in range(2):
        here = slice(128 * half, 128 * half + 128)
        row, col = iota((128, 128), 0), iota((128, 128), 1)
        fine = mul(x, (row == 64 * half + col // 2).astype(F32))
        scr[pl.ds(0, 160, stride=2), :] = fine
        scr[pl.ds(1, 160, stride=2), :] = fine
        for k, read in ((0, below), (7, above)):
            at = 80 * (k // 2)
            v[k, 0:40, here] = read(4 + half) + scr[at : at + 40, :]
            v[k, 40:80, here] = read(6 + half) + scr[at + 40 : at + 80, :]
        for k in range(1, 7):
            at = 80 * (k // 2)
            v[k, :, here] = u2[k, :, here] + scr[at : at + 80, :]

    def post1(q, carry):
        def chunk(r0, n):
            here = pl.ds(r0, CHUNK)
            x, near = near_chunk(v, q + 1, c1, c2, c3, q, r0, n)
            w[q + 1, here, :] = x + (1.0 / THETA) * (g[q, here, :] * (f[q, here, :] + near) - x)

        chunked(80, chunk)
        return carry

    lax.fori_loop(0, 6, post1, 0)

    def post2(q, carry):
        for r0 in range(8, 72, CHUNK):
            here = pl.ds(r0, CHUNK)
            x, near = near_chunk(w, q + 1, c1, c2, c3, q, r0, 80)
            step = KEEP * (x - v[q + 1, here, :]) + GAIN * (g[q, here, :] * (f[q, here, :] + near) - x)
            out[q - 1, pl.ds(r0 - 8, CHUNK), :] = x + step
        return carry

    lax.fori_loop(1, 5, post2, 0)


def shift(x, axis, by):
    count = lax.axis_size(axis)
    return lax.ppermute(x, axis, [(i, (i + by) % count) for i in range(count)])


def sibling(x):
    return lax.ppermute(x, "wide", [(i, i ^ 1) for i in range(lax.axis_size("wide"))])


def across(x):
    count = lax.axis_size("wide")
    return lax.ppermute(x, "wide", [(i, (i + 1 if i % 2 else i - 1) % count) for i in range(count)])


def body(source, coef_first, coef_second, coef_third):
    wide = lax.axis_size("wide")
    n3, n4 = wide // 2, wide // 4
    big = (80, 256)
    inputs = (source, coef_first, coef_second, coef_third)

    up, down = call(
        start_kernel,
        [(16, 8, 256), (16, 8, 256)],
        [pltpu.SemaphoreType.DMA((8,))],
        {k: pltpu.HBM for k in range(4)},
        limit=60,
    )(*inputs)
    low, high = shift(up, "narrow", 1), shift(down, "narrow", -1)

    own, coef1, far, sib = call(
        pad_kernel, [(16,) + big, (6, 40, 128), (600, 256), (600, 256)], [(2,) + big, (160, 128)]
    )(jnp.concatenate(inputs, axis=0), low, high)
    far, sib = across(far), sibling(sib)

    f, c1, c2, c3, g, u2, w1, out_far, out_sib, _ = call(
        fine_pre_kernel,
        [(6,) + big, (7,) + big, (6,) + big, (6,) + big, (6,) + big, (8,) + big]
        + [(18, 40, 128), (8, 40, 128), (8, 40, 128), (2, 40, 128)],
        [(8,) + big, (4,) + big, (160, 128)],
    )(own, coef1, far, sib)
    far1, sib1 = across(out_far), sibling(out_sib)
    (coefs,) = call(coarse_coef_kernel, [(32, 128)], [(80, 128)])(w1)

    six = (6, 40, 128)
    f1w, g1w, u2m, f2, up, down = call(
        middle_pre_kernel, [six, six, six, (40, 128), (56, 128), (56, 128)], [six, (40, 128)]
    )(out_far, far1, sib1, w1, coefs)
    low, high, far = shift(up, "narrow", 1), shift(down, "narrow", -1), shift(f2, "narrow", 2)

    own2, msg = call(coarse_start_kernel, [(6, 64, 128), (240, 128)])(f2, low, high, far, u2m)
    sib = sibling(msg)
    (swap,) = call(coarse_swap_kernel, [(384, 128)])(own2, msg, sib, w1)
    near = across(swap)
    (tiles,) = call(coarse_tiles_kernel, [(3, 8, 128)], [(64, 128)])(msg, sib)
    near, tiles = lax.optimization_barrier((near, tiles))
    other = sibling(near)
    w2, u2w, late = call(
        coarse_pre_kernel, [(21, 64, 128), (4, 64, 128), (32, 128)], [(6, 64, 128)]
    )(own2, sib, near, other)
    (send,) = call(coarse_send_kernel, [(n3, 2, 8, 128)], [(64, 128)])(w2, u2w, tiles)
    late = across(late)
    cores = [[k for k in range(wide) if k % 2 == c] for c in range(2)]
    parts = lax.all_to_all(send, "wide", split_axis=0, concat_axis=0, tiled=True, axis_index_groups=cores)
    theirs, late_sib = sibling(parts), sibling(late)

    three, four = (n3, 8, 128), (n4, 8, 128)
    (fine2,) = call(
        bottom_kernel,
        [(192, 128)],
        [three, (n3 + 1, 8, 128), three, three, three, three, (n3 + 2, 8, 128), (n3 + 2, 8, 128), four, four]
        + [(n4 + 1, 8, 128), four, four, four, (n4 + 2, 8, 128), (n4 + 2, 8, 128), four, (32, 128)],
    )(parts, theirs)
    (e2,) = call(coarse_post_kernel, [(2, 64, 128)])(fine2, w2, u2w, late, late_sib)
    far = across(e2)

    e1, edge, send = call(
        middle_post_kernel,
        [(2, 40, 128), (40, 128), (40, 128)],
        [(4, 40, 128), (7, 40, 128), (7, 40, 128), (7, 40, 128)],
    )(e2, far, msg, sib, near, f1w, g1w, w1)
    other1 = sibling(send)

    (out,) = call(
        fine_post_kernel, [(4, 64, 256)], [(8,) + big, (8,) + big, (320, 128)]
    )(e1, edge, other1, far1, sib1, f, c1, c2, c3, g, u2)
    return out


def solution(mesh):
    spec = P("wide", "narrow", None)
    return jax.shard_map(body, mesh=mesh, in_specs=(spec,) * 4, out_specs=spec, check_vma=False)
```

```python
import functools

import jax
import jax.numpy as jnp
from jax import lax
from jax.experimental import pallas as pl
from jax.experimental.pallas import tpu as pltpu
from jax.sharding import PartitionSpec as P

THETA = 1.125
DELTA = 0.875
RATIO = THETA / DELTA
SIG = [0.0002 * 4.0**level for level in range(5)]
F32 = jnp.float32


def factors(degree):
    rho, out = 1.0 / RATIO, []
    for _ in range(degree - 1):
        new = 1.0 / (2.0 * RATIO - rho)
        out.append((new * rho, 2.0 * new / DELTA))
        rho = new
    return out


(KEEP, GAIN), = factors(2)


def roll(x, by, axis):
    return pltpu.roll(x, by % x.shape[axis], axis)


def gather_sum(below, here, above, c1, h1, c2, c3):
    first = c1 * below + h1 * above
    second = c2 * roll(here, 1, 0) + roll(c2 * here, -1, 0)
    third = c3 * roll(here, 1, 1) + roll(c3 * here, -1, 1)
    return first + second + third


def diagonal(sig, c1, h1, c2, c3):
    return sig + c1 + h1 + c2 + roll(c2, -1, 0) + c3 + roll(c3, -1, 1)


def iota(shape, dim):
    return lax.broadcasted_iota(jnp.int32, shape, dim)


def pairs_of_lanes(lanes, period, even=False):
    row, col = iota((lanes, 128), 0), iota((lanes, 128), 1) % period
    hit = row == 2 * col if even else row // 2 == col
    return hit.astype(F32)


def copies_of_lanes(lanes_in, lanes_out):
    row, col = iota((lanes_in, lanes_out), 0), iota((lanes_in, lanes_out), 1)
    return (row == col // 2).astype(F32)


def pieces(x):
    out = []
    for _ in range(3):
        part = x.astype(jnp.bfloat16)
        out.append(part)
        x = x - part.astype(F32)
    return out


def mul(x, ones):
    ones = ones.astype(jnp.bfloat16)
    high, mid, low = [jnp.dot(part, ones, preferred_element_type=F32) for part in pieces(x)]
    return high + (mid + low)


def mul_left(ones, x):
    ones = ones.astype(jnp.bfloat16)
    high, mid, low = [jnp.dot(ones, part, preferred_element_type=F32) for part in pieces(x)]
    return high + (mid + low)


def pair_rows(x, scratch, start=0, count=None, even=False):
    rows = x.shape[0]
    count = rows // 2 if count is None else count
    scratch[0:rows, :] = x
    first = scratch[pl.ds(start, count, stride=2), :]
    if even:
        return first
    return first + scratch[pl.ds(start + 1, count, stride=2), :]


def twice_rows(x, scratch):
    rows = x.shape[0]
    scratch[pl.ds(0, rows, stride=2), :] = x
    scratch[pl.ds(1, rows, stride=2), :] = x
    return scratch[0 : 2 * rows, :]


def coarse_coefs(planes, scratch, lanes, period, start=0, count=None):
    both = pairs_of_lanes(lanes, period)
    alone = pairs_of_lanes(lanes, period, even=True)
    return (
        0.25 * pair_rows(mul(planes[0], both), scratch, start, count),
        0.25 * pair_rows(mul(planes[1], both), scratch, start, count, even=True),
        0.25 * pair_rows(mul(planes[2], alone), scratch, start, count),
    )


def spread_block(x, block, width):
    lane = iota(x.shape, 1)
    x = jnp.where(lane // width == block, x, 0.0)
    while width < 128:
        x = x + pltpu.roll(x, width, 1)
        width *= 2
    return x


def smooth_two(u1, below, above, f, g, c1, h1, c2, c3):
    near = gather_sum(below, u1, above, c1, h1, c2, c3)
    return (1.0 + KEEP) * u1 + GAIN * (g * (f + near) - u1)


def first_post(v, below, above, f, g, c1, h1, c2, c3):
    near = gather_sum(below, v, above, c1, h1, c2, c3)
    return v + (1.0 / THETA) * (g * (f + near) - v)


def second_post(u, v, below, above, f, g, c1, h1, c2, c3):
    near = gather_sum(below, u, above, c1, h1, c2, c3)
    return u + KEEP * (u - v) + GAIN * (g * (f + near) - u)


def call(kernel, outs, scratch=(), places=(), out_places=(), limit=4):
    places, out_places = dict(places), dict(out_places)

    def run(*args):
        in_specs = [pl.BlockSpec(memory_space=places.get(i, pltpu.VMEM)) for i in range(len(args))]
        return pl.pallas_call(
            kernel,
            out_shape=[jax.ShapeDtypeStruct(s, F32) for s in outs],
            in_specs=in_specs,
            out_specs=[pl.BlockSpec(memory_space=out_places.get(i, pltpu.VMEM)) for i in range(len(outs))],
            scratch_shapes=[pltpu.VMEM(s, F32) if isinstance(s, tuple) else s for s in scratch],
            compiler_params=pltpu.CompilerParams(vmem_limit_bytes=limit * 2**20),
        )(*args)

    return run


def two_blocks(x):
    half = x.shape[0] // 2
    return jnp.where(iota((half, 128), 1) < 64, x[:half], x[half:])


def start_kernel(f, c1, c2, c3, up, down, sems):
    copies = []
    for a, ref in enumerate((f, c1, c2, c3)):
        for k, (out, row) in enumerate(((up, 56), (down, 0))):
            copy = pltpu.make_async_copy(ref.at[:, pl.ds(row, 8), :], out.at[pl.ds(4 * a, 4)], sems.at[2 * a + k])
            copy.start()
            copies.append(copy)
    for copy in copies:
        copy.wait()


def pad_kernel(inner, low, high, own, coef1, out_far, out_sib, first, scr):
    for a in range(16):
        own[a, 0:8] = low[a]
        own[a, 8:72] = inner[a]
        own[a, 72:80] = high[a]
    par = lax.rem(lax.axis_index("wide"), 2)
    for k in range(2):
        diag = diagonal(SIG[0], own[5 + k], own[6 + k], own[9 + k], own[13 + k])
        first[k] = own[1 + k] / diag / THETA
    for out, up in ((out_far, par), (out_sib, 1 - par)):
        for a in range(4):
            out[80 * a : 80 * a + 80] = own[4 * a + 3 * up]
        out[320:400] = own[5]
        out[400:480] = first[up]
    k1 = jnp.concatenate([own[4], own[6]], axis=0)
    k2 = jnp.concatenate([own[8] + own[9], own[10] + own[11]], axis=0)
    k3 = jnp.concatenate([own[12] + own[13], own[14] + own[15]], axis=0)
    coarse = coarse_coefs((k1, k2, k3), scr, 256, 128)
    for a in range(3):
        for p in range(2):
            coef1[2 * a + p] = coarse[a][40 * p : 40 * p + 40]
    for out in (out_far, out_sib):
        for k in range(6):
            row, lane = 480 + 40 * (k // 2), 128 * (k % 2)
            out[row : row + 40, lane : lane + 128] = coef1[k]


def block(index):
    row, lane = 480 + 40 * (index // 2), 128 * (index % 2)
    return slice(row, row + 40), slice(lane, lane + 128)


def sides(far, sib):
    odd = lax.rem(lax.axis_index("wide"), 2) == 1

    def below(*at):
        return jnp.where(odd, sib[at], far[at])

    def above(*at):
        return jnp.where(odd, far[at], sib[at])

    return below, above


CHUNK = 16


def chunked(rows, body):
    for r0 in range(0, rows, CHUNK):
        body(r0, rows)


def near_chunk(u, p, c1, c2, c3, q, r0, rows):
    here = pl.ds(r0, CHUNK)
    x = u[p, here, :]
    if r0 > 0:
        lower = u[p, pl.ds(r0 - 1, CHUNK), :]
    else:
        lower = roll(x, 1, 0)
    if r0 + CHUNK < rows:
        after = pl.ds(r0 + 1, CHUNK)
        upper = c2[q, after, :] * u[p, after, :]
    else:
        upper = roll(c2[q, here, :] * x, -1, 0)
    k3 = c3[q, here, :]
    first = c1[q, here, :] * u[p - 1, here, :] + c1[q + 1, here, :] * u[p + 1, here, :]
    second = c2[q, here, :] * lower + upper
    third = k3 * roll(x, 1, 1) + roll(k3 * x, -1, 1)
    return x, first + second + third


def diag_chunk(c1, c2, c3, q, r0, rows):
    here = pl.ds(r0, CHUNK)
    k2, k3 = c2[q, here, :], c3[q, here, :]
    if r0 + CHUNK < rows:
        h2 = c2[q, pl.ds(r0 + 1, CHUNK), :]
    else:
        h2 = roll(k2, -1, 0)
    return SIG[0] + c1[q, here, :] + c1[q + 1, here, :] + k2 + h2 + k3 + roll(k3, -1, 1)


def fine_pre_kernel(own, coef1, far, sib, f, c1, c2, c3, g, u2, w1, out_far, out_sib, f1, u1, res, scr):
    below, above = sides(far, sib)
    for a, ref in enumerate((f, c1, c2, c3)):
        here = slice(80 * a, 80 * a + 80)
        ref[0] = below(here)
        ref[1:5] = own[4 * a : 4 * a + 4]
        ref[5] = above(here)
    c1[6] = above(slice(320, 400))
    u1[0] = below(slice(400, 480))
    u1[7] = above(slice(400, 480))

    def smooth_first(q, carry):
        def rows(r0, n):
            here = pl.ds(r0, CHUNK)
            inverse = 1.0 / diag_chunk(c1, c2, c3, q, r0, n)
            g[q, here, :] = inverse
            u1[q + 1, here, :] = f[q, here, :] * inverse * (1.0 / THETA)

        chunked(80, rows)
        return carry

    lax.fori_loop(0, 6, smooth_first, 0)

    def smooth_second(q, carry):
        def rows(r0, n):
            here = pl.ds(r0, CHUNK)
            x, near = near_chunk(u1, q + 1, c1, c2, c3, q, r0, n)
            u2[q + 1, here, :] = (1.0 + KEEP) * x + GAIN * (g[q, here, :] * (f[q, here, :] + near) - x)

        chunked(80, rows)
        return carry

    u2[0] = u1[0]
    u2[7] = u1[7]
    lax.fori_loop(0, 6, smooth_second, 0)

    def residual(q, carry):
        def rows(r0, n):
            here = pl.ds(r0, CHUNK)
            x, near = near_chunk(u2, q + 1, c1, c2, c3, q, r0, n)
            res[q - 1, here, :] = f[q, here, :] + near - diag_chunk(c1, c2, c3, q, r0, n) * x

        chunked(80, rows)
        return carry

    lax.fori_loop(1, 5, residual, 0)

    both = pairs_of_lanes(256, 128)
    sums = jnp.concatenate([res[0] + res[1], res[2] + res[3]], axis=0)
    coarse = 0.5 * pair_rows(mul(sums, both), scr)
    f1[0] = coarse[:40]
    f1[1] = coarse[40:]
    for a in range(3):
        for p in range(2):
            w1[6 * a + p] = below(*block(2 * a + p))
            w1[6 * a + 2 + p] = coef1[2 * a + p]
            w1[6 * a + 4 + p] = above(*block(2 * a + p))
    for p in range(2):
        k = p + 2
        inverse = 1.0 / diagonal(SIG[1], w1[k], w1[k + 1], w1[6 + k], w1[12 + k])
        for out in (out_far, out_sib):
            out[p] = f1[p]
            out[2 + p] = inverse
    par = lax.rem(lax.axis_index("wide"), 2)
    for out, plane in ((out_far, 3 + par), (out_sib, 4 - par)):
        out[4] = u2[plane, 0:40, 0:128]
        out[5] = u2[plane, 0:40, 128:256]
        out[6] = u2[plane, 40:80, 0:128]
        out[7] = u2[plane, 40:80, 128:256]


def coarse_coef_kernel(w1, out, scr):
    k1 = jnp.concatenate([w1[2], w1[4]], axis=0)
    k2, k3 = w1[8] + w1[9], w1[14] + w1[15]
    both, alone = pairs_of_lanes(128, 64), pairs_of_lanes(128, 64, even=True)
    k1 = 0.25 * pair_rows(mul(k1, both), scr)
    k2 = 0.25 * pair_rows(mul(k2, both), scr, even=True)
    k3 = 0.25 * pair_rows(mul(k3, alone), scr)
    for k, x in enumerate((k1[2:18], k1[22:38], k2[2:18], k3[2:18])):
        out[8 * k : 8 * k + 8] = two_blocks(x)


def middle_pre_kernel(own, far, sib, w1, coefs, f, g, u2, f2, up, down, u1, scr):
    below, above = sides(far, sib)
    for k, read in enumerate((below, own.__getitem__, above)):
        for p in range(2):
            f[2 * k + p] = read(p)
            g[2 * k + p] = read(2 + p)
    for p in range(6):
        u1[p] = f[p] * g[p] * (1.0 / THETA)
    u2[0] = u1[0]
    u2[5] = u1[5]
    for p in range(1, 5):
        u2[p] = smooth_two(u1[p], u1[p - 1], u1[p + 1], f[p], g[p], w1[p], w1[p + 1], w1[6 + p], w1[12 + p])
    total = 0.0
    for p in (2, 3):
        k1, h1, k2, k3 = w1[p], w1[p + 1], w1[6 + p], w1[12 + p]
        near = gather_sum(u2[p - 1], u2[p], u2[p + 1], k1, h1, k2, k3)
        total = total + (f[p] + near - diagonal(SIG[1], k1, h1, k2, k3) * u2[p])
    coarse = 0.5 * pair_rows(mul(total, pairs_of_lanes(128, 64)), scr, 4, 16)
    f2[0:8] = two_blocks(coarse)
    f2[8:40] = coefs[...]
    for p in range(2):
        up[40 + 8 * p : 48 + 8 * p] = u2[2 + p, 28:36]
        down[40 + 8 * p : 48 + 8 * p] = u2[2 + p, 4:12]
    up[0:40] = f2[...]
    down[0:40] = f2[...]


def both_halves(x):
    return jnp.concatenate([spread_block(x, 0, 64), spread_block(x, 1, 64)], axis=0)


def coarse_start_kernel(f2, low, high, far, u2fine, own, msg):
    n = lax.axis_index("narrow")
    for piece, by in ((f2, 0), (high, 1), (far, 2), (low, 3)):
        at = pl.multiple_of(16 * lax.rem(n + by, 4), 16)
        for k in range(5):
            own[k, pl.ds(at, 16), :] = both_halves(piece[8 * k : 8 * k + 8])
    own[5] = 1.0 / diagonal(SIG[2], own[1], own[2], own[3], own[4])
    for k, plane in enumerate((0, 5, 1, 3, 4)):
        msg[32 * k : 32 * k + 32] = two_blocks(own[plane])
    for p in range(2):
        at = 160 + 40 * p
        msg[at : at + 40] = u2fine[2 + p]
        msg[at : at + 4] = low[44 + 8 * p : 48 + 8 * p]
        msg[at + 36 : at + 40] = high[40 + 8 * p : 44 + 8 * p]


def coarse_tiles_kernel(msg, sib, tiles, scr):
    odd = lax.rem(lax.axis_index("wide"), 2) == 1
    for a in range(3):
        here = slice(64 + 32 * a, 96 + 32 * a)
        x = jnp.where(odd, sib[here], msg[here]) if a == 0 else msg[here] + sib[here]
        scr[...] = 0.25 * mul(both_halves(x), pairs_of_lanes(128, 32, even=a == 2))
        tiles[a] = tile_of(scr, a == 1)


def tile_of(scr, even=False):
    block = iota((8, 128), 1) // 32
    packed = 0.0
    for q in range(4):
        part = scr[pl.ds(2 * q, 8, stride=8), :]
        if not even:
            part = part + scr[pl.ds(2 * q + 1, 8, stride=8), :]
        packed = jnp.where(block == q, part, packed)
    return packed


def coarse_swap_kernel(own, msg, sib, w1, out):
    out[0:160] = msg[0:160]
    out[160:192] = sib[0:32] * sib[32:64] * (1.0 / THETA)
    out[192:224] = two_blocks(own[2])
    out[224:304] = msg[160:240]
    par = lax.rem(lax.axis_index("wide"), 2)
    out[304:344] = sib[pl.ds(pl.multiple_of(160 + 40 * par, 8), 40), :]
    out[344:384] = w1[4]


def coarse_pre_kernel(own, sib, near, other, w, u2, late, u1):
    odd = lax.rem(lax.axis_index("wide"), 2) == 1

    def below(k):
        here = slice(32 * k, 32 * k + 32)
        return both_halves(jnp.where(odd, other[here], near[here]))

    def above(k):
        here = slice(32 * k, 32 * k + 32)
        return both_halves(jnp.where(odd, near[here], other[here]))

    for a, (base, plane) in enumerate(((0, 0), (4, 5), (8, 1), (13, 3), (17, 4))):
        mine, theirs = own[plane], both_halves(sib[32 * a : 32 * a + 32])
        w[base] = below(a)
        w[base + 1] = jnp.where(odd, theirs, mine)
        w[base + 2] = jnp.where(odd, mine, theirs)
        w[base + 3] = above(a)
    w[12] = above(6)
    u1[0] = below(5)
    u1[5] = above(5)
    for k in range(4):
        u1[k + 1] = w[k] * w[4 + k] * (1.0 / THETA)
    for k in range(4):
        u2[k] = smooth_two(u1[k + 1], u1[k], u1[k + 2], w[k], w[4 + k], w[8 + k], w[9 + k], w[13 + k], w[17 + k])
    late[...] = two_blocks(jnp.where(odd, u2[1], u2[2]))


def coarse_send_kernel(w, u2, tiles, send, scr):
    odd = lax.rem(lax.axis_index("wide"), 2) == 1
    total = 0.0
    for k in (1, 2):
        args = (w[8 + k], w[9 + k], w[13 + k], w[17 + k])
        near = gather_sum(u2[k - 1], u2[k], u2[k + 1], *args)
        total = total + (w[k] + near - diagonal(SIG[2], *args) * u2[k])
    scr[...] = 0.5 * mul(total, pairs_of_lanes(128, 32))
    first = jnp.where(odd, tiles[1], tile_of(scr))
    second = jnp.where(odd, tiles[2], tiles[0])
    for k in range(send.shape[0]):
        send[k, 0] = first
        send[k, 1] = second


def packed_sum(below, x, above, c1, h1, c2, c3, width, blocks):
    lane = iota(x.shape, 2)
    block, inner = lane // width % blocks, lane % width

    def second_down(x):
        x = pltpu.roll(x, width, 2)
        return jnp.where(block == 0, pltpu.roll(x, 1, 1), x)

    def second_up(x):
        x = pltpu.roll(x, 128 - width, 2)
        return jnp.where(block == blocks - 1, pltpu.roll(x, 7, 1), x)

    def third_down(x):
        return jnp.where(inner == 0, pltpu.roll(x, 129 - width, 2), pltpu.roll(x, 1, 2))

    def third_up(x):
        return jnp.where(inner == width - 1, pltpu.roll(x, width - 1, 2), pltpu.roll(x, 127, 2))

    first = c1 * below + h1 * above
    second = c2 * second_down(x) + second_up(c2 * x)
    third = c3 * third_down(x) + third_up(c3 * x)
    return first + second + third


def packed_diagonal(sig, c1, h1, c2, c3, width, blocks):
    lane = iota(c1.shape, 2)
    block, inner = lane // width % blocks, lane % width
    h2 = pltpu.roll(c2, 128 - width, 2)
    h2 = jnp.where(block == blocks - 1, pltpu.roll(h2, 7, 1), h2)
    h3 = jnp.where(inner == width - 1, pltpu.roll(c3, width - 1, 2), pltpu.roll(c3, 127, 2))
    return sig + c1 + h1 + c2 + h2 + c3 + h3


def fold_matrix(even2=False, even3=False):
    k, j = iota((128, 128), 0), iota((128, 128), 1)
    k2, k3, j2, j3 = k // 32, k % 32, j // 16 % 2, j % 16
    hit2 = k2 == 2 * j2 if even2 else k2 // 2 == j2
    hit3 = k3 == 2 * j3 if even3 else k3 // 2 == j3
    return (hit2 & hit3).astype(F32)


def wrap(ref, count):
    ref[0] = ref[count]
    ref[count + 1] = ref[1]


def around(j, n):
    return lax.rem(j + n, n)


STEP = 8
THREE, FOUR = (32, 4), (16, 2)


def bottom_kernel(mine, theirs, e2,
                  f3, c1, c2, c3, d3, g3, u1, u2, res, f4, d1, d2, e3, g4, ua, ub, st, scr):
    n3, n4 = f3.shape[0], f4.shape[0]

    def loop(body):
        def step(c, carry):
            body(pl.multiple_of(c * STEP, STEP))
            return carry

        lax.fori_loop(0, n3 // STEP, step, 0)

    odd = lax.rem(lax.axis_index("wide"), 2) == 1

    def load(j):
        here = pl.ds(j, STEP)
        a, b, c, d = mine[here, 0], mine[here, 1], theirs[here, 0], theirs[here, 1]
        f3[here] = jnp.where(odd, c, a)
        c1[here] = jnp.where(odd, d, b)
        c2[here] = jnp.where(odd, a, c)
        c3[here] = jnp.where(odd, b, d)

    loop(load)
    c1[n3] = c1[0]

    def start(j):
        here = pl.ds(j, STEP)
        diag = packed_diagonal(SIG[3], c1[here], c1[pl.ds(j + 1, STEP)], c2[here], c3[here], *THREE)
        inverse = 1.0 / diag
        d3[here] = diag
        g3[here] = inverse
        u1[pl.ds(j + 1, STEP)] = f3[here] * inverse * (1.0 / THETA)

    loop(start)
    wrap(u1, n3)

    def near3(u, j):
        here = pl.ds(j, STEP)
        x = u[pl.ds(j + 1, STEP)]
        args = (c1[here], c1[pl.ds(j + 1, STEP)], c2[here], c3[here])
        return here, x, packed_sum(u[here], x, u[pl.ds(j + 2, STEP)], *args, *THREE)

    def pre(j):
        here, x, near = near3(u1, j)
        u2[pl.ds(j + 1, STEP)] = (1.0 + KEEP) * x + GAIN * (g3[here] * (f3[here] + near) - x)

    loop(pre)
    wrap(u2, n3)

    def residual(j):
        here, x, near = near3(u2, j)
        left = (f3[here] + near - d3[here] * x).reshape(STEP // 2, 2, 8, 128)
        res[pl.ds(j // 2, STEP // 2)] = left[:, 0] + left[:, 1]

    loop(residual)

    def fold(x, *even):
        return mul(x.reshape(8 * n4, 128), fold_matrix(*even)).reshape(n4, 8, 128)

    def halves(ref):
        x = ref[0:n3].reshape(n4, 2, 8, 128)
        return x[:, 0], x[:, 1]

    f4[...] = 0.5 * fold(res[...])
    d1[0:n4] = 0.25 * fold(halves(c1)[0])
    d1[n4] = d1[0]
    d2[...] = 0.25 * fold(sum(halves(c2)), True, False)
    e3[...] = 0.25 * fold(sum(halves(c3)), False, True)
    coefs4 = (d1[0:n4], d1[1 : n4 + 1], d2[...], e3[...])
    g4[...] = 1.0 / packed_diagonal(SIG[4], *coefs4, *FOUR)
    x = f4[...] * g4[...] * (1.0 / THETA)
    ua[1 : n4 + 1] = x
    wrap(ua, n4)
    st[...] = x
    src, dst = ua, ub
    for keep, gain in factors(4):
        x = src[1 : n4 + 1]
        near = packed_sum(src[0:n4], x, src[2 : n4 + 2], d1[0:n4], d1[1 : n4 + 1], d2[...], e3[...], *FOUR)
        step = keep * st[...] + gain * (g4[...] * (f4[...] + near) - x)
        st[...] = step
        dst[1 : n4 + 1] = x + step
        wrap(dst, n4)
        src, dst = dst, src

    j0 = around(lax.axis_index("wide") // 2 - 1, n3)
    k, j = iota((128, 128), 0), iota((128, 128), 1)
    unfold = (k == 16 * (j // 64) + j % 32 // 2).astype(F32)
    coarse = jnp.concatenate([src[1 + around(around(j0 - 2, n3) // 2 + m, n4)] for m in range(4)], axis=0)
    scr[0:32] = mul(coarse, unfold)
    shifted = lax.rem(around(j0 - 2, n3), 2)
    js = [around(j0 - 2 + m, n3) for m in range(7)]
    v = [u2[1 + js[m]] + scr[pl.ds(pl.multiple_of(8 * ((shifted + m) // 2), 8), 8), :] for m in range(7)]
    v = jnp.stack(v)

    def window(ref, first, count, by=0):
        return jnp.stack([ref[js[m] + by] for m in range(first, first + count)])

    def args(first, count):
        return window(c1, first, count), window(c1, first, count, 1), window(c2, first, count), window(c3, first, count)

    f, g = window(f3, 1, 5), window(g3, 1, 5)
    near = packed_sum(v[0:5], v[1:6], v[2:7], *args(1, 5), *THREE)
    w = v[1:6] + (1.0 / THETA) * (g * (f + near) - v[1:6])
    near = packed_sum(w[0:3], w[1:4], w[2:5], *args(2, 3), *THREE)
    x = w[1:4] + KEEP * (w[1:4] - v[2:5]) + GAIN * (g[1:4] * (f[1:4] + near) - w[1:4])
    x = x.reshape(24, 128)
    for q in range(4):
        fine = mul(x, (k == 32 * q + j % 64 // 2).astype(F32))
        e2[pl.ds(2 * q, 24, stride=8), :] = fine
        e2[pl.ds(2 * q + 1, 24, stride=8), :] = fine


def coarse_post_kernel(e2, win, u2, late, out):
    par = lax.rem(lax.axis_index("wide"), 2)
    odd = par == 1
    late = both_halves(late[...])
    v = [jnp.where(odd, u2[0], late), u2[par], u2[1 + par], u2[2 + par], jnp.where(odd, late, u2[3])]
    v = [v[m] + e2[pl.ds(pl.multiple_of(64 * ((m + par) // 2), 64), 64), :] for m in range(5)]

    def args(m):
        k = m + par
        return win[k], win[4 + k], win[8 + k], win[9 + k], win[13 + k], win[17 + k]

    w = [first_post(v[m + 1], v[m], v[m + 2], *args(m)) for m in range(3)]
    out[...] = second_post(w[1], v[2], w[0], w[2], *args(1))


def pair_kernel(a, b, out):
    out[0] = a[...]
    out[1] = b[...]


def middle_post_kernel(e2, e2sib, far, msg, sib, near, f, g, w1, own, edge, send, fine, c1, v, w):
    n, par = lax.axis_index("narrow"), lax.rem(lax.axis_index("wide"), 2)
    odd = par == 1
    row, col = iota((40, 64), 0), iota((40, 64), 1)
    pick = (col == lax.rem(16 * n + (row + 4) // 2 + 60, 64)).astype(F32)
    lanes = copies_of_lanes(128, 128)
    e2, e2sib, near0, near1 = e2[...], e2sib[...], far[0], far[1]
    for k, (upper, lower) in enumerate(((e2sib, near1), (e2, near0), (near0, e2), (near1, e2sib))):
        fine[k] = mul(mul_left(pick, jnp.where(odd, upper, lower)), lanes)
    c1[0:6] = w1[0:6]
    c1[6] = near[344:384]
    ours = [msg[160 + 40 * p : 200 + 40 * p] for p in range(2)]
    sibs = [sib[160 + 40 * p : 200 + 40 * p] for p in range(2)]
    next_chip = [near[224 + 40 * p : 264 + 40 * p] for p in range(3)]
    upper = sibs + ours + next_chip
    lower = [next_chip[2]] + next_chip[:2] + ours + sibs
    for i in range(7):
        v[i] = jnp.where(odd, upper[i], lower[i]) + fine[(i + 1 - par) // 2]

    def args(i):
        k = i - 1 + par
        return f[k], g[k], c1[k], c1[k + 1], w1[6 + k], w1[12 + k]

    for i in range(1, 6):
        w[i] = first_post(v[i], v[i - 1], v[i + 1], *args(i))
    out = [second_post(w[i], v[i], w[i - 1], w[i + 1], *args(i)) for i in (2, 3, 4)]
    own[0] = jnp.where(odd, out[0], out[1])
    own[1] = jnp.where(odd, out[1], out[2])
    edge[...] = jnp.where(odd, out[2], out[0])
    send[...] = jnp.where(odd, out[0], out[2])


def fine_post_kernel(e1, edge, other, far, sib, f, c1, c2, c3, g, u2, out, v, w, scr):
    below, above = sides(edge, other)
    x = jnp.concatenate([below(...), e1[0], e1[1], above(...)], axis=0)
    below, above = sides(far, sib)
    for half in range(2):
        here = slice(128 * half, 128 * half + 128)
        row, col = iota((128, 128), 0), iota((128, 128), 1)
        fine = mul(x, (row == 64 * half + col // 2).astype(F32))
        scr[pl.ds(0, 160, stride=2), :] = fine
        scr[pl.ds(1, 160, stride=2), :] = fine
        for k, read in ((0, below), (7, above)):
            at = 80 * (k // 2)
            v[k, 0:40, here] = read(4 + half) + scr[at : at + 40, :]
            v[k, 40:80, here] = read(6 + half) + scr[at + 40 : at + 80, :]
        for k in range(1, 7):
            at = 80 * (k // 2)
            v[k, :, here] = u2[k, :, here] + scr[at : at + 80, :]

    def post1(q, carry):
        def chunk(r0, n):
            here = pl.ds(r0, CHUNK)
            x, near = near_chunk(v, q + 1, c1, c2, c3, q, r0, n)
            w[q + 1, here, :] = x + (1.0 / THETA) * (g[q, here, :] * (f[q, here, :] + near) - x)

        chunked(80, chunk)
        return carry

    lax.fori_loop(0, 6, post1, 0)

    def post2(q, carry):
        for r0 in range(8, 72, CHUNK):
            here = pl.ds(r0, CHUNK)
            x, near = near_chunk(w, q + 1, c1, c2, c3, q, r0, 80)
            step = KEEP * (x - v[q + 1, here, :]) + GAIN * (g[q, here, :] * (f[q, here, :] + near) - x)
            out[q - 1, pl.ds(r0 - 8, CHUNK), :] = x + step
        return carry

    lax.fori_loop(1, 5, post2, 0)


def shift(x, axis, by):
    count = lax.axis_size(axis)
    return lax.ppermute(x, axis, [(i, (i + by) % count) for i in range(count)])


def sibling(x):
    return lax.ppermute(x, "wide", [(i, i ^ 1) for i in range(lax.axis_size("wide"))])


def across(x):
    count = lax.axis_size("wide")
    return lax.ppermute(x, "wide", [(i, (i + 1 if i % 2 else i - 1) % count) for i in range(count)])


def body(source, coef_first, coef_second, coef_third):
    wide = lax.axis_size("wide")
    n3, n4 = wide // 2, wide // 4
    big = (80, 256)
    inputs = (source, coef_first, coef_second, coef_third)

    up, down = call(
        start_kernel,
        [(16, 8, 256), (16, 8, 256)],
        [pltpu.SemaphoreType.DMA((8,))],
        {k: pltpu.HBM for k in range(4)},
        limit=60,
    )(*inputs)
    low, high = shift(up, "narrow", 1), shift(down, "narrow", -1)

    own, coef1, far, sib = call(
        pad_kernel, [(16,) + big, (6, 40, 128), (600, 256), (600, 256)], [(2,) + big, (160, 128)]
    )(jnp.concatenate(inputs, axis=0), low, high)
    far, sib = across(far), sibling(sib)

    f, c1, c2, c3, g, u2, w1, out_far, out_sib, _ = call(
        fine_pre_kernel,
        [(6,) + big, (7,) + big, (6,) + big, (6,) + big, (6,) + big, (8,) + big]
        + [(18, 40, 128), (8, 40, 128), (8, 40, 128), (2, 40, 128)],
        [(8,) + big, (4,) + big, (160, 128)],
    )(own, coef1, far, sib)
    far1, sib1 = across(out_far), sibling(out_sib)
    (coefs,) = call(coarse_coef_kernel, [(32, 128)], [(80, 128)])(w1)

    six = (6, 40, 128)
    f1w, g1w, u2m, f2, up, down = call(
        middle_pre_kernel, [six, six, six, (40, 128), (56, 128), (56, 128)], [six, (40, 128)]
    )(out_far, far1, sib1, w1, coefs)
    low, high, far = shift(up, "narrow", 1), shift(down, "narrow", -1), shift(f2, "narrow", 2)

    own2, msg = call(coarse_start_kernel, [(6, 64, 128), (240, 128)])(f2, low, high, far, u2m)
    sib = sibling(msg)
    (swap,) = call(coarse_swap_kernel, [(384, 128)])(own2, msg, sib, w1)
    near = across(swap)
    (tiles,) = call(coarse_tiles_kernel, [(3, 8, 128)], [(64, 128)])(msg, sib)
    near, tiles = lax.optimization_barrier((near, tiles))
    other = sibling(near)
    w2, u2w, late = call(
        coarse_pre_kernel, [(21, 64, 128), (4, 64, 128), (32, 128)], [(6, 64, 128)]
    )(own2, sib, near, other)
    (send,) = call(coarse_send_kernel, [(n3, 2, 8, 128)], [(64, 128)])(w2, u2w, tiles)
    cores = [[k for k in range(wide) if k % 2 == c] for c in range(2)]
    parts = lax.all_to_all(send, "wide", split_axis=0, concat_axis=0, tiled=True, axis_index_groups=cores)
    theirs, late = sibling(parts), across(late)

    three, four = (n3, 8, 128), (n4, 8, 128)
    (fine2,) = call(
        bottom_kernel,
        [(192, 128)],
        [three, (n3 + 1, 8, 128), three, three, three, three, (n3 + 2, 8, 128), (n3 + 2, 8, 128), four, four]
        + [(n4 + 1, 8, 128), four, four, four, (n4 + 2, 8, 128), (n4 + 2, 8, 128), four, (32, 128)],
    )(parts, theirs)
    (e2,) = call(coarse_post_kernel, [(64, 128)])(fine2, w2, u2w, late)
    e2sib = sibling(e2)
    (both,) = call(pair_kernel, [(2, 64, 128)])(e2, e2sib)
    far = across(both)

    e1, edge, send = call(
        middle_post_kernel,
        [(2, 40, 128), (40, 128), (40, 128)],
        [(4, 40, 128), (7, 40, 128), (7, 40, 128), (7, 40, 128)],
    )(e2, e2sib, far, msg, sib, near, f1w, g1w, w1)
    other1 = sibling(send)

    (out,) = call(
        fine_post_kernel, [(4, 64, 256)], [(8,) + big, (8,) + big, (320, 128)]
    )(e1, edge, other1, far1, sib1, f, c1, c2, c3, g, u2)
    return out


def solution(mesh):
    spec = P("wide", "narrow", None)
    return jax.shard_map(body, mesh=mesh, in_specs=(spec,) * 4, out_specs=spec, check_vma=False)
```

```python
import functools

import jax
import jax.numpy as jnp
from jax import lax
from jax.experimental import pallas as pl
from jax.experimental.pallas import tpu as pltpu
from jax.sharding import PartitionSpec as P

THETA = 1.125
DELTA = 0.875
RATIO = THETA / DELTA
SIG = [0.0002 * 4.0**level for level in range(5)]
F32 = jnp.float32


def factors(degree):
    rho, out = 1.0 / RATIO, []
    for _ in range(degree - 1):
        new = 1.0 / (2.0 * RATIO - rho)
        out.append((new * rho, 2.0 * new / DELTA))
        rho = new
    return out


(KEEP, GAIN), = factors(2)


def roll(x, by, axis):
    return pltpu.roll(x, by % x.shape[axis], axis)


def gather_sum(below, here, above, c1, h1, c2, c3):
    first = c1 * below + h1 * above
    second = c2 * roll(here, 1, 0) + roll(c2 * here, -1, 0)
    third = c3 * roll(here, 1, 1) + roll(c3 * here, -1, 1)
    return first + second + third


def diagonal(sig, c1, h1, c2, c3):
    return sig + c1 + h1 + c2 + roll(c2, -1, 0) + c3 + roll(c3, -1, 1)


def iota(shape, dim):
    return lax.broadcasted_iota(jnp.int32, shape, dim)


def pairs_of_lanes(lanes, period, even=False):
    row, col = iota((lanes, 128), 0), iota((lanes, 128), 1) % period
    hit = row == 2 * col if even else row // 2 == col
    return hit.astype(F32)


def copies_of_lanes(lanes_in, lanes_out):
    row, col = iota((lanes_in, lanes_out), 0), iota((lanes_in, lanes_out), 1)
    return (row == col // 2).astype(F32)


def pieces(x):
    out = []
    for _ in range(3):
        part = x.astype(jnp.bfloat16)
        out.append(part)
        x = x - part.astype(F32)
    return out


def mul(x, ones):
    ones = ones.astype(jnp.bfloat16)
    high, mid, low = [jnp.dot(part, ones, preferred_element_type=F32) for part in pieces(x)]
    return high + (mid + low)


def mul_left(ones, x):
    ones = ones.astype(jnp.bfloat16)
    high, mid, low = [jnp.dot(ones, part, preferred_element_type=F32) for part in pieces(x)]
    return high + (mid + low)


def pair_rows(x, scratch, start=0, count=None, even=False):
    rows = x.shape[0]
    count = rows // 2 if count is None else count
    scratch[0:rows, :] = x
    first = scratch[pl.ds(start, count, stride=2), :]
    if even:
        return first
    return first + scratch[pl.ds(start + 1, count, stride=2), :]


def twice_rows(x, scratch):
    rows = x.shape[0]
    scratch[pl.ds(0, rows, stride=2), :] = x
    scratch[pl.ds(1, rows, stride=2), :] = x
    return scratch[0 : 2 * rows, :]


def coarse_coefs(planes, scratch, lanes, period, start=0, count=None):
    both = pairs_of_lanes(lanes, period)
    alone = pairs_of_lanes(lanes, period, even=True)
    return (
        0.25 * pair_rows(mul(planes[0], both), scratch, start, count),
        0.25 * pair_rows(mul(planes[1], both), scratch, start, count, even=True),
        0.25 * pair_rows(mul(planes[2], alone), scratch, start, count),
    )


def spread_block(x, block, width):
    lane = iota(x.shape, 1)
    x = jnp.where(lane // width == block, x, 0.0)
    while width < 128:
        x = x + pltpu.roll(x, width, 1)
        width *= 2
    return x


def smooth_two(u1, below, above, f, g, c1, h1, c2, c3):
    near = gather_sum(below, u1, above, c1, h1, c2, c3)
    return (1.0 + KEEP) * u1 + GAIN * (g * (f + near) - u1)


def first_post(v, below, above, f, g, c1, h1, c2, c3):
    near = gather_sum(below, v, above, c1, h1, c2, c3)
    return v + (1.0 / THETA) * (g * (f + near) - v)


def second_post(u, v, below, above, f, g, c1, h1, c2, c3):
    near = gather_sum(below, u, above, c1, h1, c2, c3)
    return u + KEEP * (u - v) + GAIN * (g * (f + near) - u)


def call(kernel, outs, scratch=(), places=(), out_places=(), limit=4):
    places, out_places = dict(places), dict(out_places)

    def run(*args):
        in_specs = [pl.BlockSpec(memory_space=places.get(i, pltpu.VMEM)) for i in range(len(args))]
        return pl.pallas_call(
            kernel,
            out_shape=[jax.ShapeDtypeStruct(s, F32) for s in outs],
            in_specs=in_specs,
            out_specs=[pl.BlockSpec(memory_space=out_places.get(i, pltpu.VMEM)) for i in range(len(outs))],
            scratch_shapes=[pltpu.VMEM(s, F32) if isinstance(s, tuple) else s for s in scratch],
            compiler_params=pltpu.CompilerParams(vmem_limit_bytes=limit * 2**20),
        )(*args)

    return run


def two_blocks(x):
    half = x.shape[0] // 2
    return jnp.where(iota((half, 128), 1) < 64, x[:half], x[half:])


def start_kernel(f, c1, c2, c3, up, down, sems):
    copies = []
    for a, ref in enumerate((f, c1, c2, c3)):
        for k, (out, row) in enumerate(((up, 56), (down, 0))):
            copy = pltpu.make_async_copy(ref.at[:, pl.ds(row, 8), :], out.at[pl.ds(4 * a, 4)], sems.at[2 * a + k])
            copy.start()
            copies.append(copy)
    for copy in copies:
        copy.wait()


def pad_kernel(inner, low, high, own, coef1, out_far, out_sib, first, scr):
    for a in range(16):
        own[a, 0:8] = low[a]
        own[a, 8:72] = inner[a]
        own[a, 72:80] = high[a]
    par = lax.rem(lax.axis_index("wide"), 2)
    for k in range(2):
        diag = diagonal(SIG[0], own[5 + k], own[6 + k], own[9 + k], own[13 + k])
        first[k] = own[1 + k] / diag / THETA
    for out, up in ((out_far, par), (out_sib, 1 - par)):
        for a in range(4):
            out[80 * a : 80 * a + 80] = own[4 * a + 3 * up]
        out[320:400] = own[5]
        out[400:480] = first[up]
    k1 = jnp.concatenate([own[4], own[6]], axis=0)
    k2 = jnp.concatenate([own[8] + own[9], own[10] + own[11]], axis=0)
    k3 = jnp.concatenate([own[12] + own[13], own[14] + own[15]], axis=0)
    coarse = coarse_coefs((k1, k2, k3), scr, 256, 128)
    for a in range(3):
        for p in range(2):
            coef1[2 * a + p] = coarse[a][40 * p : 40 * p + 40]
    for out in (out_far, out_sib):
        for k in range(6):
            row, lane = 480 + 40 * (k // 2), 128 * (k % 2)
            out[row : row + 40, lane : lane + 128] = coef1[k]


def block(index):
    row, lane = 480 + 40 * (index // 2), 128 * (index % 2)
    return slice(row, row + 40), slice(lane, lane + 128)


def sides(far, sib):
    odd = lax.rem(lax.axis_index("wide"), 2) == 1

    def below(*at):
        return jnp.where(odd, sib[at], far[at])

    def above(*at):
        return jnp.where(odd, far[at], sib[at])

    return below, above


CHUNK = 16


def chunked(rows, body):
    for r0 in range(0, rows, CHUNK):
        body(r0, rows)


def near_chunk(u, p, c1, c2, c3, q, r0, rows):
    here = pl.ds(r0, CHUNK)
    x = u[p, here, :]
    if r0 > 0:
        lower = u[p, pl.ds(r0 - 1, CHUNK), :]
    else:
        lower = roll(x, 1, 0)
    if r0 + CHUNK < rows:
        after = pl.ds(r0 + 1, CHUNK)
        upper = c2[q, after, :] * u[p, after, :]
    else:
        upper = roll(c2[q, here, :] * x, -1, 0)
    k3 = c3[q, here, :]
    first = c1[q, here, :] * u[p - 1, here, :] + c1[q + 1, here, :] * u[p + 1, here, :]
    second = c2[q, here, :] * lower + upper
    third = k3 * roll(x, 1, 1) + roll(k3 * x, -1, 1)
    return x, first + second + third


def diag_chunk(c1, c2, c3, q, r0, rows):
    here = pl.ds(r0, CHUNK)
    k2, k3 = c2[q, here, :], c3[q, here, :]
    if r0 + CHUNK < rows:
        h2 = c2[q, pl.ds(r0 + 1, CHUNK), :]
    else:
        h2 = roll(k2, -1, 0)
    return SIG[0] + c1[q, here, :] + c1[q + 1, here, :] + k2 + h2 + k3 + roll(k3, -1, 1)


def fine_pre_kernel(own, coef1, far, sib, f, c1, c2, c3, g, u2, w1, out_far, out_sib, f1, u1, res, scr):
    below, above = sides(far, sib)
    for a, ref in enumerate((f, c1, c2, c3)):
        here = slice(80 * a, 80 * a + 80)
        ref[0] = below(here)
        ref[1:5] = own[4 * a : 4 * a + 4]
        ref[5] = above(here)
    c1[6] = above(slice(320, 400))
    u1[0] = below(slice(400, 480))
    u1[7] = above(slice(400, 480))

    def smooth_first(q, carry):
        def rows(r0, n):
            here = pl.ds(r0, CHUNK)
            inverse = 1.0 / diag_chunk(c1, c2, c3, q, r0, n)
            g[q, here, :] = inverse
            u1[q + 1, here, :] = f[q, here, :] * inverse * (1.0 / THETA)

        chunked(80, rows)
        return carry

    lax.fori_loop(0, 6, smooth_first, 0)

    def smooth_second(q, carry):
        def rows(r0, n):
            here = pl.ds(r0, CHUNK)
            x, near = near_chunk(u1, q + 1, c1, c2, c3, q, r0, n)
            u2[q + 1, here, :] = (1.0 + KEEP) * x + GAIN * (g[q, here, :] * (f[q, here, :] + near) - x)

        chunked(80, rows)
        return carry

    u2[0] = u1[0]
    u2[7] = u1[7]
    lax.fori_loop(0, 6, smooth_second, 0)

    def residual(q, carry):
        def rows(r0, n):
            here = pl.ds(r0, CHUNK)
            x, near = near_chunk(u2, q + 1, c1, c2, c3, q, r0, n)
            res[q - 1, here, :] = f[q, here, :] + near - diag_chunk(c1, c2, c3, q, r0, n) * x

        chunked(80, rows)
        return carry

    lax.fori_loop(1, 5, residual, 0)

    both = pairs_of_lanes(256, 128)
    sums = jnp.concatenate([res[0] + res[1], res[2] + res[3]], axis=0)
    coarse = 0.5 * pair_rows(mul(sums, both), scr)
    f1[0] = coarse[:40]
    f1[1] = coarse[40:]
    for a in range(3):
        for p in range(2):
            w1[6 * a + p] = below(*block(2 * a + p))
            w1[6 * a + 2 + p] = coef1[2 * a + p]
            w1[6 * a + 4 + p] = above(*block(2 * a + p))
    for p in range(2):
        k = p + 2
        inverse = 1.0 / diagonal(SIG[1], w1[k], w1[k + 1], w1[6 + k], w1[12 + k])
        for out in (out_far, out_sib):
            out[p] = f1[p]
            out[2 + p] = inverse
    par = lax.rem(lax.axis_index("wide"), 2)
    for out, plane in ((out_far, 3 + par), (out_sib, 4 - par)):
        out[4] = u2[plane, 0:40, 0:128]
        out[5] = u2[plane, 0:40, 128:256]
        out[6] = u2[plane, 40:80, 0:128]
        out[7] = u2[plane, 40:80, 128:256]


def coarse_coef_kernel(w1, out, scr):
    k1 = jnp.concatenate([w1[2], w1[4]], axis=0)
    k2, k3 = w1[8] + w1[9], w1[14] + w1[15]
    both, alone = pairs_of_lanes(128, 64), pairs_of_lanes(128, 64, even=True)
    k1 = 0.25 * pair_rows(mul(k1, both), scr)
    k2 = 0.25 * pair_rows(mul(k2, both), scr, even=True)
    k3 = 0.25 * pair_rows(mul(k3, alone), scr)
    for k, x in enumerate((k1[2:18], k1[22:38], k2[2:18], k3[2:18])):
        out[8 * k : 8 * k + 8] = two_blocks(x)


def middle_pre_kernel(own, far, sib, w1, coefs, f, g, u2, f2, up, down, u1, scr):
    below, above = sides(far, sib)
    for k, read in enumerate((below, own.__getitem__, above)):
        for p in range(2):
            f[2 * k + p] = read(p)
            g[2 * k + p] = read(2 + p)
    for p in range(6):
        u1[p] = f[p] * g[p] * (1.0 / THETA)
    u2[0] = u1[0]
    u2[5] = u1[5]
    for p in range(1, 5):
        u2[p] = smooth_two(u1[p], u1[p - 1], u1[p + 1], f[p], g[p], w1[p], w1[p + 1], w1[6 + p], w1[12 + p])
    total = 0.0
    for p in (2, 3):
        k1, h1, k2, k3 = w1[p], w1[p + 1], w1[6 + p], w1[12 + p]
        near = gather_sum(u2[p - 1], u2[p], u2[p + 1], k1, h1, k2, k3)
        total = total + (f[p] + near - diagonal(SIG[1], k1, h1, k2, k3) * u2[p])
    coarse = 0.5 * pair_rows(mul(total, pairs_of_lanes(128, 64)), scr, 4, 16)
    f2[0:8] = two_blocks(coarse)
    f2[8:40] = coefs[...]
    for p in range(2):
        up[40 + 8 * p : 48 + 8 * p] = u2[2 + p, 28:36]
        down[40 + 8 * p : 48 + 8 * p] = u2[2 + p, 4:12]
    up[0:40] = f2[...]
    down[0:40] = f2[...]


def both_halves(x):
    return jnp.concatenate([spread_block(x, 0, 64), spread_block(x, 1, 64)], axis=0)


def coarse_start_kernel(f2, low, high, far, u2fine, own, msg):
    n = lax.axis_index("narrow")
    for piece, by in ((f2, 0), (high, 1), (far, 2), (low, 3)):
        at = pl.multiple_of(16 * lax.rem(n + by, 4), 16)
        for k in range(5):
            own[k, pl.ds(at, 16), :] = both_halves(piece[8 * k : 8 * k + 8])
    own[5] = 1.0 / diagonal(SIG[2], own[1], own[2], own[3], own[4])
    for k, plane in enumerate((0, 5, 1, 3, 4)):
        msg[32 * k : 32 * k + 32] = two_blocks(own[plane])
    for p in range(2):
        at = 160 + 40 * p
        msg[at : at + 40] = u2fine[2 + p]
        msg[at : at + 4] = low[44 + 8 * p : 48 + 8 * p]
        msg[at + 36 : at + 40] = high[40 + 8 * p : 44 + 8 * p]


def coarse_tiles_kernel(msg, sib, tiles, scr):
    odd = lax.rem(lax.axis_index("wide"), 2) == 1
    for a in range(3):
        here = slice(64 + 32 * a, 96 + 32 * a)
        x = jnp.where(odd, sib[here], msg[here]) if a == 0 else msg[here] + sib[here]
        scr[...] = 0.25 * mul(both_halves(x), pairs_of_lanes(128, 32, even=a == 2))
        tiles[a] = tile_of(scr, a == 1)


def tile_of(scr, even=False):
    block = iota((8, 128), 1) // 32
    packed = 0.0
    for q in range(4):
        part = scr[pl.ds(2 * q, 8, stride=8), :]
        if not even:
            part = part + scr[pl.ds(2 * q + 1, 8, stride=8), :]
        packed = jnp.where(block == q, part, packed)
    return packed


def coarse_swap_kernel(own, msg, sib, w1, out):
    out[0:160] = msg[0:160]
    out[160:192] = sib[0:32] * sib[32:64] * (1.0 / THETA)
    out[192:224] = two_blocks(own[2])
    out[224:304] = msg[160:240]
    par = lax.rem(lax.axis_index("wide"), 2)
    out[304:344] = sib[pl.ds(pl.multiple_of(160 + 40 * par, 8), 40), :]
    out[344:384] = w1[4]


def coarse_pre_kernel(own, sib, near, other, w, u2, late, u1):
    odd = lax.rem(lax.axis_index("wide"), 2) == 1

    def below(k):
        here = slice(32 * k, 32 * k + 32)
        return both_halves(jnp.where(odd, other[here], near[here]))

    def above(k):
        here = slice(32 * k, 32 * k + 32)
        return both_halves(jnp.where(odd, near[here], other[here]))

    for a, (base, plane) in enumerate(((0, 0), (4, 5), (8, 1), (13, 3), (17, 4))):
        mine, theirs = own[plane], both_halves(sib[32 * a : 32 * a + 32])
        w[base] = below(a)
        w[base + 1] = jnp.where(odd, theirs, mine)
        w[base + 2] = jnp.where(odd, mine, theirs)
        w[base + 3] = above(a)
    w[12] = above(6)
    u1[0] = below(5)
    u1[5] = above(5)
    for k in range(4):
        u1[k + 1] = w[k] * w[4 + k] * (1.0 / THETA)
    for k in range(4):
        u2[k] = smooth_two(u1[k + 1], u1[k], u1[k + 2], w[k], w[4 + k], w[8 + k], w[9 + k], w[13 + k], w[17 + k])
    late[...] = two_blocks(jnp.where(odd, u2[1], u2[2]))


def coarse_send_kernel(w, u2, tiles, send, scr):
    odd = lax.rem(lax.axis_index("wide"), 2) == 1
    total = 0.0
    for k in (1, 2):
        args = (w[8 + k], w[9 + k], w[13 + k], w[17 + k])
        near = gather_sum(u2[k - 1], u2[k], u2[k + 1], *args)
        total = total + (w[k] + near - diagonal(SIG[2], *args) * u2[k])
    scr[...] = 0.5 * mul(total, pairs_of_lanes(128, 32))
    first = jnp.where(odd, tiles[1], tile_of(scr))
    second = jnp.where(odd, tiles[2], tiles[0])
    for k in range(send.shape[0]):
        send[k, 0] = first
        send[k, 1] = second


def packed_sum(below, x, above, c1, h1, c2, c3, width, blocks):
    lane = iota(x.shape, 2)
    block, inner = lane // width % blocks, lane % width

    def second_down(x):
        x = pltpu.roll(x, width, 2)
        return jnp.where(block == 0, pltpu.roll(x, 1, 1), x)

    def second_up(x):
        x = pltpu.roll(x, 128 - width, 2)
        return jnp.where(block == blocks - 1, pltpu.roll(x, 7, 1), x)

    def third_down(x):
        return jnp.where(inner == 0, pltpu.roll(x, 129 - width, 2), pltpu.roll(x, 1, 2))

    def third_up(x):
        return jnp.where(inner == width - 1, pltpu.roll(x, width - 1, 2), pltpu.roll(x, 127, 2))

    first = c1 * below + h1 * above
    second = c2 * second_down(x) + second_up(c2 * x)
    third = c3 * third_down(x) + third_up(c3 * x)
    return first + second + third


def packed_diagonal(sig, c1, h1, c2, c3, width, blocks):
    lane = iota(c1.shape, 2)
    block, inner = lane // width % blocks, lane % width
    h2 = pltpu.roll(c2, 128 - width, 2)
    h2 = jnp.where(block == blocks - 1, pltpu.roll(h2, 7, 1), h2)
    h3 = jnp.where(inner == width - 1, pltpu.roll(c3, width - 1, 2), pltpu.roll(c3, 127, 2))
    return sig + c1 + h1 + c2 + h2 + c3 + h3


def fold_matrix(even2=False, even3=False):
    k, j = iota((128, 128), 0), iota((128, 128), 1)
    k2, k3, j2, j3 = k // 32, k % 32, j // 16 % 2, j % 16
    hit2 = k2 == 2 * j2 if even2 else k2 // 2 == j2
    hit3 = k3 == 2 * j3 if even3 else k3 // 2 == j3
    return (hit2 & hit3).astype(F32)


def wrap(ref, count):
    ref[0] = ref[count]
    ref[count + 1] = ref[1]


def around(j, n):
    return lax.rem(j + n, n)


STEP = 32
THREE, FOUR = (32, 4), (16, 2)


def bottom_kernel(mine, theirs, e2,
                  f3, c1, c2, c3, d3, g3, u1, u2, res, f4, d1, d2, e3, g4, ua, ub, st, scr):
    n3, n4 = f3.shape[0], f4.shape[0]

    def loop(body):
        def step(c, carry):
            body(pl.multiple_of(c * STEP, STEP))
            return carry

        lax.fori_loop(0, n3 // STEP, step, 0)

    odd = lax.rem(lax.axis_index("wide"), 2) == 1

    def load(j):
        here = pl.ds(j, STEP)
        a, b, c, d = mine[here, 0], mine[here, 1], theirs[here, 0], theirs[here, 1]
        f3[here] = jnp.where(odd, c, a)
        c1[here] = jnp.where(odd, d, b)
        c2[here] = jnp.where(odd, a, c)
        c3[here] = jnp.where(odd, b, d)

    loop(load)
    c1[n3] = c1[0]

    def start(j):
        here = pl.ds(j, STEP)
        diag = packed_diagonal(SIG[3], c1[here], c1[pl.ds(j + 1, STEP)], c2[here], c3[here], *THREE)
        inverse = 1.0 / diag
        d3[here] = diag
        g3[here] = inverse
        u1[pl.ds(j + 1, STEP)] = f3[here] * inverse * (1.0 / THETA)

    loop(start)
    wrap(u1, n3)

    def near3(u, j):
        here = pl.ds(j, STEP)
        x = u[pl.ds(j + 1, STEP)]
        args = (c1[here], c1[pl.ds(j + 1, STEP)], c2[here], c3[here])
        return here, x, packed_sum(u[here], x, u[pl.ds(j + 2, STEP)], *args, *THREE)

    def pre(j):
        here, x, near = near3(u1, j)
        u2[pl.ds(j + 1, STEP)] = (1.0 + KEEP) * x + GAIN * (g3[here] * (f3[here] + near) - x)

    loop(pre)
    wrap(u2, n3)

    def residual(j):
        here, x, near = near3(u2, j)
        left = (f3[here] + near - d3[here] * x).reshape(STEP // 2, 2, 8, 128)
        res[pl.ds(j // 2, STEP // 2)] = left[:, 0] + left[:, 1]

    loop(residual)

    def fold(x, *even):
        return mul(x.reshape(8 * n4, 128), fold_matrix(*even)).reshape(n4, 8, 128)

    def halves(ref):
        x = ref[0:n3].reshape(n4, 2, 8, 128)
        return x[:, 0], x[:, 1]

    f4[...] = 0.5 * fold(res[...])
    d1[0:n4] = 0.25 * fold(halves(c1)[0])
    d1[n4] = d1[0]
    d2[...] = 0.25 * fold(sum(halves(c2)), True, False)
    e3[...] = 0.25 * fold(sum(halves(c3)), False, True)
    coefs4 = (d1[0:n4], d1[1 : n4 + 1], d2[...], e3[...])
    g4[...] = 1.0 / packed_diagonal(SIG[4], *coefs4, *FOUR)
    x = f4[...] * g4[...] * (1.0 / THETA)
    ua[1 : n4 + 1] = x
    wrap(ua, n4)
    st[...] = x
    src, dst = ua, ub
    for keep, gain in factors(4):
        x = src[1 : n4 + 1]
        near = packed_sum(src[0:n4], x, src[2 : n4 + 2], d1[0:n4], d1[1 : n4 + 1], d2[...], e3[...], *FOUR)
        step = keep * st[...] + gain * (g4[...] * (f4[...] + near) - x)
        st[...] = step
        dst[1 : n4 + 1] = x + step
        wrap(dst, n4)
        src, dst = dst, src

    j0 = around(lax.axis_index("wide") // 2 - 1, n3)
    k, j = iota((128, 128), 0), iota((128, 128), 1)
    unfold = (k == 16 * (j // 64) + j % 32 // 2).astype(F32)
    coarse = jnp.concatenate([src[1 + around(around(j0 - 2, n3) // 2 + m, n4)] for m in range(4)], axis=0)
    scr[0:32] = mul(coarse, unfold)
    shifted = lax.rem(around(j0 - 2, n3), 2)
    js = [around(j0 - 2 + m, n3) for m in range(7)]
    v = [u2[1 + js[m]] + scr[pl.ds(pl.multiple_of(8 * ((shifted + m) // 2), 8), 8), :] for m in range(7)]
    v = jnp.stack(v)

    def window(ref, first, count, by=0):
        return jnp.stack([ref[js[m] + by] for m in range(first, first + count)])

    def args(first, count):
        return window(c1, first, count), window(c1, first, count, 1), window(c2, first, count), window(c3, first, count)

    f, g = window(f3, 1, 5), window(g3, 1, 5)
    near = packed_sum(v[0:5], v[1:6], v[2:7], *args(1, 5), *THREE)
    w = v[1:6] + (1.0 / THETA) * (g * (f + near) - v[1:6])
    near = packed_sum(w[0:3], w[1:4], w[2:5], *args(2, 3), *THREE)
    x = w[1:4] + KEEP * (w[1:4] - v[2:5]) + GAIN * (g[1:4] * (f[1:4] + near) - w[1:4])
    x = x.reshape(24, 128)
    for q in range(4):
        fine = mul(x, (k == 32 * q + j % 64 // 2).astype(F32))
        e2[pl.ds(2 * q, 24, stride=8), :] = fine
        e2[pl.ds(2 * q + 1, 24, stride=8), :] = fine


def coarse_post_kernel(e2, win, u2, late, out):
    par = lax.rem(lax.axis_index("wide"), 2)
    odd = par == 1
    late = both_halves(late[...])
    v = [jnp.where(odd, u2[0], late), u2[par], u2[1 + par], u2[2 + par], jnp.where(odd, late, u2[3])]
    v = [v[m] + e2[pl.ds(pl.multiple_of(64 * ((m + par) // 2), 64), 64), :] for m in range(5)]

    def args(m):
        k = m + par
        return win[k], win[4 + k], win[8 + k], win[9 + k], win[13 + k], win[17 + k]

    w = [first_post(v[m + 1], v[m], v[m + 2], *args(m)) for m in range(3)]
    out[...] = second_post(w[1], v[2], w[0], w[2], *args(1))


def pair_kernel(a, b, out):
    out[0] = a[...]
    out[1] = b[...]


def middle_post_kernel(e2, e2sib, far, msg, sib, near, f, g, w1, own, edge, send, fine, c1, v, w):
    n, par = lax.axis_index("narrow"), lax.rem(lax.axis_index("wide"), 2)
    odd = par == 1
    row, col = iota((40, 64), 0), iota((40, 64), 1)
    pick = (col == lax.rem(16 * n + (row + 4) // 2 + 60, 64)).astype(F32)
    lanes = copies_of_lanes(128, 128)
    e2, e2sib, near0, near1 = e2[...], e2sib[...], far[0], far[1]
    for k, (upper, lower) in enumerate(((e2sib, near1), (e2, near0), (near0, e2), (near1, e2sib))):
        fine[k] = mul(mul_left(pick, jnp.where(odd, upper, lower)), lanes)
    c1[0:6] = w1[0:6]
    c1[6] = near[344:384]
    ours = [msg[160 + 40 * p : 200 + 40 * p] for p in range(2)]
    sibs = [sib[160 + 40 * p : 200 + 40 * p] for p in range(2)]
    next_chip = [near[224 + 40 * p : 264 + 40 * p] for p in range(3)]
    upper = sibs + ours + next_chip
    lower = [next_chip[2]] + next_chip[:2] + ours + sibs
    for i in range(7):
        v[i] = jnp.where(odd, upper[i], lower[i]) + fine[(i + 1 - par) // 2]

    def args(i):
        k = i - 1 + par
        return f[k], g[k], c1[k], c1[k + 1], w1[6 + k], w1[12 + k]

    for i in range(1, 6):
        w[i] = first_post(v[i], v[i - 1], v[i + 1], *args(i))
    out = [second_post(w[i], v[i], w[i - 1], w[i + 1], *args(i)) for i in (2, 3, 4)]
    own[0] = jnp.where(odd, out[0], out[1])
    own[1] = jnp.where(odd, out[1], out[2])
    edge[...] = jnp.where(odd, out[2], out[0])
    send[...] = jnp.where(odd, out[0], out[2])


def fine_post_kernel(e1, edge, other, far, sib, f, c1, c2, c3, g, u2, out, v, w, scr):
    below, above = sides(edge, other)
    x = jnp.concatenate([below(...), e1[0], e1[1], above(...)], axis=0)
    below, above = sides(far, sib)
    for half in range(2):
        here = slice(128 * half, 128 * half + 128)
        row, col = iota((128, 128), 0), iota((128, 128), 1)
        fine = mul(x, (row == 64 * half + col // 2).astype(F32))
        scr[pl.ds(0, 160, stride=2), :] = fine
        scr[pl.ds(1, 160, stride=2), :] = fine
        for k, read in ((0, below), (7, above)):
            at = 80 * (k // 2)
            v[k, 0:40, here] = read(4 + half) + scr[at : at + 40, :]
            v[k, 40:80, here] = read(6 + half) + scr[at + 40 : at + 80, :]
        for k in range(1, 7):
            at = 80 * (k // 2)
            v[k, :, here] = u2[k, :, here] + scr[at : at + 80, :]

    def post1(q, carry):
        def chunk(r0, n):
            here = pl.ds(r0, CHUNK)
            x, near = near_chunk(v, q + 1, c1, c2, c3, q, r0, n)
            w[q + 1, here, :] = x + (1.0 / THETA) * (g[q, here, :] * (f[q, here, :] + near) - x)

        chunked(80, chunk)
        return carry

    lax.fori_loop(0, 6, post1, 0)

    def post2(q, carry):
        for r0 in range(8, 72, CHUNK):
            here = pl.ds(r0, CHUNK)
            x, near = near_chunk(w, q + 1, c1, c2, c3, q, r0, 80)
            step = KEEP * (x - v[q + 1, here, :]) + GAIN * (g[q, here, :] * (f[q, here, :] + near) - x)
            out[q - 1, pl.ds(r0 - 8, CHUNK), :] = x + step
        return carry

    lax.fori_loop(1, 5, post2, 0)


def shift(x, axis, by):
    count = lax.axis_size(axis)
    return lax.ppermute(x, axis, [(i, (i + by) % count) for i in range(count)])


def sibling(x):
    return lax.ppermute(x, "wide", [(i, i ^ 1) for i in range(lax.axis_size("wide"))])


def across(x):
    count = lax.axis_size("wide")
    return lax.ppermute(x, "wide", [(i, (i + 1 if i % 2 else i - 1) % count) for i in range(count)])


def body(source, coef_first, coef_second, coef_third):
    wide = lax.axis_size("wide")
    n3, n4 = wide // 2, wide // 4
    big = (80, 256)
    inputs = (source, coef_first, coef_second, coef_third)

    up, down = call(
        start_kernel,
        [(16, 8, 256), (16, 8, 256)],
        [pltpu.SemaphoreType.DMA((8,))],
        {k: pltpu.HBM for k in range(4)},
        limit=60,
    )(*inputs)
    low, high = shift(up, "narrow", 1), shift(down, "narrow", -1)

    own, coef1, far, sib = call(
        pad_kernel, [(16,) + big, (6, 40, 128), (600, 256), (600, 256)], [(2,) + big, (160, 128)]
    )(jnp.concatenate(inputs, axis=0), low, high)
    far, sib = across(far), sibling(sib)

    f, c1, c2, c3, g, u2, w1, out_far, out_sib = call(
        fine_pre_kernel,
        [(6,) + big, (7,) + big, (6,) + big, (6,) + big, (6,) + big, (8,) + big]
        + [(18, 40, 128), (8, 40, 128), (8, 40, 128)],
        [(2, 40, 128), (8,) + big, (4,) + big, (160, 128)],
    )(own, coef1, far, sib)
    far1, sib1 = across(out_far), sibling(out_sib)
    (coefs,) = call(coarse_coef_kernel, [(32, 128)], [(80, 128)])(w1)

    six = (6, 40, 128)
    f1w, g1w, u2m, f2, up, down = call(
        middle_pre_kernel, [six, six, six, (40, 128), (56, 128), (56, 128)], [six, (40, 128)]
    )(out_far, far1, sib1, w1, coefs)
    low, high, far = shift(up, "narrow", 1), shift(down, "narrow", -1), shift(f2, "narrow", 2)

    own2, msg = call(coarse_start_kernel, [(6, 64, 128), (240, 128)])(f2, low, high, far, u2m)
    sib = sibling(msg)
    (swap,) = call(coarse_swap_kernel, [(384, 128)])(own2, msg, sib, w1)
    near = across(swap)
    (tiles,) = call(coarse_tiles_kernel, [(3, 8, 128)], [(64, 128)])(msg, sib)
    near, tiles = lax.optimization_barrier((near, tiles))
    other = sibling(near)
    w2, u2w, late = call(
        coarse_pre_kernel, [(21, 64, 128), (4, 64, 128), (32, 128)], [(6, 64, 128)]
    )(own2, sib, near, other)
    (send,) = call(coarse_send_kernel, [(n3, 2, 8, 128)], [(64, 128)])(w2, u2w, tiles)
    cores = [[k for k in range(wide) if k % 2 == c] for c in range(2)]
    parts = lax.all_to_all(send, "wide", split_axis=0, concat_axis=0, tiled=True, axis_index_groups=cores)
    theirs, late = sibling(parts), across(late)

    three, four = (n3, 8, 128), (n4, 8, 128)
    (fine2,) = call(
        bottom_kernel,
        [(192, 128)],
        [three, (n3 + 1, 8, 128), three, three, three, three, (n3 + 2, 8, 128), (n3 + 2, 8, 128), four, four]
        + [(n4 + 1, 8, 128), four, four, four, (n4 + 2, 8, 128), (n4 + 2, 8, 128), four, (32, 128)],
    )(parts, theirs)
    (e2,) = call(coarse_post_kernel, [(64, 128)])(fine2, w2, u2w, late)
    e2sib = sibling(e2)
    (both,) = call(pair_kernel, [(2, 64, 128)])(e2, e2sib)
    far = across(both)

    e1, edge, send = call(
        middle_post_kernel,
        [(2, 40, 128), (40, 128), (40, 128)],
        [(4, 40, 128), (7, 40, 128), (7, 40, 128), (7, 40, 128)],
    )(e2, e2sib, far, msg, sib, near, f1w, g1w, w1)
    other1 = sibling(send)

    (out,) = call(
        fine_post_kernel, [(4, 64, 256)], [(8,) + big, (8,) + big, (320, 128)]
    )(e1, edge, other1, far1, sib1, f, c1, c2, c3, g, u2)
    return out


def solution(mesh):
    spec = P("wide", "narrow", None)
    return jax.shard_map(body, mesh=mesh, in_specs=(spec,) * 4, out_specs=spec, check_vma=False)
```

```python
import functools

import jax
import jax.numpy as jnp
from jax import lax
from jax.experimental import pallas as pl
from jax.experimental.pallas import tpu as pltpu
from jax.sharding import PartitionSpec as P

THETA = 1.125
DELTA = 0.875
RATIO = THETA / DELTA
SIG = [0.0002 * 4.0**level for level in range(5)]
F32 = jnp.float32


def factors(degree):
    rho, out = 1.0 / RATIO, []
    for _ in range(degree - 1):
        new = 1.0 / (2.0 * RATIO - rho)
        out.append((new * rho, 2.0 * new / DELTA))
        rho = new
    return out


(KEEP, GAIN), = factors(2)


def roll(x, by, axis):
    return pltpu.roll(x, by % x.shape[axis], axis)


def gather_sum(below, here, above, c1, h1, c2, c3):
    first = c1 * below + h1 * above
    second = c2 * roll(here, 1, 0) + roll(c2 * here, -1, 0)
    third = c3 * roll(here, 1, 1) + roll(c3 * here, -1, 1)
    return first + second + third


def diagonal(sig, c1, h1, c2, c3):
    return sig + c1 + h1 + c2 + roll(c2, -1, 0) + c3 + roll(c3, -1, 1)


def iota(shape, dim):
    return lax.broadcasted_iota(jnp.int32, shape, dim)


def pairs_of_lanes(lanes, period, even=False):
    row, col = iota((lanes, 128), 0), iota((lanes, 128), 1) % period
    hit = row == 2 * col if even else row // 2 == col
    return hit.astype(F32)


def copies_of_lanes(lanes_in, lanes_out):
    row, col = iota((lanes_in, lanes_out), 0), iota((lanes_in, lanes_out), 1)
    return (row == col // 2).astype(F32)


def pieces(x):
    out = []
    for _ in range(3):
        part = x.astype(jnp.bfloat16)
        out.append(part)
        x = x - part.astype(F32)
    return out


def mul(x, ones):
    ones = ones.astype(jnp.bfloat16)
    high, mid, low = [jnp.dot(part, ones, preferred_element_type=F32) for part in pieces(x)]
    return high + (mid + low)


def mul_left(ones, x):
    ones = ones.astype(jnp.bfloat16)
    high, mid, low = [jnp.dot(ones, part, preferred_element_type=F32) for part in pieces(x)]
    return high + (mid + low)


def pair_rows(x, scratch, start=0, count=None, even=False):
    rows = x.shape[0]
    count = rows // 2 if count is None else count
    scratch[0:rows, :] = x
    first = scratch[pl.ds(start, count, stride=2), :]
    if even:
        return first
    return first + scratch[pl.ds(start + 1, count, stride=2), :]


def twice_rows(x, scratch):
    rows = x.shape[0]
    scratch[pl.ds(0, rows, stride=2), :] = x
    scratch[pl.ds(1, rows, stride=2), :] = x
    return scratch[0 : 2 * rows, :]


def coarse_coefs(planes, scratch, lanes, period, start=0, count=None):
    both = pairs_of_lanes(lanes, period)
    alone = pairs_of_lanes(lanes, period, even=True)
    return (
        0.25 * pair_rows(mul(planes[0], both), scratch, start, count),
        0.25 * pair_rows(mul(planes[1], both), scratch, start, count, even=True),
        0.25 * pair_rows(mul(planes[2], alone), scratch, start, count),
    )


def spread_block(x, block, width):
    lane = iota(x.shape, 1)
    x = jnp.where(lane // width == block, x, 0.0)
    while width < 128:
        x = x + pltpu.roll(x, width, 1)
        width *= 2
    return x


def smooth_two(u1, below, above, f, g, c1, h1, c2, c3):
    near = gather_sum(below, u1, above, c1, h1, c2, c3)
    return (1.0 + KEEP) * u1 + GAIN * (g * (f + near) - u1)


def first_post(v, below, above, f, g, c1, h1, c2, c3):
    near = gather_sum(below, v, above, c1, h1, c2, c3)
    return v + (1.0 / THETA) * (g * (f + near) - v)


def second_post(u, v, below, above, f, g, c1, h1, c2, c3):
    near = gather_sum(below, u, above, c1, h1, c2, c3)
    return u + KEEP * (u - v) + GAIN * (g * (f + near) - u)


def call(kernel, outs, scratch=(), places=(), out_places=(), limit=4):
    places, out_places = dict(places), dict(out_places)

    def run(*args):
        in_specs = [pl.BlockSpec(memory_space=places.get(i, pltpu.VMEM)) for i in range(len(args))]
        return pl.pallas_call(
            kernel,
            out_shape=[jax.ShapeDtypeStruct(s, F32) for s in outs],
            in_specs=in_specs,
            out_specs=[pl.BlockSpec(memory_space=out_places.get(i, pltpu.VMEM)) for i in range(len(outs))],
            scratch_shapes=[pltpu.VMEM(s, F32) if isinstance(s, tuple) else s for s in scratch],
            compiler_params=pltpu.CompilerParams(vmem_limit_bytes=limit * 2**20),
        )(*args)

    return run


def two_blocks(x):
    half = x.shape[0] // 2
    return jnp.where(iota((half, 128), 1) < 64, x[:half], x[half:])


def start_kernel(f, c1, c2, c3, up, down, sems):
    copies = []
    for a, ref in enumerate((f, c1, c2, c3)):
        for k, (out, row) in enumerate(((up, 56), (down, 0))):
            copy = pltpu.make_async_copy(ref.at[:, pl.ds(row, 8), :], out.at[pl.ds(4 * a, 4)], sems.at[2 * a + k])
            copy.start()
            copies.append(copy)
    for copy in copies:
        copy.wait()


def pad_kernel(inner, low, high, own, coef1, out_far, out_sib, first, scr):
    for a in range(16):
        own[a, 0:8] = low[a]
        own[a, 8:72] = inner[a]
        own[a, 72:80] = high[a]
    par = lax.rem(lax.axis_index("wide"), 2)
    for k in range(2):
        diag = diagonal(SIG[0], own[5 + k], own[6 + k], own[9 + k], own[13 + k])
        first[k] = own[1 + k] / diag / THETA
    for out, up in ((out_far, par), (out_sib, 1 - par)):
        for a in range(4):
            out[80 * a : 80 * a + 80] = own[4 * a + 3 * up]
        out[320:400] = own[5]
        out[400:480] = first[up]
    k1 = jnp.concatenate([own[4], own[6]], axis=0)
    k2 = jnp.concatenate([own[8] + own[9], own[10] + own[11]], axis=0)
    k3 = jnp.concatenate([own[12] + own[13], own[14] + own[15]], axis=0)
    coarse = coarse_coefs((k1, k2, k3), scr, 256, 128)
    for a in range(3):
        for p in range(2):
            coef1[2 * a + p] = coarse[a][40 * p : 40 * p + 40]
    for out in (out_far, out_sib):
        for k in range(6):
            row, lane = 480 + 40 * (k // 2), 128 * (k % 2)
            out[row : row + 40, lane : lane + 128] = coef1[k]


def block(index):
    row, lane = 480 + 40 * (index // 2), 128 * (index % 2)
    return slice(row, row + 40), slice(lane, lane + 128)


def sides(far, sib):
    odd = lax.rem(lax.axis_index("wide"), 2) == 1

    def below(*at):
        return jnp.where(odd, sib[at], far[at])

    def above(*at):
        return jnp.where(odd, far[at], sib[at])

    return below, above


CHUNK = 16


def chunked(rows, body):
    for r0 in range(0, rows, CHUNK):
        body(r0, rows)


def near_chunk(u, p, c1, c2, c3, q, r0, rows):
    here = pl.ds(r0, CHUNK)
    x = u[p, here, :]
    if r0 > 0:
        lower = u[p, pl.ds(r0 - 1, CHUNK), :]
    else:
        lower = roll(x, 1, 0)
    if r0 + CHUNK < rows:
        after = pl.ds(r0 + 1, CHUNK)
        upper = c2[q, after, :] * u[p, after, :]
    else:
        upper = roll(c2[q, here, :] * x, -1, 0)
    k3 = c3[q, here, :]
    first = c1[q, here, :] * u[p - 1, here, :] + c1[q + 1, here, :] * u[p + 1, here, :]
    second = c2[q, here, :] * lower + upper
    third = k3 * roll(x, 1, 1) + roll(k3 * x, -1, 1)
    return x, first + second + third


def diag_chunk(c1, c2, c3, q, r0, rows):
    here = pl.ds(r0, CHUNK)
    k2, k3 = c2[q, here, :], c3[q, here, :]
    if r0 + CHUNK < rows:
        h2 = c2[q, pl.ds(r0 + 1, CHUNK), :]
    else:
        h2 = roll(k2, -1, 0)
    return SIG[0] + c1[q, here, :] + c1[q + 1, here, :] + k2 + h2 + k3 + roll(k3, -1, 1)


def fine_pre_kernel(own, coef1, far, sib, f_out, c1_out, c2_out, c3_out, g, u2, w1, out_far, out_sib,
                    f, c1, c2, c3, f1, u1, res, scr, sems):
    below, above = sides(far, sib)
    copies = []
    for a, ref in enumerate((f, c1, c2, c3)):
        here = slice(80 * a, 80 * a + 80)
        ref[0] = below(here)
        ref[1:5] = own[4 * a : 4 * a + 4]
        ref[5] = above(here)
        if a == 1:
            ref[6] = above(slice(320, 400))
        copies.append(pltpu.make_async_copy(ref, (f_out, c1_out, c2_out, c3_out)[a], sems.at[a]))
        copies[a].start()
    u1[0] = below(slice(400, 480))
    u1[7] = above(slice(400, 480))

    def smooth_first(q, carry):
        def rows(r0, n):
            here = pl.ds(r0, CHUNK)
            inverse = 1.0 / diag_chunk(c1, c2, c3, q, r0, n)
            g[q, here, :] = inverse
            u1[q + 1, here, :] = f[q, here, :] * inverse * (1.0 / THETA)

        chunked(80, rows)
        return carry

    lax.fori_loop(0, 6, smooth_first, 0)

    def smooth_second(q, carry):
        def rows(r0, n):
            here = pl.ds(r0, CHUNK)
            x, near = near_chunk(u1, q + 1, c1, c2, c3, q, r0, n)
            u2[q + 1, here, :] = (1.0 + KEEP) * x + GAIN * (g[q, here, :] * (f[q, here, :] + near) - x)

        chunked(80, rows)
        return carry

    u2[0] = u1[0]
    u2[7] = u1[7]
    lax.fori_loop(0, 6, smooth_second, 0)

    def residual(q, carry):
        def rows(r0, n):
            here = pl.ds(r0, CHUNK)
            x, near = near_chunk(u2, q + 1, c1, c2, c3, q, r0, n)
            res[q - 1, here, :] = f[q, here, :] + near - diag_chunk(c1, c2, c3, q, r0, n) * x

        chunked(80, rows)
        return carry

    lax.fori_loop(1, 5, residual, 0)

    both = pairs_of_lanes(256, 128)
    sums = jnp.concatenate([res[0] + res[1], res[2] + res[3]], axis=0)
    coarse = 0.5 * pair_rows(mul(sums, both), scr)
    f1[0] = coarse[:40]
    f1[1] = coarse[40:]
    for a in range(3):
        for p in range(2):
            w1[6 * a + p] = below(*block(2 * a + p))
            w1[6 * a + 2 + p] = coef1[2 * a + p]
            w1[6 * a + 4 + p] = above(*block(2 * a + p))
    for p in range(2):
        k = p + 2
        inverse = 1.0 / diagonal(SIG[1], w1[k], w1[k + 1], w1[6 + k], w1[12 + k])
        for out in (out_far, out_sib):
            out[p] = f1[p]
            out[2 + p] = inverse
    par = lax.rem(lax.axis_index("wide"), 2)
    for out, plane in ((out_far, 3 + par), (out_sib, 4 - par)):
        out[4] = u2[plane, 0:40, 0:128]
        out[5] = u2[plane, 0:40, 128:256]
        out[6] = u2[plane, 40:80, 0:128]
        out[7] = u2[plane, 40:80, 128:256]
    for copy in copies:
        copy.wait()


def coarse_coef_kernel(w1, out, scr):
    k1 = jnp.concatenate([w1[2], w1[4]], axis=0)
    k2, k3 = w1[8] + w1[9], w1[14] + w1[15]
    both, alone = pairs_of_lanes(128, 64), pairs_of_lanes(128, 64, even=True)
    k1 = 0.25 * pair_rows(mul(k1, both), scr)
    k2 = 0.25 * pair_rows(mul(k2, both), scr, even=True)
    k3 = 0.25 * pair_rows(mul(k3, alone), scr)
    for k, x in enumerate((k1[2:18], k1[22:38], k2[2:18], k3[2:18])):
        out[8 * k : 8 * k + 8] = two_blocks(x)


def middle_pre_kernel(own, far, sib, w1, coefs, f, g, u2, f2, up, down, u1, scr):
    below, above = sides(far, sib)
    for k, read in enumerate((below, own.__getitem__, above)):
        for p in range(2):
            f[2 * k + p] = read(p)
            g[2 * k + p] = read(2 + p)
    for p in range(6):
        u1[p] = f[p] * g[p] * (1.0 / THETA)
    u2[0] = u1[0]
    u2[5] = u1[5]
    for p in range(1, 5):
        u2[p] = smooth_two(u1[p], u1[p - 1], u1[p + 1], f[p], g[p], w1[p], w1[p + 1], w1[6 + p], w1[12 + p])
    total = 0.0
    for p in (2, 3):
        k1, h1, k2, k3 = w1[p], w1[p + 1], w1[6 + p], w1[12 + p]
        near = gather_sum(u2[p - 1], u2[p], u2[p + 1], k1, h1, k2, k3)
        total = total + (f[p] + near - diagonal(SIG[1], k1, h1, k2, k3) * u2[p])
    coarse = 0.5 * pair_rows(mul(total, pairs_of_lanes(128, 64)), scr, 4, 16)
    f2[0:8] = two_blocks(coarse)
    f2[8:40] = coefs[...]
    for p in range(2):
        up[40 + 8 * p : 48 + 8 * p] = u2[2 + p, 28:36]
        down[40 + 8 * p : 48 + 8 * p] = u2[2 + p, 4:12]
    up[0:40] = f2[...]
    down[0:40] = f2[...]


def both_halves(x):
    return jnp.concatenate([spread_block(x, 0, 64), spread_block(x, 1, 64)], axis=0)


def coarse_start_kernel(f2, low, high, far, u2fine, own, msg):
    n = lax.axis_index("narrow")
    for piece, by in ((f2, 0), (high, 1), (far, 2), (low, 3)):
        at = pl.multiple_of(16 * lax.rem(n + by, 4), 16)
        for k in range(5):
            own[k, pl.ds(at, 16), :] = both_halves(piece[8 * k : 8 * k + 8])
    own[5] = 1.0 / diagonal(SIG[2], own[1], own[2], own[3], own[4])
    for k, plane in enumerate((0, 5, 1, 3, 4)):
        msg[32 * k : 32 * k + 32] = two_blocks(own[plane])
    for p in range(2):
        at = 160 + 40 * p
        msg[at : at + 40] = u2fine[2 + p]
        msg[at : at + 4] = low[44 + 8 * p : 48 + 8 * p]
        msg[at + 36 : at + 40] = high[40 + 8 * p : 44 + 8 * p]


def coarse_tiles_kernel(msg, sib, tiles, scr):
    odd = lax.rem(lax.axis_index("wide"), 2) == 1
    for a in range(3):
        here = slice(64 + 32 * a, 96 + 32 * a)
        x = jnp.where(odd, sib[here], msg[here]) if a == 0 else msg[here] + sib[here]
        scr[...] = 0.25 * mul(both_halves(x), pairs_of_lanes(128, 32, even=a == 2))
        tiles[a] = tile_of(scr, a == 1)


def tile_of(scr, even=False):
    block = iota((8, 128), 1) // 32
    packed = 0.0
    for q in range(4):
        part = scr[pl.ds(2 * q, 8, stride=8), :]
        if not even:
            part = part + scr[pl.ds(2 * q + 1, 8, stride=8), :]
        packed = jnp.where(block == q, part, packed)
    return packed


def coarse_swap_kernel(own, msg, sib, w1, out):
    out[0:160] = msg[0:160]
    out[160:192] = sib[0:32] * sib[32:64] * (1.0 / THETA)
    out[192:224] = two_blocks(own[2])
    out[224:304] = msg[160:240]
    par = lax.rem(lax.axis_index("wide"), 2)
    out[304:344] = sib[pl.ds(pl.multiple_of(160 + 40 * par, 8), 40), :]
    out[344:384] = w1[4]


def coarse_pre_kernel(own, sib, near, other, w, u2, late, u1):
    odd = lax.rem(lax.axis_index("wide"), 2) == 1

    def below(k):
        here = slice(32 * k, 32 * k + 32)
        return both_halves(jnp.where(odd, other[here], near[here]))

    def above(k):
        here = slice(32 * k, 32 * k + 32)
        return both_halves(jnp.where(odd, near[here], other[here]))

    for a, (base, plane) in enumerate(((0, 0), (4, 5), (8, 1), (13, 3), (17, 4))):
        mine, theirs = own[plane], both_halves(sib[32 * a : 32 * a + 32])
        w[base] = below(a)
        w[base + 1] = jnp.where(odd, theirs, mine)
        w[base + 2] = jnp.where(odd, mine, theirs)
        w[base + 3] = above(a)
    w[12] = above(6)
    u1[0] = below(5)
    u1[5] = above(5)
    for k in range(4):
        u1[k + 1] = w[k] * w[4 + k] * (1.0 / THETA)
    for k in range(4):
        u2[k] = smooth_two(u1[k + 1], u1[k], u1[k + 2], w[k], w[4 + k], w[8 + k], w[9 + k], w[13 + k], w[17 + k])
    late[...] = two_blocks(jnp.where(odd, u2[1], u2[2]))


def coarse_send_kernel(w, u2, tiles, send, scr):
    odd = lax.rem(lax.axis_index("wide"), 2) == 1
    total = 0.0
    for k in (1, 2):
        args = (w[8 + k], w[9 + k], w[13 + k], w[17 + k])
        near = gather_sum(u2[k - 1], u2[k], u2[k + 1], *args)
        total = total + (w[k] + near - diagonal(SIG[2], *args) * u2[k])
    scr[...] = 0.5 * mul(total, pairs_of_lanes(128, 32))
    first = jnp.where(odd, tiles[1], tile_of(scr))
    second = jnp.where(odd, tiles[2], tiles[0])
    for k in range(send.shape[0]):
        send[k, 0] = first
        send[k, 1] = second


def packed_sum(below, x, above, c1, h1, c2, c3, width, blocks):
    lane = iota(x.shape, 2)
    block, inner = lane // width % blocks, lane % width

    def second_down(x):
        x = pltpu.roll(x, width, 2)
        return jnp.where(block == 0, pltpu.roll(x, 1, 1), x)

    def second_up(x):
        x = pltpu.roll(x, 128 - width, 2)
        return jnp.where(block == blocks - 1, pltpu.roll(x, 7, 1), x)

    def third_down(x):
        return jnp.where(inner == 0, pltpu.roll(x, 129 - width, 2), pltpu.roll(x, 1, 2))

    def third_up(x):
        return jnp.where(inner == width - 1, pltpu.roll(x, width - 1, 2), pltpu.roll(x, 127, 2))

    first = c1 * below + h1 * above
    second = c2 * second_down(x) + second_up(c2 * x)
    third = c3 * third_down(x) + third_up(c3 * x)
    return first + second + third


def packed_diagonal(sig, c1, h1, c2, c3, width, blocks):
    lane = iota(c1.shape, 2)
    block, inner = lane // width % blocks, lane % width
    h2 = pltpu.roll(c2, 128 - width, 2)
    h2 = jnp.where(block == blocks - 1, pltpu.roll(h2, 7, 1), h2)
    h3 = jnp.where(inner == width - 1, pltpu.roll(c3, width - 1, 2), pltpu.roll(c3, 127, 2))
    return sig + c1 + h1 + c2 + h2 + c3 + h3


def fold_matrix(even2=False, even3=False):
    k, j = iota((128, 128), 0), iota((128, 128), 1)
    k2, k3, j2, j3 = k // 32, k % 32, j // 16 % 2, j % 16
    hit2 = k2 == 2 * j2 if even2 else k2 // 2 == j2
    hit3 = k3 == 2 * j3 if even3 else k3 // 2 == j3
    return (hit2 & hit3).astype(F32)


def wrap(ref, count):
    ref[0] = ref[count]
    ref[count + 1] = ref[1]


def around(j, n):
    return lax.rem(j + n, n)


STEP = 32
THREE, FOUR = (32, 4), (16, 2)


def bottom_kernel(mine, theirs, e2,
                  f3, c1, c2, c3, d3, g3, u1, u2, res, f4, d1, d2, e3, g4, ua, ub, st, scr):
    n3, n4 = f3.shape[0], f4.shape[0]

    def loop(body):
        def step(c, carry):
            body(pl.multiple_of(c * STEP, STEP))
            return carry

        lax.fori_loop(0, n3 // STEP, step, 0)

    odd = lax.rem(lax.axis_index("wide"), 2) == 1

    def load(j):
        here = pl.ds(j, STEP)
        a, b, c, d = mine[here, 0], mine[here, 1], theirs[here, 0], theirs[here, 1]
        f3[here] = jnp.where(odd, c, a)
        c1[here] = jnp.where(odd, d, b)
        c2[here] = jnp.where(odd, a, c)
        c3[here] = jnp.where(odd, b, d)

    loop(load)
    c1[n3] = c1[0]

    def start(j):
        here = pl.ds(j, STEP)
        diag = packed_diagonal(SIG[3], c1[here], c1[pl.ds(j + 1, STEP)], c2[here], c3[here], *THREE)
        inverse = 1.0 / diag
        d3[here] = diag
        g3[here] = inverse
        u1[pl.ds(j + 1, STEP)] = f3[here] * inverse * (1.0 / THETA)

    loop(start)
    wrap(u1, n3)

    def near3(u, j):
        here = pl.ds(j, STEP)
        x = u[pl.ds(j + 1, STEP)]
        args = (c1[here], c1[pl.ds(j + 1, STEP)], c2[here], c3[here])
        return here, x, packed_sum(u[here], x, u[pl.ds(j + 2, STEP)], *args, *THREE)

    def pre(j):
        here, x, near = near3(u1, j)
        u2[pl.ds(j + 1, STEP)] = (1.0 + KEEP) * x + GAIN * (g3[here] * (f3[here] + near) - x)

    loop(pre)
    wrap(u2, n3)

    def residual(j):
        here, x, near = near3(u2, j)
        left = (f3[here] + near - d3[here] * x).reshape(STEP // 2, 2, 8, 128)
        res[pl.ds(j // 2, STEP // 2)] = left[:, 0] + left[:, 1]

    loop(residual)

    def fold(x, *even):
        return mul(x.reshape(8 * n4, 128), fold_matrix(*even)).reshape(n4, 8, 128)

    def halves(ref):
        x = ref[0:n3].reshape(n4, 2, 8, 128)
        return x[:, 0], x[:, 1]

    f4[...] = 0.5 * fold(res[...])
    d1[0:n4] = 0.25 * fold(halves(c1)[0])
    d1[n4] = d1[0]
    d2[...] = 0.25 * fold(sum(halves(c2)), True, False)
    e3[...] = 0.25 * fold(sum(halves(c3)), False, True)
    coefs4 = (d1[0:n4], d1[1 : n4 + 1], d2[...], e3[...])
    g4[...] = 1.0 / packed_diagonal(SIG[4], *coefs4, *FOUR)
    x = f4[...] * g4[...] * (1.0 / THETA)
    ua[1 : n4 + 1] = x
    wrap(ua, n4)
    st[...] = x
    src, dst = ua, ub
    for keep, gain in factors(4):
        x = src[1 : n4 + 1]
        near = packed_sum(src[0:n4], x, src[2 : n4 + 2], d1[0:n4], d1[1 : n4 + 1], d2[...], e3[...], *FOUR)
        step = keep * st[...] + gain * (g4[...] * (f4[...] + near) - x)
        st[...] = step
        dst[1 : n4 + 1] = x + step
        wrap(dst, n4)
        src, dst = dst, src

    j0 = around(lax.axis_index("wide") // 2 - 1, n3)
    k, j = iota((128, 128), 0), iota((128, 128), 1)
    unfold = (k == 16 * (j // 64) + j % 32 // 2).astype(F32)
    coarse = jnp.concatenate([src[1 + around(around(j0 - 2, n3) // 2 + m, n4)] for m in range(4)], axis=0)
    scr[0:32] = mul(coarse, unfold)
    shifted = lax.rem(around(j0 - 2, n3), 2)
    js = [around(j0 - 2 + m, n3) for m in range(7)]
    v = [u2[1 + js[m]] + scr[pl.ds(pl.multiple_of(8 * ((shifted + m) // 2), 8), 8), :] for m in range(7)]
    v = jnp.stack(v)

    def window(ref, first, count, by=0):
        return jnp.stack([ref[js[m] + by] for m in range(first, first + count)])

    def args(first, count):
        return window(c1, first, count), window(c1, first, count, 1), window(c2, first, count), window(c3, first, count)

    f, g = window(f3, 1, 5), window(g3, 1, 5)
    near = packed_sum(v[0:5], v[1:6], v[2:7], *args(1, 5), *THREE)
    w = v[1:6] + (1.0 / THETA) * (g * (f + near) - v[1:6])
    near = packed_sum(w[0:3], w[1:4], w[2:5], *args(2, 3), *THREE)
    x = w[1:4] + KEEP * (w[1:4] - v[2:5]) + GAIN * (g[1:4] * (f[1:4] + near) - w[1:4])
    x = x.reshape(24, 128)
    for q in range(4):
        fine = mul(x, (k == 32 * q + j % 64 // 2).astype(F32))
        e2[pl.ds(2 * q, 24, stride=8), :] = fine
        e2[pl.ds(2 * q + 1, 24, stride=8), :] = fine


def coarse_post_kernel(e2, win, u2, late, late_sib, out):
    below, above = sides(late, late_sib)
    v = [both_halves(below(...)), u2[0], u2[1], u2[2], u2[3], both_halves(above(...))]
    v = [v[m] + e2[64 * (m // 2) : 64 * (m // 2) + 64, :] for m in range(6)]

    def args(k):
        return win[k], win[4 + k], win[8 + k], win[9 + k], win[13 + k], win[17 + k]

    w = [first_post(v[m + 1], v[m], v[m + 2], *args(m)) for m in range(4)]
    for p in range(2):
        out[p] = second_post(w[p + 1], v[p + 2], w[p], w[p + 2], *args(p + 1))


def middle_post_kernel(e2, far, msg, sib, near, f, g, w1, own, edge, send, fine, c1, v, w):
    n, par = lax.axis_index("narrow"), lax.rem(lax.axis_index("wide"), 2)
    odd = par == 1
    row, col = iota((40, 64), 0), iota((40, 64), 1)
    pick = (col == lax.rem(16 * n + (row + 4) // 2 + 60, 64)).astype(F32)
    lanes = copies_of_lanes(128, 128)
    planes = (e2[0], e2[1], far[0], far[1])
    for k in range(4):
        fine[k] = mul(mul_left(pick, jnp.where(odd, planes[k], planes[(k + 2) % 4])), lanes)
    c1[0:6] = w1[0:6]
    c1[6] = near[344:384]
    ours = [msg[160 + 40 * p : 200 + 40 * p] for p in range(2)]
    sibs = [sib[160 + 40 * p : 200 + 40 * p] for p in range(2)]
    next_chip = [near[224 + 40 * p : 264 + 40 * p] for p in range(3)]
    upper = sibs + ours + next_chip
    lower = [next_chip[2]] + next_chip[:2] + ours + sibs
    for i in range(7):
        v[i] = jnp.where(odd, upper[i], lower[i]) + fine[(i + 1 - par) // 2]

    def args(i):
        k = i - 1 + par
        return f[k], g[k], c1[k], c1[k + 1], w1[6 + k], w1[12 + k]

    for i in range(1, 6):
        w[i] = first_post(v[i], v[i - 1], v[i + 1], *args(i))
    out = [second_post(w[i], v[i], w[i - 1], w[i + 1], *args(i)) for i in (2, 3, 4)]
    own[0] = jnp.where(odd, out[0], out[1])
    own[1] = jnp.where(odd, out[1], out[2])
    edge[...] = jnp.where(odd, out[2], out[0])
    send[...] = jnp.where(odd, out[0], out[2])


def fine_post_kernel(e1, edge, other, far, sib, f, c1, c2, c3, g, u2, out, v, w, scr):
    below, above = sides(edge, other)
    x = jnp.concatenate([below(...), e1[0], e1[1], above(...)], axis=0)
    below, above = sides(far, sib)
    for half in range(2):
        here = slice(128 * half, 128 * half + 128)
        row, col = iota((128, 128), 0), iota((128, 128), 1)
        fine = mul(x, (row == 64 * half + col // 2).astype(F32))
        scr[pl.ds(0, 160, stride=2), :] = fine
        scr[pl.ds(1, 160, stride=2), :] = fine
        for k, read in ((0, below), (7, above)):
            at = 80 * (k // 2)
            v[k, 0:40, here] = read(4 + half) + scr[at : at + 40, :]
            v[k, 40:80, here] = read(6 + half) + scr[at + 40 : at + 80, :]
        for k in range(1, 7):
            at = 80 * (k // 2)
            v[k, :, here] = u2[k, :, here] + scr[at : at + 80, :]

    def post1(q, carry):
        def chunk(r0, n):
            here = pl.ds(r0, CHUNK)
            x, near = near_chunk(v, q + 1, c1, c2, c3, q, r0, n)
            w[q + 1, here, :] = x + (1.0 / THETA) * (g[q, here, :] * (f[q, here, :] + near) - x)

        chunked(80, chunk)
        return carry

    lax.fori_loop(0, 6, post1, 0)

    def post2(q, carry):
        for r0 in range(8, 72, CHUNK):
            here = pl.ds(r0, CHUNK)
            x, near = near_chunk(w, q + 1, c1, c2, c3, q, r0, 80)
            step = KEEP * (x - v[q + 1, here, :]) + GAIN * (g[q, here, :] * (f[q, here, :] + near) - x)
            out[q - 1, pl.ds(r0 - 8, CHUNK), :] = x + step
        return carry

    lax.fori_loop(1, 5, post2, 0)


def shift(x, axis, by):
    count = lax.axis_size(axis)
    return lax.ppermute(x, axis, [(i, (i + by) % count) for i in range(count)])


def sibling(x):
    return lax.ppermute(x, "wide", [(i, i ^ 1) for i in range(lax.axis_size("wide"))])


def across(x):
    count = lax.axis_size("wide")
    return lax.ppermute(x, "wide", [(i, (i + 1 if i % 2 else i - 1) % count) for i in range(count)])


def body(source, coef_first, coef_second, coef_third):
    wide = lax.axis_size("wide")
    n3, n4 = wide // 2, wide // 4
    big = (80, 256)
    inputs = (source, coef_first, coef_second, coef_third)

    up, down = call(
        start_kernel,
        [(16, 8, 256), (16, 8, 256)],
        [pltpu.SemaphoreType.DMA((8,))],
        {k: pltpu.HBM for k in range(4)},
        limit=60,
    )(*inputs)
    low, high = shift(up, "narrow", 1), shift(down, "narrow", -1)

    own, coef1, far, sib = call(
        pad_kernel, [(16,) + big, (6, 40, 128), (600, 256), (600, 256)], [(2,) + big, (160, 128)]
    )(jnp.concatenate(inputs, axis=0), low, high)
    far, sib = across(far), sibling(sib)

    f, c1, c2, c3, g, u2, w1, out_far, out_sib = call(
        fine_pre_kernel,
        [(6,) + big, (7,) + big, (6,) + big, (6,) + big, (6,) + big, (8,) + big]
        + [(18, 40, 128), (8, 40, 128), (8, 40, 128)],
        [(6,) + big, (7,) + big, (6,) + big, (6,) + big]
        + [(2, 40, 128), (8,) + big, (4,) + big, (160, 128), pltpu.SemaphoreType.DMA((4,))],
        out_places={k: pltpu.HBM for k in range(4)},
        limit=6,
    )(own, coef1, far, sib)
    far1, sib1 = across(out_far), sibling(out_sib)
    (coefs,) = call(coarse_coef_kernel, [(32, 128)], [(80, 128)])(w1)

    six = (6, 40, 128)
    f1w, g1w, u2m, f2, up, down = call(
        middle_pre_kernel, [six, six, six, (40, 128), (56, 128), (56, 128)], [six, (40, 128)]
    )(out_far, far1, sib1, w1, coefs)
    low, high, far = shift(up, "narrow", 1), shift(down, "narrow", -1), shift(f2, "narrow", 2)

    own2, msg = call(coarse_start_kernel, [(6, 64, 128), (240, 128)])(f2, low, high, far, u2m)
    sib = sibling(msg)
    (swap,) = call(coarse_swap_kernel, [(384, 128)])(own2, msg, sib, w1)
    near = across(swap)
    (tiles,) = call(coarse_tiles_kernel, [(3, 8, 128)], [(64, 128)])(msg, sib)
    near, tiles = lax.optimization_barrier((near, tiles))
    other = sibling(near)
    w2, u2w, late = call(
        coarse_pre_kernel, [(21, 64, 128), (4, 64, 128), (32, 128)], [(6, 64, 128)]
    )(own2, sib, near, other)
    (send,) = call(coarse_send_kernel, [(n3, 2, 8, 128)], [(64, 128)])(w2, u2w, tiles)
    late = across(late)
    cores = [[k for k in range(wide) if k % 2 == c] for c in range(2)]
    parts = lax.all_to_all(send, "wide", split_axis=0, concat_axis=0, tiled=True, axis_index_groups=cores)
    parts, late = lax.optimization_barrier((parts, late))
    theirs, late_sib = sibling(parts), sibling(late)

    three, four = (n3, 8, 128), (n4, 8, 128)
    (fine2,) = call(
        bottom_kernel,
        [(192, 128)],
        [three, (n3 + 1, 8, 128), three, three, three, three, (n3 + 2, 8, 128), (n3 + 2, 8, 128), four, four]
        + [(n4 + 1, 8, 128), four, four, four, (n4 + 2, 8, 128), (n4 + 2, 8, 128), four, (32, 128)],
    )(parts, theirs)
    (e2,) = call(coarse_post_kernel, [(2, 64, 128)])(fine2, w2, u2w, late, late_sib)
    far = across(e2)

    e1, edge, send = call(
        middle_post_kernel,
        [(2, 40, 128), (40, 128), (40, 128)],
        [(4, 40, 128), (7, 40, 128), (7, 40, 128), (7, 40, 128)],
    )(e2, far, msg, sib, near, f1w, g1w, w1)
    other1 = sibling(send)

    (out,) = call(
        fine_post_kernel, [(4, 64, 256)], [(8,) + big, (8,) + big, (320, 128)]
    )(e1, edge, other1, far1, sib1, f, c1, c2, c3, g, u2)
    return out


def solution(mesh):
    spec = P("wide", "narrow", None)
    return jax.shard_map(body, mesh=mesh, in_specs=(spec,) * 4, out_specs=spec, check_vma=False)
```

```python
import functools

import jax
import jax.numpy as jnp
from jax import lax
from jax.experimental import pallas as pl
from jax.experimental.pallas import tpu as pltpu
from jax.sharding import PartitionSpec as P

THETA = 1.125
DELTA = 0.875
RATIO = THETA / DELTA
SIG = [0.0002 * 4.0**level for level in range(5)]
F32 = jnp.float32


def factors(degree):
    rho, out = 1.0 / RATIO, []
    for _ in range(degree - 1):
        new = 1.0 / (2.0 * RATIO - rho)
        out.append((new * rho, 2.0 * new / DELTA))
        rho = new
    return out


(KEEP, GAIN), = factors(2)


def roll(x, by, axis):
    return pltpu.roll(x, by % x.shape[axis], axis)


def gather_sum(below, here, above, c1, h1, c2, c3):
    first = c1 * below + h1 * above
    second = c2 * roll(here, 1, 0) + roll(c2 * here, -1, 0)
    third = c3 * roll(here, 1, 1) + roll(c3 * here, -1, 1)
    return first + second + third


def diagonal(sig, c1, h1, c2, c3):
    return sig + c1 + h1 + c2 + roll(c2, -1, 0) + c3 + roll(c3, -1, 1)


def iota(shape, dim):
    return lax.broadcasted_iota(jnp.int32, shape, dim)


def pairs_of_lanes(lanes, period, even=False):
    row, col = iota((lanes, 128), 0), iota((lanes, 128), 1) % period
    hit = row == 2 * col if even else row // 2 == col
    return hit.astype(F32)


def copies_of_lanes(lanes_in, lanes_out):
    row, col = iota((lanes_in, lanes_out), 0), iota((lanes_in, lanes_out), 1)
    return (row == col // 2).astype(F32)


def pieces(x):
    out = []
    for _ in range(3):
        part = x.astype(jnp.bfloat16)
        out.append(part)
        x = x - part.astype(F32)
    return out


def mul(x, ones):
    ones = ones.astype(jnp.bfloat16)
    high, mid, low = [jnp.dot(part, ones, preferred_element_type=F32) for part in pieces(x)]
    return high + (mid + low)


def mul_left(ones, x):
    ones = ones.astype(jnp.bfloat16)
    high, mid, low = [jnp.dot(ones, part, preferred_element_type=F32) for part in pieces(x)]
    return high + (mid + low)


def pair_rows(x, scratch, start=0, count=None, even=False):
    rows = x.shape[0]
    count = rows // 2 if count is None else count
    scratch[0:rows, :] = x
    first = scratch[pl.ds(start, count, stride=2), :]
    if even:
        return first
    return first + scratch[pl.ds(start + 1, count, stride=2), :]


def twice_rows(x, scratch):
    rows = x.shape[0]
    scratch[pl.ds(0, rows, stride=2), :] = x
    scratch[pl.ds(1, rows, stride=2), :] = x
    return scratch[0 : 2 * rows, :]


def coarse_coefs(planes, scratch, lanes, period, start=0, count=None):
    both = pairs_of_lanes(lanes, period)
    alone = pairs_of_lanes(lanes, period, even=True)
    return (
        0.25 * pair_rows(mul(planes[0], both), scratch, start, count),
        0.25 * pair_rows(mul(planes[1], both), scratch, start, count, even=True),
        0.25 * pair_rows(mul(planes[2], alone), scratch, start, count),
    )


def spread_block(x, block, width):
    lane = iota(x.shape, 1)
    x = jnp.where(lane // width == block, x, 0.0)
    while width < 128:
        x = x + pltpu.roll(x, width, 1)
        width *= 2
    return x


def smooth_two(u1, below, above, f, g, c1, h1, c2, c3):
    near = gather_sum(below, u1, above, c1, h1, c2, c3)
    return (1.0 + KEEP) * u1 + GAIN * (g * (f + near) - u1)


def first_post(v, below, above, f, g, c1, h1, c2, c3):
    near = gather_sum(below, v, above, c1, h1, c2, c3)
    return v + (1.0 / THETA) * (g * (f + near) - v)


def second_post(u, v, below, above, f, g, c1, h1, c2, c3):
    near = gather_sum(below, u, above, c1, h1, c2, c3)
    return u + KEEP * (u - v) + GAIN * (g * (f + near) - u)


def call(kernel, outs, scratch=(), places=(), out_places=(), limit=4):
    places, out_places = dict(places), dict(out_places)

    def run(*args):
        in_specs = [pl.BlockSpec(memory_space=places.get(i, pltpu.VMEM)) for i in range(len(args))]
        return pl.pallas_call(
            kernel,
            out_shape=[jax.ShapeDtypeStruct(s, F32) for s in outs],
            in_specs=in_specs,
            out_specs=[pl.BlockSpec(memory_space=out_places.get(i, pltpu.VMEM)) for i in range(len(outs))],
            scratch_shapes=[pltpu.VMEM(s, F32) if isinstance(s, tuple) else s for s in scratch],
            compiler_params=pltpu.CompilerParams(vmem_limit_bytes=limit * 2**20),
        )(*args)

    return run


def two_blocks(x):
    half = x.shape[0] // 2
    return jnp.where(iota((half, 128), 1) < 64, x[:half], x[half:])


def start_kernel(f, c1, c2, c3, up, down, sems):
    copies = []
    for a, ref in enumerate((f, c1, c2, c3)):
        for k, (out, row) in enumerate(((up, 56), (down, 0))):
            copy = pltpu.make_async_copy(ref.at[:, pl.ds(row, 8), :], out.at[pl.ds(4 * a, 4)], sems.at[2 * a + k])
            copy.start()
            copies.append(copy)
    for copy in copies:
        copy.wait()


def pad_kernel(inner, low, high, own, coef1, out_far, out_sib, first, scr):
    for a in range(16):
        own[a, 0:8] = low[a]
        own[a, 8:72] = inner[a]
        own[a, 72:80] = high[a]
    par = lax.rem(lax.axis_index("wide"), 2)
    for k in range(2):
        diag = diagonal(SIG[0], own[5 + k], own[6 + k], own[9 + k], own[13 + k])
        first[k] = own[1 + k] / diag / THETA
    for out, up in ((out_far, par), (out_sib, 1 - par)):
        for a in range(4):
            out[80 * a : 80 * a + 80] = own[4 * a + 3 * up]
        out[320:400] = own[5]
        out[400:480] = first[up]
    k1 = jnp.concatenate([own[4], own[6]], axis=0)
    k2 = jnp.concatenate([own[8] + own[9], own[10] + own[11]], axis=0)
    k3 = jnp.concatenate([own[12] + own[13], own[14] + own[15]], axis=0)
    coarse = coarse_coefs((k1, k2, k3), scr, 256, 128)
    for a in range(3):
        for p in range(2):
            coef1[2 * a + p] = coarse[a][40 * p : 40 * p + 40]
    for out in (out_far, out_sib):
        for k in range(6):
            row, lane = 480 + 40 * (k // 2), 128 * (k % 2)
            out[row : row + 40, lane : lane + 128] = coef1[k]


def block(index):
    row, lane = 480 + 40 * (index // 2), 128 * (index % 2)
    return slice(row, row + 40), slice(lane, lane + 128)


def sides(far, sib):
    odd = lax.rem(lax.axis_index("wide"), 2) == 1

    def below(*at):
        return jnp.where(odd, sib[at], far[at])

    def above(*at):
        return jnp.where(odd, far[at], sib[at])

    return below, above


CHUNK = 16


def chunked(rows, body):
    for r0 in range(0, rows, CHUNK):
        body(r0, rows)


def near_chunk(u, p, c1, c2, c3, q, r0, rows):
    here = pl.ds(r0, CHUNK)
    x = u[p, here, :]
    if r0 > 0:
        lower = u[p, pl.ds(r0 - 1, CHUNK), :]
    else:
        lower = roll(x, 1, 0)
    if r0 + CHUNK < rows:
        after = pl.ds(r0 + 1, CHUNK)
        upper = c2[q, after, :] * u[p, after, :]
    else:
        upper = roll(c2[q, here, :] * x, -1, 0)
    k3 = c3[q, here, :]
    first = c1[q, here, :] * u[p - 1, here, :] + c1[q + 1, here, :] * u[p + 1, here, :]
    second = c2[q, here, :] * lower + upper
    third = k3 * roll(x, 1, 1) + roll(k3 * x, -1, 1)
    return x, first + second + third


def diag_chunk(c1, c2, c3, q, r0, rows):
    here = pl.ds(r0, CHUNK)
    k2, k3 = c2[q, here, :], c3[q, here, :]
    if r0 + CHUNK < rows:
        h2 = c2[q, pl.ds(r0 + 1, CHUNK), :]
    else:
        h2 = roll(k2, -1, 0)
    return SIG[0] + c1[q, here, :] + c1[q + 1, here, :] + k2 + h2 + k3 + roll(k3, -1, 1)


def fine_pre_kernel(own, coef1, far, sib, f, c1, c2, c3, u2, w1, out_far, out_sib, g, f1, u1, res, scr):
    below, above = sides(far, sib)
    for a, ref in enumerate((f, c1, c2, c3)):
        here = slice(80 * a, 80 * a + 80)
        ref[0] = below(here)
        ref[1:5] = own[4 * a : 4 * a + 4]
        ref[5] = above(here)
    c1[6] = above(slice(320, 400))
    u1[0] = below(slice(400, 480))
    u1[7] = above(slice(400, 480))

    def smooth_first(q, carry):
        def rows(r0, n):
            here = pl.ds(r0, CHUNK)
            inverse = 1.0 / diag_chunk(c1, c2, c3, q, r0, n)
            g[q, here, :] = inverse
            u1[q + 1, here, :] = f[q, here, :] * inverse * (1.0 / THETA)

        chunked(80, rows)
        return carry

    lax.fori_loop(0, 6, smooth_first, 0)

    def smooth_second(q, carry):
        def rows(r0, n):
            here = pl.ds(r0, CHUNK)
            x, near = near_chunk(u1, q + 1, c1, c2, c3, q, r0, n)
            u2[q, here, :] = (1.0 + KEEP) * x + GAIN * (g[q, here, :] * (f[q, here, :] + near) - x)

        chunked(80, rows)
        return carry

    lax.fori_loop(0, 6, smooth_second, 0)

    def residual(q, carry):
        def rows(r0, n):
            here = pl.ds(r0, CHUNK)
            x, near = near_chunk(u2, q, c1, c2, c3, q, r0, n)
            res[q - 1, here, :] = f[q, here, :] + near - diag_chunk(c1, c2, c3, q, r0, n) * x

        chunked(80, rows)
        return carry

    lax.fori_loop(1, 5, residual, 0)

    both = pairs_of_lanes(256, 128)
    sums = jnp.concatenate([res[0] + res[1], res[2] + res[3]], axis=0)
    coarse = 0.5 * pair_rows(mul(sums, both), scr)
    f1[0] = coarse[:40]
    f1[1] = coarse[40:]
    for a in range(3):
        for p in range(2):
            w1[6 * a + p] = below(*block(2 * a + p))
            w1[6 * a + 2 + p] = coef1[2 * a + p]
            w1[6 * a + 4 + p] = above(*block(2 * a + p))
    for p in range(2):
        k = p + 2
        inverse = 1.0 / diagonal(SIG[1], w1[k], w1[k + 1], w1[6 + k], w1[12 + k])
        for out in (out_far, out_sib):
            out[p] = f1[p]
            out[2 + p] = inverse
    par = lax.rem(lax.axis_index("wide"), 2)
    for out, plane in ((out_far, 2 + par), (out_sib, 3 - par)):
        out[4] = u2[plane, 0:40, 0:128]
        out[5] = u2[plane, 0:40, 128:256]
        out[6] = u2[plane, 40:80, 0:128]
        out[7] = u2[plane, 40:80, 128:256]


def coarse_coef_kernel(w1, out, scr):
    k1 = jnp.concatenate([w1[2], w1[4]], axis=0)
    k2, k3 = w1[8] + w1[9], w1[14] + w1[15]
    both, alone = pairs_of_lanes(128, 64), pairs_of_lanes(128, 64, even=True)
    k1 = 0.25 * pair_rows(mul(k1, both), scr)
    k2 = 0.25 * pair_rows(mul(k2, both), scr, even=True)
    k3 = 0.25 * pair_rows(mul(k3, alone), scr)
    for k, x in enumerate((k1[2:18], k1[22:38], k2[2:18], k3[2:18])):
        out[8 * k : 8 * k + 8] = two_blocks(x)


def middle_pre_kernel(own, far, sib, w1, coefs, f, g, u2, f2, up, down, outer, u1, scr):
    below, above = sides(far, sib)
    for k, read in enumerate((below, own.__getitem__, above)):
        for p in range(2):
            f[2 * k + p] = read(p)
            g[2 * k + p] = read(2 + p)
    for k, read in enumerate((below, above)):
        outer[k, 0:40, 0:128] = read(4)
        outer[k, 0:40, 128:256] = read(5)
        outer[k, 40:80, 0:128] = read(6)
        outer[k, 40:80, 128:256] = read(7)
    for p in range(6):
        u1[p] = f[p] * g[p] * (1.0 / THETA)
    u2[0] = u1[0]
    u2[5] = u1[5]
    for p in range(1, 5):
        u2[p] = smooth_two(u1[p], u1[p - 1], u1[p + 1], f[p], g[p], w1[p], w1[p + 1], w1[6 + p], w1[12 + p])
    total = 0.0
    for p in (2, 3):
        k1, h1, k2, k3 = w1[p], w1[p + 1], w1[6 + p], w1[12 + p]
        near = gather_sum(u2[p - 1], u2[p], u2[p + 1], k1, h1, k2, k3)
        total = total + (f[p] + near - diagonal(SIG[1], k1, h1, k2, k3) * u2[p])
    coarse = 0.5 * pair_rows(mul(total, pairs_of_lanes(128, 64)), scr, 4, 16)
    f2[0:8] = two_blocks(coarse)
    f2[8:40] = coefs[...]
    for p in range(2):
        up[40 + 8 * p : 48 + 8 * p] = u2[2 + p, 28:36]
        down[40 + 8 * p : 48 + 8 * p] = u2[2 + p, 4:12]
    up[0:40] = f2[...]
    down[0:40] = f2[...]


def both_halves(x):
    return jnp.concatenate([spread_block(x, 0, 64), spread_block(x, 1, 64)], axis=0)


def coarse_start_kernel(f2, low, high, far, u2fine, own, msg):
    n = lax.axis_index("narrow")
    for piece, by in ((f2, 0), (high, 1), (far, 2), (low, 3)):
        at = pl.multiple_of(16 * lax.rem(n + by, 4), 16)
        for k in range(5):
            own[k, pl.ds(at, 16), :] = both_halves(piece[8 * k : 8 * k + 8])
    own[5] = 1.0 / diagonal(SIG[2], own[1], own[2], own[3], own[4])
    for k, plane in enumerate((0, 5, 1, 3, 4)):
        msg[32 * k : 32 * k + 32] = two_blocks(own[plane])
    for p in range(2):
        at = 160 + 40 * p
        msg[at : at + 40] = u2fine[2 + p]
        msg[at : at + 4] = low[44 + 8 * p : 48 + 8 * p]
        msg[at + 36 : at + 40] = high[40 + 8 * p : 44 + 8 * p]


def coarse_tiles_kernel(msg, sib, tiles, scr):
    odd = lax.rem(lax.axis_index("wide"), 2) == 1
    for a in range(3):
        here = slice(64 + 32 * a, 96 + 32 * a)
        x = jnp.where(odd, sib[here], msg[here]) if a == 0 else msg[here] + sib[here]
        scr[...] = 0.25 * mul(both_halves(x), pairs_of_lanes(128, 32, even=a == 2))
        tiles[a] = tile_of(scr, a == 1)


def tile_of(scr, even=False):
    block = iota((8, 128), 1) // 32
    packed = 0.0
    for q in range(4):
        part = scr[pl.ds(2 * q, 8, stride=8), :]
        if not even:
            part = part + scr[pl.ds(2 * q + 1, 8, stride=8), :]
        packed = jnp.where(block == q, part, packed)
    return packed


def coarse_swap_kernel(own, msg, sib, w1, out):
    out[0:160] = msg[0:160]
    out[160:192] = sib[0:32] * sib[32:64] * (1.0 / THETA)
    out[192:224] = two_blocks(own[2])
    out[224:304] = msg[160:240]
    par = lax.rem(lax.axis_index("wide"), 2)
    out[304:344] = sib[pl.ds(pl.multiple_of(160 + 40 * par, 8), 40), :]
    out[344:384] = w1[4]


def coarse_pre_kernel(own, sib, near, other, w, u2, late, u1):
    odd = lax.rem(lax.axis_index("wide"), 2) == 1

    def below(k):
        here = slice(32 * k, 32 * k + 32)
        return both_halves(jnp.where(odd, other[here], near[here]))

    def above(k):
        here = slice(32 * k, 32 * k + 32)
        return both_halves(jnp.where(odd, near[here], other[here]))

    for a, (base, plane) in enumerate(((0, 0), (4, 5), (8, 1), (13, 3), (17, 4))):
        mine, theirs = own[plane], both_halves(sib[32 * a : 32 * a + 32])
        w[base] = below(a)
        w[base + 1] = jnp.where(odd, theirs, mine)
        w[base + 2] = jnp.where(odd, mine, theirs)
        w[base + 3] = above(a)
    w[12] = above(6)
    u1[0] = below(5)
    u1[5] = above(5)
    for k in range(4):
        u1[k + 1] = w[k] * w[4 + k] * (1.0 / THETA)
    for k in range(4):
        u2[k] = smooth_two(u1[k + 1], u1[k], u1[k + 2], w[k], w[4 + k], w[8 + k], w[9 + k], w[13 + k], w[17 + k])
    late[...] = two_blocks(jnp.where(odd, u2[1], u2[2]))


def coarse_send_kernel(w, u2, tiles, send, scr):
    odd = lax.rem(lax.axis_index("wide"), 2) == 1
    total = 0.0
    for k in (1, 2):
        args = (w[8 + k], w[9 + k], w[13 + k], w[17 + k])
        near = gather_sum(u2[k - 1], u2[k], u2[k + 1], *args)
        total = total + (w[k] + near - diagonal(SIG[2], *args) * u2[k])
    scr[...] = 0.5 * mul(total, pairs_of_lanes(128, 32))
    first = jnp.where(odd, tiles[1], tile_of(scr))
    second = jnp.where(odd, tiles[2], tiles[0])
    for k in range(send.shape[0]):
        send[k, 0] = first
        send[k, 1] = second


def packed_sum(below, x, above, c1, h1, c2, c3, width, blocks):
    lane = iota(x.shape, 2)
    block, inner = lane // width % blocks, lane % width

    def second_down(x):
        x = pltpu.roll(x, width, 2)
        return jnp.where(block == 0, pltpu.roll(x, 1, 1), x)

    def second_up(x):
        x = pltpu.roll(x, 128 - width, 2)
        return jnp.where(block == blocks - 1, pltpu.roll(x, 7, 1), x)

    def third_down(x):
        return jnp.where(inner == 0, pltpu.roll(x, 129 - width, 2), pltpu.roll(x, 1, 2))

    def third_up(x):
        return jnp.where(inner == width - 1, pltpu.roll(x, width - 1, 2), pltpu.roll(x, 127, 2))

    first = c1 * below + h1 * above
    second = c2 * second_down(x) + second_up(c2 * x)
    third = c3 * third_down(x) + third_up(c3 * x)
    return first + second + third


def packed_diagonal(sig, c1, h1, c2, c3, width, blocks):
    lane = iota(c1.shape, 2)
    block, inner = lane // width % blocks, lane % width
    h2 = pltpu.roll(c2, 128 - width, 2)
    h2 = jnp.where(block == blocks - 1, pltpu.roll(h2, 7, 1), h2)
    h3 = jnp.where(inner == width - 1, pltpu.roll(c3, width - 1, 2), pltpu.roll(c3, 127, 2))
    return sig + c1 + h1 + c2 + h2 + c3 + h3


def fold_matrix(even2=False, even3=False):
    k, j = iota((128, 128), 0), iota((128, 128), 1)
    k2, k3, j2, j3 = k // 32, k % 32, j // 16 % 2, j % 16
    hit2 = k2 == 2 * j2 if even2 else k2 // 2 == j2
    hit3 = k3 == 2 * j3 if even3 else k3 // 2 == j3
    return (hit2 & hit3).astype(F32)


def wrap(ref, count):
    ref[0] = ref[count]
    ref[count + 1] = ref[1]


def around(j, n):
    return lax.rem(j + n, n)


STEP = 32
THREE, FOUR = (32, 4), (16, 2)


def bottom_kernel(mine, theirs, e2,
                  f3, c1, c2, c3, d3, g3, u1, u2, res, f4, d1, d2, e3, g4, ua, ub, st, scr):
    n3, n4 = f3.shape[0], f4.shape[0]

    def loop(body):
        def step(c, carry):
            body(pl.multiple_of(c * STEP, STEP))
            return carry

        lax.fori_loop(0, n3 // STEP, step, 0)

    odd = lax.rem(lax.axis_index("wide"), 2) == 1

    def load(j):
        here = pl.ds(j, STEP)
        a, b, c, d = mine[here, 0], mine[here, 1], theirs[here, 0], theirs[here, 1]
        f3[here] = jnp.where(odd, c, a)
        c1[here] = jnp.where(odd, d, b)
        c2[here] = jnp.where(odd, a, c)
        c3[here] = jnp.where(odd, b, d)

    loop(load)
    c1[n3] = c1[0]

    def start(j):
        here = pl.ds(j, STEP)
        diag = packed_diagonal(SIG[3], c1[here], c1[pl.ds(j + 1, STEP)], c2[here], c3[here], *THREE)
        inverse = 1.0 / diag
        d3[here] = diag
        g3[here] = inverse
        u1[pl.ds(j + 1, STEP)] = f3[here] * inverse * (1.0 / THETA)

    loop(start)
    wrap(u1, n3)

    def near3(u, j):
        here = pl.ds(j, STEP)
        x = u[pl.ds(j + 1, STEP)]
        args = (c1[here], c1[pl.ds(j + 1, STEP)], c2[here], c3[here])
        return here, x, packed_sum(u[here], x, u[pl.ds(j + 2, STEP)], *args, *THREE)

    def pre(j):
        here, x, near = near3(u1, j)
        u2[pl.ds(j + 1, STEP)] = (1.0 + KEEP) * x + GAIN * (g3[here] * (f3[here] + near) - x)

    loop(pre)
    wrap(u2, n3)

    def residual(j):
        here, x, near = near3(u2, j)
        left = (f3[here] + near - d3[here] * x).reshape(STEP // 2, 2, 8, 128)
        res[pl.ds(j // 2, STEP // 2)] = left[:, 0] + left[:, 1]

    loop(residual)

    def fold(x, *even):
        return mul(x.reshape(8 * n4, 128), fold_matrix(*even)).reshape(n4, 8, 128)

    def halves(ref):
        x = ref[0:n3].reshape(n4, 2, 8, 128)
        return x[:, 0], x[:, 1]

    f4[...] = 0.5 * fold(res[...])
    d1[0:n4] = 0.25 * fold(halves(c1)[0])
    d1[n4] = d1[0]
    d2[...] = 0.25 * fold(sum(halves(c2)), True, False)
    e3[...] = 0.25 * fold(sum(halves(c3)), False, True)
    coefs4 = (d1[0:n4], d1[1 : n4 + 1], d2[...], e3[...])
    g4[...] = 1.0 / packed_diagonal(SIG[4], *coefs4, *FOUR)
    x = f4[...] * g4[...] * (1.0 / THETA)
    ua[1 : n4 + 1] = x
    wrap(ua, n4)
    st[...] = x
    src, dst = ua, ub
    for keep, gain in factors(4):
        x = src[1 : n4 + 1]
        near = packed_sum(src[0:n4], x, src[2 : n4 + 2], d1[0:n4], d1[1 : n4 + 1], d2[...], e3[...], *FOUR)
        step = keep * st[...] + gain * (g4[...] * (f4[...] + near) - x)
        st[...] = step
        dst[1 : n4 + 1] = x + step
        wrap(dst, n4)
        src, dst = dst, src

    j0 = around(lax.axis_index("wide") // 2 - 1, n3)
    k, j = iota((128, 128), 0), iota((128, 128), 1)
    unfold = (k == 16 * (j // 64) + j % 32 // 2).astype(F32)
    coarse = jnp.concatenate([src[1 + around(around(j0 - 2, n3) // 2 + m, n4)] for m in range(4)], axis=0)
    scr[0:32] = mul(coarse, unfold)
    shifted = lax.rem(around(j0 - 2, n3), 2)
    js = [around(j0 - 2 + m, n3) for m in range(7)]
    v = [u2[1 + js[m]] + scr[pl.ds(pl.multiple_of(8 * ((shifted + m) // 2), 8), 8), :] for m in range(7)]
    v = jnp.stack(v)

    def window(ref, first, count, by=0):
        return jnp.stack([ref[js[m] + by] for m in range(first, first + count)])

    def args(first, count):
        return window(c1, first, count), window(c1, first, count, 1), window(c2, first, count), window(c3, first, count)

    f, g = window(f3, 1, 5), window(g3, 1, 5)
    near = packed_sum(v[0:5], v[1:6], v[2:7], *args(1, 5), *THREE)
    w = v[1:6] + (1.0 / THETA) * (g * (f + near) - v[1:6])
    near = packed_sum(w[0:3], w[1:4], w[2:5], *args(2, 3), *THREE)
    x = w[1:4] + KEEP * (w[1:4] - v[2:5]) + GAIN * (g[1:4] * (f[1:4] + near) - w[1:4])
    x = x.reshape(24, 128)
    for q in range(4):
        fine = mul(x, (k == 32 * q + j % 64 // 2).astype(F32))
        e2[pl.ds(2 * q, 24, stride=8), :] = fine
        e2[pl.ds(2 * q + 1, 24, stride=8), :] = fine


def coarse_post_kernel(e2, win, u2, late, late_sib, out):
    below, above = sides(late, late_sib)
    v = [both_halves(below(...)), u2[0], u2[1], u2[2], u2[3], both_halves(above(...))]
    v = [v[m] + e2[64 * (m // 2) : 64 * (m // 2) + 64, :] for m in range(6)]

    def args(k):
        return win[k], win[4 + k], win[8 + k], win[9 + k], win[13 + k], win[17 + k]

    w = [first_post(v[m + 1], v[m], v[m + 2], *args(m)) for m in range(4)]
    for p in range(2):
        out[p] = second_post(w[p + 1], v[p + 2], w[p], w[p + 2], *args(p + 1))


def middle_post_kernel(e2, far, msg, sib, near, f, g, w1, own, edge, send, fine, c1, v, w):
    n, par = lax.axis_index("narrow"), lax.rem(lax.axis_index("wide"), 2)
    odd = par == 1
    row, col = iota((40, 64), 0), iota((40, 64), 1)
    pick = (col == lax.rem(16 * n + (row + 4) // 2 + 60, 64)).astype(F32)
    lanes = copies_of_lanes(128, 128)
    planes = (e2[0], e2[1], far[0], far[1])
    for k in range(4):
        fine[k] = mul(mul_left(pick, jnp.where(odd, planes[k], planes[(k + 2) % 4])), lanes)
    c1[0:6] = w1[0:6]
    c1[6] = near[344:384]
    ours = [msg[160 + 40 * p : 200 + 40 * p] for p in range(2)]
    sibs = [sib[160 + 40 * p : 200 + 40 * p] for p in range(2)]
    next_chip = [near[224 + 40 * p : 264 + 40 * p] for p in range(3)]
    upper = sibs + ours + next_chip
    lower = [next_chip[2]] + next_chip[:2] + ours + sibs
    for i in range(7):
        v[i] = jnp.where(odd, upper[i], lower[i]) + fine[(i + 1 - par) // 2]

    def args(i):
        k = i - 1 + par
        return f[k], g[k], c1[k], c1[k + 1], w1[6 + k], w1[12 + k]

    for i in range(1, 6):
        w[i] = first_post(v[i], v[i - 1], v[i + 1], *args(i))
    out = [second_post(w[i], v[i], w[i - 1], w[i + 1], *args(i)) for i in (2, 3, 4)]
    own[0] = jnp.where(odd, out[0], out[1])
    own[1] = jnp.where(odd, out[1], out[2])
    edge[...] = jnp.where(odd, out[2], out[0])
    send[...] = jnp.where(odd, out[0], out[2])


def fine_post_kernel(e1, edge, other, outer, f, c1, c2, c3, u2, out, g, v, w, scr):
    below, above = sides(edge, other)
    x = jnp.concatenate([below(...), e1[0], e1[1], above(...)], axis=0)
    for half in range(2):
        here = slice(128 * half, 128 * half + 128)
        row, col = iota((128, 128), 0), iota((128, 128), 1)
        fine = mul(x, (row == 64 * half + col // 2).astype(F32))
        scr[pl.ds(0, 160, stride=2), :] = fine
        scr[pl.ds(1, 160, stride=2), :] = fine
        for k in range(8):
            at = 80 * (k // 2)
            base = u2[k - 1, :, here] if 0 < k < 7 else outer[k // 7, :, here]
            v[k, :, here] = base + scr[at : at + 80, :]

    def post1(q, carry):
        def chunk(r0, n):
            here = pl.ds(r0, CHUNK)
            x, near = near_chunk(v, q + 1, c1, c2, c3, q, r0, n)
            inverse = 1.0 / diag_chunk(c1, c2, c3, q, r0, n)
            g[q, here, :] = inverse
            w[q + 1, here, :] = x + (1.0 / THETA) * (inverse * (f[q, here, :] + near) - x)

        chunked(80, chunk)
        return carry

    lax.fori_loop(0, 6, post1, 0)

    def post2(q, carry):
        for r0 in range(8, 72, CHUNK):
            here = pl.ds(r0, CHUNK)
            x, near = near_chunk(w, q + 1, c1, c2, c3, q, r0, 80)
            step = KEEP * (x - v[q + 1, here, :]) + GAIN * (g[q, here, :] * (f[q, here, :] + near) - x)
            out[q - 1, pl.ds(r0 - 8, CHUNK), :] = x + step
        return carry

    lax.fori_loop(1, 5, post2, 0)


def shift(x, axis, by):
    count = lax.axis_size(axis)
    return lax.ppermute(x, axis, [(i, (i + by) % count) for i in range(count)])


def sibling(x):
    return lax.ppermute(x, "wide", [(i, i ^ 1) for i in range(lax.axis_size("wide"))])


def across(x):
    count = lax.axis_size("wide")
    return lax.ppermute(x, "wide", [(i, (i + 1 if i % 2 else i - 1) % count) for i in range(count)])


def body(source, coef_first, coef_second, coef_third):
    wide = lax.axis_size("wide")
    n3, n4 = wide // 2, wide // 4
    big = (80, 256)
    inputs = (source, coef_first, coef_second, coef_third)

    up, down = call(
        start_kernel,
        [(16, 8, 256), (16, 8, 256)],
        [pltpu.SemaphoreType.DMA((8,))],
        {k: pltpu.HBM for k in range(4)},
        limit=60,
    )(*inputs)
    low, high = shift(up, "narrow", 1), shift(down, "narrow", -1)

    own, coef1, far, sib = call(
        pad_kernel, [(16,) + big, (6, 40, 128), (600, 256), (600, 256)], [(2,) + big, (160, 128)]
    )(jnp.concatenate(inputs, axis=0), low, high)
    far, sib = across(far), sibling(sib)

    f, c1, c2, c3, u2, w1, out_far, out_sib = call(
        fine_pre_kernel,
        [(6,) + big, (7,) + big, (6,) + big, (6,) + big, (6,) + big]
        + [(18, 40, 128), (8, 40, 128), (8, 40, 128)],
        [(6,) + big, (2, 40, 128), (8,) + big, (4,) + big, (160, 128)],
    )(own, coef1, far, sib)
    far1, sib1 = across(out_far), sibling(out_sib)
    (coefs,) = call(coarse_coef_kernel, [(32, 128)], [(80, 128)])(w1)

    six = (6, 40, 128)
    f1w, g1w, u2m, f2, up, down, outer = call(
        middle_pre_kernel, [six, six, six, (40, 128), (56, 128), (56, 128), (2,) + big], [six, (40, 128)]
    )(out_far, far1, sib1, w1, coefs)
    low, high, far = shift(up, "narrow", 1), shift(down, "narrow", -1), shift(f2, "narrow", 2)

    own2, msg = call(coarse_start_kernel, [(6, 64, 128), (240, 128)])(f2, low, high, far, u2m)
    sib = sibling(msg)
    (swap,) = call(coarse_swap_kernel, [(384, 128)])(own2, msg, sib, w1)
    near = across(swap)
    (tiles,) = call(coarse_tiles_kernel, [(3, 8, 128)], [(64, 128)])(msg, sib)
    near, tiles = lax.optimization_barrier((near, tiles))
    other = sibling(near)
    w2, u2w, late = call(
        coarse_pre_kernel, [(21, 64, 128), (4, 64, 128), (32, 128)], [(6, 64, 128)]
    )(own2, sib, near, other)
    (send,) = call(coarse_send_kernel, [(n3, 2, 8, 128)], [(64, 128)])(w2, u2w, tiles)
    late = across(late)
    cores = [[k for k in range(wide) if k % 2 == c] for c in range(2)]
    parts = lax.all_to_all(send, "wide", split_axis=0, concat_axis=0, tiled=True, axis_index_groups=cores)
    parts, late = lax.optimization_barrier((parts, late))
    theirs, late_sib = sibling(parts), sibling(late)

    three, four = (n3, 8, 128), (n4, 8, 128)
    (fine2,) = call(
        bottom_kernel,
        [(192, 128)],
        [three, (n3 + 1, 8, 128), three, three, three, three, (n3 + 2, 8, 128), (n3 + 2, 8, 128), four, four]
        + [(n4 + 1, 8, 128), four, four, four, (n4 + 2, 8, 128), (n4 + 2, 8, 128), four, (32, 128)],
    )(parts, theirs)
    (e2,) = call(coarse_post_kernel, [(2, 64, 128)])(fine2, w2, u2w, late, late_sib)
    far = across(e2)

    e1, edge, send = call(
        middle_post_kernel,
        [(2, 40, 128), (40, 128), (40, 128)],
        [(4, 40, 128), (7, 40, 128), (7, 40, 128), (7, 40, 128)],
    )(e2, far, msg, sib, near, f1w, g1w, w1)
    other1 = sibling(send)

    (out,) = call(
        fine_post_kernel, [(4, 64, 256)], [(6,) + big, (8,) + big, (8,) + big, (320, 128)]
    )(e1, edge, other1, outer, f, c1, c2, c3, u2)
    return out


def solution(mesh):
    spec = P("wide", "narrow", None)
    return jax.shard_map(body, mesh=mesh, in_specs=(spec,) * 4, out_specs=spec, check_vma=False)
```

```python
import functools

import jax
import jax.numpy as jnp
from jax import lax
from jax.experimental import pallas as pl
from jax.experimental.pallas import tpu as pltpu
from jax.sharding import PartitionSpec as P

THETA = 1.125
DELTA = 0.875
RATIO = THETA / DELTA
SIG = [0.0002 * 4.0**level for level in range(5)]
F32 = jnp.float32


def factors(degree):
    rho, out = 1.0 / RATIO, []
    for _ in range(degree - 1):
        new = 1.0 / (2.0 * RATIO - rho)
        out.append((new * rho, 2.0 * new / DELTA))
        rho = new
    return out


(KEEP, GAIN), = factors(2)


def roll(x, by, axis):
    return pltpu.roll(x, by % x.shape[axis], axis)


def gather_sum(below, here, above, c1, h1, c2, c3):
    first = c1 * below + h1 * above
    second = c2 * roll(here, 1, 0) + roll(c2 * here, -1, 0)
    third = c3 * roll(here, 1, 1) + roll(c3 * here, -1, 1)
    return first + second + third


def diagonal(sig, c1, h1, c2, c3):
    return sig + c1 + h1 + c2 + roll(c2, -1, 0) + c3 + roll(c3, -1, 1)


def iota(shape, dim):
    return lax.broadcasted_iota(jnp.int32, shape, dim)


def pairs_of_lanes(lanes, period, even=False):
    row, col = iota((lanes, 128), 0), iota((lanes, 128), 1) % period
    hit = row == 2 * col if even else row // 2 == col
    return hit.astype(F32)


def copies_of_lanes(lanes_in, lanes_out):
    row, col = iota((lanes_in, lanes_out), 0), iota((lanes_in, lanes_out), 1)
    return (row == col // 2).astype(F32)


def pieces(x):
    out = []
    for _ in range(3):
        part = x.astype(jnp.bfloat16)
        out.append(part)
        x = x - part.astype(F32)
    return out


def mul(x, ones):
    ones = ones.astype(jnp.bfloat16)
    high, mid, low = [jnp.dot(part, ones, preferred_element_type=F32) for part in pieces(x)]
    return high + (mid + low)


def mul_left(ones, x):
    ones = ones.astype(jnp.bfloat16)
    high, mid, low = [jnp.dot(ones, part, preferred_element_type=F32) for part in pieces(x)]
    return high + (mid + low)


def pair_rows(x, scratch, start=0, count=None, even=False):
    rows = x.shape[0]
    count = rows // 2 if count is None else count
    scratch[0:rows, :] = x
    first = scratch[pl.ds(start, count, stride=2), :]
    if even:
        return first
    return first + scratch[pl.ds(start + 1, count, stride=2), :]


def twice_rows(x, scratch):
    rows = x.shape[0]
    scratch[pl.ds(0, rows, stride=2), :] = x
    scratch[pl.ds(1, rows, stride=2), :] = x
    return scratch[0 : 2 * rows, :]


def coarse_coefs(planes, scratch, lanes, period, start=0, count=None):
    both = pairs_of_lanes(lanes, period)
    alone = pairs_of_lanes(lanes, period, even=True)
    return (
        0.25 * pair_rows(mul(planes[0], both), scratch, start, count),
        0.25 * pair_rows(mul(planes[1], both), scratch, start, count, even=True),
        0.25 * pair_rows(mul(planes[2], alone), scratch, start, count),
    )


def spread_block(x, block, width):
    lane = iota(x.shape, 1)
    x = jnp.where(lane // width == block, x, 0.0)
    while width < 128:
        x = x + pltpu.roll(x, width, 1)
        width *= 2
    return x


def smooth_two(u1, below, above, f, g, c1, h1, c2, c3):
    near = gather_sum(below, u1, above, c1, h1, c2, c3)
    return (1.0 + KEEP) * u1 + GAIN * (g * (f + near) - u1)


def first_post(v, below, above, f, g, c1, h1, c2, c3):
    near = gather_sum(below, v, above, c1, h1, c2, c3)
    return v + (1.0 / THETA) * (g * (f + near) - v)


def second_post(u, v, below, above, f, g, c1, h1, c2, c3):
    near = gather_sum(below, u, above, c1, h1, c2, c3)
    return u + KEEP * (u - v) + GAIN * (g * (f + near) - u)


def call(kernel, outs, scratch=(), places=(), out_places=(), limit=4):
    places, out_places = dict(places), dict(out_places)

    def run(*args):
        in_specs = [pl.BlockSpec(memory_space=places.get(i, pltpu.VMEM)) for i in range(len(args))]
        return pl.pallas_call(
            kernel,
            out_shape=[jax.ShapeDtypeStruct(s, F32) for s in outs],
            in_specs=in_specs,
            out_specs=[pl.BlockSpec(memory_space=out_places.get(i, pltpu.VMEM)) for i in range(len(outs))],
            scratch_shapes=[pltpu.VMEM(s, F32) if isinstance(s, tuple) else s for s in scratch],
            compiler_params=pltpu.CompilerParams(vmem_limit_bytes=limit * 2**20),
        )(*args)

    return run


def two_blocks(x):
    half = x.shape[0] // 2
    return jnp.where(iota((half, 128), 1) < 64, x[:half], x[half:])


def start_kernel(f, c1, c2, c3, up, down, out_far, out_sib, rows, planes, sems):
    par = lax.rem(lax.axis_index("wide"), 2)
    moves = []
    for k, (out, row) in enumerate(((up, 56), (down, 0))):
        for a, ref in enumerate((f, c1, c2, c3)):
            moves.append((ref.at[:, pl.ds(row, 8), :], rows.at[k, pl.ds(4 * a, 4)], out.at[pl.ds(4 * a, 4)]))
    for k, (out, upward) in enumerate(((out_far, par), (out_sib, 1 - par))):
        for a, ref in enumerate((f, c1, c2, c3, c1)):
            plane = 3 * upward if a < 4 else 1
            moves.append((ref.at[pl.ds(plane, 1)], planes.at[k, pl.ds(a, 1)], out.at[pl.ds(a, 1)]))
    first = [pltpu.make_async_copy(src, mid, sems.at[0, k]) for k, (src, mid, _) in enumerate(moves)]
    second = [pltpu.make_async_copy(mid, dst, sems.at[1, k]) for k, (_, mid, dst) in enumerate(moves)]
    for copy in first:
        copy.start()
    for one, two in zip(first, second):
        one.wait()
        two.start()
    for copy in second:
        copy.wait()


def pad_kernel(inner, low, high, own, coef1, out_far, out_sib, first, scr):
    for a in range(16):
        own[a, 0:8] = low[a]
        own[a, 8:72] = inner[a]
        own[a, 72:80] = high[a]
    par = lax.rem(lax.axis_index("wide"), 2)
    for k in range(2):
        diag = diagonal(SIG[0], own[5 + k], own[6 + k], own[9 + k], own[13 + k])
        first[k] = own[1 + k] / diag / THETA
    for out, up in ((out_far, par), (out_sib, 1 - par)):
        for a in range(5):
            plane = 4 * a + 3 * up if a < 4 else 5
            out[16 * a : 16 * a + 8] = own[plane, 0:8]
            out[16 * a + 8 : 16 * a + 16] = own[plane, 72:80]
        out[80:160] = first[up]
    k1 = jnp.concatenate([own[4], own[6]], axis=0)
    k2 = jnp.concatenate([own[8] + own[9], own[10] + own[11]], axis=0)
    k3 = jnp.concatenate([own[12] + own[13], own[14] + own[15]], axis=0)
    coarse = coarse_coefs((k1, k2, k3), scr, 256, 128)
    for a in range(3):
        for p in range(2):
            coef1[2 * a + p] = coarse[a][40 * p : 40 * p + 40]
    for out in (out_far, out_sib):
        for k in range(6):
            row, lane = 160 + 40 * (k // 2), 128 * (k % 2)
            out[row : row + 40, lane : lane + 128] = coef1[k]


def block(index):
    row, lane = 160 + 40 * (index // 2), 128 * (index % 2)
    return slice(row, row + 40), slice(lane, lane + 128)


def sides(far, sib):
    odd = lax.rem(lax.axis_index("wide"), 2) == 1

    def below(*at):
        return jnp.where(odd, sib[at], far[at])

    def above(*at):
        return jnp.where(odd, far[at], sib[at])

    return below, above


CHUNK = 16


def chunked(rows, body):
    for r0 in range(0, rows, CHUNK):
        body(r0, rows)


def near_chunk(u, p, c1, c2, c3, q, r0, rows):
    here = pl.ds(r0, CHUNK)
    x = u[p, here, :]
    if r0 > 0:
        lower = u[p, pl.ds(r0 - 1, CHUNK), :]
    else:
        lower = roll(x, 1, 0)
    if r0 + CHUNK < rows:
        after = pl.ds(r0 + 1, CHUNK)
        upper = c2[q, after, :] * u[p, after, :]
    else:
        upper = roll(c2[q, here, :] * x, -1, 0)
    k3 = c3[q, here, :]
    first = c1[q, here, :] * u[p - 1, here, :] + c1[q + 1, here, :] * u[p + 1, here, :]
    second = c2[q, here, :] * lower + upper
    third = k3 * roll(x, 1, 1) + roll(k3 * x, -1, 1)
    return x, first + second + third


def diag_chunk(c1, c2, c3, q, r0, rows):
    here = pl.ds(r0, CHUNK)
    k2, k3 = c2[q, here, :], c3[q, here, :]
    if r0 + CHUNK < rows:
        h2 = c2[q, pl.ds(r0 + 1, CHUNK), :]
    else:
        h2 = roll(k2, -1, 0)
    return SIG[0] + c1[q, here, :] + c1[q + 1, here, :] + k2 + h2 + k3 + roll(k3, -1, 1)


def fine_pre_kernel(own, coef1, far_raw, sib_raw, far, sib, f, c1, c2, c3, u2, w1, out_far, out_sib, g, f1, u1, res, scr):
    below, above = sides(far, sib)
    below_raw, above_raw = sides(far_raw, sib_raw)
    for a, ref in enumerate((f, c1, c2, c3)):
        ref[1:5] = own[4 * a : 4 * a + 4]
    for a, ref, q, raw, rest in (
        [(a, ref, 0, below_raw, below) for a, ref in enumerate((f, c1, c2, c3))]
        + [(a, ref, 5, above_raw, above) for a, ref in enumerate((f, c1, c2, c3))]
        + [(4, c1, 6, above_raw, above)]
    ):
        ref[q, 0:8] = rest(slice(16 * a, 16 * a + 8))
        ref[q, 8:72] = raw(a)
        ref[q, 72:80] = rest(slice(16 * a + 8, 16 * a + 16))
    u1[0] = below(slice(80, 160))
    u1[7] = above(slice(80, 160))

    def smooth_first(q, carry):
        def rows(r0, n):
            here = pl.ds(r0, CHUNK)
            inverse = 1.0 / diag_chunk(c1, c2, c3, q, r0, n)
            g[q, here, :] = inverse
            u1[q + 1, here, :] = f[q, here, :] * inverse * (1.0 / THETA)

        chunked(80, rows)
        return carry

    lax.fori_loop(0, 6, smooth_first, 0)

    def smooth_second(q, carry):
        def rows(r0, n):
            here = pl.ds(r0, CHUNK)
            x, near = near_chunk(u1, q + 1, c1, c2, c3, q, r0, n)
            u2[q, here, :] = (1.0 + KEEP) * x + GAIN * (g[q, here, :] * (f[q, here, :] + near) - x)

        chunked(80, rows)
        return carry

    lax.fori_loop(0, 6, smooth_second, 0)

    def residual(q, carry):
        def rows(r0, n):
            here = pl.ds(r0, CHUNK)
            x, near = near_chunk(u2, q, c1, c2, c3, q, r0, n)
            res[q - 1, here, :] = f[q, here, :] + near - diag_chunk(c1, c2, c3, q, r0, n) * x

        chunked(80, rows)
        return carry

    lax.fori_loop(1, 5, residual, 0)

    both = pairs_of_lanes(256, 128)
    sums = jnp.concatenate([res[0] + res[1], res[2] + res[3]], axis=0)
    coarse = 0.5 * pair_rows(mul(sums, both), scr)
    f1[0] = coarse[:40]
    f1[1] = coarse[40:]
    for a in range(3):
        for p in range(2):
            w1[6 * a + p] = below(*block(2 * a + p))
            w1[6 * a + 2 + p] = coef1[2 * a + p]
            w1[6 * a + 4 + p] = above(*block(2 * a + p))
    for p in range(2):
        k = p + 2
        inverse = 1.0 / diagonal(SIG[1], w1[k], w1[k + 1], w1[6 + k], w1[12 + k])
        for out in (out_far, out_sib):
            out[p] = f1[p]
            out[2 + p] = inverse
    par = lax.rem(lax.axis_index("wide"), 2)
    for out, plane in ((out_far, 2 + par), (out_sib, 3 - par)):
        out[4] = u2[plane, 0:40, 0:128]
        out[5] = u2[plane, 0:40, 128:256]
        out[6] = u2[plane, 40:80, 0:128]
        out[7] = u2[plane, 40:80, 128:256]


def coarse_coef_kernel(w1, out, scr):
    k1 = jnp.concatenate([w1[2], w1[4]], axis=0)
    k2, k3 = w1[8] + w1[9], w1[14] + w1[15]
    both, alone = pairs_of_lanes(128, 64), pairs_of_lanes(128, 64, even=True)
    k1 = 0.25 * pair_rows(mul(k1, both), scr)
    k2 = 0.25 * pair_rows(mul(k2, both), scr, even=True)
    k3 = 0.25 * pair_rows(mul(k3, alone), scr)
    for k, x in enumerate((k1[2:18], k1[22:38], k2[2:18], k3[2:18])):
        out[8 * k : 8 * k + 8] = two_blocks(x)


def middle_pre_kernel(own, far, sib, w1, coefs, f, g, u2, f2, up, down, outer, u1, scr):
    below, above = sides(far, sib)
    for k, read in enumerate((below, own.__getitem__, above)):
        for p in range(2):
            f[2 * k + p] = read(p)
            g[2 * k + p] = read(2 + p)
    for k, read in enumerate((below, above)):
        outer[k, 0:40, 0:128] = read(4)
        outer[k, 0:40, 128:256] = read(5)
        outer[k, 40:80, 0:128] = read(6)
        outer[k, 40:80, 128:256] = read(7)
    for p in range(6):
        u1[p] = f[p] * g[p] * (1.0 / THETA)
    u2[0] = u1[0]
    u2[5] = u1[5]
    for p in range(1, 5):
        u2[p] = smooth_two(u1[p], u1[p - 1], u1[p + 1], f[p], g[p], w1[p], w1[p + 1], w1[6 + p], w1[12 + p])
    total = 0.0
    for p in (2, 3):
        k1, h1, k2, k3 = w1[p], w1[p + 1], w1[6 + p], w1[12 + p]
        near = gather_sum(u2[p - 1], u2[p], u2[p + 1], k1, h1, k2, k3)
        total = total + (f[p] + near - diagonal(SIG[1], k1, h1, k2, k3) * u2[p])
    coarse = 0.5 * pair_rows(mul(total, pairs_of_lanes(128, 64)), scr, 4, 16)
    f2[0:8] = two_blocks(coarse)
    f2[8:40] = coefs[...]
    for p in range(2):
        up[40 + 8 * p : 48 + 8 * p] = u2[2 + p, 28:36]
        down[40 + 8 * p : 48 + 8 * p] = u2[2 + p, 4:12]
    up[0:40] = f2[...]
    down[0:40] = f2[...]


def both_halves(x):
    return jnp.concatenate([spread_block(x, 0, 64), spread_block(x, 1, 64)], axis=0)


def coarse_start_kernel(f2, low, high, far, u2fine, own, msg):
    n = lax.axis_index("narrow")
    for piece, by in ((f2, 0), (high, 1), (far, 2), (low, 3)):
        at = pl.multiple_of(16 * lax.rem(n + by, 4), 16)
        for k in range(5):
            own[k, pl.ds(at, 16), :] = both_halves(piece[8 * k : 8 * k + 8])
    own[5] = 1.0 / diagonal(SIG[2], own[1], own[2], own[3], own[4])
    for k, plane in enumerate((0, 5, 1, 3, 4)):
        msg[32 * k : 32 * k + 32] = two_blocks(own[plane])
    for p in range(2):
        at = 160 + 40 * p
        msg[at : at + 40] = u2fine[2 + p]
        msg[at : at + 4] = low[44 + 8 * p : 48 + 8 * p]
        msg[at + 36 : at + 40] = high[40 + 8 * p : 44 + 8 * p]


def coarse_tiles_kernel(msg, sib, tiles, scr):
    odd = lax.rem(lax.axis_index("wide"), 2) == 1
    for a in range(3):
        here = slice(64 + 32 * a, 96 + 32 * a)
        x = jnp.where(odd, sib[here], msg[here]) if a == 0 else msg[here] + sib[here]
        scr[...] = 0.25 * mul(both_halves(x), pairs_of_lanes(128, 32, even=a == 2))
        tiles[a] = tile_of(scr, a == 1)


def tile_of(scr, even=False):
    block = iota((8, 128), 1) // 32
    packed = 0.0
    for q in range(4):
        part = scr[pl.ds(2 * q, 8, stride=8), :]
        if not even:
            part = part + scr[pl.ds(2 * q + 1, 8, stride=8), :]
        packed = jnp.where(block == q, part, packed)
    return packed


def coarse_swap_kernel(own, msg, sib, w1, out):
    out[0:160] = msg[0:160]
    out[160:192] = sib[0:32] * sib[32:64] * (1.0 / THETA)
    out[192:224] = two_blocks(own[2])
    out[224:304] = msg[160:240]
    par = lax.rem(lax.axis_index("wide"), 2)
    out[304:344] = sib[pl.ds(pl.multiple_of(160 + 40 * par, 8), 40), :]
    out[344:384] = w1[4]


def coarse_pre_kernel(own, sib, near, other, w, u2, late, u1):
    odd = lax.rem(lax.axis_index("wide"), 2) == 1

    def below(k):
        here = slice(32 * k, 32 * k + 32)
        return both_halves(jnp.where(odd, other[here], near[here]))

    def above(k):
        here = slice(32 * k, 32 * k + 32)
        return both_halves(jnp.where(odd, near[here], other[here]))

    for a, (base, plane) in enumerate(((0, 0), (4, 5), (8, 1), (13, 3), (17, 4))):
        mine, theirs = own[plane], both_halves(sib[32 * a : 32 * a + 32])
        w[base] = below(a)
        w[base + 1] = jnp.where(odd, theirs, mine)
        w[base + 2] = jnp.where(odd, mine, theirs)
        w[base + 3] = above(a)
    w[12] = above(6)
    u1[0] = below(5)
    u1[5] = above(5)
    for k in range(4):
        u1[k + 1] = w[k] * w[4 + k] * (1.0 / THETA)
    for k in range(4):
        u2[k] = smooth_two(u1[k + 1], u1[k], u1[k + 2], w[k], w[4 + k], w[8 + k], w[9 + k], w[13 + k], w[17 + k])
    late[...] = two_blocks(jnp.where(odd, u2[1], u2[2]))


def coarse_send_kernel(w, u2, tiles, send, scr):
    odd = lax.rem(lax.axis_index("wide"), 2) == 1
    total = 0.0
    for k in (1, 2):
        args = (w[8 + k], w[9 + k], w[13 + k], w[17 + k])
        near = gather_sum(u2[k - 1], u2[k], u2[k + 1], *args)
        total = total + (w[k] + near - diagonal(SIG[2], *args) * u2[k])
    scr[...] = 0.5 * mul(total, pairs_of_lanes(128, 32))
    first = jnp.where(odd, tiles[1], tile_of(scr))
    second = jnp.where(odd, tiles[2], tiles[0])
    for k in range(send.shape[0]):
        send[k, 0] = first
        send[k, 1] = second


def packed_sum(below, x, above, c1, h1, c2, c3, width, blocks):
    lane = iota(x.shape, 2)
    block, inner = lane // width % blocks, lane % width

    def second_down(x):
        x = pltpu.roll(x, width, 2)
        return jnp.where(block == 0, pltpu.roll(x, 1, 1), x)

    def second_up(x):
        x = pltpu.roll(x, 128 - width, 2)
        return jnp.where(block == blocks - 1, pltpu.roll(x, 7, 1), x)

    def third_down(x):
        return jnp.where(inner == 0, pltpu.roll(x, 129 - width, 2), pltpu.roll(x, 1, 2))

    def third_up(x):
        return jnp.where(inner == width - 1, pltpu.roll(x, width - 1, 2), pltpu.roll(x, 127, 2))

    first = c1 * below + h1 * above
    second = c2 * second_down(x) + second_up(c2 * x)
    third = c3 * third_down(x) + third_up(c3 * x)
    return first + second + third


def packed_diagonal(sig, c1, h1, c2, c3, width, blocks):
    lane = iota(c1.shape, 2)
    block, inner = lane // width % blocks, lane % width
    h2 = pltpu.roll(c2, 128 - width, 2)
    h2 = jnp.where(block == blocks - 1, pltpu.roll(h2, 7, 1), h2)
    h3 = jnp.where(inner == width - 1, pltpu.roll(c3, width - 1, 2), pltpu.roll(c3, 127, 2))
    return sig + c1 + h1 + c2 + h2 + c3 + h3


def fold_matrix(even2=False, even3=False):
    k, j = iota((128, 128), 0), iota((128, 128), 1)
    k2, k3, j2, j3 = k // 32, k % 32, j // 16 % 2, j % 16
    hit2 = k2 == 2 * j2 if even2 else k2 // 2 == j2
    hit3 = k3 == 2 * j3 if even3 else k3 // 2 == j3
    return (hit2 & hit3).astype(F32)


def wrap(ref, count):
    ref[0] = ref[count]
    ref[count + 1] = ref[1]


def around(j, n):
    return lax.rem(j + n, n)


STEP = 32
THREE, FOUR = (32, 4), (16, 2)


def bottom_kernel(mine, theirs, e2,
                  f3, c1, c2, c3, d3, g3, u1, u2, res, f4, d1, d2, e3, g4, ua, ub, st, scr):
    n3, n4 = f3.shape[0], f4.shape[0]

    def loop(body):
        def step(c, carry):
            body(pl.multiple_of(c * STEP, STEP))
            return carry

        lax.fori_loop(0, n3 // STEP, step, 0)

    odd = lax.rem(lax.axis_index("wide"), 2) == 1

    def load(j):
        here = pl.ds(j, STEP)
        a, b, c, d = mine[here, 0], mine[here, 1], theirs[here, 0], theirs[here, 1]
        f3[here] = jnp.where(odd, c, a)
        c1[here] = jnp.where(odd, d, b)
        c2[here] = jnp.where(odd, a, c)
        c3[here] = jnp.where(odd, b, d)

    loop(load)
    c1[n3] = c1[0]

    def start(j):
        here = pl.ds(j, STEP)
        diag = packed_diagonal(SIG[3], c1[here], c1[pl.ds(j + 1, STEP)], c2[here], c3[here], *THREE)
        inverse = 1.0 / diag
        d3[here] = diag
        g3[here] = inverse
        u1[pl.ds(j + 1, STEP)] = f3[here] * inverse * (1.0 / THETA)

    loop(start)
    wrap(u1, n3)

    def near3(u, j):
        here = pl.ds(j, STEP)
        x = u[pl.ds(j + 1, STEP)]
        args = (c1[here], c1[pl.ds(j + 1, STEP)], c2[here], c3[here])
        return here, x, packed_sum(u[here], x, u[pl.ds(j + 2, STEP)], *args, *THREE)

    def pre(j):
        here, x, near = near3(u1, j)
        u2[pl.ds(j + 1, STEP)] = (1.0 + KEEP) * x + GAIN * (g3[here] * (f3[here] + near) - x)

    loop(pre)
    wrap(u2, n3)

    def residual(j):
        here, x, near = near3(u2, j)
        left = (f3[here] + near - d3[here] * x).reshape(STEP // 2, 2, 8, 128)
        res[pl.ds(j // 2, STEP // 2)] = left[:, 0] + left[:, 1]

    loop(residual)

    def fold(x, *even):
        return mul(x.reshape(8 * n4, 128), fold_matrix(*even)).reshape(n4, 8, 128)

    def halves(ref):
        x = ref[0:n3].reshape(n4, 2, 8, 128)
        return x[:, 0], x[:, 1]

    f4[...] = 0.5 * fold(res[...])
    d1[0:n4] = 0.25 * fold(halves(c1)[0])
    d1[n4] = d1[0]
    d2[...] = 0.25 * fold(sum(halves(c2)), True, False)
    e3[...] = 0.25 * fold(sum(halves(c3)), False, True)
    coefs4 = (d1[0:n4], d1[1 : n4 + 1], d2[...], e3[...])
    g4[...] = 1.0 / packed_diagonal(SIG[4], *coefs4, *FOUR)
    x = f4[...] * g4[...] * (1.0 / THETA)
    ua[1 : n4 + 1] = x
    wrap(ua, n4)
    st[...] = x
    src, dst = ua, ub
    for keep, gain in factors(4):
        x = src[1 : n4 + 1]
        near = packed_sum(src[0:n4], x, src[2 : n4 + 2], d1[0:n4], d1[1 : n4 + 1], d2[...], e3[...], *FOUR)
        step = keep * st[...] + gain * (g4[...] * (f4[...] + near) - x)
        st[...] = step
        dst[1 : n4 + 1] = x + step
        wrap(dst, n4)
        src, dst = dst, src

    j0 = around(lax.axis_index("wide") // 2 - 1, n3)
    k, j = iota((128, 128), 0), iota((128, 128), 1)
    unfold = (k == 16 * (j // 64) + j % 32 // 2).astype(F32)
    coarse = jnp.concatenate([src[1 + around(around(j0 - 2, n3) // 2 + m, n4)] for m in range(4)], axis=0)
    scr[0:32] = mul(coarse, unfold)
    shifted = lax.rem(around(j0 - 2, n3), 2)
    js = [around(j0 - 2 + m, n3) for m in range(7)]
    v = [u2[1 + js[m]] + scr[pl.ds(pl.multiple_of(8 * ((shifted + m) // 2), 8), 8), :] for m in range(7)]
    v = jnp.stack(v)

    def window(ref, first, count, by=0):
        return jnp.stack([ref[js[m] + by] for m in range(first, first + count)])

    def args(first, count):
        return window(c1, first, count), window(c1, first, count, 1), window(c2, first, count), window(c3, first, count)

    f, g = window(f3, 1, 5), window(g3, 1, 5)
    near = packed_sum(v[0:5], v[1:6], v[2:7], *args(1, 5), *THREE)
    w = v[1:6] + (1.0 / THETA) * (g * (f + near) - v[1:6])
    near = packed_sum(w[0:3], w[1:4], w[2:5], *args(2, 3), *THREE)
    x = w[1:4] + KEEP * (w[1:4] - v[2:5]) + GAIN * (g[1:4] * (f[1:4] + near) - w[1:4])
    x = x.reshape(24, 128)
    for q in range(4):
        fine = mul(x, (k == 32 * q + j % 64 // 2).astype(F32))
        e2[pl.ds(2 * q, 24, stride=8), :] = fine
        e2[pl.ds(2 * q + 1, 24, stride=8), :] = fine


def coarse_post_kernel(e2, win, u2, late, late_sib, out):
    below, above = sides(late, late_sib)
    v = [both_halves(below(...)), u2[0], u2[1], u2[2], u2[3], both_halves(above(...))]
    v = [v[m] + e2[64 * (m // 2) : 64 * (m // 2) + 64, :] for m in range(6)]

    def args(k):
        return win[k], win[4 + k], win[8 + k], win[9 + k], win[13 + k], win[17 + k]

    w = [first_post(v[m + 1], v[m], v[m + 2], *args(m)) for m in range(4)]
    for p in range(2):
        out[p] = second_post(w[p + 1], v[p + 2], w[p], w[p + 2], *args(p + 1))


def middle_post_kernel(e2, far, msg, sib, near, f, g, w1, own, edge, send, fine, c1, v, w):
    n, par = lax.axis_index("narrow"), lax.rem(lax.axis_index("wide"), 2)
    odd = par == 1
    row, col = iota((40, 64), 0), iota((40, 64), 1)
    pick = (col == lax.rem(16 * n + (row + 4) // 2 + 60, 64)).astype(F32)
    lanes = copies_of_lanes(128, 128)
    planes = (e2[0], e2[1], far[0], far[1])
    for k in range(4):
        fine[k] = mul(mul_left(pick, jnp.where(odd, planes[k], planes[(k + 2) % 4])), lanes)
    c1[0:6] = w1[0:6]
    c1[6] = near[344:384]
    ours = [msg[160 + 40 * p : 200 + 40 * p] for p in range(2)]
    sibs = [sib[160 + 40 * p : 200 + 40 * p] for p in range(2)]
    next_chip = [near[224 + 40 * p : 264 + 40 * p] for p in range(3)]
    upper = sibs + ours + next_chip
    lower = [next_chip[2]] + next_chip[:2] + ours + sibs
    for i in range(7):
        v[i] = jnp.where(odd, upper[i], lower[i]) + fine[(i + 1 - par) // 2]

    def args(i):
        k = i - 1 + par
        return f[k], g[k], c1[k], c1[k + 1], w1[6 + k], w1[12 + k]

    for i in range(1, 6):
        w[i] = first_post(v[i], v[i - 1], v[i + 1], *args(i))
    out = [second_post(w[i], v[i], w[i - 1], w[i + 1], *args(i)) for i in (2, 3, 4)]
    own[0] = jnp.where(odd, out[0], out[1])
    own[1] = jnp.where(odd, out[1], out[2])
    edge[...] = jnp.where(odd, out[2], out[0])
    send[...] = jnp.where(odd, out[0], out[2])


def fine_post_kernel(e1, edge, other, outer, f, c1, c2, c3, u2, out, g, v, w, scr):
    below, above = sides(edge, other)
    x = jnp.concatenate([below(...), e1[0], e1[1], above(...)], axis=0)
    for half in range(2):
        here = slice(128 * half, 128 * half + 128)
        row, col = iota((128, 128), 0), iota((128, 128), 1)
        fine = mul(x, (row == 64 * half + col // 2).astype(F32))
        scr[pl.ds(0, 160, stride=2), :] = fine
        scr[pl.ds(1, 160, stride=2), :] = fine
        for k in range(8):
            at = 80 * (k // 2)
            base = u2[k - 1, :, here] if 0 < k < 7 else outer[k // 7, :, here]
            v[k, :, here] = base + scr[at : at + 80, :]

    def post1(q, carry):
        def chunk(r0, n):
            here = pl.ds(r0, CHUNK)
            x, near = near_chunk(v, q + 1, c1, c2, c3, q, r0, n)
            inverse = 1.0 / diag_chunk(c1, c2, c3, q, r0, n)
            g[q, here, :] = inverse
            w[q + 1, here, :] = x + (1.0 / THETA) * (inverse * (f[q, here, :] + near) - x)

        chunked(80, chunk)
        return carry

    lax.fori_loop(0, 6, post1, 0)

    def post2(q, carry):
        for r0 in range(8, 72, CHUNK):
            here = pl.ds(r0, CHUNK)
            x, near = near_chunk(w, q + 1, c1, c2, c3, q, r0, 80)
            step = KEEP * (x - v[q + 1, here, :]) + GAIN * (g[q, here, :] * (f[q, here, :] + near) - x)
            out[q - 1, pl.ds(r0 - 8, CHUNK), :] = x + step
        return carry

    lax.fori_loop(1, 5, post2, 0)


def shift(x, axis, by):
    count = lax.axis_size(axis)
    return lax.ppermute(x, axis, [(i, (i + by) % count) for i in range(count)])


def sibling(x):
    return lax.ppermute(x, "wide", [(i, i ^ 1) for i in range(lax.axis_size("wide"))])


def across(x):
    count = lax.axis_size("wide")
    return lax.ppermute(x, "wide", [(i, (i + 1 if i % 2 else i - 1) % count) for i in range(count)])


def body(source, coef_first, coef_second, coef_third):
    wide = lax.axis_size("wide")
    n3, n4 = wide // 2, wide // 4
    big = (80, 256)
    inputs = (source, coef_first, coef_second, coef_third)

    up, down, far_raw, sib_raw = call(
        start_kernel,
        [(16, 8, 256), (16, 8, 256), (5, 64, 256), (5, 64, 256)],
        [(2, 16, 8, 256), (2, 5, 64, 256), pltpu.SemaphoreType.DMA((2, 18))],
        {k: pltpu.HBM for k in range(4)},
        {k: pltpu.HBM for k in range(4)},
        limit=60,
    )(*inputs)
    far_raw, sib_raw = across(far_raw), sibling(sib_raw)
    low, high = shift(up, "narrow", 1), shift(down, "narrow", -1)

    own, coef1, far, sib = call(
        pad_kernel, [(16,) + big, (6, 40, 128), (280, 256), (280, 256)], [(2,) + big, (160, 128)]
    )(jnp.concatenate(inputs, axis=0), low, high)
    far, sib = across(far), sibling(sib)

    f, c1, c2, c3, u2, w1, out_far, out_sib = call(
        fine_pre_kernel,
        [(6,) + big, (7,) + big, (6,) + big, (6,) + big, (6,) + big]
        + [(18, 40, 128), (8, 40, 128), (8, 40, 128)],
        [(6,) + big, (2, 40, 128), (8,) + big, (4,) + big, (160, 128)],
    )(own, coef1, far_raw, sib_raw, far, sib)
    far1, sib1 = across(out_far), sibling(out_sib)
    (coefs,) = call(coarse_coef_kernel, [(32, 128)], [(80, 128)])(w1)

    six = (6, 40, 128)
    f1w, g1w, u2m, f2, up, down, outer = call(
        middle_pre_kernel, [six, six, six, (40, 128), (56, 128), (56, 128), (2,) + big], [six, (40, 128)]
    )(out_far, far1, sib1, w1, coefs)
    low, high, far = shift(up, "narrow", 1), shift(down, "narrow", -1), shift(f2, "narrow", 2)

    own2, msg = call(coarse_start_kernel, [(6, 64, 128), (240, 128)])(f2, low, high, far, u2m)
    sib = sibling(msg)
    (swap,) = call(coarse_swap_kernel, [(384, 128)])(own2, msg, sib, w1)
    near = across(swap)
    (tiles,) = call(coarse_tiles_kernel, [(3, 8, 128)], [(64, 128)])(msg, sib)
    near, tiles = lax.optimization_barrier((near, tiles))
    other = sibling(near)
    w2, u2w, late = call(
        coarse_pre_kernel, [(21, 64, 128), (4, 64, 128), (32, 128)], [(6, 64, 128)]
    )(own2, sib, near, other)
    (send,) = call(coarse_send_kernel, [(n3, 2, 8, 128)], [(64, 128)])(w2, u2w, tiles)
    late = across(late)
    cores = [[k for k in range(wide) if k % 2 == c] for c in range(2)]
    parts = lax.all_to_all(send, "wide", split_axis=0, concat_axis=0, tiled=True, axis_index_groups=cores)
    parts, late = lax.optimization_barrier((parts, late))
    theirs, late_sib = sibling(parts), sibling(late)

    three, four = (n3, 8, 128), (n4, 8, 128)
    (fine2,) = call(
        bottom_kernel,
        [(192, 128)],
        [three, (n3 + 1, 8, 128), three, three, three, three, (n3 + 2, 8, 128), (n3 + 2, 8, 128), four, four]
        + [(n4 + 1, 8, 128), four, four, four, (n4 + 2, 8, 128), (n4 + 2, 8, 128), four, (32, 128)],
    )(parts, theirs)
    (e2,) = call(coarse_post_kernel, [(2, 64, 128)])(fine2, w2, u2w, late, late_sib)
    far = across(e2)

    e1, edge, send = call(
        middle_post_kernel,
        [(2, 40, 128), (40, 128), (40, 128)],
        [(4, 40, 128), (7, 40, 128), (7, 40, 128), (7, 40, 128)],
    )(e2, far, msg, sib, near, f1w, g1w, w1)
    other1 = sibling(send)

    (out,) = call(
        fine_post_kernel, [(4, 64, 256)], [(6,) + big, (8,) + big, (8,) + big, (320, 128)]
    )(e1, edge, other1, outer, f, c1, c2, c3, u2)
    return out


def solution(mesh):
    spec = P("wide", "narrow", None)
    return jax.shard_map(body, mesh=mesh, in_specs=(spec,) * 4, out_specs=spec, check_vma=False)
```

```python
import functools

import jax
import jax.numpy as jnp
from jax import lax
from jax.experimental import pallas as pl
from jax.experimental.pallas import tpu as pltpu
from jax.sharding import PartitionSpec as P

THETA = 1.125
DELTA = 0.875
RATIO = THETA / DELTA
SIG = [0.0002 * 4.0**level for level in range(5)]
F32 = jnp.float32


def factors(degree):
    rho, out = 1.0 / RATIO, []
    for _ in range(degree - 1):
        new = 1.0 / (2.0 * RATIO - rho)
        out.append((new * rho, 2.0 * new / DELTA))
        rho = new
    return out


(KEEP, GAIN), = factors(2)


def roll(x, by, axis):
    return pltpu.roll(x, by % x.shape[axis], axis)


def gather_sum(below, here, above, c1, h1, c2, c3):
    first = c1 * below + h1 * above
    second = c2 * roll(here, 1, 0) + roll(c2 * here, -1, 0)
    third = c3 * roll(here, 1, 1) + roll(c3 * here, -1, 1)
    return first + second + third


def diagonal(sig, c1, h1, c2, c3):
    return sig + c1 + h1 + c2 + roll(c2, -1, 0) + c3 + roll(c3, -1, 1)


def iota(shape, dim):
    return lax.broadcasted_iota(jnp.int32, shape, dim)


def pairs_of_lanes(lanes, period, even=False):
    row, col = iota((lanes, 128), 0), iota((lanes, 128), 1) % period
    hit = row == 2 * col if even else row // 2 == col
    return hit.astype(F32)


def copies_of_lanes(lanes_in, lanes_out):
    row, col = iota((lanes_in, lanes_out), 0), iota((lanes_in, lanes_out), 1)
    return (row == col // 2).astype(F32)


def pieces(x):
    out = []
    for _ in range(3):
        part = x.astype(jnp.bfloat16)
        out.append(part)
        x = x - part.astype(F32)
    return out


def mul(x, ones):
    ones = ones.astype(jnp.bfloat16)
    high, mid, low = [jnp.dot(part, ones, preferred_element_type=F32) for part in pieces(x)]
    return high + (mid + low)


def mul_left(ones, x):
    ones = ones.astype(jnp.bfloat16)
    high, mid, low = [jnp.dot(ones, part, preferred_element_type=F32) for part in pieces(x)]
    return high + (mid + low)


def pair_rows(x, scratch, start=0, count=None, even=False):
    rows = x.shape[0]
    count = rows // 2 if count is None else count
    scratch[0:rows, :] = x
    first = scratch[pl.ds(start, count, stride=2), :]
    if even:
        return first
    return first + scratch[pl.ds(start + 1, count, stride=2), :]


def twice_rows(x, scratch):
    rows = x.shape[0]
    scratch[pl.ds(0, rows, stride=2), :] = x
    scratch[pl.ds(1, rows, stride=2), :] = x
    return scratch[0 : 2 * rows, :]


def coarse_coefs(planes, scratch, lanes, period, start=0, count=None):
    both = pairs_of_lanes(lanes, period)
    alone = pairs_of_lanes(lanes, period, even=True)
    return (
        0.25 * pair_rows(mul(planes[0], both), scratch, start, count),
        0.25 * pair_rows(mul(planes[1], both), scratch, start, count, even=True),
        0.25 * pair_rows(mul(planes[2], alone), scratch, start, count),
    )


def spread_block(x, block, width):
    lane = iota(x.shape, 1)
    x = jnp.where(lane // width == block, x, 0.0)
    while width < 128:
        x = x + pltpu.roll(x, width, 1)
        width *= 2
    return x


def smooth_two(u1, below, above, f, g, c1, h1, c2, c3):
    near = gather_sum(below, u1, above, c1, h1, c2, c3)
    return (1.0 + KEEP) * u1 + GAIN * (g * (f + near) - u1)


def first_post(v, below, above, f, g, c1, h1, c2, c3):
    near = gather_sum(below, v, above, c1, h1, c2, c3)
    return v + (1.0 / THETA) * (g * (f + near) - v)


def second_post(u, v, below, above, f, g, c1, h1, c2, c3):
    near = gather_sum(below, u, above, c1, h1, c2, c3)
    return u + KEEP * (u - v) + GAIN * (g * (f + near) - u)


def call(kernel, outs, scratch=(), places=(), out_places=(), limit=4):
    places, out_places = dict(places), dict(out_places)

    def run(*args):
        in_specs = [pl.BlockSpec(memory_space=places.get(i, pltpu.VMEM)) for i in range(len(args))]
        return pl.pallas_call(
            kernel,
            out_shape=[jax.ShapeDtypeStruct(s, F32) for s in outs],
            in_specs=in_specs,
            out_specs=[pl.BlockSpec(memory_space=out_places.get(i, pltpu.VMEM)) for i in range(len(outs))],
            scratch_shapes=[pltpu.VMEM(s, F32) if isinstance(s, tuple) else s for s in scratch],
            compiler_params=pltpu.CompilerParams(vmem_limit_bytes=limit * 2**20),
        )(*args)

    return run


def two_blocks(x):
    half = x.shape[0] // 2
    return jnp.where(iota((half, 128), 1) < 64, x[:half], x[half:])


def start_kernel(f, c1, c2, c3, up, down, out_far, out_sib, rows, planes, sems):
    par = lax.rem(lax.axis_index("wide"), 2)
    moves = []
    for k, (out, row) in enumerate(((up, 56), (down, 0))):
        for a, ref in enumerate((f, c1, c2, c3)):
            moves.append((ref.at[:, pl.ds(row, 8), :], rows.at[k, pl.ds(4 * a, 4)], out.at[pl.ds(4 * a, 4)]))
    for k, (out, upward) in enumerate(((out_far, par), (out_sib, 1 - par))):
        for a, ref in enumerate((f, c1, c2, c3, c1)):
            plane = 3 * upward if a < 4 else 1
            moves.append((ref.at[pl.ds(plane, 1)], planes.at[k, pl.ds(a, 1)], out.at[pl.ds(a, 1)]))
    first = [pltpu.make_async_copy(src, mid, sems.at[0, k]) for k, (src, mid, _) in enumerate(moves)]
    second = [pltpu.make_async_copy(mid, dst, sems.at[1, k]) for k, (_, mid, dst) in enumerate(moves)]
    for copy in first:
        copy.start()
    for one, two in zip(first, second):
        one.wait()
        two.start()
    for copy in second:
        copy.wait()


def pad_kernel(inner, low, high, own, coef1, out_far, out_sib, first, scr):
    for a in range(16):
        own[a, 0:8] = low[a]
        own[a, 8:72] = inner[a]
        own[a, 72:80] = high[a]
    par = lax.rem(lax.axis_index("wide"), 2)
    for k in range(2):
        diag = diagonal(SIG[0], own[5 + k], own[6 + k], own[9 + k], own[13 + k])
        first[k] = own[1 + k] / diag / THETA
    for out, up in ((out_far, par), (out_sib, 1 - par)):
        for a in range(5):
            plane = 4 * a + 3 * up if a < 4 else 5
            out[16 * a : 16 * a + 8] = own[plane, 0:8]
            out[16 * a + 8 : 16 * a + 16] = own[plane, 72:80]
        out[80:160] = first[up]
    k1 = jnp.concatenate([own[4], own[6]], axis=0)
    k2 = jnp.concatenate([own[8] + own[9], own[10] + own[11]], axis=0)
    k3 = jnp.concatenate([own[12] + own[13], own[14] + own[15]], axis=0)
    coarse = coarse_coefs((k1, k2, k3), scr, 256, 128)
    for a in range(3):
        for p in range(2):
            coef1[2 * a + p] = coarse[a][40 * p : 40 * p + 40]
    for out in (out_far, out_sib):
        for k in range(6):
            row, lane = 160 + 40 * (k // 2), 128 * (k % 2)
            out[row : row + 40, lane : lane + 128] = coef1[k]


def block(index):
    row, lane = 160 + 40 * (index // 2), 128 * (index % 2)
    return slice(row, row + 40), slice(lane, lane + 128)


def sides(far, sib):
    odd = lax.rem(lax.axis_index("wide"), 2) == 1

    def below(*at):
        return jnp.where(odd, sib[at], far[at])

    def above(*at):
        return jnp.where(odd, far[at], sib[at])

    return below, above


CHUNK = 16


def chunked(rows, body):
    for r0 in range(0, rows, CHUNK):
        body(r0, rows)


def near_chunk(u, p, c1, c2, c3, q, r0, rows):
    here = pl.ds(r0, CHUNK)
    x = u[p, here, :]
    if r0 > 0:
        lower = u[p, pl.ds(r0 - 1, CHUNK), :]
    else:
        lower = roll(x, 1, 0)
    if r0 + CHUNK < rows:
        after = pl.ds(r0 + 1, CHUNK)
        upper = c2[q, after, :] * u[p, after, :]
    else:
        upper = roll(c2[q, here, :] * x, -1, 0)
    k3 = c3[q, here, :]
    first = c1[q, here, :] * u[p - 1, here, :] + c1[q + 1, here, :] * u[p + 1, here, :]
    second = c2[q, here, :] * lower + upper
    third = k3 * roll(x, 1, 1) + roll(k3 * x, -1, 1)
    return x, first + second + third


def diag_chunk(c1, c2, c3, q, r0, rows):
    here = pl.ds(r0, CHUNK)
    k2, k3 = c2[q, here, :], c3[q, here, :]
    if r0 + CHUNK < rows:
        h2 = c2[q, pl.ds(r0 + 1, CHUNK), :]
    else:
        h2 = roll(k2, -1, 0)
    return SIG[0] + c1[q, here, :] + c1[q + 1, here, :] + k2 + h2 + k3 + roll(k3, -1, 1)


def fine_pre_kernel(own, coef1, far_raw, sib_raw, far, sib, halo, u2, w1, out_far, out_sib, f, c1, c2, c3, g, f1, u1, res, scr):
    below, above = sides(far, sib)
    below_raw, above_raw = sides(far_raw, sib_raw)
    for a, ref in enumerate((f, c1, c2, c3)):
        ref[1:5] = own[4 * a : 4 * a + 4]
    for a, ref, q, raw, rest in (
        [(a, ref, 0, below_raw, below) for a, ref in enumerate((f, c1, c2, c3))]
        + [(a, ref, 5, above_raw, above) for a, ref in enumerate((f, c1, c2, c3))]
        + [(4, c1, 6, above_raw, above)]
    ):
        ref[q, 0:8] = rest(slice(16 * a, 16 * a + 8))
        ref[q, 8:72] = raw(a)
        ref[q, 72:80] = rest(slice(16 * a + 8, 16 * a + 16))
    for a, ref in enumerate((f, c1, c2, c3)):
        halo[a] = ref[0]
        halo[4 + a] = ref[5]
    halo[8] = c1[6]
    u1[0] = below(slice(80, 160))
    u1[7] = above(slice(80, 160))

    def smooth_first(q, carry):
        def rows(r0, n):
            here = pl.ds(r0, CHUNK)
            inverse = 1.0 / diag_chunk(c1, c2, c3, q, r0, n)
            g[q, here, :] = inverse
            u1[q + 1, here, :] = f[q, here, :] * inverse * (1.0 / THETA)

        chunked(80, rows)
        return carry

    lax.fori_loop(0, 6, smooth_first, 0)

    def smooth_second(q, carry):
        def rows(r0, n):
            here = pl.ds(r0, CHUNK)
            x, near = near_chunk(u1, q + 1, c1, c2, c3, q, r0, n)
            u2[q, here, :] = (1.0 + KEEP) * x + GAIN * (g[q, here, :] * (f[q, here, :] + near) - x)

        chunked(80, rows)
        return carry

    lax.fori_loop(0, 6, smooth_second, 0)

    def residual(q, carry):
        def rows(r0, n):
            here = pl.ds(r0, CHUNK)
            x, near = near_chunk(u2, q, c1, c2, c3, q, r0, n)
            res[q - 1, here, :] = f[q, here, :] + near - diag_chunk(c1, c2, c3, q, r0, n) * x

        chunked(80, rows)
        return carry

    lax.fori_loop(1, 5, residual, 0)

    both = pairs_of_lanes(256, 128)
    sums = jnp.concatenate([res[0] + res[1], res[2] + res[3]], axis=0)
    coarse = 0.5 * pair_rows(mul(sums, both), scr)
    f1[0] = coarse[:40]
    f1[1] = coarse[40:]
    for a in range(3):
        for p in range(2):
            w1[6 * a + p] = below(*block(2 * a + p))
            w1[6 * a + 2 + p] = coef1[2 * a + p]
            w1[6 * a + 4 + p] = above(*block(2 * a + p))
    for p in range(2):
        k = p + 2
        inverse = 1.0 / diagonal(SIG[1], w1[k], w1[k + 1], w1[6 + k], w1[12 + k])
        for out in (out_far, out_sib):
            out[p] = f1[p]
            out[2 + p] = inverse
    par = lax.rem(lax.axis_index("wide"), 2)
    for out, plane in ((out_far, 2 + par), (out_sib, 3 - par)):
        out[4] = u2[plane, 0:40, 0:128]
        out[5] = u2[plane, 0:40, 128:256]
        out[6] = u2[plane, 40:80, 0:128]
        out[7] = u2[plane, 40:80, 128:256]


def coarse_coef_kernel(w1, out, scr):
    k1 = jnp.concatenate([w1[2], w1[4]], axis=0)
    k2, k3 = w1[8] + w1[9], w1[14] + w1[15]
    both, alone = pairs_of_lanes(128, 64), pairs_of_lanes(128, 64, even=True)
    k1 = 0.25 * pair_rows(mul(k1, both), scr)
    k2 = 0.25 * pair_rows(mul(k2, both), scr, even=True)
    k3 = 0.25 * pair_rows(mul(k3, alone), scr)
    for k, x in enumerate((k1[2:18], k1[22:38], k2[2:18], k3[2:18])):
        out[8 * k : 8 * k + 8] = two_blocks(x)


def middle_pre_kernel(own, far, sib, w1, coefs, f, g, u2, f2, up, down, outer, u1, scr):
    below, above = sides(far, sib)
    for k, read in enumerate((below, own.__getitem__, above)):
        for p in range(2):
            f[2 * k + p] = read(p)
            g[2 * k + p] = read(2 + p)
    for k, read in enumerate((below, above)):
        outer[k, 0:40, 0:128] = read(4)
        outer[k, 0:40, 128:256] = read(5)
        outer[k, 40:80, 0:128] = read(6)
        outer[k, 40:80, 128:256] = read(7)
    for p in range(6):
        u1[p] = f[p] * g[p] * (1.0 / THETA)
    u2[0] = u1[0]
    u2[5] = u1[5]
    for p in range(1, 5):
        u2[p] = smooth_two(u1[p], u1[p - 1], u1[p + 1], f[p], g[p], w1[p], w1[p + 1], w1[6 + p], w1[12 + p])
    total = 0.0
    for p in (2, 3):
        k1, h1, k2, k3 = w1[p], w1[p + 1], w1[6 + p], w1[12 + p]
        near = gather_sum(u2[p - 1], u2[p], u2[p + 1], k1, h1, k2, k3)
        total = total + (f[p] + near - diagonal(SIG[1], k1, h1, k2, k3) * u2[p])
    coarse = 0.5 * pair_rows(mul(total, pairs_of_lanes(128, 64)), scr, 4, 16)
    f2[0:8] = two_blocks(coarse)
    f2[8:40] = coefs[...]
    for p in range(2):
        up[40 + 8 * p : 48 + 8 * p] = u2[2 + p, 28:36]
        down[40 + 8 * p : 48 + 8 * p] = u2[2 + p, 4:12]
    up[0:40] = f2[...]
    down[0:40] = f2[...]


def both_halves(x):
    return jnp.concatenate([spread_block(x, 0, 64), spread_block(x, 1, 64)], axis=0)


def coarse_start_kernel(f2, low, high, far, u2fine, own, msg):
    n = lax.axis_index("narrow")
    for piece, by in ((f2, 0), (high, 1), (far, 2), (low, 3)):
        at = pl.multiple_of(16 * lax.rem(n + by, 4), 16)
        for k in range(5):
            own[k, pl.ds(at, 16), :] = both_halves(piece[8 * k : 8 * k + 8])
    own[5] = 1.0 / diagonal(SIG[2], own[1], own[2], own[3], own[4])
    for k, plane in enumerate((0, 5, 1, 3, 4)):
        msg[32 * k : 32 * k + 32] = two_blocks(own[plane])
    for p in range(2):
        at = 160 + 40 * p
        msg[at : at + 40] = u2fine[2 + p]
        msg[at : at + 4] = low[44 + 8 * p : 48 + 8 * p]
        msg[at + 36 : at + 40] = high[40 + 8 * p : 44 + 8 * p]


def coarse_tiles_kernel(msg, sib, tiles, scr):
    odd = lax.rem(lax.axis_index("wide"), 2) == 1
    for a in range(3):
        here = slice(64 + 32 * a, 96 + 32 * a)
        x = jnp.where(odd, sib[here], msg[here]) if a == 0 else msg[here] + sib[here]
        scr[...] = 0.25 * mul(both_halves(x), pairs_of_lanes(128, 32, even=a == 2))
        tiles[a] = tile_of(scr, a == 1)


def tile_of(scr, even=False):
    block = iota((8, 128), 1) // 32
    packed = 0.0
    for q in range(4):
        part = scr[pl.ds(2 * q, 8, stride=8), :]
        if not even:
            part = part + scr[pl.ds(2 * q + 1, 8, stride=8), :]
        packed = jnp.where(block == q, part, packed)
    return packed


def coarse_swap_kernel(own, msg, sib, w1, out):
    out[0:160] = msg[0:160]
    out[160:192] = sib[0:32] * sib[32:64] * (1.0 / THETA)
    out[192:224] = two_blocks(own[2])
    out[224:304] = msg[160:240]
    par = lax.rem(lax.axis_index("wide"), 2)
    out[304:344] = sib[pl.ds(pl.multiple_of(160 + 40 * par, 8), 40), :]
    out[344:384] = w1[4]


def coarse_pre_kernel(own, msg, sib, near, other, w, u2, late, fine, u1):
    for p in range(2):
        fine[p] = sib[160 + 40 * p : 200 + 40 * p]
        fine[2 + p] = msg[160 + 40 * p : 200 + 40 * p]
    for p in range(4):
        fine[4 + p] = near[224 + 40 * p : 264 + 40 * p]
    odd = lax.rem(lax.axis_index("wide"), 2) == 1

    def below(k):
        here = slice(32 * k, 32 * k + 32)
        return both_halves(jnp.where(odd, other[here], near[here]))

    def above(k):
        here = slice(32 * k, 32 * k + 32)
        return both_halves(jnp.where(odd, near[here], other[here]))

    for a, (base, plane) in enumerate(((0, 0), (4, 5), (8, 1), (13, 3), (17, 4))):
        mine, theirs = own[plane], both_halves(sib[32 * a : 32 * a + 32])
        w[base] = below(a)
        w[base + 1] = jnp.where(odd, theirs, mine)
        w[base + 2] = jnp.where(odd, mine, theirs)
        w[base + 3] = above(a)
    w[12] = above(6)
    u1[0] = below(5)
    u1[5] = above(5)
    for k in range(4):
        u1[k + 1] = w[k] * w[4 + k] * (1.0 / THETA)
    for k in range(4):
        u2[k] = smooth_two(u1[k + 1], u1[k], u1[k + 2], w[k], w[4 + k], w[8 + k], w[9 + k], w[13 + k], w[17 + k])
    late[...] = two_blocks(jnp.where(odd, u2[1], u2[2]))


def coarse_send_kernel(w, u2, tiles, send, scr):
    odd = lax.rem(lax.axis_index("wide"), 2) == 1
    total = 0.0
    for k in (1, 2):
        args = (w[8 + k], w[9 + k], w[13 + k], w[17 + k])
        near = gather_sum(u2[k - 1], u2[k], u2[k + 1], *args)
        total = total + (w[k] + near - diagonal(SIG[2], *args) * u2[k])
    scr[...] = 0.5 * mul(total, pairs_of_lanes(128, 32))
    first = jnp.where(odd, tiles[1], tile_of(scr))
    second = jnp.where(odd, tiles[2], tiles[0])
    for k in range(send.shape[0]):
        send[k, 0] = first
        send[k, 1] = second


def packed_sum(below, x, above, c1, h1, c2, c3, width, blocks):
    lane = iota(x.shape, 2)
    block, inner = lane // width % blocks, lane % width

    def second_down(x):
        x = pltpu.roll(x, width, 2)
        return jnp.where(block == 0, pltpu.roll(x, 1, 1), x)

    def second_up(x):
        x = pltpu.roll(x, 128 - width, 2)
        return jnp.where(block == blocks - 1, pltpu.roll(x, 7, 1), x)

    def third_down(x):
        return jnp.where(inner == 0, pltpu.roll(x, 129 - width, 2), pltpu.roll(x, 1, 2))

    def third_up(x):
        return jnp.where(inner == width - 1, pltpu.roll(x, width - 1, 2), pltpu.roll(x, 127, 2))

    first = c1 * below + h1 * above
    second = c2 * second_down(x) + second_up(c2 * x)
    third = c3 * third_down(x) + third_up(c3 * x)
    return first + second + third


def packed_diagonal(sig, c1, h1, c2, c3, width, blocks):
    lane = iota(c1.shape, 2)
    block, inner = lane // width % blocks, lane % width
    h2 = pltpu.roll(c2, 128 - width, 2)
    h2 = jnp.where(block == blocks - 1, pltpu.roll(h2, 7, 1), h2)
    h3 = jnp.where(inner == width - 1, pltpu.roll(c3, width - 1, 2), pltpu.roll(c3, 127, 2))
    return sig + c1 + h1 + c2 + h2 + c3 + h3


def fold_matrix(even2=False, even3=False):
    k, j = iota((128, 128), 0), iota((128, 128), 1)
    k2, k3, j2, j3 = k // 32, k % 32, j // 16 % 2, j % 16
    hit2 = k2 == 2 * j2 if even2 else k2 // 2 == j2
    hit3 = k3 == 2 * j3 if even3 else k3 // 2 == j3
    return (hit2 & hit3).astype(F32)


def wrap(ref, count):
    ref[0] = ref[count]
    ref[count + 1] = ref[1]


def around(j, n):
    return lax.rem(j + n, n)


STEP = 32
THREE, FOUR = (32, 4), (16, 2)


def bottom_kernel(mine, theirs, e2,
                  f3, c1, c2, c3, d3, g3, u1, u2, res, f4, d1, d2, e3, g4, ua, ub, st, scr):
    n3, n4 = f3.shape[0], f4.shape[0]

    def loop(body):
        def step(c, carry):
            body(pl.multiple_of(c * STEP, STEP))
            return carry

        lax.fori_loop(0, n3 // STEP, step, 0)

    odd = lax.rem(lax.axis_index("wide"), 2) == 1

    def load(j):
        here = pl.ds(j, STEP)
        a, b, c, d = mine[here, 0], mine[here, 1], theirs[here, 0], theirs[here, 1]
        f3[here] = jnp.where(odd, c, a)
        c1[here] = jnp.where(odd, d, b)
        c2[here] = jnp.where(odd, a, c)
        c3[here] = jnp.where(odd, b, d)

    loop(load)
    c1[n3] = c1[0]

    def start(j):
        here = pl.ds(j, STEP)
        diag = packed_diagonal(SIG[3], c1[here], c1[pl.ds(j + 1, STEP)], c2[here], c3[here], *THREE)
        inverse = 1.0 / diag
        d3[here] = diag
        g3[here] = inverse
        u1[pl.ds(j + 1, STEP)] = f3[here] * inverse * (1.0 / THETA)

    loop(start)
    wrap(u1, n3)

    def near3(u, j):
        here = pl.ds(j, STEP)
        x = u[pl.ds(j + 1, STEP)]
        args = (c1[here], c1[pl.ds(j + 1, STEP)], c2[here], c3[here])
        return here, x, packed_sum(u[here], x, u[pl.ds(j + 2, STEP)], *args, *THREE)

    def pre(j):
        here, x, near = near3(u1, j)
        u2[pl.ds(j + 1, STEP)] = (1.0 + KEEP) * x + GAIN * (g3[here] * (f3[here] + near) - x)

    loop(pre)
    wrap(u2, n3)

    def residual(j):
        here, x, near = near3(u2, j)
        left = (f3[here] + near - d3[here] * x).reshape(STEP // 2, 2, 8, 128)
        res[pl.ds(j // 2, STEP // 2)] = left[:, 0] + left[:, 1]

    loop(residual)

    def fold(x, *even):
        return mul(x.reshape(8 * n4, 128), fold_matrix(*even)).reshape(n4, 8, 128)

    def halves(ref):
        x = ref[0:n3].reshape(n4, 2, 8, 128)
        return x[:, 0], x[:, 1]

    f4[...] = 0.5 * fold(res[...])
    d1[0:n4] = 0.25 * fold(halves(c1)[0])
    d1[n4] = d1[0]
    d2[...] = 0.25 * fold(sum(halves(c2)), True, False)
    e3[...] = 0.25 * fold(sum(halves(c3)), False, True)
    coefs4 = (d1[0:n4], d1[1 : n4 + 1], d2[...], e3[...])
    g4[...] = 1.0 / packed_diagonal(SIG[4], *coefs4, *FOUR)
    x = f4[...] * g4[...] * (1.0 / THETA)
    ua[1 : n4 + 1] = x
    wrap(ua, n4)
    st[...] = x
    src, dst = ua, ub
    for keep, gain in factors(4):
        x = src[1 : n4 + 1]
        near = packed_sum(src[0:n4], x, src[2 : n4 + 2], d1[0:n4], d1[1 : n4 + 1], d2[...], e3[...], *FOUR)
        step = keep * st[...] + gain * (g4[...] * (f4[...] + near) - x)
        st[...] = step
        dst[1 : n4 + 1] = x + step
        wrap(dst, n4)
        src, dst = dst, src

    j0 = around(lax.axis_index("wide") // 2 - 1, n3)
    k, j = iota((128, 128), 0), iota((128, 128), 1)
    unfold = (k == 16 * (j // 64) + j % 32 // 2).astype(F32)
    coarse = jnp.concatenate([src[1 + around(around(j0 - 2, n3) // 2 + m, n4)] for m in range(4)], axis=0)
    scr[0:32] = mul(coarse, unfold)
    shifted = lax.rem(around(j0 - 2, n3), 2)
    js = [around(j0 - 2 + m, n3) for m in range(7)]
    v = [u2[1 + js[m]] + scr[pl.ds(pl.multiple_of(8 * ((shifted + m) // 2), 8), 8), :] for m in range(7)]
    v = jnp.stack(v)

    def window(ref, first, count, by=0):
        return jnp.stack([ref[js[m] + by] for m in range(first, first + count)])

    def args(first, count):
        return window(c1, first, count), window(c1, first, count, 1), window(c2, first, count), window(c3, first, count)

    f, g = window(f3, 1, 5), window(g3, 1, 5)
    near = packed_sum(v[0:5], v[1:6], v[2:7], *args(1, 5), *THREE)
    w = v[1:6] + (1.0 / THETA) * (g * (f + near) - v[1:6])
    near = packed_sum(w[0:3], w[1:4], w[2:5], *args(2, 3), *THREE)
    x = w[1:4] + KEEP * (w[1:4] - v[2:5]) + GAIN * (g[1:4] * (f[1:4] + near) - w[1:4])
    x = x.reshape(24, 128)
    for q in range(4):
        fine = mul(x, (k == 32 * q + j % 64 // 2).astype(F32))
        e2[pl.ds(2 * q, 24, stride=8), :] = fine
        e2[pl.ds(2 * q + 1, 24, stride=8), :] = fine


def coarse_post_kernel(e2, win, u2, late, late_sib, out):
    below, above = sides(late, late_sib)
    v = [both_halves(below(...)), u2[0], u2[1], u2[2], u2[3], both_halves(above(...))]
    v = [v[m] + e2[64 * (m // 2) : 64 * (m // 2) + 64, :] for m in range(6)]

    def args(k):
        return win[k], win[4 + k], win[8 + k], win[9 + k], win[13 + k], win[17 + k]

    w = [first_post(v[m + 1], v[m], v[m + 2], *args(m)) for m in range(4)]
    for p in range(2):
        out[p] = second_post(w[p + 1], v[p + 2], w[p], w[p + 2], *args(p + 1))


def middle_post_kernel(e2, far, u2, f, g, w1, own, edge, send, fine, c1, v, w):
    n, par = lax.axis_index("narrow"), lax.rem(lax.axis_index("wide"), 2)
    odd = par == 1
    row, col = iota((40, 64), 0), iota((40, 64), 1)
    pick = (col == lax.rem(16 * n + (row + 4) // 2 + 60, 64)).astype(F32)
    lanes = copies_of_lanes(128, 128)
    planes = (e2[0], e2[1], far[0], far[1])
    for k in range(4):
        fine[k] = mul(mul_left(pick, jnp.where(odd, planes[k], planes[(k + 2) % 4])), lanes)
    c1[0:6] = w1[0:6]
    c1[6] = u2[7]
    sibs, ours, next_chip = ([u2[k] for k in some] for some in ((0, 1), (2, 3), (4, 5, 6)))
    upper = sibs + ours + next_chip
    lower = [next_chip[2]] + next_chip[:2] + ours + sibs
    for i in range(7):
        v[i] = jnp.where(odd, upper[i], lower[i]) + fine[(i + 1 - par) // 2]

    def args(i):
        k = i - 1 + par
        return f[k], g[k], c1[k], c1[k + 1], w1[6 + k], w1[12 + k]

    for i in range(1, 6):
        w[i] = first_post(v[i], v[i - 1], v[i + 1], *args(i))
    out = [second_post(w[i], v[i], w[i - 1], w[i + 1], *args(i)) for i in (2, 3, 4)]
    own[0] = jnp.where(odd, out[0], out[1])
    own[1] = jnp.where(odd, out[1], out[2])
    edge[...] = jnp.where(odd, out[2], out[0])
    send[...] = jnp.where(odd, out[0], out[2])


def fine_post_kernel(e1, edge, other, outer, inner, low, high, halo, u2, out, f, c1, c2, c3, g, v, w, scr):
    for a, ref in enumerate((f, c1, c2, c3)):
        ref[0] = halo[a]
        ref[5] = halo[4 + a]
        for p in range(4):
            ref[p + 1, 0:8] = low[4 * a + p]
            ref[p + 1, 8:72] = inner[4 * a + p]
            ref[p + 1, 72:80] = high[4 * a + p]
    c1[6] = halo[8]
    below, above = sides(edge, other)
    x = jnp.concatenate([below(...), e1[0], e1[1], above(...)], axis=0)
    for half in range(2):
        here = slice(128 * half, 128 * half + 128)
        row, col = iota((128, 128), 0), iota((128, 128), 1)
        fine = mul(x, (row == 64 * half + col // 2).astype(F32))
        scr[pl.ds(0, 160, stride=2), :] = fine
        scr[pl.ds(1, 160, stride=2), :] = fine
        for k in range(8):
            at = 80 * (k // 2)
            base = u2[k - 1, :, here] if 0 < k < 7 else outer[k // 7, :, here]
            v[k, :, here] = base + scr[at : at + 80, :]

    def post1(q, carry):
        def chunk(r0, n):
            here = pl.ds(r0, CHUNK)
            x, near = near_chunk(v, q + 1, c1, c2, c3, q, r0, n)
            inverse = 1.0 / diag_chunk(c1, c2, c3, q, r0, n)
            g[q, here, :] = inverse
            w[q + 1, here, :] = x + (1.0 / THETA) * (inverse * (f[q, here, :] + near) - x)

        chunked(80, chunk)
        return carry

    lax.fori_loop(0, 6, post1, 0)

    def post2(q, carry):
        for r0 in range(8, 72, CHUNK):
            here = pl.ds(r0, CHUNK)
            x, near = near_chunk(w, q + 1, c1, c2, c3, q, r0, 80)
            step = KEEP * (x - v[q + 1, here, :]) + GAIN * (g[q, here, :] * (f[q, here, :] + near) - x)
            out[q - 1, pl.ds(r0 - 8, CHUNK), :] = x + step
        return carry

    lax.fori_loop(1, 5, post2, 0)


def shift(x, axis, by):
    count = lax.axis_size(axis)
    return lax.ppermute(x, axis, [(i, (i + by) % count) for i in range(count)])


def sibling(x):
    return lax.ppermute(x, "wide", [(i, i ^ 1) for i in range(lax.axis_size("wide"))])


def across(x):
    count = lax.axis_size("wide")
    return lax.ppermute(x, "wide", [(i, (i + 1 if i % 2 else i - 1) % count) for i in range(count)])


def body(source, coef_first, coef_second, coef_third):
    wide = lax.axis_size("wide")
    n3, n4 = wide // 2, wide // 4
    big = (80, 256)
    inputs = (source, coef_first, coef_second, coef_third)

    up, down, far_raw, sib_raw = call(
        start_kernel,
        [(16, 8, 256), (16, 8, 256), (5, 64, 256), (5, 64, 256)],
        [(2, 16, 8, 256), (2, 5, 64, 256), pltpu.SemaphoreType.DMA((2, 18))],
        {k: pltpu.HBM for k in range(4)},
        {k: pltpu.HBM for k in range(4)},
        limit=60,
    )(*inputs)
    far_raw, sib_raw = across(far_raw), sibling(sib_raw)
    low0, high0 = shift(up, "narrow", 1), shift(down, "narrow", -1)

    own, coef1, far, sib = call(
        pad_kernel, [(16,) + big, (6, 40, 128), (280, 256), (280, 256)], [(2,) + big, (160, 128)]
    )(jnp.concatenate(inputs, axis=0), low0, high0)
    far, sib = across(far), sibling(sib)

    windows = [(6,) + big, (7,) + big, (6,) + big, (6,) + big]
    halo, u2, w1, out_far, out_sib = call(
        fine_pre_kernel,
        [(9,) + big, (6,) + big, (18, 40, 128), (8, 40, 128), (8, 40, 128)],
        windows + [(6,) + big, (2, 40, 128), (8,) + big, (4,) + big, (160, 128)],
        limit=6,
    )(own, coef1, far_raw, sib_raw, far, sib)
    far1, sib1 = across(out_far), sibling(out_sib)
    (coefs,) = call(coarse_coef_kernel, [(32, 128)], [(80, 128)])(w1)

    six = (6, 40, 128)
    f1w, g1w, u2m, f2, up, down, outer = call(
        middle_pre_kernel, [six, six, six, (40, 128), (56, 128), (56, 128), (2,) + big], [six, (40, 128)]
    )(out_far, far1, sib1, w1, coefs)
    low, high, far = shift(up, "narrow", 1), shift(down, "narrow", -1), shift(f2, "narrow", 2)

    own2, msg = call(coarse_start_kernel, [(6, 64, 128), (240, 128)])(f2, low, high, far, u2m)
    sib = sibling(msg)
    (swap,) = call(coarse_swap_kernel, [(384, 128)])(own2, msg, sib, w1)
    near = across(swap)
    (tiles,) = call(coarse_tiles_kernel, [(3, 8, 128)], [(64, 128)])(msg, sib)
    near, tiles = lax.optimization_barrier((near, tiles))
    other = sibling(near)
    w2, u2w, late, fine1 = call(
        coarse_pre_kernel, [(21, 64, 128), (4, 64, 128), (32, 128), (8, 40, 128)], [(6, 64, 128)]
    )(own2, msg, sib, near, other)
    (send,) = call(coarse_send_kernel, [(n3, 2, 8, 128)], [(64, 128)])(w2, u2w, tiles)
    late = across(late)
    cores = [[k for k in range(wide) if k % 2 == c] for c in range(2)]
    parts = lax.all_to_all(send, "wide", split_axis=0, concat_axis=0, tiled=True, axis_index_groups=cores)
    parts, late = lax.optimization_barrier((parts, late))
    theirs, late_sib = sibling(parts), sibling(late)

    three, four = (n3, 8, 128), (n4, 8, 128)
    (fine2,) = call(
        bottom_kernel,
        [(192, 128)],
        [three, (n3 + 1, 8, 128), three, three, three, three, (n3 + 2, 8, 128), (n3 + 2, 8, 128), four, four]
        + [(n4 + 1, 8, 128), four, four, four, (n4 + 2, 8, 128), (n4 + 2, 8, 128), four, (32, 128)],
    )(parts, theirs)
    (e2,) = call(coarse_post_kernel, [(2, 64, 128)])(fine2, w2, u2w, late, late_sib)
    e2, *again = lax.optimization_barrier((e2,) + inputs)
    far = across(e2)

    e1, edge, send = call(
        middle_post_kernel,
        [(2, 40, 128), (40, 128), (40, 128)],
        [(4, 40, 128), (7, 40, 128), (7, 40, 128), (7, 40, 128)],
    )(e2, far, fine1, f1w, g1w, w1)
    other1 = sibling(send)

    (out,) = call(
        fine_post_kernel,
        [(4, 64, 256)],
        windows + [(6,) + big, (8,) + big, (8,) + big, (320, 128)],
        limit=6,
    )(e1, edge, other1, outer, jnp.concatenate(again, axis=0), low0, high0, halo, u2)
    return out


def solution(mesh):
    spec = P("wide", "narrow", None)
    return jax.shard_map(body, mesh=mesh, in_specs=(spec,) * 4, out_specs=spec, check_vma=False)
```

```python
import functools

import jax
import jax.numpy as jnp
from jax import lax
from jax.experimental import pallas as pl
from jax.experimental.pallas import tpu as pltpu
from jax.sharding import PartitionSpec as P

THETA = 1.125
DELTA = 0.875
RATIO = THETA / DELTA
SIG = [0.0002 * 4.0**level for level in range(5)]
F32 = jnp.float32


def factors(degree):
    rho, out = 1.0 / RATIO, []
    for _ in range(degree - 1):
        new = 1.0 / (2.0 * RATIO - rho)
        out.append((new * rho, 2.0 * new / DELTA))
        rho = new
    return out


(KEEP, GAIN), = factors(2)


def roll(x, by, axis):
    return pltpu.roll(x, by % x.shape[axis], axis)


def gather_sum(below, here, above, c1, h1, c2, c3):
    first = c1 * below + h1 * above
    second = c2 * roll(here, 1, 0) + roll(c2 * here, -1, 0)
    third = c3 * roll(here, 1, 1) + roll(c3 * here, -1, 1)
    return first + second + third


def diagonal(sig, c1, h1, c2, c3):
    return sig + c1 + h1 + c2 + roll(c2, -1, 0) + c3 + roll(c3, -1, 1)


def iota(shape, dim):
    return lax.broadcasted_iota(jnp.int32, shape, dim)


def pairs_of_lanes(lanes, period, even=False):
    row, col = iota((lanes, 128), 0), iota((lanes, 128), 1) % period
    hit = row == 2 * col if even else row // 2 == col
    return hit.astype(F32)


def copies_of_lanes(lanes_in, lanes_out):
    row, col = iota((lanes_in, lanes_out), 0), iota((lanes_in, lanes_out), 1)
    return (row == col // 2).astype(F32)


def pieces(x):
    out = []
    for _ in range(3):
        part = x.astype(jnp.bfloat16)
        out.append(part)
        x = x - part.astype(F32)
    return out


def mul(x, ones):
    ones = ones.astype(jnp.bfloat16)
    high, mid, low = [jnp.dot(part, ones, preferred_element_type=F32) for part in pieces(x)]
    return high + (mid + low)


def mul_left(ones, x):
    ones = ones.astype(jnp.bfloat16)
    high, mid, low = [jnp.dot(ones, part, preferred_element_type=F32) for part in pieces(x)]
    return high + (mid + low)


def pair_rows(x, scratch, start=0, count=None, even=False):
    rows = x.shape[0]
    count = rows // 2 if count is None else count
    scratch[0:rows, :] = x
    first = scratch[pl.ds(start, count, stride=2), :]
    if even:
        return first
    return first + scratch[pl.ds(start + 1, count, stride=2), :]


def twice_rows(x, scratch):
    rows = x.shape[0]
    scratch[pl.ds(0, rows, stride=2), :] = x
    scratch[pl.ds(1, rows, stride=2), :] = x
    return scratch[0 : 2 * rows, :]


def coarse_coefs(planes, scratch, lanes, period, start=0, count=None):
    both = pairs_of_lanes(lanes, period)
    alone = pairs_of_lanes(lanes, period, even=True)
    return (
        0.25 * pair_rows(mul(planes[0], both), scratch, start, count),
        0.25 * pair_rows(mul(planes[1], both), scratch, start, count, even=True),
        0.25 * pair_rows(mul(planes[2], alone), scratch, start, count),
    )


def spread_block(x, block, width):
    lane = iota(x.shape, 1)
    x = jnp.where(lane // width == block, x, 0.0)
    while width < 128:
        x = x + pltpu.roll(x, width, 1)
        width *= 2
    return x


def smooth_two(u1, below, above, f, g, c1, h1, c2, c3):
    near = gather_sum(below, u1, above, c1, h1, c2, c3)
    return (1.0 + KEEP) * u1 + GAIN * (g * (f + near) - u1)


def first_post(v, below, above, f, g, c1, h1, c2, c3):
    near = gather_sum(below, v, above, c1, h1, c2, c3)
    return v + (1.0 / THETA) * (g * (f + near) - v)


def second_post(u, v, below, above, f, g, c1, h1, c2, c3):
    near = gather_sum(below, u, above, c1, h1, c2, c3)
    return u + KEEP * (u - v) + GAIN * (g * (f + near) - u)


def call(kernel, outs, scratch=(), places=(), out_places=(), limit=4):
    places, out_places = dict(places), dict(out_places)

    def run(*args):
        in_specs = [pl.BlockSpec(memory_space=places.get(i, pltpu.VMEM)) for i in range(len(args))]
        return pl.pallas_call(
            kernel,
            out_shape=[jax.ShapeDtypeStruct(s, F32) for s in outs],
            in_specs=in_specs,
            out_specs=[pl.BlockSpec(memory_space=out_places.get(i, pltpu.VMEM)) for i in range(len(outs))],
            scratch_shapes=[pltpu.VMEM(s, F32) if isinstance(s, tuple) else s for s in scratch],
            compiler_params=pltpu.CompilerParams(vmem_limit_bytes=limit * 2**20),
        )(*args)

    return run


def two_blocks(x):
    half = x.shape[0] // 2
    return jnp.where(iota((half, 128), 1) < 64, x[:half], x[half:])


def start_kernel(f, c1, c2, c3, up, down, out_far, out_sib, rows, planes, sems):
    par = lax.rem(lax.axis_index("wide"), 2)
    moves = []
    for k, (out, row) in enumerate(((up, 56), (down, 0))):
        for a, ref in enumerate((f, c1, c2, c3)):
            moves.append((ref.at[:, pl.ds(row, 8), :], rows.at[k, pl.ds(4 * a, 4)], out.at[pl.ds(4 * a, 4)]))
    for k, (out, upward) in enumerate(((out_far, par), (out_sib, 1 - par))):
        for a, ref in enumerate((f, c1, c2, c3, c1)):
            plane = 3 * upward if a < 4 else 1
            moves.append((ref.at[pl.ds(plane, 1)], planes.at[k, pl.ds(a, 1)], out.at[pl.ds(a, 1)]))
    first = [pltpu.make_async_copy(src, mid, sems.at[0, k]) for k, (src, mid, _) in enumerate(moves)]
    second = [pltpu.make_async_copy(mid, dst, sems.at[1, k]) for k, (_, mid, dst) in enumerate(moves)]
    for copy in first:
        copy.start()
    for one, two in zip(first, second):
        one.wait()
        two.start()
    for copy in second:
        copy.wait()


def pad_kernel(inner, low, high, own, coef1, out_far, out_sib, first, scr):
    for a in range(16):
        own[a, 0:8] = low[a]
        own[a, 8:72] = inner[a]
        own[a, 72:80] = high[a]
    par = lax.rem(lax.axis_index("wide"), 2)
    for k in range(2):
        diag = diagonal(SIG[0], own[5 + k], own[6 + k], own[9 + k], own[13 + k])
        first[k] = own[1 + k] / diag / THETA
    for out, up in ((out_far, par), (out_sib, 1 - par)):
        for a in range(5):
            plane = 4 * a + 3 * up if a < 4 else 5
            out[16 * a : 16 * a + 8] = own[plane, 0:8]
            out[16 * a + 8 : 16 * a + 16] = own[plane, 72:80]
        out[80:160] = first[up]
    k1 = jnp.concatenate([own[4], own[6]], axis=0)
    k2 = jnp.concatenate([own[8] + own[9], own[10] + own[11]], axis=0)
    k3 = jnp.concatenate([own[12] + own[13], own[14] + own[15]], axis=0)
    coarse = coarse_coefs((k1, k2, k3), scr, 256, 128)
    for a in range(3):
        for p in range(2):
            coef1[2 * a + p] = coarse[a][40 * p : 40 * p + 40]
    for out in (out_far, out_sib):
        for k in range(6):
            row, lane = 160 + 40 * (k // 2), 128 * (k % 2)
            out[row : row + 40, lane : lane + 128] = coef1[k]


def block(index):
    row, lane = 160 + 40 * (index // 2), 128 * (index % 2)
    return slice(row, row + 40), slice(lane, lane + 128)


def sides(far, sib):
    odd = lax.rem(lax.axis_index("wide"), 2) == 1

    def below(*at):
        return jnp.where(odd, sib[at], far[at])

    def above(*at):
        return jnp.where(odd, far[at], sib[at])

    return below, above


CHUNK = 16


def chunked(rows, body):
    for r0 in range(0, rows, CHUNK):
        body(r0, rows)


def near_chunk(u, p, c1, c2, c3, q, r0, rows):
    here = pl.ds(r0, CHUNK)
    x = u[p, here, :]
    if r0 > 0:
        lower = u[p, pl.ds(r0 - 1, CHUNK), :]
    else:
        lower = roll(x, 1, 0)
    if r0 + CHUNK < rows:
        after = pl.ds(r0 + 1, CHUNK)
        upper = c2[q, after, :] * u[p, after, :]
    else:
        upper = roll(c2[q, here, :] * x, -1, 0)
    k3 = c3[q, here, :]
    first = c1[q, here, :] * u[p - 1, here, :] + c1[q + 1, here, :] * u[p + 1, here, :]
    second = c2[q, here, :] * lower + upper
    third = k3 * roll(x, 1, 1) + roll(k3 * x, -1, 1)
    return x, first + second + third


def diag_chunk(c1, c2, c3, q, r0, rows):
    here = pl.ds(r0, CHUNK)
    k2, k3 = c2[q, here, :], c3[q, here, :]
    if r0 + CHUNK < rows:
        h2 = c2[q, pl.ds(r0 + 1, CHUNK), :]
    else:
        h2 = roll(k2, -1, 0)
    return SIG[0] + c1[q, here, :] + c1[q + 1, here, :] + k2 + h2 + k3 + roll(k3, -1, 1)


def fine_pre_kernel(own, coef1, far_raw, sib_raw, far, sib, halo, u2, w1, out_far, out_sib, f, c1, c2, c3, g, f1, u1, res, scr):
    below, above = sides(far, sib)
    below_raw, above_raw = sides(far_raw, sib_raw)
    for a, ref in enumerate((f, c1, c2, c3)):
        ref[1:5] = own[4 * a : 4 * a + 4]
    for a, ref, q, raw, rest in (
        [(a, ref, 0, below_raw, below) for a, ref in enumerate((f, c1, c2, c3))]
        + [(a, ref, 5, above_raw, above) for a, ref in enumerate((f, c1, c2, c3))]
        + [(4, c1, 6, above_raw, above)]
    ):
        ref[q, 0:8] = rest(slice(16 * a, 16 * a + 8))
        ref[q, 8:72] = raw(a)
        ref[q, 72:80] = rest(slice(16 * a + 8, 16 * a + 16))
    for a, ref in enumerate((f, c1, c2, c3)):
        halo[a] = ref[0]
        halo[4 + a] = ref[5]
    halo[8] = c1[6]
    u1[0] = below(slice(80, 160))
    u1[7] = above(slice(80, 160))

    def smooth_first(q, carry):
        def rows(r0, n):
            here = pl.ds(r0, CHUNK)
            inverse = 1.0 / diag_chunk(c1, c2, c3, q, r0, n)
            g[q, here, :] = inverse
            u1[q + 1, here, :] = f[q, here, :] * inverse * (1.0 / THETA)

        chunked(80, rows)
        return carry

    lax.fori_loop(0, 6, smooth_first, 0)

    def smooth_second(q, carry):
        def rows(r0, n):
            here = pl.ds(r0, CHUNK)
            x, near = near_chunk(u1, q + 1, c1, c2, c3, q, r0, n)
            u2[q, here, :] = (1.0 + KEEP) * x + GAIN * (g[q, here, :] * (f[q, here, :] + near) - x)

        chunked(80, rows)
        return carry

    lax.fori_loop(0, 6, smooth_second, 0)

    def residual(q, carry):
        def rows(r0, n):
            here = pl.ds(r0, CHUNK)
            x, near = near_chunk(u2, q, c1, c2, c3, q, r0, n)
            res[q - 1, here, :] = f[q, here, :] + near - diag_chunk(c1, c2, c3, q, r0, n) * x

        chunked(80, rows)
        return carry

    lax.fori_loop(1, 5, residual, 0)

    both = pairs_of_lanes(256, 128)
    sums = jnp.concatenate([res[0] + res[1], res[2] + res[3]], axis=0)
    coarse = 0.5 * pair_rows(mul(sums, both), scr)
    f1[0] = coarse[:40]
    f1[1] = coarse[40:]
    for a in range(3):
        for p in range(2):
            w1[6 * a + p] = below(*block(2 * a + p))
            w1[6 * a + 2 + p] = coef1[2 * a + p]
            w1[6 * a + 4 + p] = above(*block(2 * a + p))
    for p in range(2):
        k = p + 2
        inverse = 1.0 / diagonal(SIG[1], w1[k], w1[k + 1], w1[6 + k], w1[12 + k])
        for out in (out_far, out_sib):
            out[p] = f1[p]
            out[2 + p] = inverse
    par = lax.rem(lax.axis_index("wide"), 2)
    for out, plane in ((out_far, 2 + par), (out_sib, 3 - par)):
        out[4] = u2[plane, 0:40, 0:128]
        out[5] = u2[plane, 0:40, 128:256]
        out[6] = u2[plane, 40:80, 0:128]
        out[7] = u2[plane, 40:80, 128:256]


def coarse_coef_kernel(w1, out, scr):
    k1 = jnp.concatenate([w1[2], w1[4]], axis=0)
    k2, k3 = w1[8] + w1[9], w1[14] + w1[15]
    both, alone = pairs_of_lanes(128, 64), pairs_of_lanes(128, 64, even=True)
    k1 = 0.25 * pair_rows(mul(k1, both), scr)
    k2 = 0.25 * pair_rows(mul(k2, both), scr, even=True)
    k3 = 0.25 * pair_rows(mul(k3, alone), scr)
    for k, x in enumerate((k1[2:18], k1[22:38], k2[2:18], k3[2:18])):
        out[8 * k : 8 * k + 8] = two_blocks(x)


def middle_pre_kernel(own, far, sib, w1, coefs, f, g, u2, f2, up, down, outer, u1, scr):
    below, above = sides(far, sib)
    for k, read in enumerate((below, own.__getitem__, above)):
        for p in range(2):
            f[2 * k + p] = read(p)
            g[2 * k + p] = read(2 + p)
    for k, read in enumerate((below, above)):
        outer[k, 0:40, 0:128] = read(4)
        outer[k, 0:40, 128:256] = read(5)
        outer[k, 40:80, 0:128] = read(6)
        outer[k, 40:80, 128:256] = read(7)
    for p in range(6):
        u1[p] = f[p] * g[p] * (1.0 / THETA)
    u2[0] = u1[0]
    u2[5] = u1[5]
    for p in range(1, 5):
        u2[p] = smooth_two(u1[p], u1[p - 1], u1[p + 1], f[p], g[p], w1[p], w1[p + 1], w1[6 + p], w1[12 + p])
    total = 0.0
    for p in (2, 3):
        k1, h1, k2, k3 = w1[p], w1[p + 1], w1[6 + p], w1[12 + p]
        near = gather_sum(u2[p - 1], u2[p], u2[p + 1], k1, h1, k2, k3)
        total = total + (f[p] + near - diagonal(SIG[1], k1, h1, k2, k3) * u2[p])
    coarse = 0.5 * pair_rows(mul(total, pairs_of_lanes(128, 64)), scr, 4, 16)
    f2[0:8] = two_blocks(coarse)
    f2[8:40] = coefs[...]
    for p in range(2):
        up[40 + 8 * p : 48 + 8 * p] = u2[2 + p, 28:36]
        down[40 + 8 * p : 48 + 8 * p] = u2[2 + p, 4:12]
    up[0:40] = f2[...]
    down[0:40] = f2[...]


def both_halves(x):
    return jnp.concatenate([spread_block(x, 0, 64), spread_block(x, 1, 64)], axis=0)


def coarse_start_kernel(f2, low, high, far, u2fine, own, msg):
    n = lax.axis_index("narrow")
    for piece, by in ((f2, 0), (high, 1), (far, 2), (low, 3)):
        at = pl.multiple_of(16 * lax.rem(n + by, 4), 16)
        for k in range(5):
            own[k, pl.ds(at, 16), :] = both_halves(piece[8 * k : 8 * k + 8])
    own[5] = 1.0 / diagonal(SIG[2], own[1], own[2], own[3], own[4])
    for k, plane in enumerate((0, 5, 1, 3, 4)):
        msg[32 * k : 32 * k + 32] = two_blocks(own[plane])
    for p in range(2):
        at = 160 + 40 * p
        msg[at : at + 40] = u2fine[2 + p]
        msg[at : at + 4] = low[44 + 8 * p : 48 + 8 * p]
        msg[at + 36 : at + 40] = high[40 + 8 * p : 44 + 8 * p]


def coarse_tiles_kernel(msg, sib, tiles, scr):
    odd = lax.rem(lax.axis_index("wide"), 2) == 1
    for a in range(3):
        here = slice(64 + 32 * a, 96 + 32 * a)
        x = jnp.where(odd, sib[here], msg[here]) if a == 0 else msg[here] + sib[here]
        scr[...] = 0.25 * mul(both_halves(x), pairs_of_lanes(128, 32, even=a == 2))
        tiles[a] = tile_of(scr, a == 1)


def tile_of(scr, even=False):
    block = iota((8, 128), 1) // 32
    packed = 0.0
    for q in range(4):
        part = scr[pl.ds(2 * q, 8, stride=8), :]
        if not even:
            part = part + scr[pl.ds(2 * q + 1, 8, stride=8), :]
        packed = jnp.where(block == q, part, packed)
    return packed


def coarse_swap_kernel(own, msg, sib, out):
    out[0:160] = msg[0:160]
    out[160:192] = sib[0:32] * sib[32:64] * (1.0 / THETA)
    out[192:224] = two_blocks(own[2])


def coarse_pre_kernel(own, msg, sib, near, other, w1, w, u2, late, fine, u1):
    for p in range(2):
        fine[p] = sib[160 + 40 * p : 200 + 40 * p]
        fine[2 + p] = msg[160 + 40 * p : 200 + 40 * p]
    late[32:112] = msg[160:240]
    late[112:152] = fine[lax.rem(lax.axis_index("wide"), 2)]
    late[152:192] = w1[4]
    odd = lax.rem(lax.axis_index("wide"), 2) == 1

    def below(k):
        here = slice(32 * k, 32 * k + 32)
        return both_halves(jnp.where(odd, other[here], near[here]))

    def above(k):
        here = slice(32 * k, 32 * k + 32)
        return both_halves(jnp.where(odd, near[here], other[here]))

    for a, (base, plane) in enumerate(((0, 0), (4, 5), (8, 1), (13, 3), (17, 4))):
        mine, theirs = own[plane], both_halves(sib[32 * a : 32 * a + 32])
        w[base] = below(a)
        w[base + 1] = jnp.where(odd, theirs, mine)
        w[base + 2] = jnp.where(odd, mine, theirs)
        w[base + 3] = above(a)
    w[12] = above(6)
    u1[0] = below(5)
    u1[5] = above(5)
    for k in range(4):
        u1[k + 1] = w[k] * w[4 + k] * (1.0 / THETA)
    for k in range(4):
        u2[k] = smooth_two(u1[k + 1], u1[k], u1[k + 2], w[k], w[4 + k], w[8 + k], w[9 + k], w[13 + k], w[17 + k])
    late[0:32] = two_blocks(jnp.where(odd, u2[1], u2[2]))


def coarse_send_kernel(w, u2, tiles, send, scr):
    odd = lax.rem(lax.axis_index("wide"), 2) == 1
    total = 0.0
    for k in (1, 2):
        args = (w[8 + k], w[9 + k], w[13 + k], w[17 + k])
        near = gather_sum(u2[k - 1], u2[k], u2[k + 1], *args)
        total = total + (w[k] + near - diagonal(SIG[2], *args) * u2[k])
    scr[...] = 0.5 * mul(total, pairs_of_lanes(128, 32))
    first = jnp.where(odd, tiles[1], tile_of(scr))
    second = jnp.where(odd, tiles[2], tiles[0])
    for k in range(send.shape[0]):
        send[k, 0] = first
        send[k, 1] = second


def packed_sum(below, x, above, c1, h1, c2, c3, width, blocks):
    lane = iota(x.shape, 2)
    block, inner = lane // width % blocks, lane % width

    def second_down(x):
        x = pltpu.roll(x, width, 2)
        return jnp.where(block == 0, pltpu.roll(x, 1, 1), x)

    def second_up(x):
        x = pltpu.roll(x, 128 - width, 2)
        return jnp.where(block == blocks - 1, pltpu.roll(x, 7, 1), x)

    def third_down(x):
        return jnp.where(inner == 0, pltpu.roll(x, 129 - width, 2), pltpu.roll(x, 1, 2))

    def third_up(x):
        return jnp.where(inner == width - 1, pltpu.roll(x, width - 1, 2), pltpu.roll(x, 127, 2))

    first = c1 * below + h1 * above
    second = c2 * second_down(x) + second_up(c2 * x)
    third = c3 * third_down(x) + third_up(c3 * x)
    return first + second + third


def packed_diagonal(sig, c1, h1, c2, c3, width, blocks):
    lane = iota(c1.shape, 2)
    block, inner = lane // width % blocks, lane % width
    h2 = pltpu.roll(c2, 128 - width, 2)
    h2 = jnp.where(block == blocks - 1, pltpu.roll(h2, 7, 1), h2)
    h3 = jnp.where(inner == width - 1, pltpu.roll(c3, width - 1, 2), pltpu.roll(c3, 127, 2))
    return sig + c1 + h1 + c2 + h2 + c3 + h3


def fold_matrix(even2=False, even3=False):
    k, j = iota((128, 128), 0), iota((128, 128), 1)
    k2, k3, j2, j3 = k // 32, k % 32, j // 16 % 2, j % 16
    hit2 = k2 == 2 * j2 if even2 else k2 // 2 == j2
    hit3 = k3 == 2 * j3 if even3 else k3 // 2 == j3
    return (hit2 & hit3).astype(F32)


def wrap(ref, count):
    ref[0] = ref[count]
    ref[count + 1] = ref[1]


def around(j, n):
    return lax.rem(j + n, n)


STEP = 32
THREE, FOUR = (32, 4), (16, 2)


def bottom_kernel(mine, theirs, e2,
                  f3, c1, c2, c3, d3, g3, u1, u2, res, f4, d1, d2, e3, g4, ua, ub, st, scr):
    n3, n4 = f3.shape[0], f4.shape[0]

    def loop(body):
        def step(c, carry):
            body(pl.multiple_of(c * STEP, STEP))
            return carry

        lax.fori_loop(0, n3 // STEP, step, 0)

    odd = lax.rem(lax.axis_index("wide"), 2) == 1

    def load(j):
        here = pl.ds(j, STEP)
        a, b, c, d = mine[here, 0], mine[here, 1], theirs[here, 0], theirs[here, 1]
        f3[here] = jnp.where(odd, c, a)
        c1[here] = jnp.where(odd, d, b)
        c2[here] = jnp.where(odd, a, c)
        c3[here] = jnp.where(odd, b, d)

    loop(load)
    c1[n3] = c1[0]

    def start(j):
        here = pl.ds(j, STEP)
        diag = packed_diagonal(SIG[3], c1[here], c1[pl.ds(j + 1, STEP)], c2[here], c3[here], *THREE)
        inverse = 1.0 / diag
        d3[here] = diag
        g3[here] = inverse
        u1[pl.ds(j + 1, STEP)] = f3[here] * inverse * (1.0 / THETA)

    loop(start)
    wrap(u1, n3)

    def near3(u, j):
        here = pl.ds(j, STEP)
        x = u[pl.ds(j + 1, STEP)]
        args = (c1[here], c1[pl.ds(j + 1, STEP)], c2[here], c3[here])
        return here, x, packed_sum(u[here], x, u[pl.ds(j + 2, STEP)], *args, *THREE)

    def pre(j):
        here, x, near = near3(u1, j)
        u2[pl.ds(j + 1, STEP)] = (1.0 + KEEP) * x + GAIN * (g3[here] * (f3[here] + near) - x)

    loop(pre)
    wrap(u2, n3)

    def residual(j):
        here, x, near = near3(u2, j)
        left = (f3[here] + near - d3[here] * x).reshape(STEP // 2, 2, 8, 128)
        res[pl.ds(j // 2, STEP // 2)] = left[:, 0] + left[:, 1]

    loop(residual)

    def fold(x, *even):
        return mul(x.reshape(8 * n4, 128), fold_matrix(*even)).reshape(n4, 8, 128)

    def halves(ref):
        x = ref[0:n3].reshape(n4, 2, 8, 128)
        return x[:, 0], x[:, 1]

    f4[...] = 0.5 * fold(res[...])
    d1[0:n4] = 0.25 * fold(halves(c1)[0])
    d1[n4] = d1[0]
    d2[...] = 0.25 * fold(sum(halves(c2)), True, False)
    e3[...] = 0.25 * fold(sum(halves(c3)), False, True)
    coefs4 = (d1[0:n4], d1[1 : n4 + 1], d2[...], e3[...])
    g4[...] = 1.0 / packed_diagonal(SIG[4], *coefs4, *FOUR)
    x = f4[...] * g4[...] * (1.0 / THETA)
    ua[1 : n4 + 1] = x
    wrap(ua, n4)
    st[...] = x
    src, dst = ua, ub
    for keep, gain in factors(4):
        x = src[1 : n4 + 1]
        near = packed_sum(src[0:n4], x, src[2 : n4 + 2], d1[0:n4], d1[1 : n4 + 1], d2[...], e3[...], *FOUR)
        step = keep * st[...] + gain * (g4[...] * (f4[...] + near) - x)
        st[...] = step
        dst[1 : n4 + 1] = x + step
        wrap(dst, n4)
        src, dst = dst, src

    j0 = around(lax.axis_index("wide") // 2 - 1, n3)
    k, j = iota((128, 128), 0), iota((128, 128), 1)
    unfold = (k == 16 * (j // 64) + j % 32 // 2).astype(F32)
    coarse = jnp.concatenate([src[1 + around(around(j0 - 2, n3) // 2 + m, n4)] for m in range(4)], axis=0)
    scr[0:32] = mul(coarse, unfold)
    shifted = lax.rem(around(j0 - 2, n3), 2)
    js = [around(j0 - 2 + m, n3) for m in range(7)]
    v = [u2[1 + js[m]] + scr[pl.ds(pl.multiple_of(8 * ((shifted + m) // 2), 8), 8), :] for m in range(7)]
    v = jnp.stack(v)

    def window(ref, first, count, by=0):
        return jnp.stack([ref[js[m] + by] for m in range(first, first + count)])

    def args(first, count):
        return window(c1, first, count), window(c1, first, count, 1), window(c2, first, count), window(c3, first, count)

    f, g = window(f3, 1, 5), window(g3, 1, 5)
    near = packed_sum(v[0:5], v[1:6], v[2:7], *args(1, 5), *THREE)
    w = v[1:6] + (1.0 / THETA) * (g * (f + near) - v[1:6])
    near = packed_sum(w[0:3], w[1:4], w[2:5], *args(2, 3), *THREE)
    x = w[1:4] + KEEP * (w[1:4] - v[2:5]) + GAIN * (g[1:4] * (f[1:4] + near) - w[1:4])
    x = x.reshape(24, 128)
    for q in range(4):
        fine = mul(x, (k == 32 * q + j % 64 // 2).astype(F32))
        e2[pl.ds(2 * q, 24, stride=8), :] = fine
        e2[pl.ds(2 * q + 1, 24, stride=8), :] = fine


def coarse_post_kernel(e2, win, u2, late, late_sib, out):
    below, above = sides(late, late_sib)
    half = slice(0, 32)
    v = [both_halves(below(half)), u2[0], u2[1], u2[2], u2[3], both_halves(above(half))]
    v = [v[m] + e2[64 * (m // 2) : 64 * (m // 2) + 64, :] for m in range(6)]

    def args(k):
        return win[k], win[4 + k], win[8 + k], win[9 + k], win[13 + k], win[17 + k]

    w = [first_post(v[m + 1], v[m], v[m + 2], *args(m)) for m in range(4)]
    for p in range(2):
        x = second_post(w[p + 1], v[p + 2], w[p], w[p + 2], *args(p + 1))
        out[p] = pltpu.roll(x, lax.rem(72 - 16 * lax.axis_index("narrow"), 64), 0)[0:32]


def middle_post_kernel(e2, far, u2, late, f, g, w1, own, edge, send, fine, c1, v, w):
    par = lax.rem(lax.axis_index("wide"), 2)
    odd = par == 1
    row, col = iota((40, 32), 0), iota((40, 32), 1)
    pick = (col == (row + 4) // 2 + 4).astype(F32)
    lanes = copies_of_lanes(128, 128)
    planes = (e2[0], e2[1], far[0], far[1])
    for k in range(4):
        fine[k] = mul(mul_left(pick, jnp.where(odd, planes[k], planes[(k + 2) % 4])), lanes)
    c1[0:6] = w1[0:6]
    c1[6] = late[152:192]
    sibs, ours = [u2[0], u2[1]], [u2[2], u2[3]]
    next_chip = [late[32 + 40 * p : 72 + 40 * p] for p in range(3)]
    upper = sibs + ours + next_chip
    lower = [next_chip[2]] + next_chip[:2] + ours + sibs
    for i in range(7):
        v[i] = jnp.where(odd, upper[i], lower[i]) + fine[(i + 1 - par) // 2]

    def args(i):
        k = i - 1 + par
        return f[k], g[k], c1[k], c1[k + 1], w1[6 + k], w1[12 + k]

    for i in range(1, 6):
        w[i] = first_post(v[i], v[i - 1], v[i + 1], *args(i))
    out = [second_post(w[i], v[i], w[i - 1], w[i + 1], *args(i)) for i in (2, 3, 4)]
    own[0] = jnp.where(odd, out[0], out[1])
    own[1] = jnp.where(odd, out[1], out[2])
    edge[...] = jnp.where(odd, out[2], out[0])
    send[...] = jnp.where(odd, out[0], out[2])


def fine_post_kernel(e1, edge, other, outer, inner, low, high, halo, u2, out, f, c1, c2, c3, g, v, w, scr):
    for a, ref in enumerate((f, c1, c2, c3)):
        ref[0] = halo[a]
        ref[5] = halo[4 + a]
        for p in range(4):
            ref[p + 1, 0:8] = low[4 * a + p]
            ref[p + 1, 8:72] = inner[4 * a + p]
            ref[p + 1, 72:80] = high[4 * a + p]
    c1[6] = halo[8]
    below, above = sides(edge, other)
    x = jnp.concatenate([below(...), e1[0], e1[1], above(...)], axis=0)
    for half in range(2):
        here = slice(128 * half, 128 * half + 128)
        row, col = iota((128, 128), 0), iota((128, 128), 1)
        fine = mul(x, (row == 64 * half + col // 2).astype(F32))
        scr[pl.ds(0, 160, stride=2), :] = fine
        scr[pl.ds(1, 160, stride=2), :] = fine
        for k in range(8):
            at = 80 * (k // 2)
            base = u2[k - 1, :, here] if 0 < k < 7 else outer[k // 7, :, here]
            v[k, :, here] = base + scr[at : at + 80, :]

    def post1(q, carry):
        def chunk(r0, n):
            here = pl.ds(r0, CHUNK)
            x, near = near_chunk(v, q + 1, c1, c2, c3, q, r0, n)
            inverse = 1.0 / diag_chunk(c1, c2, c3, q, r0, n)
            g[q, here, :] = inverse
            w[q + 1, here, :] = x + (1.0 / THETA) * (inverse * (f[q, here, :] + near) - x)

        chunked(80, chunk)
        return carry

    lax.fori_loop(0, 6, post1, 0)

    def post2(q, carry):
        for r0 in range(8, 72, CHUNK):
            here = pl.ds(r0, CHUNK)
            x, near = near_chunk(w, q + 1, c1, c2, c3, q, r0, 80)
            step = KEEP * (x - v[q + 1, here, :]) + GAIN * (g[q, here, :] * (f[q, here, :] + near) - x)
            out[q - 1, pl.ds(r0 - 8, CHUNK), :] = x + step
        return carry

    lax.fori_loop(1, 5, post2, 0)


def shift(x, axis, by):
    count = lax.axis_size(axis)
    return lax.ppermute(x, axis, [(i, (i + by) % count) for i in range(count)])


def sibling(x):
    return lax.ppermute(x, "wide", [(i, i ^ 1) for i in range(lax.axis_size("wide"))])


def across(x):
    count = lax.axis_size("wide")
    return lax.ppermute(x, "wide", [(i, (i + 1 if i % 2 else i - 1) % count) for i in range(count)])


def body(source, coef_first, coef_second, coef_third):
    wide = lax.axis_size("wide")
    n3, n4 = wide // 2, wide // 4
    big = (80, 256)
    inputs = (source, coef_first, coef_second, coef_third)

    up, down, far_raw, sib_raw = call(
        start_kernel,
        [(16, 8, 256), (16, 8, 256), (5, 64, 256), (5, 64, 256)],
        [(2, 16, 8, 256), (2, 5, 64, 256), pltpu.SemaphoreType.DMA((2, 18))],
        {k: pltpu.HBM for k in range(4)},
        {k: pltpu.HBM for k in range(4)},
        limit=60,
    )(*inputs)
    far_raw, sib_raw = across(far_raw), sibling(sib_raw)
    low0, high0 = shift(up, "narrow", 1), shift(down, "narrow", -1)

    own, coef1, far, sib = call(
        pad_kernel, [(16,) + big, (6, 40, 128), (280, 256), (280, 256)], [(2,) + big, (160, 128)]
    )(jnp.concatenate(inputs, axis=0), low0, high0)
    far, sib = across(far), sibling(sib)

    windows = [(6,) + big, (7,) + big, (6,) + big, (6,) + big]
    halo, u2, w1, out_far, out_sib = call(
        fine_pre_kernel,
        [(9,) + big, (6,) + big, (18, 40, 128), (8, 40, 128), (8, 40, 128)],
        windows + [(6,) + big, (2, 40, 128), (8,) + big, (4,) + big, (160, 128)],
        limit=6,
    )(own, coef1, far_raw, sib_raw, far, sib)
    far1, sib1 = across(out_far), sibling(out_sib)
    (coefs,) = call(coarse_coef_kernel, [(32, 128)], [(80, 128)])(w1)

    six = (6, 40, 128)
    f1w, g1w, u2m, f2, up, down, outer = call(
        middle_pre_kernel, [six, six, six, (40, 128), (56, 128), (56, 128), (2,) + big], [six, (40, 128)]
    )(out_far, far1, sib1, w1, coefs)
    low, high, far = shift(up, "narrow", 1), shift(down, "narrow", -1), shift(f2, "narrow", 2)

    own2, msg = call(coarse_start_kernel, [(6, 64, 128), (240, 128)])(f2, low, high, far, u2m)
    sib = sibling(msg)
    (swap,) = call(coarse_swap_kernel, [(224, 128)])(own2, msg, sib)
    near = across(swap)
    (tiles,) = call(coarse_tiles_kernel, [(3, 8, 128)], [(64, 128)])(msg, sib)
    near, tiles = lax.optimization_barrier((near, tiles))
    other = sibling(near)
    w2, u2w, late, fine1 = call(
        coarse_pre_kernel, [(21, 64, 128), (4, 64, 128), (192, 128), (4, 40, 128)], [(6, 64, 128)]
    )(own2, msg, sib, near, other, w1)
    (send,) = call(coarse_send_kernel, [(n3, 2, 8, 128)], [(64, 128)])(w2, u2w, tiles)
    late = across(late)
    cores = [[k for k in range(wide) if k % 2 == c] for c in range(2)]
    parts = lax.all_to_all(send, "wide", split_axis=0, concat_axis=0, tiled=True, axis_index_groups=cores)
    parts, late = lax.optimization_barrier((parts, late))
    theirs, late_sib = sibling(parts), sibling(late)

    three, four = (n3, 8, 128), (n4, 8, 128)
    (fine2,) = call(
        bottom_kernel,
        [(192, 128)],
        [three, (n3 + 1, 8, 128), three, three, three, three, (n3 + 2, 8, 128), (n3 + 2, 8, 128), four, four]
        + [(n4 + 1, 8, 128), four, four, four, (n4 + 2, 8, 128), (n4 + 2, 8, 128), four, (32, 128)],
    )(parts, theirs)
    (e2,) = call(coarse_post_kernel, [(2, 32, 128)])(fine2, w2, u2w, late, late_sib)
    e2, *again = lax.optimization_barrier((e2,) + inputs)
    far = across(e2)

    e1, edge, send = call(
        middle_post_kernel,
        [(2, 40, 128), (40, 128), (40, 128)],
        [(4, 40, 128), (7, 40, 128), (7, 40, 128), (7, 40, 128)],
    )(e2, far, fine1, late, f1w, g1w, w1)
    other1 = sibling(send)

    (out,) = call(
        fine_post_kernel,
        [(4, 64, 256)],
        windows + [(6,) + big, (8,) + big, (8,) + big, (320, 128)],
        limit=6,
    )(e1, edge, other1, outer, jnp.concatenate(again, axis=0), low0, high0, halo, u2)
    return out


def solution(mesh):
    spec = P("wide", "narrow", None)
    return jax.shard_map(body, mesh=mesh, in_specs=(spec,) * 4, out_specs=spec, check_vma=False)
```

```python
import functools

import jax
import jax.numpy as jnp
from jax import lax
from jax.experimental import pallas as pl
from jax.experimental.pallas import tpu as pltpu
from jax.sharding import PartitionSpec as P

THETA = 1.125
DELTA = 0.875
RATIO = THETA / DELTA
SIG = [0.0002 * 4.0**level for level in range(5)]
F32 = jnp.float32


def factors(degree):
    rho, out = 1.0 / RATIO, []
    for _ in range(degree - 1):
        new = 1.0 / (2.0 * RATIO - rho)
        out.append((new * rho, 2.0 * new / DELTA))
        rho = new
    return out


(KEEP, GAIN), = factors(2)


def roll(x, by, axis):
    return pltpu.roll(x, by % x.shape[axis], axis)


def gather_sum(below, here, above, c1, h1, c2, c3):
    first = c1 * below + h1 * above
    second = c2 * roll(here, 1, 0) + roll(c2 * here, -1, 0)
    third = c3 * roll(here, 1, 1) + roll(c3 * here, -1, 1)
    return first + second + third


def diagonal(sig, c1, h1, c2, c3):
    return sig + c1 + h1 + c2 + roll(c2, -1, 0) + c3 + roll(c3, -1, 1)


def iota(shape, dim):
    return lax.broadcasted_iota(jnp.int32, shape, dim)


def pairs_of_lanes(lanes, period, even=False):
    row, col = iota((lanes, 128), 0), iota((lanes, 128), 1) % period
    hit = row == 2 * col if even else row // 2 == col
    return hit.astype(F32)


def copies_of_lanes(lanes_in, lanes_out):
    row, col = iota((lanes_in, lanes_out), 0), iota((lanes_in, lanes_out), 1)
    return (row == col // 2).astype(F32)


def pieces(x):
    out = []
    for _ in range(3):
        part = x.astype(jnp.bfloat16)
        out.append(part)
        x = x - part.astype(F32)
    return out


def mul(x, ones):
    ones = ones.astype(jnp.bfloat16)
    high, mid, low = [jnp.dot(part, ones, preferred_element_type=F32) for part in pieces(x)]
    return high + (mid + low)


def mul_left(ones, x):
    ones = ones.astype(jnp.bfloat16)
    high, mid, low = [jnp.dot(ones, part, preferred_element_type=F32) for part in pieces(x)]
    return high + (mid + low)


def pair_rows(x, scratch, start=0, count=None, even=False):
    rows = x.shape[0]
    count = rows // 2 if count is None else count
    scratch[0:rows, :] = x
    first = scratch[pl.ds(start, count, stride=2), :]
    if even:
        return first
    return first + scratch[pl.ds(start + 1, count, stride=2), :]


def twice_rows(x, scratch):
    rows = x.shape[0]
    scratch[pl.ds(0, rows, stride=2), :] = x
    scratch[pl.ds(1, rows, stride=2), :] = x
    return scratch[0 : 2 * rows, :]


def coarse_coefs(planes, scratch, lanes, period, start=0, count=None):
    both = pairs_of_lanes(lanes, period)
    alone = pairs_of_lanes(lanes, period, even=True)
    return (
        0.25 * pair_rows(mul(planes[0], both), scratch, start, count),
        0.25 * pair_rows(mul(planes[1], both), scratch, start, count, even=True),
        0.25 * pair_rows(mul(planes[2], alone), scratch, start, count),
    )


def spread_block(x, block, width):
    lane = iota(x.shape, 1)
    x = jnp.where(lane // width == block, x, 0.0)
    while width < 128:
        x = x + pltpu.roll(x, width, 1)
        width *= 2
    return x


def smooth_two(u1, below, above, f, g, c1, h1, c2, c3):
    near = gather_sum(below, u1, above, c1, h1, c2, c3)
    return (1.0 + KEEP) * u1 + GAIN * (g * (f + near) - u1)


def first_post(v, below, above, f, g, c1, h1, c2, c3):
    near = gather_sum(below, v, above, c1, h1, c2, c3)
    return v + (1.0 / THETA) * (g * (f + near) - v)


def second_post(u, v, below, above, f, g, c1, h1, c2, c3):
    near = gather_sum(below, u, above, c1, h1, c2, c3)
    return u + KEEP * (u - v) + GAIN * (g * (f + near) - u)


def call(kernel, outs, scratch=(), places=(), out_places=(), limit=4):
    places, out_places = dict(places), dict(out_places)

    def run(*args):
        in_specs = [pl.BlockSpec(memory_space=places.get(i, pltpu.VMEM)) for i in range(len(args))]
        return pl.pallas_call(
            kernel,
            out_shape=[jax.ShapeDtypeStruct(s, F32) for s in outs],
            in_specs=in_specs,
            out_specs=[pl.BlockSpec(memory_space=out_places.get(i, pltpu.VMEM)) for i in range(len(outs))],
            scratch_shapes=[pltpu.VMEM(s, F32) if isinstance(s, tuple) else s for s in scratch],
            compiler_params=pltpu.CompilerParams(vmem_limit_bytes=limit * 2**20),
        )(*args)

    return run


def two_blocks(x):
    half = x.shape[0] // 2
    return jnp.where(iota((half, 128), 1) < 64, x[:half], x[half:])


def start_kernel(f, c1, c2, c3, up, down, out_far, out_sib, rows, planes, sems):
    par = lax.rem(lax.axis_index("wide"), 2)
    moves = []
    for k, (out, row) in enumerate(((up, 56), (down, 0))):
        for a, ref in enumerate((f, c1, c2, c3)):
            moves.append((ref.at[:, pl.ds(row, 8), :], rows.at[k, pl.ds(4 * a, 4)], out.at[pl.ds(4 * a, 4)]))
    for k, (out, upward) in enumerate(((out_far, par), (out_sib, 1 - par))):
        for a, ref in enumerate((f, c1, c2, c3, c1)):
            plane = 3 * upward if a < 4 else 1
            moves.append((ref.at[pl.ds(plane, 1)], planes.at[k, pl.ds(a, 1)], out.at[pl.ds(a, 1)]))
    first = [pltpu.make_async_copy(src, mid, sems.at[0, k]) for k, (src, mid, _) in enumerate(moves)]
    second = [pltpu.make_async_copy(mid, dst, sems.at[1, k]) for k, (_, mid, dst) in enumerate(moves)]
    for copy in first:
        copy.start()
    for one, two in zip(first, second):
        one.wait()
        two.start()
    for copy in second:
        copy.wait()


def pad_kernel(inner, low, high, own, coef1, out_far, out_sib, first, scr):
    for a in range(16):
        own[a, 0:8] = low[a]
        own[a, 8:72] = inner[a]
        own[a, 72:80] = high[a]
    par = lax.rem(lax.axis_index("wide"), 2)
    for k in range(2):
        diag = diagonal(SIG[0], own[5 + k], own[6 + k], own[9 + k], own[13 + k])
        first[k] = own[1 + k] / diag / THETA
    for out, up in ((out_far, par), (out_sib, 1 - par)):
        for a in range(5):
            plane = 4 * a + 3 * up if a < 4 else 5
            out[16 * a : 16 * a + 8] = own[plane, 0:8]
            out[16 * a + 8 : 16 * a + 16] = own[plane, 72:80]
        out[80:160] = first[up]
    k1 = jnp.concatenate([own[4], own[6]], axis=0)
    k2 = jnp.concatenate([own[8] + own[9], own[10] + own[11]], axis=0)
    k3 = jnp.concatenate([own[12] + own[13], own[14] + own[15]], axis=0)
    coarse = coarse_coefs((k1, k2, k3), scr, 256, 128)
    for a in range(3):
        for p in range(2):
            coef1[2 * a + p] = coarse[a][40 * p : 40 * p + 40]
    for out in (out_far, out_sib):
        for k in range(6):
            row, lane = 160 + 40 * (k // 2), 128 * (k % 2)
            out[row : row + 40, lane : lane + 128] = coef1[k]


def block(index):
    row, lane = 160 + 40 * (index // 2), 128 * (index % 2)
    return slice(row, row + 40), slice(lane, lane + 128)


def sides(far, sib):
    odd = lax.rem(lax.axis_index("wide"), 2) == 1

    def below(*at):
        return jnp.where(odd, sib[at], far[at])

    def above(*at):
        return jnp.where(odd, far[at], sib[at])

    return below, above


CHUNK = 16


def chunked(rows, body):
    for r0 in range(0, rows, CHUNK):
        body(r0, rows)


def near_chunk(u, p, c1, c2, c3, q, r0, rows):
    here = pl.ds(r0, CHUNK)
    x = u[p, here, :]
    if r0 > 0:
        lower = u[p, pl.ds(r0 - 1, CHUNK), :]
    else:
        lower = roll(x, 1, 0)
    if r0 + CHUNK < rows:
        after = pl.ds(r0 + 1, CHUNK)
        upper = c2[q, after, :] * u[p, after, :]
    else:
        upper = roll(c2[q, here, :] * x, -1, 0)
    k3 = c3[q, here, :]
    first = c1[q, here, :] * u[p - 1, here, :] + c1[q + 1, here, :] * u[p + 1, here, :]
    second = c2[q, here, :] * lower + upper
    third = k3 * roll(x, 1, 1) + roll(k3 * x, -1, 1)
    return x, first + second + third


def diag_chunk(c1, c2, c3, q, r0, rows):
    here = pl.ds(r0, CHUNK)
    k2, k3 = c2[q, here, :], c3[q, here, :]
    if r0 + CHUNK < rows:
        h2 = c2[q, pl.ds(r0 + 1, CHUNK), :]
    else:
        h2 = roll(k2, -1, 0)
    return SIG[0] + c1[q, here, :] + c1[q + 1, here, :] + k2 + h2 + k3 + roll(k3, -1, 1)


def fine_pre_kernel(own, coef1, far_raw, sib_raw, far, sib, halo, u2, w1, out_far, out_sib, f, c1, c2, c3, g, f1, u1, res, scr):
    below, above = sides(far, sib)
    below_raw, above_raw = sides(far_raw, sib_raw)
    for a, ref in enumerate((f, c1, c2, c3)):
        ref[1:5] = own[4 * a : 4 * a + 4]
    for a, ref, q, raw, rest in (
        [(a, ref, 0, below_raw, below) for a, ref in enumerate((f, c1, c2, c3))]
        + [(a, ref, 5, above_raw, above) for a, ref in enumerate((f, c1, c2, c3))]
        + [(4, c1, 6, above_raw, above)]
    ):
        ref[q, 0:8] = rest(slice(16 * a, 16 * a + 8))
        ref[q, 8:72] = raw(a)
        ref[q, 72:80] = rest(slice(16 * a + 8, 16 * a + 16))
    for a, ref in enumerate((f, c1, c2, c3)):
        halo[a] = ref[0]
        halo[4 + a] = ref[5]
    halo[8] = c1[6]
    u1[0] = below(slice(80, 160))
    u1[7] = above(slice(80, 160))

    def smooth_first(q, carry):
        def rows(r0, n):
            here = pl.ds(r0, CHUNK)
            inverse = 1.0 / diag_chunk(c1, c2, c3, q, r0, n)
            g[q, here, :] = inverse
            u1[q + 1, here, :] = f[q, here, :] * inverse * (1.0 / THETA)

        chunked(80, rows)
        return carry

    lax.fori_loop(0, 6, smooth_first, 0)

    def smooth_second(q, carry):
        def rows(r0, n):
            here = pl.ds(r0, CHUNK)
            x, near = near_chunk(u1, q + 1, c1, c2, c3, q, r0, n)
            u2[q, here, :] = (1.0 + KEEP) * x + GAIN * (g[q, here, :] * (f[q, here, :] + near) - x)

        chunked(80, rows)
        return carry

    lax.fori_loop(0, 6, smooth_second, 0)

    def residual(q, carry):
        def rows(r0, n):
            here = pl.ds(r0, CHUNK)
            x, near = near_chunk(u2, q, c1, c2, c3, q, r0, n)
            res[q - 1, here, :] = f[q, here, :] + near - diag_chunk(c1, c2, c3, q, r0, n) * x

        chunked(80, rows)
        return carry

    lax.fori_loop(1, 5, residual, 0)

    both = pairs_of_lanes(256, 128)
    sums = jnp.concatenate([res[0] + res[1], res[2] + res[3]], axis=0)
    coarse = 0.5 * pair_rows(mul(sums, both), scr)
    f1[0] = coarse[:40]
    f1[1] = coarse[40:]
    for a in range(3):
        for p in range(2):
            w1[6 * a + p] = below(*block(2 * a + p))
            w1[6 * a + 2 + p] = coef1[2 * a + p]
            w1[6 * a + 4 + p] = above(*block(2 * a + p))
    for p in range(2):
        k = p + 2
        inverse = 1.0 / diagonal(SIG[1], w1[k], w1[k + 1], w1[6 + k], w1[12 + k])
        for out in (out_far, out_sib):
            out[p] = f1[p]
            out[2 + p] = inverse
    par = lax.rem(lax.axis_index("wide"), 2)
    for out, plane in ((out_far, 2 + par), (out_sib, 3 - par)):
        out[4] = u2[plane, 0:40, 0:128]
        out[5] = u2[plane, 0:40, 128:256]
        out[6] = u2[plane, 40:80, 0:128]
        out[7] = u2[plane, 40:80, 128:256]


def coarse_coef_kernel(w1, out, scr):
    k1 = jnp.concatenate([w1[2], w1[4]], axis=0)
    k2, k3 = w1[8] + w1[9], w1[14] + w1[15]
    both, alone = pairs_of_lanes(128, 64), pairs_of_lanes(128, 64, even=True)
    k1 = 0.25 * pair_rows(mul(k1, both), scr)
    k2 = 0.25 * pair_rows(mul(k2, both), scr, even=True)
    k3 = 0.25 * pair_rows(mul(k3, alone), scr)
    for k, x in enumerate((k1[2:18], k1[22:38], k2[2:18], k3[2:18])):
        out[8 * k : 8 * k + 8] = two_blocks(x)


def middle_pre_kernel(own, far, sib, w1, coefs, f, g, u2, f2, up, down, outer, u1, scr):
    below, above = sides(far, sib)
    for k, read in enumerate((below, own.__getitem__, above)):
        for p in range(2):
            f[2 * k + p] = read(p)
            g[2 * k + p] = read(2 + p)
    for k, read in enumerate((below, above)):
        outer[k, 0:40, 0:128] = read(4)
        outer[k, 0:40, 128:256] = read(5)
        outer[k, 40:80, 0:128] = read(6)
        outer[k, 40:80, 128:256] = read(7)
    for p in range(6):
        u1[p] = f[p] * g[p] * (1.0 / THETA)
    u2[0] = u1[0]
    u2[5] = u1[5]
    for p in range(1, 5):
        u2[p] = smooth_two(u1[p], u1[p - 1], u1[p + 1], f[p], g[p], w1[p], w1[p + 1], w1[6 + p], w1[12 + p])
    total = 0.0
    for p in (2, 3):
        k1, h1, k2, k3 = w1[p], w1[p + 1], w1[6 + p], w1[12 + p]
        near = gather_sum(u2[p - 1], u2[p], u2[p + 1], k1, h1, k2, k3)
        total = total + (f[p] + near - diagonal(SIG[1], k1, h1, k2, k3) * u2[p])
    coarse = 0.5 * pair_rows(mul(total, pairs_of_lanes(128, 64)), scr, 4, 16)
    f2[0:8] = two_blocks(coarse)
    f2[8:40] = coefs[...]
    for p in range(2):
        up[40 + 8 * p : 48 + 8 * p] = u2[2 + p, 28:36]
        down[40 + 8 * p : 48 + 8 * p] = u2[2 + p, 4:12]
    up[0:40] = f2[...]
    down[0:40] = f2[...]


def both_halves(x):
    return jnp.concatenate([spread_block(x, 0, 64), spread_block(x, 1, 64)], axis=0)


def coarse_start_kernel(f2, low, high, far, u2fine, own, msg):
    n = lax.axis_index("narrow")
    for piece, by in ((f2, 0), (high, 1), (far, 2), (low, 3)):
        at = pl.multiple_of(16 * lax.rem(n + by, 4), 16)
        for k in range(5):
            own[k, pl.ds(at, 16), :] = both_halves(piece[8 * k : 8 * k + 8])
    own[5] = 1.0 / diagonal(SIG[2], own[1], own[2], own[3], own[4])
    for k, plane in enumerate((0, 5, 1, 3, 4)):
        msg[32 * k : 32 * k + 32] = two_blocks(own[plane])
    for p in range(2):
        at = 160 + 40 * p
        msg[at : at + 40] = u2fine[2 + p]
        msg[at : at + 4] = low[44 + 8 * p : 48 + 8 * p]
        msg[at + 36 : at + 40] = high[40 + 8 * p : 44 + 8 * p]


def coarse_tiles_kernel(msg, sib, tiles, scr):
    odd = lax.rem(lax.axis_index("wide"), 2) == 1
    for a in range(3):
        here = slice(64 + 32 * a, 96 + 32 * a)
        x = jnp.where(odd, sib[here], msg[here]) if a == 0 else msg[here] + sib[here]
        scr[...] = 0.25 * mul(both_halves(x), pairs_of_lanes(128, 32, even=a == 2))
        tiles[a] = tile_of(scr, a == 1)


def tile_of(scr, even=False):
    block = iota((8, 128), 1) // 32
    packed = 0.0
    for q in range(4):
        part = scr[pl.ds(2 * q, 8, stride=8), :]
        if not even:
            part = part + scr[pl.ds(2 * q + 1, 8, stride=8), :]
        packed = jnp.where(block == q, part, packed)
    return packed


def coarse_swap_kernel(own, msg, sib, w1, out):
    out[0:160] = msg[0:160]
    out[160:192] = sib[0:32] * sib[32:64] * (1.0 / THETA)
    out[192:224] = two_blocks(own[2])
    out[224:304] = msg[160:240]
    par = lax.rem(lax.axis_index("wide"), 2)
    out[304:344] = sib[pl.ds(pl.multiple_of(160 + 40 * par, 8), 40), :]
    out[344:384] = w1[4]


def coarse_pre_kernel(own, msg, sib, near, other, w, u2, late, fine, u1):
    for p in range(2):
        fine[p] = sib[160 + 40 * p : 200 + 40 * p]
        fine[2 + p] = msg[160 + 40 * p : 200 + 40 * p]
    for p in range(4):
        fine[4 + p] = near[224 + 40 * p : 264 + 40 * p]
    odd = lax.rem(lax.axis_index("wide"), 2) == 1

    def below(k):
        here = slice(32 * k, 32 * k + 32)
        return both_halves(jnp.where(odd, other[here], near[here]))

    def above(k):
        here = slice(32 * k, 32 * k + 32)
        return both_halves(jnp.where(odd, near[here], other[here]))

    for a, (base, plane) in enumerate(((0, 0), (4, 5), (8, 1), (13, 3), (17, 4))):
        mine, theirs = own[plane], both_halves(sib[32 * a : 32 * a + 32])
        w[base] = below(a)
        w[base + 1] = jnp.where(odd, theirs, mine)
        w[base + 2] = jnp.where(odd, mine, theirs)
        w[base + 3] = above(a)
    w[12] = above(6)
    u1[0] = below(5)
    u1[5] = above(5)
    for k in range(4):
        u1[k + 1] = w[k] * w[4 + k] * (1.0 / THETA)
    for k in range(4):
        u2[k] = smooth_two(u1[k + 1], u1[k], u1[k + 2], w[k], w[4 + k], w[8 + k], w[9 + k], w[13 + k], w[17 + k])
    late[...] = two_blocks(jnp.where(odd, u2[1], u2[2]))


def coarse_send_kernel(w, u2, tiles, send, scr):
    odd = lax.rem(lax.axis_index("wide"), 2) == 1
    total = 0.0
    for k in (1, 2):
        args = (w[8 + k], w[9 + k], w[13 + k], w[17 + k])
        near = gather_sum(u2[k - 1], u2[k], u2[k + 1], *args)
        total = total + (w[k] + near - diagonal(SIG[2], *args) * u2[k])
    scr[...] = 0.5 * mul(total, pairs_of_lanes(128, 32))
    first = jnp.where(odd, tiles[1], tile_of(scr))
    second = jnp.where(odd, tiles[2], tiles[0])
    for k in range(send.shape[0]):
        send[k, 0] = first
        send[k, 1] = second


def packed_sum(below, x, above, c1, h1, c2, c3, width, blocks):
    lane = iota(x.shape, 2)
    block, inner = lane // width % blocks, lane % width

    def second_down(x):
        x = pltpu.roll(x, width, 2)
        return jnp.where(block == 0, pltpu.roll(x, 1, 1), x)

    def second_up(x):
        x = pltpu.roll(x, 128 - width, 2)
        return jnp.where(block == blocks - 1, pltpu.roll(x, 7, 1), x)

    def third_down(x):
        return jnp.where(inner == 0, pltpu.roll(x, 129 - width, 2), pltpu.roll(x, 1, 2))

    def third_up(x):
        return jnp.where(inner == width - 1, pltpu.roll(x, width - 1, 2), pltpu.roll(x, 127, 2))

    first = c1 * below + h1 * above
    second = c2 * second_down(x) + second_up(c2 * x)
    third = c3 * third_down(x) + third_up(c3 * x)
    return first + second + third


def packed_diagonal(sig, c1, h1, c2, c3, width, blocks):
    lane = iota(c1.shape, 2)
    block, inner = lane // width % blocks, lane % width
    h2 = pltpu.roll(c2, 128 - width, 2)
    h2 = jnp.where(block == blocks - 1, pltpu.roll(h2, 7, 1), h2)
    h3 = jnp.where(inner == width - 1, pltpu.roll(c3, width - 1, 2), pltpu.roll(c3, 127, 2))
    return sig + c1 + h1 + c2 + h2 + c3 + h3


def fold_matrix(even2=False, even3=False):
    k, j = iota((128, 128), 0), iota((128, 128), 1)
    k2, k3, j2, j3 = k // 32, k % 32, j // 16 % 2, j % 16
    hit2 = k2 == 2 * j2 if even2 else k2 // 2 == j2
    hit3 = k3 == 2 * j3 if even3 else k3 // 2 == j3
    return (hit2 & hit3).astype(F32)


def wrap(ref, count):
    ref[0] = ref[count]
    ref[count + 1] = ref[1]


def around(j, n):
    return lax.rem(j + n, n)


STEP = 32
THREE, FOUR = (32, 4), (16, 2)


def bottom_kernel(mine, theirs, e2,
                  f3, c1, c2, c3, d3, g3, u1, u2, res, f4, d1, d2, e3, g4, ua, ub, st, scr):
    n3, n4 = f3.shape[0], f4.shape[0]

    def loop(body):
        def step(c, carry):
            body(pl.multiple_of(c * STEP, STEP))
            return carry

        lax.fori_loop(0, n3 // STEP, step, 0)

    odd = lax.rem(lax.axis_index("wide"), 2) == 1

    def load(j):
        here = pl.ds(j, STEP)
        a, b, c, d = mine[here, 0], mine[here, 1], theirs[here, 0], theirs[here, 1]
        f3[here] = jnp.where(odd, c, a)
        c1[here] = jnp.where(odd, d, b)
        c2[here] = jnp.where(odd, a, c)
        c3[here] = jnp.where(odd, b, d)

    loop(load)
    c1[n3] = c1[0]

    def start(j):
        here = pl.ds(j, STEP)
        diag = packed_diagonal(SIG[3], c1[here], c1[pl.ds(j + 1, STEP)], c2[here], c3[here], *THREE)
        inverse = 1.0 / diag
        d3[here] = diag
        g3[here] = inverse
        u1[pl.ds(j + 1, STEP)] = f3[here] * inverse * (1.0 / THETA)

    loop(start)
    wrap(u1, n3)

    def near3(u, j):
        here = pl.ds(j, STEP)
        x = u[pl.ds(j + 1, STEP)]
        args = (c1[here], c1[pl.ds(j + 1, STEP)], c2[here], c3[here])
        return here, x, packed_sum(u[here], x, u[pl.ds(j + 2, STEP)], *args, *THREE)

    def pre(j):
        here, x, near = near3(u1, j)
        u2[pl.ds(j + 1, STEP)] = (1.0 + KEEP) * x + GAIN * (g3[here] * (f3[here] + near) - x)

    loop(pre)
    wrap(u2, n3)

    def residual(j):
        here, x, near = near3(u2, j)
        left = (f3[here] + near - d3[here] * x).reshape(STEP // 2, 2, 8, 128)
        res[pl.ds(j // 2, STEP // 2)] = left[:, 0] + left[:, 1]

    loop(residual)

    def fold(x, *even):
        return mul(x.reshape(8 * n4, 128), fold_matrix(*even)).reshape(n4, 8, 128)

    def halves(ref):
        x = ref[0:n3].reshape(n4, 2, 8, 128)
        return x[:, 0], x[:, 1]

    f4[...] = 0.5 * fold(res[...])
    d1[0:n4] = 0.25 * fold(halves(c1)[0])
    d1[n4] = d1[0]
    d2[...] = 0.25 * fold(sum(halves(c2)), True, False)
    e3[...] = 0.25 * fold(sum(halves(c3)), False, True)
    coefs4 = (d1[0:n4], d1[1 : n4 + 1], d2[...], e3[...])
    g4[...] = 1.0 / packed_diagonal(SIG[4], *coefs4, *FOUR)
    x = f4[...] * g4[...] * (1.0 / THETA)
    ua[1 : n4 + 1] = x
    wrap(ua, n4)
    st[...] = x
    src, dst = ua, ub
    for keep, gain in factors(4):
        x = src[1 : n4 + 1]
        near = packed_sum(src[0:n4], x, src[2 : n4 + 2], d1[0:n4], d1[1 : n4 + 1], d2[...], e3[...], *FOUR)
        step = keep * st[...] + gain * (g4[...] * (f4[...] + near) - x)
        st[...] = step
        dst[1 : n4 + 1] = x + step
        wrap(dst, n4)
        src, dst = dst, src

    j0 = around(lax.axis_index("wide") // 2 - 1, n3)
    k, j = iota((128, 128), 0), iota((128, 128), 1)
    unfold = (k == 16 * (j // 64) + j % 32 // 2).astype(F32)
    coarse = jnp.concatenate([src[1 + around(around(j0 - 2, n3) // 2 + m, n4)] for m in range(4)], axis=0)
    scr[0:32] = mul(coarse, unfold)
    shifted = lax.rem(around(j0 - 2, n3), 2)
    js = [around(j0 - 2 + m, n3) for m in range(7)]
    v = [u2[1 + js[m]] + scr[pl.ds(pl.multiple_of(8 * ((shifted + m) // 2), 8), 8), :] for m in range(7)]
    v = jnp.stack(v)

    def window(ref, first, count, by=0):
        return jnp.stack([ref[js[m] + by] for m in range(first, first + count)])

    def args(first, count):
        return window(c1, first, count), window(c1, first, count, 1), window(c2, first, count), window(c3, first, count)

    f, g = window(f3, 1, 5), window(g3, 1, 5)
    near = packed_sum(v[0:5], v[1:6], v[2:7], *args(1, 5), *THREE)
    w = v[1:6] + (1.0 / THETA) * (g * (f + near) - v[1:6])
    near = packed_sum(w[0:3], w[1:4], w[2:5], *args(2, 3), *THREE)
    x = w[1:4] + KEEP * (w[1:4] - v[2:5]) + GAIN * (g[1:4] * (f[1:4] + near) - w[1:4])
    x = x.reshape(24, 128)
    for q in range(4):
        fine = mul(x, (k == 32 * q + j % 64 // 2).astype(F32))
        e2[pl.ds(2 * q, 24, stride=8), :] = fine
        e2[pl.ds(2 * q + 1, 24, stride=8), :] = fine


def coarse_post_kernel(e2, win, u2, late, late_sib, out):
    below, above = sides(late, late_sib)
    v = [both_halves(below(...)), u2[0], u2[1], u2[2], u2[3], both_halves(above(...))]
    v = [v[m] + e2[64 * (m // 2) : 64 * (m // 2) + 64, :] for m in range(6)]

    def args(k):
        return win[k], win[4 + k], win[8 + k], win[9 + k], win[13 + k], win[17 + k]

    w = [first_post(v[m + 1], v[m], v[m + 2], *args(m)) for m in range(4)]
    for p in range(2):
        x = second_post(w[p + 1], v[p + 2], w[p], w[p + 2], *args(p + 1))
        out[p] = pltpu.roll(x, lax.rem(72 - 16 * lax.axis_index("narrow"), 64), 0)[0:32]


def middle_post_kernel(e2, far, u2, f, g, w1, own, edge, send, fine, c1, v, w):
    par = lax.rem(lax.axis_index("wide"), 2)
    odd = par == 1
    row, col = iota((40, 32), 0), iota((40, 32), 1)
    pick = (col == (row + 4) // 2 + 4).astype(F32)
    lanes = copies_of_lanes(128, 128)
    planes = (e2[0], e2[1], far[0], far[1])
    for k in range(4):
        fine[k] = mul(mul_left(pick, jnp.where(odd, planes[k], planes[(k + 2) % 4])), lanes)
    c1[0:6] = w1[0:6]
    c1[6] = u2[7]
    sibs, ours, next_chip = ([u2[k] for k in some] for some in ((0, 1), (2, 3), (4, 5, 6)))
    upper = sibs + ours + next_chip
    lower = [next_chip[2]] + next_chip[:2] + ours + sibs
    for i in range(7):
        v[i] = jnp.where(odd, upper[i], lower[i]) + fine[(i + 1 - par) // 2]

    def args(i):
        k = i - 1 + par
        return f[k], g[k], c1[k], c1[k + 1], w1[6 + k], w1[12 + k]

    for i in range(1, 6):
        w[i] = first_post(v[i], v[i - 1], v[i + 1], *args(i))
    out = [second_post(w[i], v[i], w[i - 1], w[i + 1], *args(i)) for i in (2, 3, 4)]
    own[0] = jnp.where(odd, out[0], out[1])
    own[1] = jnp.where(odd, out[1], out[2])
    edge[...] = jnp.where(odd, out[2], out[0])
    send[...] = jnp.where(odd, out[0], out[2])


def fine_post_kernel(e1, edge, other, outer, inner, low, high, halo, u2, result, f, c1, c2, c3, g, v, w, scr, out, sems):
    for a, ref in enumerate((f, c1, c2, c3)):
        ref[0] = halo[a]
        ref[5] = halo[4 + a]
        for p in range(4):
            ref[p + 1, 0:8] = low[4 * a + p]
            ref[p + 1, 8:72] = inner[4 * a + p]
            ref[p + 1, 72:80] = high[4 * a + p]
    c1[6] = halo[8]
    below, above = sides(edge, other)
    x = jnp.concatenate([below(...), e1[0], e1[1], above(...)], axis=0)
    for half in range(2):
        here = slice(128 * half, 128 * half + 128)
        row, col = iota((128, 128), 0), iota((128, 128), 1)
        fine = mul(x, (row == 64 * half + col // 2).astype(F32))
        scr[pl.ds(0, 160, stride=2), :] = fine
        scr[pl.ds(1, 160, stride=2), :] = fine
        for k in range(8):
            at = 80 * (k // 2)
            base = u2[k - 1, :, here] if 0 < k < 7 else outer[k // 7, :, here]
            v[k, :, here] = base + scr[at : at + 80, :]

    def post1(q, carry):
        def chunk(r0, n):
            here = pl.ds(r0, CHUNK)
            x, near = near_chunk(v, q + 1, c1, c2, c3, q, r0, n)
            inverse = 1.0 / diag_chunk(c1, c2, c3, q, r0, n)
            g[q, here, :] = inverse
            w[q + 1, here, :] = x + (1.0 / THETA) * (inverse * (f[q, here, :] + near) - x)

        chunked(80, chunk)
        return carry

    lax.fori_loop(0, 6, post1, 0)

    def post2(q, carry):
        for r0 in range(8, 72, CHUNK):
            here = pl.ds(r0, CHUNK)
            x, near = near_chunk(w, q + 1, c1, c2, c3, q, r0, 80)
            step = KEEP * (x - v[q + 1, here, :]) + GAIN * (g[q, here, :] * (f[q, here, :] + near) - x)
            out[q - 1, pl.ds(r0 - 8, CHUNK), :] = x + step
        return carry

    copies = []
    for p in range(4):
        post2(p + 1, 0)
        copies.append(pltpu.make_async_copy(out.at[pl.ds(p, 1)], result.at[pl.ds(p, 1)], sems.at[p]))
        copies[p].start()
    for copy in copies:
        copy.wait()


def shift(x, axis, by):
    count = lax.axis_size(axis)
    return lax.ppermute(x, axis, [(i, (i + by) % count) for i in range(count)])


def sibling(x):
    return lax.ppermute(x, "wide", [(i, i ^ 1) for i in range(lax.axis_size("wide"))])


def across(x):
    count = lax.axis_size("wide")
    return lax.ppermute(x, "wide", [(i, (i + 1 if i % 2 else i - 1) % count) for i in range(count)])


def body(source, coef_first, coef_second, coef_third):
    wide = lax.axis_size("wide")
    n3, n4 = wide // 2, wide // 4
    big = (80, 256)
    inputs = (source, coef_first, coef_second, coef_third)

    up, down, far_raw, sib_raw = call(
        start_kernel,
        [(16, 8, 256), (16, 8, 256), (5, 64, 256), (5, 64, 256)],
        [(2, 16, 8, 256), (2, 5, 64, 256), pltpu.SemaphoreType.DMA((2, 18))],
        {k: pltpu.HBM for k in range(4)},
        {k: pltpu.HBM for k in range(4)},
        limit=60,
    )(*inputs)
    far_raw, sib_raw = across(far_raw), sibling(sib_raw)
    low0, high0 = shift(up, "narrow", 1), shift(down, "narrow", -1)

    own, coef1, far, sib = call(
        pad_kernel, [(16,) + big, (6, 40, 128), (280, 256), (280, 256)], [(2,) + big, (160, 128)]
    )(jnp.concatenate(inputs, axis=0), low0, high0)
    far, sib = across(far), sibling(sib)

    windows = [(6,) + big, (7,) + big, (6,) + big, (6,) + big]
    halo, u2, w1, out_far, out_sib = call(
        fine_pre_kernel,
        [(9,) + big, (6,) + big, (18, 40, 128), (8, 40, 128), (8, 40, 128)],
        windows + [(6,) + big, (2, 40, 128), (8,) + big, (4,) + big, (160, 128)],
        limit=6,
    )(own, coef1, far_raw, sib_raw, far, sib)
    far1, sib1 = across(out_far), sibling(out_sib)
    (coefs,) = call(coarse_coef_kernel, [(32, 128)], [(80, 128)])(w1)

    six = (6, 40, 128)
    f1w, g1w, u2m, f2, up, down, outer = call(
        middle_pre_kernel, [six, six, six, (40, 128), (56, 128), (56, 128), (2,) + big], [six, (40, 128)]
    )(out_far, far1, sib1, w1, coefs)
    low, high, far = shift(up, "narrow", 1), shift(down, "narrow", -1), shift(f2, "narrow", 2)

    own2, msg = call(coarse_start_kernel, [(6, 64, 128), (240, 128)])(f2, low, high, far, u2m)
    sib = sibling(msg)
    (swap,) = call(coarse_swap_kernel, [(384, 128)])(own2, msg, sib, w1)
    near = across(swap)
    (tiles,) = call(coarse_tiles_kernel, [(3, 8, 128)], [(64, 128)])(msg, sib)
    near, tiles = lax.optimization_barrier((near, tiles))
    other = sibling(near)
    w2, u2w, late, fine1 = call(
        coarse_pre_kernel, [(21, 64, 128), (4, 64, 128), (32, 128), (8, 40, 128)], [(6, 64, 128)]
    )(own2, msg, sib, near, other)
    (send,) = call(coarse_send_kernel, [(n3, 2, 8, 128)], [(64, 128)])(w2, u2w, tiles)
    late = across(late)
    cores = [[k for k in range(wide) if k % 2 == c] for c in range(2)]
    parts = lax.all_to_all(send, "wide", split_axis=0, concat_axis=0, tiled=True, axis_index_groups=cores)
    parts, late = lax.optimization_barrier((parts, late))
    theirs, late_sib = sibling(parts), sibling(late)

    three, four = (n3, 8, 128), (n4, 8, 128)
    (fine2,) = call(
        bottom_kernel,
        [(192, 128)],
        [three, (n3 + 1, 8, 128), three, three, three, three, (n3 + 2, 8, 128), (n3 + 2, 8, 128), four, four]
        + [(n4 + 1, 8, 128), four, four, four, (n4 + 2, 8, 128), (n4 + 2, 8, 128), four, (32, 128)],
    )(parts, theirs)
    (e2,) = call(coarse_post_kernel, [(2, 32, 128)])(fine2, w2, u2w, late, late_sib)
    e2, *again = lax.optimization_barrier((e2,) + inputs)
    far = across(e2)

    e1, edge, send = call(
        middle_post_kernel,
        [(2, 40, 128), (40, 128), (40, 128)],
        [(4, 40, 128), (7, 40, 128), (7, 40, 128), (7, 40, 128)],
    )(e2, far, fine1, f1w, g1w, w1)
    other1 = sibling(send)

    (out,) = call(
        fine_post_kernel,
        [(4, 64, 256)],
        windows + [(6,) + big, (8,) + big, (8,) + big, (320, 128), (4, 64, 256), pltpu.SemaphoreType.DMA((4,))],
        out_places={0: pltpu.HBM},
        limit=6,
    )(e1, edge, other1, outer, jnp.concatenate(again, axis=0), low0, high0, halo, u2)
    return out


def solution(mesh):
    spec = P("wide", "narrow", None)
    return jax.shard_map(body, mesh=mesh, in_specs=(spec,) * 4, out_specs=spec, check_vma=False)
```

```python
import functools

import jax
import jax.numpy as jnp
from jax import lax
from jax.experimental import pallas as pl
from jax.experimental.pallas import tpu as pltpu
from jax.sharding import PartitionSpec as P

THETA = 1.125
DELTA = 0.875
RATIO = THETA / DELTA
SIG = [0.0002 * 4.0**level for level in range(5)]
F32 = jnp.float32


def factors(degree):
    rho, out = 1.0 / RATIO, []
    for _ in range(degree - 1):
        new = 1.0 / (2.0 * RATIO - rho)
        out.append((new * rho, 2.0 * new / DELTA))
        rho = new
    return out


(KEEP, GAIN), = factors(2)


def roll(x, by, axis):
    return pltpu.roll(x, by % x.shape[axis], axis)


def gather_sum(below, here, above, c1, h1, c2, c3):
    first = c1 * below + h1 * above
    second = c2 * roll(here, 1, 0) + roll(c2 * here, -1, 0)
    third = c3 * roll(here, 1, 1) + roll(c3 * here, -1, 1)
    return first + second + third


def diagonal(sig, c1, h1, c2, c3):
    return sig + c1 + h1 + c2 + roll(c2, -1, 0) + c3 + roll(c3, -1, 1)


def iota(shape, dim):
    return lax.broadcasted_iota(jnp.int32, shape, dim)


def pairs_of_lanes(lanes, period, even=False):
    row, col = iota((lanes, 128), 0), iota((lanes, 128), 1) % period
    hit = row == 2 * col if even else row // 2 == col
    return hit.astype(F32)


def copies_of_lanes(lanes_in, lanes_out):
    row, col = iota((lanes_in, lanes_out), 0), iota((lanes_in, lanes_out), 1)
    return (row == col // 2).astype(F32)


def pieces(x):
    out = []
    for _ in range(3):
        part = x.astype(jnp.bfloat16)
        out.append(part)
        x = x - part.astype(F32)
    return out


def mul(x, ones):
    ones = ones.astype(jnp.bfloat16)
    high, mid, low = [jnp.dot(part, ones, preferred_element_type=F32) for part in pieces(x)]
    return high + (mid + low)


def mul_left(ones, x):
    ones = ones.astype(jnp.bfloat16)
    high, mid, low = [jnp.dot(ones, part, preferred_element_type=F32) for part in pieces(x)]
    return high + (mid + low)


def pair_rows(x, scratch, start=0, count=None, even=False):
    rows = x.shape[0]
    count = rows // 2 if count is None else count
    scratch[0:rows, :] = x
    first = scratch[pl.ds(start, count, stride=2), :]
    if even:
        return first
    return first + scratch[pl.ds(start + 1, count, stride=2), :]


def twice_rows(x, scratch):
    rows = x.shape[0]
    scratch[pl.ds(0, rows, stride=2), :] = x
    scratch[pl.ds(1, rows, stride=2), :] = x
    return scratch[0 : 2 * rows, :]


def coarse_coefs(planes, scratch, lanes, period, start=0, count=None):
    both = pairs_of_lanes(lanes, period)
    alone = pairs_of_lanes(lanes, period, even=True)
    return (
        0.25 * pair_rows(mul(planes[0], both), scratch, start, count),
        0.25 * pair_rows(mul(planes[1], both), scratch, start, count, even=True),
        0.25 * pair_rows(mul(planes[2], alone), scratch, start, count),
    )


def spread_block(x, block, width):
    lane = iota(x.shape, 1)
    x = jnp.where(lane // width == block, x, 0.0)
    while width < 128:
        x = x + pltpu.roll(x, width, 1)
        width *= 2
    return x


def smooth_two(u1, below, above, f, g, c1, h1, c2, c3):
    near = gather_sum(below, u1, above, c1, h1, c2, c3)
    return (1.0 + KEEP) * u1 + GAIN * (g * (f + near) - u1)


def first_post(v, below, above, f, g, c1, h1, c2, c3):
    near = gather_sum(below, v, above, c1, h1, c2, c3)
    return v + (1.0 / THETA) * (g * (f + near) - v)


def second_post(u, v, below, above, f, g, c1, h1, c2, c3):
    near = gather_sum(below, u, above, c1, h1, c2, c3)
    return u + KEEP * (u - v) + GAIN * (g * (f + near) - u)


def call(kernel, outs, scratch=(), places=(), out_places=(), limit=4):
    places, out_places = dict(places), dict(out_places)

    def run(*args):
        in_specs = [pl.BlockSpec(memory_space=places.get(i, pltpu.VMEM)) for i in range(len(args))]
        return pl.pallas_call(
            kernel,
            out_shape=[jax.ShapeDtypeStruct(s, F32) for s in outs],
            in_specs=in_specs,
            out_specs=[pl.BlockSpec(memory_space=out_places.get(i, pltpu.VMEM)) for i in range(len(outs))],
            scratch_shapes=[pltpu.VMEM(s, F32) if isinstance(s, tuple) else s for s in scratch],
            compiler_params=pltpu.CompilerParams(vmem_limit_bytes=limit * 2**20),
        )(*args)

    return run


def two_blocks(x):
    half = x.shape[0] // 2
    return jnp.where(iota((half, 128), 1) < 64, x[:half], x[half:])


def start_kernel(f, c1, c2, c3, up, down, out_far, out_sib, rows, planes, sems):
    par = lax.rem(lax.axis_index("wide"), 2)
    moves = []
    for k, (out, row) in enumerate(((up, 56), (down, 0))):
        for a, ref in enumerate((f, c1, c2, c3)):
            moves.append((ref.at[:, pl.ds(row, 8), :], rows.at[k, pl.ds(4 * a, 4)], out.at[pl.ds(4 * a, 4)]))
    for k, (out, upward) in enumerate(((out_far, par), (out_sib, 1 - par))):
        for a, ref in enumerate((f, c1, c2, c3, c1)):
            plane = 3 * upward if a < 4 else 1
            moves.append((ref.at[pl.ds(plane, 1)], planes.at[k, pl.ds(a, 1)], out.at[pl.ds(a, 1)]))
    first = [pltpu.make_async_copy(src, mid, sems.at[0, k]) for k, (src, mid, _) in enumerate(moves)]
    second = [pltpu.make_async_copy(mid, dst, sems.at[1, k]) for k, (_, mid, dst) in enumerate(moves)]
    for copy in first:
        copy.start()
    for one, two in zip(first, second):
        one.wait()
        two.start()
    for copy in second:
        copy.wait()


def pad_kernel(inner, low, high, own, coef1, out_far, out_sib, first, scr):
    for a in range(16):
        own[a, 0:8] = low[a]
        own[a, 8:72] = inner[a]
        own[a, 72:80] = high[a]
    par = lax.rem(lax.axis_index("wide"), 2)
    for k in range(2):
        diag = diagonal(SIG[0], own[5 + k], own[6 + k], own[9 + k], own[13 + k])
        first[k] = own[1 + k] / diag / THETA
    for out, up in ((out_far, par), (out_sib, 1 - par)):
        for a in range(5):
            plane = 4 * a + 3 * up if a < 4 else 5
            out[16 * a : 16 * a + 8] = own[plane, 0:8]
            out[16 * a + 8 : 16 * a + 16] = own[plane, 72:80]
        out[80:160] = first[up]
    k1 = jnp.concatenate([own[4], own[6]], axis=0)
    k2 = jnp.concatenate([own[8] + own[9], own[10] + own[11]], axis=0)
    k3 = jnp.concatenate([own[12] + own[13], own[14] + own[15]], axis=0)
    coarse = coarse_coefs((k1, k2, k3), scr, 256, 128)
    for a in range(3):
        for p in range(2):
            coef1[2 * a + p] = coarse[a][40 * p : 40 * p + 40]
    for out in (out_far, out_sib):
        for k in range(6):
            row, lane = 160 + 40 * (k // 2), 128 * (k % 2)
            out[row : row + 40, lane : lane + 128] = coef1[k]


def block(index):
    row, lane = 160 + 40 * (index // 2), 128 * (index % 2)
    return slice(row, row + 40), slice(lane, lane + 128)


def sides(far, sib):
    odd = lax.rem(lax.axis_index("wide"), 2) == 1

    def below(*at):
        return jnp.where(odd, sib[at], far[at])

    def above(*at):
        return jnp.where(odd, far[at], sib[at])

    return below, above


CHUNK = 16


def chunked(rows, body):
    for r0 in range(0, rows, CHUNK):
        body(r0, rows)


def near_chunk(u, p, c1, c2, c3, q, r0, rows):
    here = pl.ds(r0, CHUNK)
    x = u[p, here, :]
    if r0 > 0:
        lower = u[p, pl.ds(r0 - 1, CHUNK), :]
    else:
        lower = roll(x, 1, 0)
    if r0 + CHUNK < rows:
        after = pl.ds(r0 + 1, CHUNK)
        upper = c2[q, after, :] * u[p, after, :]
    else:
        upper = roll(c2[q, here, :] * x, -1, 0)
    k3 = c3[q, here, :]
    first = c1[q, here, :] * u[p - 1, here, :] + c1[q + 1, here, :] * u[p + 1, here, :]
    second = c2[q, here, :] * lower + upper
    third = k3 * roll(x, 1, 1) + roll(k3 * x, -1, 1)
    return x, first + second + third


def diag_chunk(c1, c2, c3, q, r0, rows):
    here = pl.ds(r0, CHUNK)
    k2, k3 = c2[q, here, :], c3[q, here, :]
    if r0 + CHUNK < rows:
        h2 = c2[q, pl.ds(r0 + 1, CHUNK), :]
    else:
        h2 = roll(k2, -1, 0)
    return SIG[0] + c1[q, here, :] + c1[q + 1, here, :] + k2 + h2 + k3 + roll(k3, -1, 1)


def fine_pre_kernel(own, coef1, far_raw, sib_raw, far, sib, u2, out_far, out_sib, f, c1, c2, c3, g, f1, u1, res, scr):
    below, above = sides(far, sib)
    below_raw, above_raw = sides(far_raw, sib_raw)
    for a, ref in enumerate((f, c1, c2, c3)):
        ref[1:5] = own[4 * a : 4 * a + 4]
    for a, ref, q, raw, rest in (
        [(a, ref, 0, below_raw, below) for a, ref in enumerate((f, c1, c2, c3))]
        + [(a, ref, 5, above_raw, above) for a, ref in enumerate((f, c1, c2, c3))]
        + [(4, c1, 6, above_raw, above)]
    ):
        halo_plane(ref, q, a, raw, rest)
    u1[0] = below(slice(80, 160))
    u1[7] = above(slice(80, 160))

    def smooth_first(q, carry):
        def rows(r0, n):
            here = pl.ds(r0, CHUNK)
            inverse = 1.0 / diag_chunk(c1, c2, c3, q, r0, n)
            g[q, here, :] = inverse
            u1[q + 1, here, :] = f[q, here, :] * inverse * (1.0 / THETA)

        chunked(80, rows)
        return carry

    lax.fori_loop(0, 6, smooth_first, 0)

    def smooth_second(q, carry):
        def rows(r0, n):
            here = pl.ds(r0, CHUNK)
            x, near = near_chunk(u1, q + 1, c1, c2, c3, q, r0, n)
            u2[q, here, :] = (1.0 + KEEP) * x + GAIN * (g[q, here, :] * (f[q, here, :] + near) - x)

        chunked(80, rows)
        return carry

    lax.fori_loop(0, 6, smooth_second, 0)

    def residual(q, carry):
        def rows(r0, n):
            here = pl.ds(r0, CHUNK)
            x, near = near_chunk(u2, q, c1, c2, c3, q, r0, n)
            res[q - 1, here, :] = f[q, here, :] + near - diag_chunk(c1, c2, c3, q, r0, n) * x

        chunked(80, rows)
        return carry

    lax.fori_loop(1, 5, residual, 0)

    both = pairs_of_lanes(256, 128)
    sums = jnp.concatenate([res[0] + res[1], res[2] + res[3]], axis=0)
    coarse = 0.5 * pair_rows(mul(sums, both), scr)
    f1[0] = coarse[:40]
    f1[1] = coarse[40:]
    for p in range(2):
        face = coef1[1] if p == 0 else above(*block(0))
        inverse = 1.0 / diagonal(SIG[1], coef1[p], face, coef1[2 + p], coef1[4 + p])
        for out in (out_far, out_sib):
            out[p] = f1[p]
            out[2 + p] = inverse
    par = lax.rem(lax.axis_index("wide"), 2)
    for out, plane in ((out_far, 2 + par), (out_sib, 3 - par)):
        out[4] = u2[plane, 0:40, 0:128]
        out[5] = u2[plane, 0:40, 128:256]
        out[6] = u2[plane, 40:80, 0:128]
        out[7] = u2[plane, 40:80, 128:256]


def halo_plane(out, k, a, raw, rest):
    out[k, 0:8] = rest(slice(16 * a, 16 * a + 8))
    out[k, 8:72] = raw(a)
    out[k, 72:80] = rest(slice(16 * a + 8, 16 * a + 16))


def coarse_coef_kernel(coef1, far_raw, sib_raw, far, sib, w1, halo, out, scr):
    below, above = sides(far, sib)
    below_raw, above_raw = sides(far_raw, sib_raw)
    for a in range(4):
        halo_plane(halo, a, a, below_raw, below)
        halo_plane(halo, 4 + a, a, above_raw, above)
    halo_plane(halo, 8, 4, above_raw, above)
    for a in range(3):
        for p in range(2):
            w1[6 * a + p] = below(*block(2 * a + p))
            w1[6 * a + 2 + p] = coef1[2 * a + p]
            w1[6 * a + 4 + p] = above(*block(2 * a + p))
    k1 = jnp.concatenate([w1[2], w1[4]], axis=0)
    k2, k3 = w1[8] + w1[9], w1[14] + w1[15]
    both, alone = pairs_of_lanes(128, 64), pairs_of_lanes(128, 64, even=True)
    k1 = 0.25 * pair_rows(mul(k1, both), scr)
    k2 = 0.25 * pair_rows(mul(k2, both), scr, even=True)
    k3 = 0.25 * pair_rows(mul(k3, alone), scr)
    for k, x in enumerate((k1[2:18], k1[22:38], k2[2:18], k3[2:18])):
        out[8 * k : 8 * k + 8] = two_blocks(x)


def middle_pre_kernel(own, far, sib, w1, coefs, f, g, u2, f2, up, down, outer, u1, scr):
    below, above = sides(far, sib)
    for k, read in enumerate((below, own.__getitem__, above)):
        for p in range(2):
            f[2 * k + p] = read(p)
            g[2 * k + p] = read(2 + p)
    for k, read in enumerate((below, above)):
        outer[k, 0:40, 0:128] = read(4)
        outer[k, 0:40, 128:256] = read(5)
        outer[k, 40:80, 0:128] = read(6)
        outer[k, 40:80, 128:256] = read(7)
    for p in range(6):
        u1[p] = f[p] * g[p] * (1.0 / THETA)
    u2[0] = u1[0]
    u2[5] = u1[5]
    for p in range(1, 5):
        u2[p] = smooth_two(u1[p], u1[p - 1], u1[p + 1], f[p], g[p], w1[p], w1[p + 1], w1[6 + p], w1[12 + p])
    total = 0.0
    for p in (2, 3):
        k1, h1, k2, k3 = w1[p], w1[p + 1], w1[6 + p], w1[12 + p]
        near = gather_sum(u2[p - 1], u2[p], u2[p + 1], k1, h1, k2, k3)
        total = total + (f[p] + near - diagonal(SIG[1], k1, h1, k2, k3) * u2[p])
    coarse = 0.5 * pair_rows(mul(total, pairs_of_lanes(128, 64)), scr, 4, 16)
    f2[0:8] = two_blocks(coarse)
    f2[8:40] = coefs[...]
    for p in range(2):
        up[40 + 8 * p : 48 + 8 * p] = u2[2 + p, 28:36]
        down[40 + 8 * p : 48 + 8 * p] = u2[2 + p, 4:12]
    up[0:40] = f2[...]
    down[0:40] = f2[...]


def both_halves(x):
    return jnp.concatenate([spread_block(x, 0, 64), spread_block(x, 1, 64)], axis=0)


def coarse_start_kernel(f2, low, high, far, u2fine, own, msg):
    n = lax.axis_index("narrow")
    for piece, by in ((f2, 0), (high, 1), (far, 2), (low, 3)):
        at = pl.multiple_of(16 * lax.rem(n + by, 4), 16)
        for k in range(5):
            own[k, pl.ds(at, 16), :] = both_halves(piece[8 * k : 8 * k + 8])
    own[5] = 1.0 / diagonal(SIG[2], own[1], own[2], own[3], own[4])
    for k, plane in enumerate((0, 5, 1, 3, 4)):
        msg[32 * k : 32 * k + 32] = two_blocks(own[plane])
    for p in range(2):
        at = 160 + 40 * p
        msg[at : at + 40] = u2fine[2 + p]
        msg[at : at + 4] = low[44 + 8 * p : 48 + 8 * p]
        msg[at + 36 : at + 40] = high[40 + 8 * p : 44 + 8 * p]


def coarse_tiles_kernel(msg, sib, tiles, scr):
    odd = lax.rem(lax.axis_index("wide"), 2) == 1
    for a in range(3):
        here = slice(64 + 32 * a, 96 + 32 * a)
        x = jnp.where(odd, sib[here], msg[here]) if a == 0 else msg[here] + sib[here]
        scr[...] = 0.25 * mul(both_halves(x), pairs_of_lanes(128, 32, even=a == 2))
        tiles[a] = tile_of(scr, a == 1)


def tile_of(scr, even=False):
    block = iota((8, 128), 1) // 32
    packed = 0.0
    for q in range(4):
        part = scr[pl.ds(2 * q, 8, stride=8), :]
        if not even:
            part = part + scr[pl.ds(2 * q + 1, 8, stride=8), :]
        packed = jnp.where(block == q, part, packed)
    return packed


def coarse_swap_kernel(own, msg, sib, w1, out):
    out[0:32] = msg[0:32]
    out[32:128] = msg[64:160]
    out[128:160] = sib[0:32] * sib[32:64] * (1.0 / THETA)
    out[160:192] = two_blocks(own[2])
    out[192:272] = msg[160:240]
    par = lax.rem(lax.axis_index("wide"), 2)
    out[272:312] = sib[pl.ds(pl.multiple_of(160 + 40 * par, 8), 40), :]
    out[312:352] = w1[4]


def coarse_pre_kernel(own, msg, sib, near, other, w, u2, late, fine, u1):
    for p in range(2):
        fine[p] = sib[160 + 40 * p : 200 + 40 * p]
        fine[2 + p] = msg[160 + 40 * p : 200 + 40 * p]
    for p in range(4):
        fine[4 + p] = near[192 + 40 * p : 232 + 40 * p]
    odd = lax.rem(lax.axis_index("wide"), 2) == 1

    def below(k):
        here = slice(32 * k, 32 * k + 32)
        return both_halves(jnp.where(odd, other[here], near[here]))

    def above(k):
        here = slice(32 * k, 32 * k + 32)
        return both_halves(jnp.where(odd, near[here], other[here]))

    for a, (base, plane, slot) in enumerate(((0, 0, 0), (4, 5, None), (8, 1, 1), (13, 3, 2), (17, 4, 3))):
        mine, theirs = own[plane], both_halves(sib[32 * a : 32 * a + 32])
        w[base + 1] = jnp.where(odd, theirs, mine)
        w[base + 2] = jnp.where(odd, mine, theirs)
        if slot is not None:
            w[base] = below(slot)
            w[base + 3] = above(slot)
    w[12] = above(5)
    u1[0] = below(4)
    u1[5] = above(4)
    for k in (0, 3):
        w[4 + k] = 1.0 / diagonal(SIG[2], w[8 + k], w[9 + k], w[13 + k], w[17 + k])
    for k in range(4):
        u1[k + 1] = w[k] * w[4 + k] * (1.0 / THETA)
    for k in range(4):
        u2[k] = smooth_two(u1[k + 1], u1[k], u1[k + 2], w[k], w[4 + k], w[8 + k], w[9 + k], w[13 + k], w[17 + k])
    late[...] = two_blocks(jnp.where(odd, u2[1], u2[2]))


def coarse_send_kernel(w, u2, tiles, send, scr, stack, sems):
    odd = lax.rem(lax.axis_index("wide"), 2) == 1
    total = 0.0
    for k in (1, 2):
        args = (w[8 + k], w[9 + k], w[13 + k], w[17 + k])
        near = gather_sum(u2[k - 1], u2[k], u2[k + 1], *args)
        total = total + (w[k] + near - diagonal(SIG[2], *args) * u2[k])
    scr[...] = 0.5 * mul(total, pairs_of_lanes(128, 32))
    first = jnp.where(odd, tiles[1], tile_of(scr))
    second = jnp.where(odd, tiles[2], tiles[0])
    share = stack.shape[0]
    for k in range(share):
        stack[k, 0] = first
        stack[k, 1] = second
    copies = []
    for k in range(4):
        copies.append(pltpu.make_async_copy(stack, send.at[pl.ds(share * k, share)], sems.at[k]))
        copies[k].start()
    for copy in copies:
        copy.wait()


def packed_sum(below, x, above, c1, h1, c2, c3, width, blocks):
    lane = iota(x.shape, 2)
    block, inner = lane // width % blocks, lane % width

    def second_down(x):
        x = pltpu.roll(x, width, 2)
        return jnp.where(block == 0, pltpu.roll(x, 1, 1), x)

    def second_up(x):
        x = pltpu.roll(x, 128 - width, 2)
        return jnp.where(block == blocks - 1, pltpu.roll(x, 7, 1), x)

    def third_down(x):
        return jnp.where(inner == 0, pltpu.roll(x, 129 - width, 2), pltpu.roll(x, 1, 2))

    def third_up(x):
        return jnp.where(inner == width - 1, pltpu.roll(x, width - 1, 2), pltpu.roll(x, 127, 2))

    first = c1 * below + h1 * above
    second = c2 * second_down(x) + second_up(c2 * x)
    third = c3 * third_down(x) + third_up(c3 * x)
    return first + second + third


def packed_diagonal(sig, c1, h1, c2, c3, width, blocks):
    lane = iota(c1.shape, 2)
    block, inner = lane // width % blocks, lane % width
    h2 = pltpu.roll(c2, 128 - width, 2)
    h2 = jnp.where(block == blocks - 1, pltpu.roll(h2, 7, 1), h2)
    h3 = jnp.where(inner == width - 1, pltpu.roll(c3, width - 1, 2), pltpu.roll(c3, 127, 2))
    return sig + c1 + h1 + c2 + h2 + c3 + h3


def fold_matrix(even2=False, even3=False):
    k, j = iota((128, 128), 0), iota((128, 128), 1)
    k2, k3, j2, j3 = k // 32, k % 32, j // 16 % 2, j % 16
    hit2 = k2 == 2 * j2 if even2 else k2 // 2 == j2
    hit3 = k3 == 2 * j3 if even3 else k3 // 2 == j3
    return (hit2 & hit3).astype(F32)


def wrap(ref, count):
    ref[0] = ref[count]
    ref[count + 1] = ref[1]


def around(j, n):
    return lax.rem(j + n, n)


STEP = 32
THREE, FOUR = (32, 4), (16, 2)


def bottom_kernel(mine, theirs, e2,
                  f3, c1, c2, c3, d3, g3, u1, u2, res, f4, d1, d2, e3, g4, ua, ub, st, scr):
    n3, n4 = f3.shape[0], f4.shape[0]

    def loop(body):
        def step(c, carry):
            body(pl.multiple_of(c * STEP, STEP))
            return carry

        lax.fori_loop(0, n3 // STEP, step, 0)

    odd = lax.rem(lax.axis_index("wide"), 2) == 1

    def load(j):
        here = pl.ds(j, STEP)
        a, b, c, d = mine[here, 0], mine[here, 1], theirs[here, 0], theirs[here, 1]
        f3[here] = jnp.where(odd, c, a)
        c1[here] = jnp.where(odd, d, b)
        c2[here] = jnp.where(odd, a, c)
        c3[here] = jnp.where(odd, b, d)

    loop(load)
    c1[n3] = c1[0]

    def start(j):
        here = pl.ds(j, STEP)
        diag = packed_diagonal(SIG[3], c1[here], c1[pl.ds(j + 1, STEP)], c2[here], c3[here], *THREE)
        inverse = 1.0 / diag
        d3[here] = diag
        g3[here] = inverse
        u1[pl.ds(j + 1, STEP)] = f3[here] * inverse * (1.0 / THETA)

    loop(start)
    wrap(u1, n3)

    def near3(u, j):
        here = pl.ds(j, STEP)
        x = u[pl.ds(j + 1, STEP)]
        args = (c1[here], c1[pl.ds(j + 1, STEP)], c2[here], c3[here])
        return here, x, packed_sum(u[here], x, u[pl.ds(j + 2, STEP)], *args, *THREE)

    def pre(j):
        here, x, near = near3(u1, j)
        u2[pl.ds(j + 1, STEP)] = (1.0 + KEEP) * x + GAIN * (g3[here] * (f3[here] + near) - x)

    loop(pre)
    wrap(u2, n3)

    def residual(j):
        here, x, near = near3(u2, j)
        left = (f3[here] + near - d3[here] * x).reshape(STEP // 2, 2, 8, 128)
        res[pl.ds(j // 2, STEP // 2)] = left[:, 0] + left[:, 1]

    loop(residual)

    def fold(x, *even):
        return mul(x.reshape(8 * n4, 128), fold_matrix(*even)).reshape(n4, 8, 128)

    def halves(ref):
        x = ref[0:n3].reshape(n4, 2, 8, 128)
        return x[:, 0], x[:, 1]

    f4[...] = 0.5 * fold(res[...])
    d1[0:n4] = 0.25 * fold(halves(c1)[0])
    d1[n4] = d1[0]
    d2[...] = 0.25 * fold(sum(halves(c2)), True, False)
    e3[...] = 0.25 * fold(sum(halves(c3)), False, True)
    coefs4 = (d1[0:n4], d1[1 : n4 + 1], d2[...], e3[...])
    g4[...] = 1.0 / packed_diagonal(SIG[4], *coefs4, *FOUR)
    x = f4[...] * g4[...] * (1.0 / THETA)
    ua[1 : n4 + 1] = x
    wrap(ua, n4)
    st[...] = x
    src, dst = ua, ub
    for keep, gain in factors(4):
        x = src[1 : n4 + 1]
        near = packed_sum(src[0:n4], x, src[2 : n4 + 2], d1[0:n4], d1[1 : n4 + 1], d2[...], e3[...], *FOUR)
        step = keep * st[...] + gain * (g4[...] * (f4[...] + near) - x)
        st[...] = step
        dst[1 : n4 + 1] = x + step
        wrap(dst, n4)
        src, dst = dst, src

    j0 = around(lax.axis_index("wide") // 2 - 1, n3)
    k, j = iota((128, 128), 0), iota((128, 128), 1)
    unfold = (k == 16 * (j // 64) + j % 32 // 2).astype(F32)
    coarse = jnp.concatenate([src[1 + around(around(j0 - 2, n3) // 2 + m, n4)] for m in range(4)], axis=0)
    scr[0:32] = mul(coarse, unfold)
    shifted = lax.rem(around(j0 - 2, n3), 2)
    js = [around(j0 - 2 + m, n3) for m in range(7)]
    v = [u2[1 + js[m]] + scr[pl.ds(pl.multiple_of(8 * ((shifted + m) // 2), 8), 8), :] for m in range(7)]
    v = jnp.stack(v)

    def window(ref, first, count, by=0):
        return jnp.stack([ref[js[m] + by] for m in range(first, first + count)])

    def args(first, count):
        return window(c1, first, count), window(c1, first, count, 1), window(c2, first, count), window(c3, first, count)

    f, g = window(f3, 1, 5), window(g3, 1, 5)
    near = packed_sum(v[0:5], v[1:6], v[2:7], *args(1, 5), *THREE)
    w = v[1:6] + (1.0 / THETA) * (g * (f + near) - v[1:6])
    near = packed_sum(w[0:3], w[1:4], w[2:5], *args(2, 3), *THREE)
    x = w[1:4] + KEEP * (w[1:4] - v[2:5]) + GAIN * (g[1:4] * (f[1:4] + near) - w[1:4])
    x = x.reshape(24, 128)
    for q in range(4):
        fine = mul(x, (k == 32 * q + j % 64 // 2).astype(F32))
        e2[pl.ds(2 * q, 24, stride=8), :] = fine
        e2[pl.ds(2 * q + 1, 24, stride=8), :] = fine


def coarse_post_kernel(e2, win, u2, late, late_sib, out):
    below, above = sides(late, late_sib)
    v = [both_halves(below(...)), u2[0], u2[1], u2[2], u2[3], both_halves(above(...))]
    v = [v[m] + e2[64 * (m // 2) : 64 * (m // 2) + 64, :] for m in range(6)]

    def args(k):
        return win[k], win[4 + k], win[8 + k], win[9 + k], win[13 + k], win[17 + k]

    w = [first_post(v[m + 1], v[m], v[m + 2], *args(m)) for m in range(4)]
    for p in range(2):
        x = second_post(w[p + 1], v[p + 2], w[p], w[p + 2], *args(p + 1))
        out[p] = pltpu.roll(x, lax.rem(72 - 16 * lax.axis_index("narrow"), 64), 0)[0:32]


def middle_post_kernel(e2, far, u2, f, g, w1, own, edge, send, fine, c1, v, w):
    par = lax.rem(lax.axis_index("wide"), 2)
    odd = par == 1
    row, col = iota((40, 32), 0), iota((40, 32), 1)
    pick = (col == (row + 4) // 2 + 4).astype(F32)
    lanes = copies_of_lanes(128, 128)
    planes = (e2[0], e2[1], far[0], far[1])
    for k in range(4):
        fine[k] = mul(mul_left(pick, jnp.where(odd, planes[k], planes[(k + 2) % 4])), lanes)
    c1[0:6] = w1[0:6]
    c1[6] = u2[7]
    sibs, ours, next_chip = ([u2[k] for k in some] for some in ((0, 1), (2, 3), (4, 5, 6)))
    upper = sibs + ours + next_chip
    lower = [next_chip[2]] + next_chip[:2] + ours + sibs
    for i in range(7):
        v[i] = jnp.where(odd, upper[i], lower[i]) + fine[(i + 1 - par) // 2]

    def args(i):
        k = i - 1 + par
        return f[k], g[k], c1[k], c1[k + 1], w1[6 + k], w1[12 + k]

    for i in range(1, 6):
        w[i] = first_post(v[i], v[i - 1], v[i + 1], *args(i))
    out = [second_post(w[i], v[i], w[i - 1], w[i + 1], *args(i)) for i in (2, 3, 4)]
    own[0] = jnp.where(odd, out[0], out[1])
    own[1] = jnp.where(odd, out[1], out[2])
    edge[...] = jnp.where(odd, out[2], out[0])
    send[...] = jnp.where(odd, out[0], out[2])


def fine_post_kernel(e1, edge, other, outer, inner, low, high, halo, u2, result, f, c1, c2, c3, g, v, w, scr, out, sems):
    for a, ref in enumerate((f, c1, c2, c3)):
        ref[0] = halo[a]
        ref[5] = halo[4 + a]
        for p in range(4):
            ref[p + 1, 0:8] = low[4 * a + p]
            ref[p + 1, 8:72] = inner[4 * a + p]
            ref[p + 1, 72:80] = high[4 * a + p]
    c1[6] = halo[8]
    below, above = sides(edge, other)
    x = jnp.concatenate([below(...), e1[0], e1[1], above(...)], axis=0)
    for half in range(2):
        here = slice(128 * half, 128 * half + 128)
        row, col = iota((128, 128), 0), iota((128, 128), 1)
        fine = mul(x, (row == 64 * half + col // 2).astype(F32))
        scr[pl.ds(0, 160, stride=2), :] = fine
        scr[pl.ds(1, 160, stride=2), :] = fine
        for k in range(8):
            at = 80 * (k // 2)
            base = u2[k - 1, :, here] if 0 < k < 7 else outer[k // 7, :, here]
            v[k, :, here] = base + scr[at : at + 80, :]

    def post1(q, carry):
        def chunk(r0, n):
            here = pl.ds(r0, CHUNK)
            x, near = near_chunk(v, q + 1, c1, c2, c3, q, r0, n)
            inverse = 1.0 / diag_chunk(c1, c2, c3, q, r0, n)
            g[q, here, :] = inverse
            w[q + 1, here, :] = x + (1.0 / THETA) * (inverse * (f[q, here, :] + near) - x)

        chunked(80, chunk)
        return carry

    lax.fori_loop(0, 6, post1, 0)

    def post2(q, carry):
        for r0 in range(8, 72, CHUNK):
            here = pl.ds(r0, CHUNK)
            x, near = near_chunk(w, q + 1, c1, c2, c3, q, r0, 80)
            step = KEEP * (x - v[q + 1, here, :]) + GAIN * (g[q, here, :] * (f[q, here, :] + near) - x)
            out[q - 1, pl.ds(r0 - 8, CHUNK), :] = x + step
        return carry

    copies = []
    for p in range(4):
        post2(p + 1, 0)
        copies.append(pltpu.make_async_copy(out.at[pl.ds(p, 1)], result.at[pl.ds(p, 1)], sems.at[p]))
        copies[p].start()
    for copy in copies:
        copy.wait()


def shift(x, axis, by):
    count = lax.axis_size(axis)
    return lax.ppermute(x, axis, [(i, (i + by) % count) for i in range(count)])


def sibling(x):
    return lax.ppermute(x, "wide", [(i, i ^ 1) for i in range(lax.axis_size("wide"))])


def across(x):
    count = lax.axis_size("wide")
    return lax.ppermute(x, "wide", [(i, (i + 1 if i % 2 else i - 1) % count) for i in range(count)])


def body(source, coef_first, coef_second, coef_third):
    wide = lax.axis_size("wide")
    n3, n4 = wide // 2, wide // 4
    big = (80, 256)
    inputs = (source, coef_first, coef_second, coef_third)

    up, down, far_raw, sib_raw = call(
        start_kernel,
        [(16, 8, 256), (16, 8, 256), (5, 64, 256), (5, 64, 256)],
        [(2, 16, 8, 256), (2, 5, 64, 256), pltpu.SemaphoreType.DMA((2, 18))],
        {k: pltpu.HBM for k in range(4)},
        {k: pltpu.HBM for k in range(4)},
        limit=60,
    )(*inputs)
    far_raw, sib_raw = across(far_raw), sibling(sib_raw)
    low0, high0 = shift(up, "narrow", 1), shift(down, "narrow", -1)

    own, coef1, far, sib = call(
        pad_kernel, [(16,) + big, (6, 40, 128), (280, 256), (280, 256)], [(2,) + big, (160, 128)]
    )(jnp.concatenate(inputs, axis=0), low0, high0)
    far, sib = across(far), sibling(sib)

    windows = [(6,) + big, (7,) + big, (6,) + big, (6,) + big]
    u2, out_far, out_sib = call(
        fine_pre_kernel,
        [(6,) + big, (8, 40, 128), (8, 40, 128)],
        windows + [(6,) + big, (2, 40, 128), (8,) + big, (4,) + big, (160, 128)],
        limit=6,
    )(own, coef1, far_raw, sib_raw, far, sib)
    far1, sib1 = across(out_far), sibling(out_sib)
    w1, halo, coefs = call(
        coarse_coef_kernel, [(18, 40, 128), (9,) + big, (32, 128)], [(80, 128)]
    )(coef1, far_raw, sib_raw, far, sib)

    six = (6, 40, 128)
    f1w, g1w, u2m, f2, up, down, outer = call(
        middle_pre_kernel, [six, six, six, (40, 128), (56, 128), (56, 128), (2,) + big], [six, (40, 128)]
    )(out_far, far1, sib1, w1, coefs)
    low, high, far = shift(up, "narrow", 1), shift(down, "narrow", -1), shift(f2, "narrow", 2)

    own2, msg = call(coarse_start_kernel, [(6, 64, 128), (240, 128)])(f2, low, high, far, u2m)
    sib = sibling(msg)
    (swap,) = call(coarse_swap_kernel, [(352, 128)])(own2, msg, sib, w1)
    near = across(swap)
    (tiles,) = call(coarse_tiles_kernel, [(3, 8, 128)], [(64, 128)])(msg, sib)
    near, tiles = lax.optimization_barrier((near, tiles))
    other = sibling(near)
    w2, u2w, late, fine1 = call(
        coarse_pre_kernel, [(21, 64, 128), (4, 64, 128), (32, 128), (8, 40, 128)], [(6, 64, 128)]
    )(own2, msg, sib, near, other)
    (send,) = call(
        coarse_send_kernel,
        [(n3, 2, 8, 128)],
        [(64, 128), (n3 // 4, 2, 8, 128), pltpu.SemaphoreType.DMA((4,))],
        out_places={0: pltpu.HBM},
    )(w2, u2w, tiles)
    late = across(late)
    cores = [[k for k in range(wide) if k % 2 == c] for c in range(2)]
    parts = lax.all_to_all(send, "wide", split_axis=0, concat_axis=0, tiled=True, axis_index_groups=cores)
    parts, late = lax.optimization_barrier((parts, late))
    theirs, late_sib = sibling(parts), sibling(late)

    three, four = (n3, 8, 128), (n4, 8, 128)
    (fine2,) = call(
        bottom_kernel,
        [(192, 128)],
        [three, (n3 + 1, 8, 128), three, three, three, three, (n3 + 2, 8, 128), (n3 + 2, 8, 128), four, four]
        + [(n4 + 1, 8, 128), four, four, four, (n4 + 2, 8, 128), (n4 + 2, 8, 128), four, (32, 128)],
    )(parts, theirs)
    (e2,) = call(coarse_post_kernel, [(2, 32, 128)])(fine2, w2, u2w, late, late_sib)
    e2, *again = lax.optimization_barrier((e2,) + inputs)
    far = across(e2)

    e1, edge, send = call(
        middle_post_kernel,
        [(2, 40, 128), (40, 128), (40, 128)],
        [(4, 40, 128), (7, 40, 128), (7, 40, 128), (7, 40, 128)],
    )(e2, far, fine1, f1w, g1w, w1)
    other1 = sibling(send)

    (out,) = call(
        fine_post_kernel,
        [(4, 64, 256)],
        windows + [(6,) + big, (8,) + big, (8,) + big, (320, 128), (4, 64, 256), pltpu.SemaphoreType.DMA((4,))],
        out_places={0: pltpu.HBM},
        limit=6,
    )(e1, edge, other1, outer, jnp.concatenate(again, axis=0), low0, high0, halo, u2)
    return out


def solution(mesh):
    spec = P("wide", "narrow", None)
    return jax.shard_map(body, mesh=mesh, in_specs=(spec,) * 4, out_specs=spec, check_vma=False)
```

```python
import functools

import jax
import jax.numpy as jnp
from jax import lax
from jax.experimental import pallas as pl
from jax.experimental.pallas import tpu as pltpu
from jax.sharding import PartitionSpec as P

THETA = 1.125
DELTA = 0.875
RATIO = THETA / DELTA
SIG = [0.0002 * 4.0**level for level in range(5)]
F32 = jnp.float32


def factors(degree):
    rho, out = 1.0 / RATIO, []
    for _ in range(degree - 1):
        new = 1.0 / (2.0 * RATIO - rho)
        out.append((new * rho, 2.0 * new / DELTA))
        rho = new
    return out


(KEEP, GAIN), = factors(2)


def roll(x, by, axis):
    return pltpu.roll(x, by % x.shape[axis], axis)


def gather_sum(below, here, above, c1, h1, c2, c3):
    first = c1 * below + h1 * above
    second = c2 * roll(here, 1, 0) + roll(c2 * here, -1, 0)
    third = c3 * roll(here, 1, 1) + roll(c3 * here, -1, 1)
    return first + second + third


def diagonal(sig, c1, h1, c2, c3):
    return sig + c1 + h1 + c2 + roll(c2, -1, 0) + c3 + roll(c3, -1, 1)


def iota(shape, dim):
    return lax.broadcasted_iota(jnp.int32, shape, dim)


def pairs_of_lanes(lanes, period, even=False):
    row, col = iota((lanes, 128), 0), iota((lanes, 128), 1) % period
    hit = row == 2 * col if even else row // 2 == col
    return hit.astype(F32)


def copies_of_lanes(lanes_in, lanes_out):
    row, col = iota((lanes_in, lanes_out), 0), iota((lanes_in, lanes_out), 1)
    return (row == col // 2).astype(F32)


def pieces(x):
    out = []
    for _ in range(3):
        part = x.astype(jnp.bfloat16)
        out.append(part)
        x = x - part.astype(F32)
    return out


def mul(x, ones):
    ones = ones.astype(jnp.bfloat16)
    high, mid, low = [jnp.dot(part, ones, preferred_element_type=F32) for part in pieces(x)]
    return high + (mid + low)


def mul_left(ones, x):
    ones = ones.astype(jnp.bfloat16)
    high, mid, low = [jnp.dot(ones, part, preferred_element_type=F32) for part in pieces(x)]
    return high + (mid + low)


def pair_rows(x, scratch, start=0, count=None, even=False):
    rows = x.shape[0]
    count = rows // 2 if count is None else count
    scratch[0:rows, :] = x
    first = scratch[pl.ds(start, count, stride=2), :]
    if even:
        return first
    return first + scratch[pl.ds(start + 1, count, stride=2), :]


def twice_rows(x, scratch):
    rows = x.shape[0]
    scratch[pl.ds(0, rows, stride=2), :] = x
    scratch[pl.ds(1, rows, stride=2), :] = x
    return scratch[0 : 2 * rows, :]


def coarse_coefs(planes, scratch, lanes, period, start=0, count=None):
    both = pairs_of_lanes(lanes, period)
    alone = pairs_of_lanes(lanes, period, even=True)
    return (
        0.25 * pair_rows(mul(planes[0], both), scratch, start, count),
        0.25 * pair_rows(mul(planes[1], both), scratch, start, count, even=True),
        0.25 * pair_rows(mul(planes[2], alone), scratch, start, count),
    )


def spread_block(x, block, width):
    lane = iota(x.shape, 1)
    x = jnp.where(lane // width == block, x, 0.0)
    while width < 128:
        x = x + pltpu.roll(x, width, 1)
        width *= 2
    return x


def smooth_two(u1, below, above, f, g, c1, h1, c2, c3):
    near = gather_sum(below, u1, above, c1, h1, c2, c3)
    return (1.0 + KEEP) * u1 + GAIN * (g * (f + near) - u1)


def first_post(v, below, above, f, g, c1, h1, c2, c3):
    near = gather_sum(below, v, above, c1, h1, c2, c3)
    return v + (1.0 / THETA) * (g * (f + near) - v)


def second_post(u, v, below, above, f, g, c1, h1, c2, c3):
    near = gather_sum(below, u, above, c1, h1, c2, c3)
    return u + KEEP * (u - v) + GAIN * (g * (f + near) - u)


def call(kernel, outs, scratch=(), places=(), out_places=(), limit=4):
    places, out_places = dict(places), dict(out_places)

    def run(*args):
        in_specs = [pl.BlockSpec(memory_space=places.get(i, pltpu.VMEM)) for i in range(len(args))]
        return pl.pallas_call(
            kernel,
            out_shape=[jax.ShapeDtypeStruct(s, F32) for s in outs],
            in_specs=in_specs,
            out_specs=[pl.BlockSpec(memory_space=out_places.get(i, pltpu.VMEM)) for i in range(len(outs))],
            scratch_shapes=[pltpu.VMEM(s, F32) if isinstance(s, tuple) else s for s in scratch],
            compiler_params=pltpu.CompilerParams(vmem_limit_bytes=limit * 2**20),
        )(*args)

    return run


def two_blocks(x):
    half = x.shape[0] // 2
    return jnp.where(iota((half, 128), 1) < 64, x[:half], x[half:])


def start_kernel(f, c1, c2, c3, up, down, out_far, out_sib, rows, planes, sems):
    par = lax.rem(lax.axis_index("wide"), 2)
    moves = []
    for k, (out, row) in enumerate(((up, 56), (down, 0))):
        for a, ref in enumerate((f, c1, c2, c3)):
            moves.append((ref.at[:, pl.ds(row, 8), :], rows.at[k, pl.ds(4 * a, 4)], out.at[pl.ds(4 * a, 4)]))
    for k, (out, upward) in enumerate(((out_far, par), (out_sib, 1 - par))):
        for a, ref in enumerate((f, c1, c2, c3, c1)):
            plane = 3 * upward if a < 4 else 1
            moves.append((ref.at[pl.ds(plane, 1)], planes.at[k, pl.ds(a, 1)], out.at[pl.ds(a, 1)]))
    first = [pltpu.make_async_copy(src, mid, sems.at[0, k]) for k, (src, mid, _) in enumerate(moves)]
    second = [pltpu.make_async_copy(mid, dst, sems.at[1, k]) for k, (_, mid, dst) in enumerate(moves)]
    for copy in first:
        copy.start()
    for one, two in zip(first, second):
        one.wait()
        two.start()
    for copy in second:
        copy.wait()


def pad_kernel(inner, low, high, own, coef1, out_far, out_sib, first, scr):
    for a in range(16):
        own[a, 0:8] = low[a]
        own[a, 8:72] = inner[a]
        own[a, 72:80] = high[a]
    par = lax.rem(lax.axis_index("wide"), 2)
    for k in range(2):
        diag = diagonal(SIG[0], own[5 + k], own[6 + k], own[9 + k], own[13 + k])
        first[k] = own[1 + k] / diag / THETA
    for out, up in ((out_far, par), (out_sib, 1 - par)):
        for a in range(5):
            plane = 4 * a + 3 * up if a < 4 else 5
            out[16 * a : 16 * a + 8] = own[plane, 0:8]
            out[16 * a + 8 : 16 * a + 16] = own[plane, 72:80]
        out[80:160] = first[up]
    k1 = jnp.concatenate([own[4], own[6]], axis=0)
    k2 = jnp.concatenate([own[8] + own[9], own[10] + own[11]], axis=0)
    k3 = jnp.concatenate([own[12] + own[13], own[14] + own[15]], axis=0)
    coarse = coarse_coefs((k1, k2, k3), scr, 256, 128)
    for a in range(3):
        for p in range(2):
            coef1[2 * a + p] = coarse[a][40 * p : 40 * p + 40]
    for out in (out_far, out_sib):
        for k in range(6):
            row, lane = 160 + 40 * (k // 2), 128 * (k % 2)
            out[row : row + 40, lane : lane + 128] = coef1[k]


def block(index):
    row, lane = 160 + 40 * (index // 2), 128 * (index % 2)
    return slice(row, row + 40), slice(lane, lane + 128)


def sides(far, sib):
    odd = lax.rem(lax.axis_index("wide"), 2) == 1

    def below(*at):
        return jnp.where(odd, sib[at], far[at])

    def above(*at):
        return jnp.where(odd, far[at], sib[at])

    return below, above


CHUNK = 16


def chunked(rows, body):
    for r0 in range(0, rows, CHUNK):
        body(r0, rows)


def near_chunk(u, p, c1, c2, c3, q, r0, rows):
    here = pl.ds(r0, CHUNK)
    x = u[p, here, :]
    if r0 > 0:
        lower = u[p, pl.ds(r0 - 1, CHUNK), :]
    else:
        lower = roll(x, 1, 0)
    if r0 + CHUNK < rows:
        after = pl.ds(r0 + 1, CHUNK)
        upper = c2[q, after, :] * u[p, after, :]
    else:
        upper = roll(c2[q, here, :] * x, -1, 0)
    k3 = c3[q, here, :]
    first = c1[q, here, :] * u[p - 1, here, :] + c1[q + 1, here, :] * u[p + 1, here, :]
    second = c2[q, here, :] * lower + upper
    third = k3 * roll(x, 1, 1) + roll(k3 * x, -1, 1)
    return x, first + second + third


def diag_chunk(c1, c2, c3, q, r0, rows):
    here = pl.ds(r0, CHUNK)
    k2, k3 = c2[q, here, :], c3[q, here, :]
    if r0 + CHUNK < rows:
        h2 = c2[q, pl.ds(r0 + 1, CHUNK), :]
    else:
        h2 = roll(k2, -1, 0)
    return SIG[0] + c1[q, here, :] + c1[q + 1, here, :] + k2 + h2 + k3 + roll(k3, -1, 1)


def fine_pre_kernel(own, coef1, far_raw, sib_raw, far, sib, u2, out_far, out_sib, f, c1, c2, c3, g, f1, u1, res, scr):
    below, above = sides(far, sib)
    below_raw, above_raw = sides(far_raw, sib_raw)
    for a, ref in enumerate((f, c1, c2, c3)):
        ref[1:5] = own[4 * a : 4 * a + 4]
    for a, ref, q, raw, rest in (
        [(a, ref, 0, below_raw, below) for a, ref in enumerate((f, c1, c2, c3))]
        + [(a, ref, 5, above_raw, above) for a, ref in enumerate((f, c1, c2, c3))]
        + [(4, c1, 6, above_raw, above)]
    ):
        halo_plane(ref, q, a, raw, rest)
    u1[0] = below(slice(80, 160))
    u1[7] = above(slice(80, 160))

    def smooth_first(q, carry):
        def rows(r0, n):
            here = pl.ds(r0, CHUNK)
            inverse = 1.0 / diag_chunk(c1, c2, c3, q, r0, n)
            g[q, here, :] = inverse
            u1[q + 1, here, :] = f[q, here, :] * inverse * (1.0 / THETA)

        chunked(80, rows)
        return carry

    lax.fori_loop(0, 6, smooth_first, 0)

    def smooth_second(q, carry):
        def rows(r0, n):
            here = pl.ds(r0, CHUNK)
            x, near = near_chunk(u1, q + 1, c1, c2, c3, q, r0, n)
            u2[q, here, :] = (1.0 + KEEP) * x + GAIN * (g[q, here, :] * (f[q, here, :] + near) - x)

        chunked(80, rows)
        return carry

    lax.fori_loop(0, 6, smooth_second, 0)

    def residual(q, carry):
        def rows(r0, n):
            here = pl.ds(r0, CHUNK)
            x, near = near_chunk(u2, q, c1, c2, c3, q, r0, n)
            res[q - 1, here, :] = f[q, here, :] + near - diag_chunk(c1, c2, c3, q, r0, n) * x

        chunked(80, rows)
        return carry

    lax.fori_loop(1, 5, residual, 0)

    both = pairs_of_lanes(256, 128)
    sums = jnp.concatenate([res[0] + res[1], res[2] + res[3]], axis=0)
    coarse = 0.5 * pair_rows(mul(sums, both), scr)
    f1[0] = coarse[:40]
    f1[1] = coarse[40:]
    for p in range(2):
        face = coef1[1] if p == 0 else above(*block(0))
        inverse = 1.0 / diagonal(SIG[1], coef1[p], face, coef1[2 + p], coef1[4 + p])
        for out in (out_far, out_sib):
            out[p] = f1[p]
            out[2 + p] = inverse
    par = lax.rem(lax.axis_index("wide"), 2)
    for out, plane in ((out_far, 2 + par), (out_sib, 3 - par)):
        out[4] = u2[plane, 0:40, 0:128]
        out[5] = u2[plane, 0:40, 128:256]
        out[6] = u2[plane, 40:80, 0:128]
        out[7] = u2[plane, 40:80, 128:256]


def halo_plane(out, k, a, raw, rest):
    out[k, 0:8] = rest(slice(16 * a, 16 * a + 8))
    out[k, 8:72] = raw(a)
    out[k, 72:80] = rest(slice(16 * a + 8, 16 * a + 16))


def coarse_coef_kernel(coef1, far_raw, sib_raw, far, sib, w1, halo, out, scr):
    below, above = sides(far, sib)
    below_raw, above_raw = sides(far_raw, sib_raw)
    for a in range(4):
        halo_plane(halo, a, a, below_raw, below)
        halo_plane(halo, 4 + a, a, above_raw, above)
    halo_plane(halo, 8, 4, above_raw, above)
    for a in range(3):
        for p in range(2):
            w1[6 * a + p] = below(*block(2 * a + p))
            w1[6 * a + 2 + p] = coef1[2 * a + p]
            w1[6 * a + 4 + p] = above(*block(2 * a + p))
    k1 = jnp.concatenate([w1[2], w1[4]], axis=0)
    k2, k3 = w1[8] + w1[9], w1[14] + w1[15]
    both, alone = pairs_of_lanes(128, 64), pairs_of_lanes(128, 64, even=True)
    k1 = 0.25 * pair_rows(mul(k1, both), scr)
    k2 = 0.25 * pair_rows(mul(k2, both), scr, even=True)
    k3 = 0.25 * pair_rows(mul(k3, alone), scr)
    for k, x in enumerate((k1[2:18], k1[22:38], k2[2:18], k3[2:18])):
        out[8 * k : 8 * k + 8] = two_blocks(x)


def middle_pre_kernel(own, far, sib, w1, coefs, f, g, u2, f2, up, down, outer, u1, scr):
    below, above = sides(far, sib)
    for k, read in enumerate((below, own.__getitem__, above)):
        for p in range(2):
            f[2 * k + p] = read(p)
            g[2 * k + p] = read(2 + p)
    for k, read in enumerate((below, above)):
        outer[k, 0:40, 0:128] = read(4)
        outer[k, 0:40, 128:256] = read(5)
        outer[k, 40:80, 0:128] = read(6)
        outer[k, 40:80, 128:256] = read(7)
    for p in range(6):
        u1[p] = f[p] * g[p] * (1.0 / THETA)
    u2[0] = u1[0]
    u2[5] = u1[5]
    for p in range(1, 5):
        u2[p] = smooth_two(u1[p], u1[p - 1], u1[p + 1], f[p], g[p], w1[p], w1[p + 1], w1[6 + p], w1[12 + p])
    total = 0.0
    for p in (2, 3):
        k1, h1, k2, k3 = w1[p], w1[p + 1], w1[6 + p], w1[12 + p]
        near = gather_sum(u2[p - 1], u2[p], u2[p + 1], k1, h1, k2, k3)
        total = total + (f[p] + near - diagonal(SIG[1], k1, h1, k2, k3) * u2[p])
    coarse = 0.5 * pair_rows(mul(total, pairs_of_lanes(128, 64)), scr, 4, 16)
    f2[0:8] = two_blocks(coarse)
    f2[8:40] = coefs[...]
    for p in range(2):
        up[40 + 8 * p : 48 + 8 * p] = u2[2 + p, 28:36]
        down[40 + 8 * p : 48 + 8 * p] = u2[2 + p, 4:12]
    up[0:40] = f2[...]
    down[0:40] = f2[...]


def both_halves(x):
    return jnp.concatenate([spread_block(x, 0, 64), spread_block(x, 1, 64)], axis=0)


def coarse_start_kernel(f2, low, high, far, u2fine, own, msg):
    n = lax.axis_index("narrow")
    for piece, by in ((f2, 0), (high, 1), (far, 2), (low, 3)):
        at = pl.multiple_of(16 * lax.rem(n + by, 4), 16)
        for k in range(5):
            own[k, pl.ds(at, 16), :] = both_halves(piece[8 * k : 8 * k + 8])
    own[5] = 1.0 / diagonal(SIG[2], own[1], own[2], own[3], own[4])
    for k, plane in enumerate((0, 5, 1, 3, 4)):
        msg[32 * k : 32 * k + 32] = two_blocks(own[plane])
    for p in range(2):
        at = 160 + 40 * p
        msg[at : at + 40] = u2fine[2 + p]
        msg[at : at + 4] = low[44 + 8 * p : 48 + 8 * p]
        msg[at + 36 : at + 40] = high[40 + 8 * p : 44 + 8 * p]


def coarse_tiles_kernel(msg, sib, tiles, scr):
    odd = lax.rem(lax.axis_index("wide"), 2) == 1
    for a in range(3):
        here = slice(64 + 32 * a, 96 + 32 * a)
        x = jnp.where(odd, sib[here], msg[here]) if a == 0 else msg[here] + sib[here]
        scr[0:64, :] = 0.25 * mul(both_halves(x), pairs_of_lanes(128, 32, even=a == 2))
        tiles[a] = tile_of(scr, a == 1)


def tile_of(scr, even=False):
    block = iota((8, 128), 1) // 32
    packed = 0.0
    for q in range(4):
        part = scr[pl.ds(2 * q, 8, stride=8), :]
        if not even:
            part = part + scr[pl.ds(2 * q + 1, 8, stride=8), :]
        packed = jnp.where(block == q, part, packed)
    return packed


def coarse_swap_kernel(own, msg, sib, w1, out):
    out[0:32] = msg[0:32]
    out[32:128] = msg[64:160]
    out[128:160] = sib[0:32] * sib[32:64] * (1.0 / THETA)
    out[160:192] = two_blocks(own[2])
    out[192:272] = msg[160:240]
    par = lax.rem(lax.axis_index("wide"), 2)
    out[272:312] = sib[pl.ds(pl.multiple_of(160 + 40 * par, 8), 40), :]
    out[312:352] = w1[4]


def coarse_pre_kernel(own, msg, sib, near, other, w, u2, late, fine, u1):
    for p in range(2):
        fine[p] = sib[160 + 40 * p : 200 + 40 * p]
        fine[2 + p] = msg[160 + 40 * p : 200 + 40 * p]
    for p in range(4):
        fine[4 + p] = near[192 + 40 * p : 232 + 40 * p]
    odd = lax.rem(lax.axis_index("wide"), 2) == 1

    def below(k):
        here = slice(32 * k, 32 * k + 32)
        return both_halves(jnp.where(odd, other[here], near[here]))

    def above(k):
        here = slice(32 * k, 32 * k + 32)
        return both_halves(jnp.where(odd, near[here], other[here]))

    for a, (base, plane, slot) in enumerate(((0, 0, 0), (4, 5, None), (8, 1, 1), (13, 3, 2), (17, 4, 3))):
        mine, theirs = own[plane], both_halves(sib[32 * a : 32 * a + 32])
        w[base + 1] = jnp.where(odd, theirs, mine)
        w[base + 2] = jnp.where(odd, mine, theirs)
        if slot is not None:
            w[base] = below(slot)
            w[base + 3] = above(slot)
    w[12] = above(5)
    u1[0] = below(4)
    u1[5] = above(4)
    for k in (0, 3):
        w[4 + k] = 1.0 / diagonal(SIG[2], w[8 + k], w[9 + k], w[13 + k], w[17 + k])
    for k in range(4):
        u1[k + 1] = w[k] * w[4 + k] * (1.0 / THETA)
    for k in range(4):
        u2[k] = smooth_two(u1[k + 1], u1[k], u1[k + 2], w[k], w[4 + k], w[8 + k], w[9 + k], w[13 + k], w[17 + k])
    late[...] = two_blocks(jnp.where(odd, u2[1], u2[2]))


def coarse_send_kernel(w, u2, tiles, send, scr):
    odd = lax.rem(lax.axis_index("wide"), 2) == 1
    total = 0.0
    for k in (1, 2):
        args = (w[8 + k], w[9 + k], w[13 + k], w[17 + k])
        near = gather_sum(u2[k - 1], u2[k], u2[k + 1], *args)
        total = total + (w[k] + near - diagonal(SIG[2], *args) * u2[k])
    scr[0:64, :] = 0.5 * mul(total, pairs_of_lanes(128, 32))
    first = jnp.where(odd, tiles[1], tile_of(scr))
    second = jnp.where(odd, tiles[2], tiles[0])
    for k in range(send.shape[0]):
        send[k, 0] = first
        send[k, 1] = second


def packed_sum(below, x, above, c1, h1, c2, c3, width, blocks):
    lane = iota(x.shape, 2)
    block, inner = lane // width % blocks, lane % width

    def second_down(x):
        x = pltpu.roll(x, width, 2)
        return jnp.where(block == 0, pltpu.roll(x, 1, 1), x)

    def second_up(x):
        x = pltpu.roll(x, 128 - width, 2)
        return jnp.where(block == blocks - 1, pltpu.roll(x, 7, 1), x)

    def third_down(x):
        return jnp.where(inner == 0, pltpu.roll(x, 129 - width, 2), pltpu.roll(x, 1, 2))

    def third_up(x):
        return jnp.where(inner == width - 1, pltpu.roll(x, width - 1, 2), pltpu.roll(x, 127, 2))

    first = c1 * below + h1 * above
    second = c2 * second_down(x) + second_up(c2 * x)
    third = c3 * third_down(x) + third_up(c3 * x)
    return first + second + third


def packed_diagonal(sig, c1, h1, c2, c3, width, blocks):
    lane = iota(c1.shape, 2)
    block, inner = lane // width % blocks, lane % width
    h2 = pltpu.roll(c2, 128 - width, 2)
    h2 = jnp.where(block == blocks - 1, pltpu.roll(h2, 7, 1), h2)
    h3 = jnp.where(inner == width - 1, pltpu.roll(c3, width - 1, 2), pltpu.roll(c3, 127, 2))
    return sig + c1 + h1 + c2 + h2 + c3 + h3


def fold_matrix(even2=False, even3=False):
    k, j = iota((128, 128), 0), iota((128, 128), 1)
    k2, k3, j2, j3 = k // 32, k % 32, j // 16 % 2, j % 16
    hit2 = k2 == 2 * j2 if even2 else k2 // 2 == j2
    hit3 = k3 == 2 * j3 if even3 else k3 // 2 == j3
    return (hit2 & hit3).astype(F32)


def wrap(ref, count):
    ref[0] = ref[count]
    ref[count + 1] = ref[1]


def around(j, n):
    return lax.rem(j + n, n)


STEP = 32
THREE, FOUR = (32, 4), (16, 2)


def bottom_kernel(mine, theirs, e2,
                  f3, c1, c2, c3, d3, g3, u1, u2, res, f4, d1, d2, e3, g4, ua, ub, st, scr):
    n3, n4 = f3.shape[0], f4.shape[0]

    def loop(body):
        for j in range(0, n3, STEP):
            body(j)

    odd = lax.rem(lax.axis_index("wide"), 2) == 1

    def load(j):
        here = pl.ds(j, STEP)
        a, b, c, d = mine[here, 0], mine[here, 1], theirs[here, 0], theirs[here, 1]
        f3[here] = jnp.where(odd, c, a)
        c1[here] = jnp.where(odd, d, b)
        c2[here] = jnp.where(odd, a, c)
        c3[here] = jnp.where(odd, b, d)

    loop(load)
    c1[n3] = c1[0]

    def start(j):
        here = pl.ds(j, STEP)
        diag = packed_diagonal(SIG[3], c1[here], c1[pl.ds(j + 1, STEP)], c2[here], c3[here], *THREE)
        inverse = 1.0 / diag
        d3[here] = diag
        g3[here] = inverse
        u1[pl.ds(j + 1, STEP)] = f3[here] * inverse * (1.0 / THETA)

    loop(start)
    wrap(u1, n3)

    def near3(u, j):
        here = pl.ds(j, STEP)
        x = u[pl.ds(j + 1, STEP)]
        args = (c1[here], c1[pl.ds(j + 1, STEP)], c2[here], c3[here])
        return here, x, packed_sum(u[here], x, u[pl.ds(j + 2, STEP)], *args, *THREE)

    def pre(j):
        here, x, near = near3(u1, j)
        u2[pl.ds(j + 1, STEP)] = (1.0 + KEEP) * x + GAIN * (g3[here] * (f3[here] + near) - x)

    loop(pre)
    wrap(u2, n3)

    def residual(j):
        here, x, near = near3(u2, j)
        left = (f3[here] + near - d3[here] * x).reshape(STEP // 2, 2, 8, 128)
        res[pl.ds(j // 2, STEP // 2)] = left[:, 0] + left[:, 1]

    loop(residual)

    def fold(x, *even):
        return mul(x.reshape(8 * n4, 128), fold_matrix(*even)).reshape(n4, 8, 128)

    def halves(ref):
        x = ref[0:n3].reshape(n4, 2, 8, 128)
        return x[:, 0], x[:, 1]

    f4[...] = 0.5 * fold(res[...])
    d1[0:n4] = 0.25 * fold(halves(c1)[0])
    d1[n4] = d1[0]
    d2[...] = 0.25 * fold(sum(halves(c2)), True, False)
    e3[...] = 0.25 * fold(sum(halves(c3)), False, True)
    coefs4 = (d1[0:n4], d1[1 : n4 + 1], d2[...], e3[...])
    g4[...] = 1.0 / packed_diagonal(SIG[4], *coefs4, *FOUR)
    x = f4[...] * g4[...] * (1.0 / THETA)
    ua[1 : n4 + 1] = x
    wrap(ua, n4)
    st[...] = x
    src, dst = ua, ub
    for keep, gain in factors(4):
        x = src[1 : n4 + 1]
        near = packed_sum(src[0:n4], x, src[2 : n4 + 2], d1[0:n4], d1[1 : n4 + 1], d2[...], e3[...], *FOUR)
        step = keep * st[...] + gain * (g4[...] * (f4[...] + near) - x)
        st[...] = step
        dst[1 : n4 + 1] = x + step
        wrap(dst, n4)
        src, dst = dst, src

    j0 = around(lax.axis_index("wide") // 2 - 1, n3)
    k, j = iota((128, 128), 0), iota((128, 128), 1)
    unfold = (k == 16 * (j // 64) + j % 32 // 2).astype(F32)
    coarse = jnp.concatenate([src[1 + around(around(j0 - 2, n3) // 2 + m, n4)] for m in range(4)], axis=0)
    scr[0:32] = mul(coarse, unfold)
    shifted = lax.rem(around(j0 - 2, n3), 2)
    js = [around(j0 - 2 + m, n3) for m in range(7)]
    v = [u2[1 + js[m]] + scr[pl.ds(pl.multiple_of(8 * ((shifted + m) // 2), 8), 8), :] for m in range(7)]
    v = jnp.stack(v)

    def window(ref, first, count, by=0):
        return jnp.stack([ref[js[m] + by] for m in range(first, first + count)])

    def args(first, count):
        return window(c1, first, count), window(c1, first, count, 1), window(c2, first, count), window(c3, first, count)

    f, g = window(f3, 1, 5), window(g3, 1, 5)
    near = packed_sum(v[0:5], v[1:6], v[2:7], *args(1, 5), *THREE)
    w = v[1:6] + (1.0 / THETA) * (g * (f + near) - v[1:6])
    near = packed_sum(w[0:3], w[1:4], w[2:5], *args(2, 3), *THREE)
    x = w[1:4] + KEEP * (w[1:4] - v[2:5]) + GAIN * (g[1:4] * (f[1:4] + near) - w[1:4])
    x = x.reshape(24, 128)
    for q in range(4):
        fine = mul(x, (k == 32 * q + j % 64 // 2).astype(F32))
        e2[pl.ds(2 * q, 24, stride=8), :] = fine
        e2[pl.ds(2 * q + 1, 24, stride=8), :] = fine


def coarse_post_kernel(e2, win, u2, late, late_sib, out):
    below, above = sides(late, late_sib)
    v = [both_halves(below(...)), u2[0], u2[1], u2[2], u2[3], both_halves(above(...))]
    v = [v[m] + e2[64 * (m // 2) : 64 * (m // 2) + 64, :] for m in range(6)]

    def args(k):
        return win[k], win[4 + k], win[8 + k], win[9 + k], win[13 + k], win[17 + k]

    w = [first_post(v[m + 1], v[m], v[m + 2], *args(m)) for m in range(4)]
    for p in range(2):
        x = second_post(w[p + 1], v[p + 2], w[p], w[p + 2], *args(p + 1))
        out[p] = pltpu.roll(x, lax.rem(72 - 16 * lax.axis_index("narrow"), 64), 0)[0:32]


def middle_post_kernel(e2, far, u2, f, g, w1, own, edge, send, fine, c1, v, w):
    par = lax.rem(lax.axis_index("wide"), 2)
    odd = par == 1
    row, col = iota((40, 32), 0), iota((40, 32), 1)
    pick = (col == (row + 4) // 2 + 4).astype(F32)
    lanes = copies_of_lanes(128, 128)
    planes = (e2[0], e2[1], far[0], far[1])
    for k in range(4):
        fine[k] = mul(mul_left(pick, jnp.where(odd, planes[k], planes[(k + 2) % 4])), lanes)
    c1[0:6] = w1[0:6]
    c1[6] = u2[7]
    sibs, ours, next_chip = ([u2[k] for k in some] for some in ((0, 1), (2, 3), (4, 5, 6)))
    upper = sibs + ours + next_chip
    lower = [next_chip[2]] + next_chip[:2] + ours + sibs
    for i in range(7):
        v[i] = jnp.where(odd, upper[i], lower[i]) + fine[(i + 1 - par) // 2]

    def args(i):
        k = i - 1 + par
        return f[k], g[k], c1[k], c1[k + 1], w1[6 + k], w1[12 + k]

    for i in range(1, 6):
        w[i] = first_post(v[i], v[i - 1], v[i + 1], *args(i))
    out = [second_post(w[i], v[i], w[i - 1], w[i + 1], *args(i)) for i in (2, 3, 4)]
    own[0] = jnp.where(odd, out[0], out[1])
    own[1] = jnp.where(odd, out[1], out[2])
    edge[...] = jnp.where(odd, out[2], out[0])
    send[...] = jnp.where(odd, out[0], out[2])


def fine_post_kernel(e1, edge, other, outer, inner, low, high, halo, u2, result, f, c1, c2, c3, g, v, w, scr, out, sems):
    for a, ref in enumerate((f, c1, c2, c3)):
        ref[0] = halo[a]
        ref[5] = halo[4 + a]
        for p in range(4):
            ref[p + 1, 0:8] = low[4 * a + p]
            ref[p + 1, 8:72] = inner[4 * a + p]
            ref[p + 1, 72:80] = high[4 * a + p]
    c1[6] = halo[8]
    below, above = sides(edge, other)
    x = jnp.concatenate([below(...), e1[0], e1[1], above(...)], axis=0)
    for half in range(2):
        here = slice(128 * half, 128 * half + 128)
        row, col = iota((128, 128), 0), iota((128, 128), 1)
        fine = mul(x, (row == 64 * half + col // 2).astype(F32))
        scr[pl.ds(0, 160, stride=2), :] = fine
        scr[pl.ds(1, 160, stride=2), :] = fine
        for k in range(8):
            at = 80 * (k // 2)
            base = u2[k - 1, :, here] if 0 < k < 7 else outer[k // 7, :, here]
            v[k, :, here] = base + scr[at : at + 80, :]

    def post1(q, carry):
        def chunk(r0, n):
            here = pl.ds(r0, CHUNK)
            x, near = near_chunk(v, q + 1, c1, c2, c3, q, r0, n)
            inverse = 1.0 / diag_chunk(c1, c2, c3, q, r0, n)
            g[q, here, :] = inverse
            w[q + 1, here, :] = x + (1.0 / THETA) * (inverse * (f[q, here, :] + near) - x)

        chunked(80, chunk)
        return carry

    lax.fori_loop(0, 6, post1, 0)

    def post2(q, carry):
        for r0 in range(8, 72, CHUNK):
            here = pl.ds(r0, CHUNK)
            x, near = near_chunk(w, q + 1, c1, c2, c3, q, r0, 80)
            step = KEEP * (x - v[q + 1, here, :]) + GAIN * (g[q, here, :] * (f[q, here, :] + near) - x)
            out[q - 1, pl.ds(r0 - 8, CHUNK), :] = x + step
        return carry

    copies = []
    for p in range(4):
        post2(p + 1, 0)
        copies.append(pltpu.make_async_copy(out.at[pl.ds(p, 1)], result.at[pl.ds(p, 1)], sems.at[p]))
        copies[p].start()
    for copy in copies:
        copy.wait()


def shift(x, axis, by):
    count = lax.axis_size(axis)
    return lax.ppermute(x, axis, [(i, (i + by) % count) for i in range(count)])


def sibling(x):
    return lax.ppermute(x, "wide", [(i, i ^ 1) for i in range(lax.axis_size("wide"))])


def across(x):
    count = lax.axis_size("wide")
    return lax.ppermute(x, "wide", [(i, (i + 1 if i % 2 else i - 1) % count) for i in range(count)])


def body(source, coef_first, coef_second, coef_third):
    wide = lax.axis_size("wide")
    n3, n4 = wide // 2, wide // 4
    big = (80, 256)
    inputs = (source, coef_first, coef_second, coef_third)

    up, down, far_raw, sib_raw = call(
        start_kernel,
        [(16, 8, 256), (16, 8, 256), (5, 64, 256), (5, 64, 256)],
        [(2, 16, 8, 256), (2, 5, 64, 256), pltpu.SemaphoreType.DMA((2, 18))],
        {k: pltpu.HBM for k in range(4)},
        {k: pltpu.HBM for k in range(4)},
        limit=60,
    )(*inputs)
    far_raw, sib_raw = across(far_raw), sibling(sib_raw)
    low0, high0 = shift(up, "narrow", 1), shift(down, "narrow", -1)

    own, coef1, far, sib = call(
        pad_kernel, [(16,) + big, (6, 40, 128), (280, 256), (280, 256)], [(2,) + big, (168, 128)]
    )(jnp.concatenate(inputs, axis=0), low0, high0)
    far, sib = across(far), sibling(sib)

    windows = [(6,) + big, (7,) + big, (6,) + big, (6,) + big]
    u2, out_far, out_sib = call(
        fine_pre_kernel,
        [(6,) + big, (8, 40, 128), (8, 40, 128)],
        windows + [(6,) + big, (2, 40, 128), (8,) + big, (4,) + big, (168, 128)],
        limit=6,
    )(own, coef1, far_raw, sib_raw, far, sib)
    far1, sib1 = across(out_far), sibling(out_sib)
    w1, halo, coefs = call(
        coarse_coef_kernel, [(18, 40, 128), (9,) + big, (32, 128)], [(88, 128)]
    )(coef1, far_raw, sib_raw, far, sib)

    six = (6, 40, 128)
    f1w, g1w, u2m, f2, up, down, outer = call(
        middle_pre_kernel, [six, six, six, (40, 128), (56, 128), (56, 128), (2,) + big], [six, (48, 128)]
    )(out_far, far1, sib1, w1, coefs)
    low, high, far = shift(up, "narrow", 1), shift(down, "narrow", -1), shift(f2, "narrow", 2)

    own2, msg = call(coarse_start_kernel, [(6, 64, 128), (240, 128)])(f2, low, high, far, u2m)
    sib = sibling(msg)
    (swap,) = call(coarse_swap_kernel, [(352, 128)])(own2, msg, sib, w1)
    near = across(swap)
    (tiles,) = call(coarse_tiles_kernel, [(3, 8, 128)], [(72, 128)])(msg, sib)
    near, tiles = lax.optimization_barrier((near, tiles))
    other = sibling(near)
    w2, u2w, late, fine1 = call(
        coarse_pre_kernel, [(21, 64, 128), (4, 64, 128), (32, 128), (8, 40, 128)], [(6, 64, 128)]
    )(own2, msg, sib, near, other)
    (send,) = call(coarse_send_kernel, [(n3, 2, 8, 128)], [(72, 128)])(w2, u2w, tiles)
    late = across(late)
    cores = [[k for k in range(wide) if k % 2 == c] for c in range(2)]
    parts = lax.all_to_all(send, "wide", split_axis=0, concat_axis=0, tiled=True, axis_index_groups=cores)
    parts, late = lax.optimization_barrier((parts, late))
    theirs, late_sib = sibling(parts), sibling(late)

    three, four = (n3, 8, 128), (n4, 8, 128)
    (fine2,) = call(
        bottom_kernel,
        [(200, 128)],
        [three, (n3 + 1, 8, 128), three, three, three, three, (n3 + 2, 8, 128), (n3 + 2, 8, 128), four, four]
        + [(n4 + 1, 8, 128), four, four, four, (n4 + 2, 8, 128), (n4 + 2, 8, 128), four, (32, 128)],
    )(parts, theirs)
    (e2,) = call(coarse_post_kernel, [(2, 32, 128)])(fine2, w2, u2w, late, late_sib)
    e2, *again = lax.optimization_barrier((e2,) + inputs)
    far = across(e2)

    e1, edge, send = call(
        middle_post_kernel,
        [(2, 40, 128), (40, 128), (40, 128)],
        [(4, 40, 128), (7, 40, 128), (7, 40, 128), (7, 40, 128)],
    )(e2, far, fine1, f1w, g1w, w1)
    other1 = sibling(send)

    (out,) = call(
        fine_post_kernel,
        [(4, 64, 256)],
        windows + [(6,) + big, (8,) + big, (8,) + big, (328, 128), (4, 64, 256), pltpu.SemaphoreType.DMA((4,))],
        out_places={0: pltpu.HBM},
        limit=6,
    )(e1, edge, other1, outer, jnp.concatenate(again, axis=0), low0, high0, halo, u2)
    return out


def solution(mesh):
    spec = P("wide", "narrow", None)
    return jax.shard_map(body, mesh=mesh, in_specs=(spec,) * 4, out_specs=spec, check_vma=False)
```

```python
import functools

import jax
import jax.numpy as jnp
from jax import lax
from jax.experimental import pallas as pl
from jax.experimental.pallas import tpu as pltpu
from jax.sharding import PartitionSpec as P

THETA = 1.125
DELTA = 0.875
RATIO = THETA / DELTA
SIG = [0.0002 * 4.0**level for level in range(5)]
F32 = jnp.float32


def factors(degree):
    rho, out = 1.0 / RATIO, []
    for _ in range(degree - 1):
        new = 1.0 / (2.0 * RATIO - rho)
        out.append((new * rho, 2.0 * new / DELTA))
        rho = new
    return out


(KEEP, GAIN), = factors(2)


def roll(x, by, axis):
    return pltpu.roll(x, by % x.shape[axis], axis)


def gather_sum(below, here, above, c1, h1, c2, c3):
    first = c1 * below + h1 * above
    second = c2 * roll(here, 1, 0) + roll(c2 * here, -1, 0)
    third = c3 * roll(here, 1, 1) + roll(c3 * here, -1, 1)
    return first + second + third


def diagonal(sig, c1, h1, c2, c3):
    return sig + c1 + h1 + c2 + roll(c2, -1, 0) + c3 + roll(c3, -1, 1)


def iota(shape, dim):
    return lax.broadcasted_iota(jnp.int32, shape, dim)


def pairs_of_lanes(lanes, period, even=False):
    row, col = iota((lanes, 128), 0), iota((lanes, 128), 1) % period
    hit = row == 2 * col if even else row // 2 == col
    return hit.astype(F32)


def copies_of_lanes(lanes_in, lanes_out):
    row, col = iota((lanes_in, lanes_out), 0), iota((lanes_in, lanes_out), 1)
    return (row == col // 2).astype(F32)


def pieces(x):
    out = []
    for _ in range(3):
        part = x.astype(jnp.bfloat16)
        out.append(part)
        x = x - part.astype(F32)
    return out


def mul(x, ones):
    ones = ones.astype(jnp.bfloat16)
    high, mid, low = [jnp.dot(part, ones, preferred_element_type=F32) for part in pieces(x)]
    return high + (mid + low)


def mul_left(ones, x):
    ones = ones.astype(jnp.bfloat16)
    high, mid, low = [jnp.dot(ones, part, preferred_element_type=F32) for part in pieces(x)]
    return high + (mid + low)


def pair_rows(x, scratch, start=0, count=None, even=False):
    rows = x.shape[0]
    count = rows // 2 if count is None else count
    scratch[0:rows, :] = x
    first = scratch[pl.ds(start, count, stride=2), :]
    if even:
        return first
    return first + scratch[pl.ds(start + 1, count, stride=2), :]


def twice_rows(x, scratch):
    rows = x.shape[0]
    scratch[pl.ds(0, rows, stride=2), :] = x
    scratch[pl.ds(1, rows, stride=2), :] = x
    return scratch[0 : 2 * rows, :]


def coarse_coefs(planes, scratch, lanes, period, start=0, count=None):
    both = pairs_of_lanes(lanes, period)
    alone = pairs_of_lanes(lanes, period, even=True)
    return (
        0.25 * pair_rows(mul(planes[0], both), scratch, start, count),
        0.25 * pair_rows(mul(planes[1], both), scratch, start, count, even=True),
        0.25 * pair_rows(mul(planes[2], alone), scratch, start, count),
    )


def spread_block(x, block, width):
    lane = iota(x.shape, 1)
    x = jnp.where(lane // width == block, x, 0.0)
    while width < 128:
        x = x + pltpu.roll(x, width, 1)
        width *= 2
    return x


def smooth_two(u1, below, above, f, g, c1, h1, c2, c3):
    near = gather_sum(below, u1, above, c1, h1, c2, c3)
    return (1.0 + KEEP) * u1 + GAIN * (g * (f + near) - u1)


def first_post(v, below, above, f, g, c1, h1, c2, c3):
    near = gather_sum(below, v, above, c1, h1, c2, c3)
    return v + (1.0 / THETA) * (g * (f + near) - v)


def second_post(u, v, below, above, f, g, c1, h1, c2, c3):
    near = gather_sum(below, u, above, c1, h1, c2, c3)
    return u + KEEP * (u - v) + GAIN * (g * (f + near) - u)


def call(kernel, outs, scratch=(), places=(), out_places=(), limit=4):
    places, out_places = dict(places), dict(out_places)

    def run(*args):
        in_specs = [pl.BlockSpec(memory_space=places.get(i, pltpu.VMEM)) for i in range(len(args))]
        return pl.pallas_call(
            kernel,
            out_shape=[jax.ShapeDtypeStruct(s, F32) for s in outs],
            in_specs=in_specs,
            out_specs=[pl.BlockSpec(memory_space=out_places.get(i, pltpu.VMEM)) for i in range(len(outs))],
            scratch_shapes=[pltpu.VMEM(s, F32) if isinstance(s, tuple) else s for s in scratch],
            compiler_params=pltpu.CompilerParams(vmem_limit_bytes=limit * 2**20),
        )(*args)

    return run


def two_blocks(x):
    half = x.shape[0] // 2
    return jnp.where(iota((half, 128), 1) < 64, x[:half], x[half:])


def start_kernel(f, c1, c2, c3, up, down, out_far, out_sib, rows, planes, sems):
    par = lax.rem(lax.axis_index("wide"), 2)
    moves = []
    for k, (out, row) in enumerate(((up, 56), (down, 0))):
        for a, ref in enumerate((f, c1, c2, c3)):
            moves.append((ref.at[:, pl.ds(row, 8), :], rows.at[k, pl.ds(4 * a, 4)], out.at[pl.ds(4 * a, 4)]))
    for k, (out, upward) in enumerate(((out_far, par), (out_sib, 1 - par))):
        for a, ref in enumerate((f, c1, c2, c3, c1)):
            plane = 3 * upward if a < 4 else 1
            moves.append((ref.at[pl.ds(plane, 1)], planes.at[k, pl.ds(a, 1)], out.at[pl.ds(a, 1)]))
    first = [pltpu.make_async_copy(src, mid, sems.at[0, k]) for k, (src, mid, _) in enumerate(moves)]
    second = [pltpu.make_async_copy(mid, dst, sems.at[1, k]) for k, (_, mid, dst) in enumerate(moves)]
    for copy in first:
        copy.start()
    for one, two in zip(first, second):
        one.wait()
        two.start()
    for copy in second:
        copy.wait()


def pad_kernel(inner, low, high, own, coef1, out_far, out_sib, first, scr):
    for a in range(16):
        own[a, 0:8] = low[a]
        own[a, 8:72] = inner[a]
        own[a, 72:80] = high[a]
    par = lax.rem(lax.axis_index("wide"), 2)
    for k in range(2):
        diag = diagonal(SIG[0], own[5 + k], own[6 + k], own[9 + k], own[13 + k])
        first[k] = own[1 + k] / diag / THETA
    for out, up in ((out_far, par), (out_sib, 1 - par)):
        for a in range(5):
            plane = 4 * a + 3 * up if a < 4 else 5
            out[16 * a : 16 * a + 8] = own[plane, 0:8]
            out[16 * a + 8 : 16 * a + 16] = own[plane, 72:80]
        out[80:160] = first[up]
    k1 = jnp.concatenate([own[4], own[6]], axis=0)
    k2 = jnp.concatenate([own[8] + own[9], own[10] + own[11]], axis=0)
    k3 = jnp.concatenate([own[12] + own[13], own[14] + own[15]], axis=0)
    coarse = coarse_coefs((k1, k2, k3), scr, 256, 128)
    for a in range(3):
        for p in range(2):
            coef1[2 * a + p] = coarse[a][40 * p : 40 * p + 40]
    for out in (out_far, out_sib):
        for k in range(6):
            row, lane = 160 + 40 * (k // 2), 128 * (k % 2)
            out[row : row + 40, lane : lane + 128] = coef1[k]


def block(index):
    row, lane = 160 + 40 * (index // 2), 128 * (index % 2)
    return slice(row, row + 40), slice(lane, lane + 128)


def sides(far, sib):
    odd = lax.rem(lax.axis_index("wide"), 2) == 1

    def below(*at):
        return jnp.where(odd, sib[at], far[at])

    def above(*at):
        return jnp.where(odd, far[at], sib[at])

    return below, above


CHUNK = 16


def chunked(rows, body):
    for r0 in range(0, rows, CHUNK):
        body(r0, rows)


def near_chunk(u, p, c1, c2, c3, q, r0, rows):
    here = pl.ds(r0, CHUNK)
    x = u[p, here, :]
    if r0 > 0:
        lower = u[p, pl.ds(r0 - 1, CHUNK), :]
    else:
        lower = roll(x, 1, 0)
    if r0 + CHUNK < rows:
        after = pl.ds(r0 + 1, CHUNK)
        upper = c2[q, after, :] * u[p, after, :]
    else:
        upper = roll(c2[q, here, :] * x, -1, 0)
    k3 = c3[q, here, :]
    first = c1[q, here, :] * u[p - 1, here, :] + c1[q + 1, here, :] * u[p + 1, here, :]
    second = c2[q, here, :] * lower + upper
    third = k3 * roll(x, 1, 1) + roll(k3 * x, -1, 1)
    return x, first + second + third


def diag_chunk(c1, c2, c3, q, r0, rows):
    here = pl.ds(r0, CHUNK)
    k2, k3 = c2[q, here, :], c3[q, here, :]
    if r0 + CHUNK < rows:
        h2 = c2[q, pl.ds(r0 + 1, CHUNK), :]
    else:
        h2 = roll(k2, -1, 0)
    return SIG[0] + c1[q, here, :] + c1[q + 1, here, :] + k2 + h2 + k3 + roll(k3, -1, 1)


def fine_pre_kernel(own, coef1, far_raw, sib_raw, far, sib, u2, out_far, out_sib, f, c1, c2, c3, g, f1, u1, res, scr):
    below, above = sides(far, sib)
    below_raw, above_raw = sides(far_raw, sib_raw)
    for a, ref in enumerate((f, c1, c2, c3)):
        ref[1:5] = own[4 * a : 4 * a + 4]
    for a, ref, q, raw, rest in (
        [(a, ref, 0, below_raw, below) for a, ref in enumerate((f, c1, c2, c3))]
        + [(a, ref, 5, above_raw, above) for a, ref in enumerate((f, c1, c2, c3))]
        + [(4, c1, 6, above_raw, above)]
    ):
        halo_plane(ref, q, a, raw, rest)
    u1[0] = below(slice(80, 160))
    u1[7] = above(slice(80, 160))

    def smooth_first(q, carry):
        def rows(r0, n):
            here = pl.ds(r0, CHUNK)
            inverse = 1.0 / diag_chunk(c1, c2, c3, q, r0, n)
            g[q, here, :] = inverse
            u1[q + 1, here, :] = f[q, here, :] * inverse * (1.0 / THETA)

        chunked(80, rows)
        return carry

    lax.fori_loop(0, 6, smooth_first, 0)

    def smooth_second(q, carry):
        def rows(r0, n):
            here = pl.ds(r0, CHUNK)
            x, near = near_chunk(u1, q + 1, c1, c2, c3, q, r0, n)
            u2[q, here, :] = (1.0 + KEEP) * x + GAIN * (g[q, here, :] * (f[q, here, :] + near) - x)

        chunked(80, rows)
        return carry

    lax.fori_loop(0, 6, smooth_second, 0)

    def residual(q, carry):
        def rows(r0, n):
            here = pl.ds(r0, CHUNK)
            x, near = near_chunk(u2, q, c1, c2, c3, q, r0, n)
            res[q - 1, here, :] = f[q, here, :] + near - diag_chunk(c1, c2, c3, q, r0, n) * x

        chunked(80, rows)
        return carry

    lax.fori_loop(1, 5, residual, 0)

    both = pairs_of_lanes(256, 128)
    sums = jnp.concatenate([res[0] + res[1], res[2] + res[3]], axis=0)
    coarse = 0.5 * pair_rows(mul(sums, both), scr)
    f1[0] = coarse[:40]
    f1[1] = coarse[40:]
    for p in range(2):
        face = coef1[1] if p == 0 else above(*block(0))
        inverse = 1.0 / diagonal(SIG[1], coef1[p], face, coef1[2 + p], coef1[4 + p])
        for out in (out_far, out_sib):
            out[p] = f1[p]
            out[2 + p] = inverse
    par = lax.rem(lax.axis_index("wide"), 2)
    for out, plane in ((out_far, 2 + par), (out_sib, 3 - par)):
        out[4] = u2[plane, 0:40, 0:128]
        out[5] = u2[plane, 0:40, 128:256]
        out[6] = u2[plane, 40:80, 0:128]
        out[7] = u2[plane, 40:80, 128:256]


def halo_plane(out, k, a, raw, rest):
    out[k, 0:8] = rest(slice(16 * a, 16 * a + 8))
    out[k, 8:72] = raw(a)
    out[k, 72:80] = rest(slice(16 * a + 8, 16 * a + 16))


def coarse_coef_kernel(coef1, far_raw, sib_raw, far, sib, w1, halo, out, scr):
    below, above = sides(far, sib)
    below_raw, above_raw = sides(far_raw, sib_raw)
    for a in range(4):
        halo_plane(halo, a, a, below_raw, below)
        halo_plane(halo, 4 + a, a, above_raw, above)
    halo_plane(halo, 8, 4, above_raw, above)
    for a in range(3):
        for p in range(2):
            w1[6 * a + p] = below(*block(2 * a + p))
            w1[6 * a + 2 + p] = coef1[2 * a + p]
            w1[6 * a + 4 + p] = above(*block(2 * a + p))
    k1 = jnp.concatenate([w1[2], w1[4]], axis=0)
    k2, k3 = w1[8] + w1[9], w1[14] + w1[15]
    both, alone = pairs_of_lanes(128, 64), pairs_of_lanes(128, 64, even=True)
    k1 = 0.25 * pair_rows(mul(k1, both), scr)
    k2 = 0.25 * pair_rows(mul(k2, both), scr, even=True)
    k3 = 0.25 * pair_rows(mul(k3, alone), scr)
    for k, x in enumerate((k1[2:18], k1[22:38], k2[2:18], k3[2:18])):
        out[8 * k : 8 * k + 8] = two_blocks(x)


def middle_pre_kernel(own, far, sib, w1, coefs, f, g, u2, f2, up, down, outer, u1, scr):
    below, above = sides(far, sib)
    for k, read in enumerate((below, own.__getitem__, above)):
        for p in range(2):
            f[2 * k + p] = read(p)
            g[2 * k + p] = read(2 + p)
    for k, read in enumerate((below, above)):
        outer[k, 0:40, 0:128] = read(4)
        outer[k, 0:40, 128:256] = read(5)
        outer[k, 40:80, 0:128] = read(6)
        outer[k, 40:80, 128:256] = read(7)
    for p in range(6):
        u1[p] = f[p] * g[p] * (1.0 / THETA)
    u2[0] = u1[0]
    u2[5] = u1[5]
    for p in range(1, 5):
        u2[p] = smooth_two(u1[p], u1[p - 1], u1[p + 1], f[p], g[p], w1[p], w1[p + 1], w1[6 + p], w1[12 + p])
    total = 0.0
    for p in (2, 3):
        k1, h1, k2, k3 = w1[p], w1[p + 1], w1[6 + p], w1[12 + p]
        near = gather_sum(u2[p - 1], u2[p], u2[p + 1], k1, h1, k2, k3)
        total = total + (f[p] + near - diagonal(SIG[1], k1, h1, k2, k3) * u2[p])
    coarse = 0.5 * pair_rows(mul(total, pairs_of_lanes(128, 64)), scr, 4, 16)
    f2[0:8] = two_blocks(coarse)
    f2[8:40] = coefs[...]
    for p in range(2):
        up[40 + 8 * p : 48 + 8 * p] = u2[2 + p, 28:36]
        down[40 + 8 * p : 48 + 8 * p] = u2[2 + p, 4:12]
    up[0:40] = f2[...]
    down[0:40] = f2[...]


def both_halves(x):
    return jnp.concatenate([spread_block(x, 0, 64), spread_block(x, 1, 64)], axis=0)


def coarse_start_kernel(f2, low, high, far, u2fine, own, msg):
    n = lax.axis_index("narrow")
    for piece, by in ((f2, 0), (high, 1), (far, 2), (low, 3)):
        at = pl.multiple_of(16 * lax.rem(n + by, 4), 16)
        for k in range(5):
            own[k, pl.ds(at, 16), :] = both_halves(piece[8 * k : 8 * k + 8])
    own[5] = 1.0 / diagonal(SIG[2], own[1], own[2], own[3], own[4])
    for k, plane in enumerate((0, 5, 1, 3, 4)):
        msg[32 * k : 32 * k + 32] = two_blocks(own[plane])
    for p in range(2):
        at = 160 + 40 * p
        msg[at : at + 40] = u2fine[2 + p]
        msg[at : at + 4] = low[44 + 8 * p : 48 + 8 * p]
        msg[at + 36 : at + 40] = high[40 + 8 * p : 44 + 8 * p]


def coarse_tiles_kernel(msg, sib, tiles, scr):
    odd = lax.rem(lax.axis_index("wide"), 2) == 1
    for a in range(3):
        here = slice(64 + 32 * a, 96 + 32 * a)
        x = jnp.where(odd, sib[here], msg[here]) if a == 0 else msg[here] + sib[here]
        scr[0:64, :] = 0.25 * mul(both_halves(x), pairs_of_lanes(128, 32, even=a == 2))
        tiles[a] = tile_of(scr, a == 1)


def tile_of(scr, even=False):
    block = iota((8, 128), 1) // 32
    packed = 0.0
    for q in range(4):
        part = scr[pl.ds(2 * q, 8, stride=8), :]
        if not even:
            part = part + scr[pl.ds(2 * q + 1, 8, stride=8), :]
        packed = jnp.where(block == q, part, packed)
    return packed


def coarse_swap_kernel(own, msg, sib, w1, out):
    out[0:32] = msg[0:32]
    out[32:128] = msg[64:160]
    out[128:160] = sib[0:32] * sib[32:64] * (1.0 / THETA)
    out[160:192] = two_blocks(own[2])
    out[192:272] = msg[160:240]
    par = lax.rem(lax.axis_index("wide"), 2)
    out[272:312] = sib[pl.ds(pl.multiple_of(160 + 40 * par, 8), 40), :]
    out[312:352] = w1[4]


def coarse_pre_kernel(own, msg, sib, near, other, w, u2, late, fine, u1):
    for p in range(2):
        fine[p] = sib[160 + 40 * p : 200 + 40 * p]
        fine[2 + p] = msg[160 + 40 * p : 200 + 40 * p]
    for p in range(4):
        fine[4 + p] = near[192 + 40 * p : 232 + 40 * p]
    odd = lax.rem(lax.axis_index("wide"), 2) == 1

    def below(k):
        here = slice(32 * k, 32 * k + 32)
        return both_halves(jnp.where(odd, other[here], near[here]))

    def above(k):
        here = slice(32 * k, 32 * k + 32)
        return both_halves(jnp.where(odd, near[here], other[here]))

    for a, (base, plane, slot) in enumerate(((0, 0, 0), (4, 5, None), (8, 1, 1), (13, 3, 2), (17, 4, 3))):
        mine, theirs = own[plane], both_halves(sib[32 * a : 32 * a + 32])
        w[base + 1] = jnp.where(odd, theirs, mine)
        w[base + 2] = jnp.where(odd, mine, theirs)
        if slot is not None:
            w[base] = below(slot)
            w[base + 3] = above(slot)
    w[12] = above(5)
    u1[0] = below(4)
    u1[5] = above(4)
    for k in (0, 3):
        w[4 + k] = 1.0 / diagonal(SIG[2], w[8 + k], w[9 + k], w[13 + k], w[17 + k])
    for k in range(4):
        u1[k + 1] = w[k] * w[4 + k] * (1.0 / THETA)
    for k in range(4):
        u2[k] = smooth_two(u1[k + 1], u1[k], u1[k + 2], w[k], w[4 + k], w[8 + k], w[9 + k], w[13 + k], w[17 + k])
    late[...] = two_blocks(jnp.where(odd, u2[1], u2[2]))


def coarse_send_kernel(w, u2, tiles, send, scr):
    odd = lax.rem(lax.axis_index("wide"), 2) == 1
    total = 0.0
    for k in (1, 2):
        args = (w[8 + k], w[9 + k], w[13 + k], w[17 + k])
        near = gather_sum(u2[k - 1], u2[k], u2[k + 1], *args)
        total = total + (w[k] + near - diagonal(SIG[2], *args) * u2[k])
    scr[0:64, :] = 0.5 * mul(total, pairs_of_lanes(128, 32))
    first = jnp.where(odd, tiles[1], tile_of(scr))
    second = jnp.where(odd, tiles[2], tiles[0])
    for k in range(send.shape[0]):
        send[k, 0] = first
        send[k, 1] = second


def packed_sum(below, x, above, c1, h1, c2, c3, width, blocks):
    lane = iota(x.shape, 2)
    block, inner = lane // width % blocks, lane % width

    def second_down(x):
        x = pltpu.roll(x, width, 2)
        return jnp.where(block == 0, pltpu.roll(x, 1, 1), x)

    def second_up(x):
        x = pltpu.roll(x, 128 - width, 2)
        return jnp.where(block == blocks - 1, pltpu.roll(x, 7, 1), x)

    def third_down(x):
        return jnp.where(inner == 0, pltpu.roll(x, 129 - width, 2), pltpu.roll(x, 1, 2))

    def third_up(x):
        return jnp.where(inner == width - 1, pltpu.roll(x, width - 1, 2), pltpu.roll(x, 127, 2))

    first = c1 * below + h1 * above
    second = c2 * second_down(x) + second_up(c2 * x)
    third = c3 * third_down(x) + third_up(c3 * x)
    return first + second + third


def packed_diagonal(sig, c1, h1, c2, c3, width, blocks):
    lane = iota(c1.shape, 2)
    block, inner = lane // width % blocks, lane % width
    h2 = pltpu.roll(c2, 128 - width, 2)
    h2 = jnp.where(block == blocks - 1, pltpu.roll(h2, 7, 1), h2)
    h3 = jnp.where(inner == width - 1, pltpu.roll(c3, width - 1, 2), pltpu.roll(c3, 127, 2))
    return sig + c1 + h1 + c2 + h2 + c3 + h3


def fold_matrix(even2=False, even3=False):
    k, j = iota((128, 128), 0), iota((128, 128), 1)
    k2, k3, j2, j3 = k // 32, k % 32, j // 16 % 2, j % 16
    hit2 = k2 == 2 * j2 if even2 else k2 // 2 == j2
    hit3 = k3 == 2 * j3 if even3 else k3 // 2 == j3
    return (hit2 & hit3).astype(F32)


def wrap(ref, count):
    ref[0] = ref[count]
    ref[count + 1] = ref[1]


def around(j, n):
    return lax.rem(j + n, n)


STEP = 32
THREE, FOUR = (32, 4), (16, 2)


def bottom_kernel(mine, theirs, e2,
                  f3, c1, c2, c3, d3, g3, u1, u2, res, f4, d1, d2, e3, g4, ua, ub, st, scr):
    n3, n4 = f3.shape[0], f4.shape[0]

    def loop(body):
        for j in range(0, n3, STEP):
            body(j)

    odd = lax.rem(lax.axis_index("wide"), 2) == 1

    def load(j):
        here = pl.ds(j, STEP)
        a, b, c, d = mine[here, 0], mine[here, 1], theirs[here, 0], theirs[here, 1]
        f3[here] = jnp.where(odd, c, a)
        c1[here] = jnp.where(odd, d, b)
        c2[here] = jnp.where(odd, a, c)
        c3[here] = jnp.where(odd, b, d)

    loop(load)
    c1[n3] = c1[0]

    def start(j):
        here = pl.ds(j, STEP)
        diag = packed_diagonal(SIG[3], c1[here], c1[pl.ds(j + 1, STEP)], c2[here], c3[here], *THREE)
        inverse = 1.0 / diag
        d3[here] = diag
        g3[here] = inverse
        u1[pl.ds(j + 1, STEP)] = f3[here] * inverse * (1.0 / THETA)

    loop(start)
    wrap(u1, n3)

    def near3(u, j):
        here = pl.ds(j, STEP)
        x = u[pl.ds(j + 1, STEP)]
        args = (c1[here], c1[pl.ds(j + 1, STEP)], c2[here], c3[here])
        return here, x, packed_sum(u[here], x, u[pl.ds(j + 2, STEP)], *args, *THREE)

    def pre(j):
        here, x, near = near3(u1, j)
        u2[pl.ds(j + 1, STEP)] = (1.0 + KEEP) * x + GAIN * (g3[here] * (f3[here] + near) - x)

    loop(pre)
    wrap(u2, n3)

    def residual(j):
        here, x, near = near3(u2, j)
        left = (f3[here] + near - d3[here] * x).reshape(STEP // 2, 2, 8, 128)
        res[pl.ds(j // 2, STEP // 2)] = left[:, 0] + left[:, 1]

    loop(residual)

    def fold(x, *even):
        return mul(x.reshape(8 * n4, 128), fold_matrix(*even)).reshape(n4, 8, 128)

    def halves(ref):
        x = ref[0:n3].reshape(n4, 2, 8, 128)
        return x[:, 0], x[:, 1]

    f4[...] = 0.5 * fold(res[...])
    d1[0:n4] = 0.25 * fold(halves(c1)[0])
    d1[n4] = d1[0]
    d2[...] = 0.25 * fold(sum(halves(c2)), True, False)
    e3[...] = 0.25 * fold(sum(halves(c3)), False, True)
    coefs4 = (d1[0:n4], d1[1 : n4 + 1], d2[...], e3[...])
    g4[...] = 1.0 / packed_diagonal(SIG[4], *coefs4, *FOUR)
    x = f4[...] * g4[...] * (1.0 / THETA)
    ua[1 : n4 + 1] = x
    wrap(ua, n4)
    st[...] = x
    src, dst = ua, ub
    for keep, gain in factors(4):
        x = src[1 : n4 + 1]
        near = packed_sum(src[0:n4], x, src[2 : n4 + 2], d1[0:n4], d1[1 : n4 + 1], d2[...], e3[...], *FOUR)
        step = keep * st[...] + gain * (g4[...] * (f4[...] + near) - x)
        st[...] = step
        dst[1 : n4 + 1] = x + step
        wrap(dst, n4)
        src, dst = dst, src

    j0 = around(lax.axis_index("wide") // 2 - 1, n3)
    k, j = iota((128, 128), 0), iota((128, 128), 1)
    unfold = (k == 16 * (j // 64) + j % 32 // 2).astype(F32)
    coarse = jnp.concatenate([src[1 + around(around(j0 - 2, n3) // 2 + m, n4)] for m in range(4)], axis=0)
    scr[0:32] = mul(coarse, unfold)
    shifted = lax.rem(around(j0 - 2, n3), 2)
    js = [around(j0 - 2 + m, n3) for m in range(7)]
    v = [u2[1 + js[m]] + scr[pl.ds(pl.multiple_of(8 * ((shifted + m) // 2), 8), 8), :] for m in range(7)]
    v = jnp.stack(v)

    def window(ref, first, count, by=0):
        return jnp.stack([ref[js[m] + by] for m in range(first, first + count)])

    def args(first, count):
        return window(c1, first, count), window(c1, first, count, 1), window(c2, first, count), window(c3, first, count)

    f, g = window(f3, 1, 5), window(g3, 1, 5)
    near = packed_sum(v[0:5], v[1:6], v[2:7], *args(1, 5), *THREE)
    w = v[1:6] + (1.0 / THETA) * (g * (f + near) - v[1:6])
    near = packed_sum(w[0:3], w[1:4], w[2:5], *args(2, 3), *THREE)
    x = w[1:4] + KEEP * (w[1:4] - v[2:5]) + GAIN * (g[1:4] * (f[1:4] + near) - w[1:4])
    x = x.reshape(24, 128)
    for q in range(4):
        fine = mul(x, (k == 32 * q + j % 64 // 2).astype(F32))
        e2[pl.ds(2 * q, 24, stride=8), :] = fine
        e2[pl.ds(2 * q + 1, 24, stride=8), :] = fine


def coarse_post_kernel(e2, win, u2, late, late_sib, out, msg):
    below, above = sides(late, late_sib)
    v = [both_halves(below(...)), u2[0], u2[1], u2[2], u2[3], both_halves(above(...))]
    v = [v[m] + e2[64 * (m // 2) : 64 * (m // 2) + 64, :] for m in range(6)]

    def args(k):
        return win[k], win[4 + k], win[8 + k], win[9 + k], win[13 + k], win[17 + k]

    w = [first_post(v[m + 1], v[m], v[m + 2], *args(m)) for m in range(4)]
    for p in range(2):
        x = second_post(w[p + 1], v[p + 2], w[p], w[p + 2], *args(p + 1))
        out[p] = pltpu.roll(x, lax.rem(72 - 16 * lax.axis_index("narrow"), 64), 0)[0:32]
    msg[...] = jnp.where(iota((32, 128), 1) < 64, out[0], out[1])


def middle_post_kernel(e2, far, u2, f, g, w1, own, edge, send, fine, c1, v, w):
    par = lax.rem(lax.axis_index("wide"), 2)
    odd = par == 1
    row, col = iota((40, 32), 0), iota((40, 32), 1)
    pick = (col == (row + 4) // 2 + 4).astype(F32)
    lanes = copies_of_lanes(128, 128)
    planes = (e2[0], e2[1], spread_block(far[...], 0, 64), spread_block(far[...], 1, 64))
    for k in range(4):
        fine[k] = mul(mul_left(pick, jnp.where(odd, planes[k], planes[(k + 2) % 4])), lanes)
    c1[0:6] = w1[0:6]
    c1[6] = u2[7]
    sibs, ours, next_chip = ([u2[k] for k in some] for some in ((0, 1), (2, 3), (4, 5, 6)))
    upper = sibs + ours + next_chip
    lower = [next_chip[2]] + next_chip[:2] + ours + sibs
    for i in range(7):
        v[i] = jnp.where(odd, upper[i], lower[i]) + fine[(i + 1 - par) // 2]

    def args(i):
        k = i - 1 + par
        return f[k], g[k], c1[k], c1[k + 1], w1[6 + k], w1[12 + k]

    for i in range(1, 6):
        w[i] = first_post(v[i], v[i - 1], v[i + 1], *args(i))
    out = [second_post(w[i], v[i], w[i - 1], w[i + 1], *args(i)) for i in (2, 3, 4)]
    own[0] = jnp.where(odd, out[0], out[1])
    own[1] = jnp.where(odd, out[1], out[2])
    edge[...] = jnp.where(odd, out[2], out[0])
    send[...] = jnp.where(odd, out[0], out[2])


def fine_post_kernel(e1, edge, other, outer, inner, low, high, halo, u2, result, f, c1, c2, c3, g, v, w, scr, out, sems):
    for a, ref in enumerate((f, c1, c2, c3)):
        ref[0] = halo[a]
        ref[5] = halo[4 + a]
        for p in range(4):
            ref[p + 1, 0:8] = low[4 * a + p]
            ref[p + 1, 8:72] = inner[4 * a + p]
            ref[p + 1, 72:80] = high[4 * a + p]
    c1[6] = halo[8]
    below, above = sides(edge, other)
    x = jnp.concatenate([below(...), e1[0], e1[1], above(...)], axis=0)
    for half in range(2):
        here = slice(128 * half, 128 * half + 128)
        row, col = iota((128, 128), 0), iota((128, 128), 1)
        fine = mul(x, (row == 64 * half + col // 2).astype(F32))
        scr[pl.ds(0, 160, stride=2), :] = fine
        scr[pl.ds(1, 160, stride=2), :] = fine
        for k in range(8):
            at = 80 * (k // 2)
            base = u2[k - 1, :, here] if 0 < k < 7 else outer[k // 7, :, here]
            v[k, :, here] = base + scr[at : at + 80, :]

    def post1(q, carry):
        def chunk(r0, n):
            here = pl.ds(r0, CHUNK)
            x, near = near_chunk(v, q + 1, c1, c2, c3, q, r0, n)
            inverse = 1.0 / diag_chunk(c1, c2, c3, q, r0, n)
            g[q, here, :] = inverse
            w[q + 1, here, :] = x + (1.0 / THETA) * (inverse * (f[q, here, :] + near) - x)

        chunked(80, chunk)
        return carry

    lax.fori_loop(0, 6, post1, 0)

    def post2(q, carry):
        for r0 in range(8, 72, CHUNK):
            here = pl.ds(r0, CHUNK)
            x, near = near_chunk(w, q + 1, c1, c2, c3, q, r0, 80)
            step = KEEP * (x - v[q + 1, here, :]) + GAIN * (g[q, here, :] * (f[q, here, :] + near) - x)
            out[q - 1, pl.ds(r0 - 8, CHUNK), :] = x + step
        return carry

    copies = []
    for p in range(4):
        post2(p + 1, 0)
        copies.append(pltpu.make_async_copy(out.at[pl.ds(p, 1)], result.at[pl.ds(p, 1)], sems.at[p]))
        copies[p].start()
    for copy in copies:
        copy.wait()


def shift(x, axis, by):
    count = lax.axis_size(axis)
    return lax.ppermute(x, axis, [(i, (i + by) % count) for i in range(count)])


def sibling(x):
    return lax.ppermute(x, "wide", [(i, i ^ 1) for i in range(lax.axis_size("wide"))])


def across(x):
    count = lax.axis_size("wide")
    return lax.ppermute(x, "wide", [(i, (i + 1 if i % 2 else i - 1) % count) for i in range(count)])


def body(source, coef_first, coef_second, coef_third):
    wide = lax.axis_size("wide")
    n3, n4 = wide // 2, wide // 4
    big = (80, 256)
    inputs = (source, coef_first, coef_second, coef_third)

    up, down, far_raw, sib_raw = call(
        start_kernel,
        [(16, 8, 256), (16, 8, 256), (5, 64, 256), (5, 64, 256)],
        [(2, 16, 8, 256), (2, 5, 64, 256), pltpu.SemaphoreType.DMA((2, 18))],
        {k: pltpu.HBM for k in range(4)},
        {k: pltpu.HBM for k in range(4)},
        limit=60,
    )(*inputs)
    far_raw, sib_raw = across(far_raw), sibling(sib_raw)
    low0, high0 = shift(up, "narrow", 1), shift(down, "narrow", -1)

    own, coef1, far, sib = call(
        pad_kernel, [(16,) + big, (6, 40, 128), (280, 256), (280, 256)], [(2,) + big, (168, 128)]
    )(jnp.concatenate(inputs, axis=0), low0, high0)
    far, sib = across(far), sibling(sib)

    windows = [(6,) + big, (7,) + big, (6,) + big, (6,) + big]
    u2, out_far, out_sib = call(
        fine_pre_kernel,
        [(6,) + big, (8, 40, 128), (8, 40, 128)],
        windows + [(6,) + big, (2, 40, 128), (8,) + big, (4,) + big, (168, 128)],
        limit=6,
    )(own, coef1, far_raw, sib_raw, far, sib)
    far1, sib1 = across(out_far), sibling(out_sib)
    w1, halo, coefs = call(
        coarse_coef_kernel, [(18, 40, 128), (9,) + big, (32, 128)], [(88, 128)]
    )(coef1, far_raw, sib_raw, far, sib)

    six = (6, 40, 128)
    f1w, g1w, u2m, f2, up, down, outer = call(
        middle_pre_kernel, [six, six, six, (40, 128), (56, 128), (56, 128), (2,) + big], [six, (48, 128)]
    )(out_far, far1, sib1, w1, coefs)
    low, high, far = shift(up, "narrow", 1), shift(down, "narrow", -1), shift(f2, "narrow", 2)

    own2, msg = call(coarse_start_kernel, [(6, 64, 128), (240, 128)])(f2, low, high, far, u2m)
    sib = sibling(msg)
    (swap,) = call(coarse_swap_kernel, [(352, 128)])(own2, msg, sib, w1)
    near = across(swap)
    (tiles,) = call(coarse_tiles_kernel, [(3, 8, 128)], [(72, 128)])(msg, sib)
    near, tiles = lax.optimization_barrier((near, tiles))
    other = sibling(near)
    w2, u2w, late, fine1 = call(
        coarse_pre_kernel, [(21, 64, 128), (4, 64, 128), (32, 128), (8, 40, 128)], [(6, 64, 128)]
    )(own2, msg, sib, near, other)
    (send,) = call(coarse_send_kernel, [(n3, 2, 8, 128)], [(72, 128)])(w2, u2w, tiles)
    late = across(late)
    cores = [[k for k in range(wide) if k % 2 == c] for c in range(2)]
    parts = lax.all_to_all(send, "wide", split_axis=0, concat_axis=0, tiled=True, axis_index_groups=cores)
    parts, late = lax.optimization_barrier((parts, late))
    theirs, late_sib = sibling(parts), sibling(late)

    three, four = (n3, 8, 128), (n4, 8, 128)
    (fine2,) = call(
        bottom_kernel,
        [(200, 128)],
        [three, (n3 + 1, 8, 128), three, three, three, three, (n3 + 2, 8, 128), (n3 + 2, 8, 128), four, four]
        + [(n4 + 1, 8, 128), four, four, four, (n4 + 2, 8, 128), (n4 + 2, 8, 128), four, (32, 128)],
    )(parts, theirs)
    e2, both = call(coarse_post_kernel, [(2, 32, 128), (32, 128)])(fine2, w2, u2w, late, late_sib)
    both, *again = lax.optimization_barrier((both,) + inputs)
    far = across(both)

    e1, edge, send = call(
        middle_post_kernel,
        [(2, 40, 128), (40, 128), (40, 128)],
        [(4, 40, 128), (7, 40, 128), (7, 40, 128), (7, 40, 128)],
    )(e2, far, fine1, f1w, g1w, w1)
    other1 = sibling(send)

    (out,) = call(
        fine_post_kernel,
        [(4, 64, 256)],
        windows + [(6,) + big, (8,) + big, (8,) + big, (328, 128), (4, 64, 256), pltpu.SemaphoreType.DMA((4,))],
        out_places={0: pltpu.HBM},
        limit=6,
    )(e1, edge, other1, outer, jnp.concatenate(again, axis=0), low0, high0, halo, u2)
    return out


def solution(mesh):
    spec = P("wide", "narrow", None)
    return jax.shard_map(body, mesh=mesh, in_specs=(spec,) * 4, out_specs=spec, check_vma=False)
```

```python
import functools

import jax
import jax.numpy as jnp
from jax import lax
from jax.experimental import pallas as pl
from jax.experimental.pallas import tpu as pltpu
from jax.sharding import PartitionSpec as P

THETA = 1.125
DELTA = 0.875
RATIO = THETA / DELTA
SIG = [0.0002 * 4.0**level for level in range(5)]
F32 = jnp.float32


def factors(degree):
    rho, out = 1.0 / RATIO, []
    for _ in range(degree - 1):
        new = 1.0 / (2.0 * RATIO - rho)
        out.append((new * rho, 2.0 * new / DELTA))
        rho = new
    return out


(KEEP, GAIN), = factors(2)


def roll(x, by, axis):
    return pltpu.roll(x, by % x.shape[axis], axis)


def gather_sum(below, here, above, c1, h1, c2, c3):
    first = c1 * below + h1 * above
    second = c2 * roll(here, 1, 0) + roll(c2 * here, -1, 0)
    third = c3 * roll(here, 1, 1) + roll(c3 * here, -1, 1)
    return first + second + third


def diagonal(sig, c1, h1, c2, c3):
    return sig + c1 + h1 + c2 + roll(c2, -1, 0) + c3 + roll(c3, -1, 1)


def iota(shape, dim):
    return lax.broadcasted_iota(jnp.int32, shape, dim)


def pairs_of_lanes(lanes, period, even=False):
    row, col = iota((lanes, 128), 0), iota((lanes, 128), 1) % period
    hit = row == 2 * col if even else row // 2 == col
    return hit.astype(F32)


def copies_of_lanes(lanes_in, lanes_out):
    row, col = iota((lanes_in, lanes_out), 0), iota((lanes_in, lanes_out), 1)
    return (row == col // 2).astype(F32)


def pieces(x):
    out = []
    for _ in range(3):
        part = x.astype(jnp.bfloat16)
        out.append(part)
        x = x - part.astype(F32)
    return out


def mul(x, ones):
    ones = ones.astype(jnp.bfloat16)
    high, mid, low = [jnp.dot(part, ones, preferred_element_type=F32) for part in pieces(x)]
    return high + (mid + low)


def mul_left(ones, x):
    ones = ones.astype(jnp.bfloat16)
    high, mid, low = [jnp.dot(ones, part, preferred_element_type=F32) for part in pieces(x)]
    return high + (mid + low)


def pair_rows(x, scratch, start=0, count=None, even=False):
    rows = x.shape[0]
    count = rows // 2 if count is None else count
    scratch[0:rows, :] = x
    first = scratch[pl.ds(start, count, stride=2), :]
    if even:
        return first
    return first + scratch[pl.ds(start + 1, count, stride=2), :]


def twice_rows(x, scratch):
    rows = x.shape[0]
    scratch[pl.ds(0, rows, stride=2), :] = x
    scratch[pl.ds(1, rows, stride=2), :] = x
    return scratch[0 : 2 * rows, :]


def coarse_coefs(planes, scratch, lanes, period, start=0, count=None):
    both = pairs_of_lanes(lanes, period)
    alone = pairs_of_lanes(lanes, period, even=True)
    return (
        0.25 * pair_rows(mul(planes[0], both), scratch, start, count),
        0.25 * pair_rows(mul(planes[1], both), scratch, start, count, even=True),
        0.25 * pair_rows(mul(planes[2], alone), scratch, start, count),
    )


def spread_block(x, block, width):
    lane = iota(x.shape, 1)
    x = jnp.where(lane // width == block, x, 0.0)
    while width < 128:
        x = x + pltpu.roll(x, width, 1)
        width *= 2
    return x


def smooth_two(u1, below, above, f, g, c1, h1, c2, c3):
    near = gather_sum(below, u1, above, c1, h1, c2, c3)
    return (1.0 + KEEP) * u1 + GAIN * (g * (f + near) - u1)


def first_post(v, below, above, f, g, c1, h1, c2, c3):
    near = gather_sum(below, v, above, c1, h1, c2, c3)
    return v + (1.0 / THETA) * (g * (f + near) - v)


def second_post(u, v, below, above, f, g, c1, h1, c2, c3):
    near = gather_sum(below, u, above, c1, h1, c2, c3)
    return u + KEEP * (u - v) + GAIN * (g * (f + near) - u)


def call(kernel, outs, scratch=(), places=(), out_places=(), limit=4):
    places, out_places = dict(places), dict(out_places)

    def run(*args):
        in_specs = [pl.BlockSpec(memory_space=places.get(i, pltpu.VMEM)) for i in range(len(args))]
        return pl.pallas_call(
            kernel,
            out_shape=[jax.ShapeDtypeStruct(s, F32) for s in outs],
            in_specs=in_specs,
            out_specs=[pl.BlockSpec(memory_space=out_places.get(i, pltpu.VMEM)) for i in range(len(outs))],
            scratch_shapes=[pltpu.VMEM(s, F32) if isinstance(s, tuple) else s for s in scratch],
            compiler_params=pltpu.CompilerParams(vmem_limit_bytes=limit * 2**20),
        )(*args)

    return run


def two_blocks(x):
    half = x.shape[0] // 2
    return jnp.where(iota((half, 128), 1) < 64, x[:half], x[half:])


def start_kernel(f, c1, c2, c3, up, down, out_far, out_sib, rows, planes, sems):
    par = lax.rem(lax.axis_index("wide"), 2)
    moves = []
    for k, (out, row) in enumerate(((up, 56), (down, 0))):
        for a, ref in enumerate((f, c1, c2, c3)):
            moves.append((ref.at[:, pl.ds(row, 8), :], rows.at[k, pl.ds(4 * a, 4)], out.at[pl.ds(4 * a, 4)]))
    for k, (out, upward) in enumerate(((out_far, par), (out_sib, 1 - par))):
        for a, ref in enumerate((f, c1, c2, c3, c1)):
            plane = 3 * upward if a < 4 else 1
            moves.append((ref.at[pl.ds(plane, 1)], planes.at[k, pl.ds(a, 1)], out.at[pl.ds(a, 1)]))
    first = [pltpu.make_async_copy(src, mid, sems.at[0, k]) for k, (src, mid, _) in enumerate(moves)]
    second = [pltpu.make_async_copy(mid, dst, sems.at[1, k]) for k, (_, mid, dst) in enumerate(moves)]
    for copy in first:
        copy.start()
    for one, two in zip(first, second):
        one.wait()
        two.start()
    for copy in second:
        copy.wait()


def pad_kernel(inner, low, high, own, coef1, out_far, out_sib, first, scr):
    for a in range(16):
        own[a, 0:8] = low[a]
        own[a, 8:72] = inner[a]
        own[a, 72:80] = high[a]
    par = lax.rem(lax.axis_index("wide"), 2)
    for k in range(2):
        diag = diagonal(SIG[0], own[5 + k], own[6 + k], own[9 + k], own[13 + k])
        first[k] = own[1 + k] / diag / THETA
    for out, up in ((out_far, par), (out_sib, 1 - par)):
        for a in range(5):
            plane = 4 * a + 3 * up if a < 4 else 5
            out[16 * a : 16 * a + 8] = own[plane, 0:8]
            out[16 * a + 8 : 16 * a + 16] = own[plane, 72:80]
        out[80:160] = first[up]
    k1 = jnp.concatenate([own[4], own[6]], axis=0)
    k2 = jnp.concatenate([own[8] + own[9], own[10] + own[11]], axis=0)
    k3 = jnp.concatenate([own[12] + own[13], own[14] + own[15]], axis=0)
    coarse = coarse_coefs((k1, k2, k3), scr, 256, 128)
    for a in range(3):
        for p in range(2):
            coef1[2 * a + p] = coarse[a][40 * p : 40 * p + 40]
    for out in (out_far, out_sib):
        for k in range(6):
            row, lane = 160 + 40 * (k // 2), 128 * (k % 2)
            out[row : row + 40, lane : lane + 128] = coef1[k]


def block(index):
    row, lane = 160 + 40 * (index // 2), 128 * (index % 2)
    return slice(row, row + 40), slice(lane, lane + 128)


def sides(far, sib):
    odd = lax.rem(lax.axis_index("wide"), 2) == 1

    def below(*at):
        return jnp.where(odd, sib[at], far[at])

    def above(*at):
        return jnp.where(odd, far[at], sib[at])

    return below, above


CHUNK = 16


def chunked(rows, body):
    for r0 in range(0, rows, CHUNK):
        body(r0, rows)


def near_chunk(u, p, c1, c2, c3, q, r0, rows):
    here = pl.ds(r0, CHUNK)
    x = u[p, here, :]
    if r0 > 0:
        lower = u[p, pl.ds(r0 - 1, CHUNK), :]
    else:
        lower = roll(x, 1, 0)
    if r0 + CHUNK < rows:
        after = pl.ds(r0 + 1, CHUNK)
        upper = c2[q, after, :] * u[p, after, :]
    else:
        upper = roll(c2[q, here, :] * x, -1, 0)
    k3 = c3[q, here, :]
    first = c1[q, here, :] * u[p - 1, here, :] + c1[q + 1, here, :] * u[p + 1, here, :]
    second = c2[q, here, :] * lower + upper
    third = k3 * roll(x, 1, 1) + roll(k3 * x, -1, 1)
    return x, first + second + third


def diag_chunk(c1, c2, c3, q, r0, rows):
    here = pl.ds(r0, CHUNK)
    k2, k3 = c2[q, here, :], c3[q, here, :]
    if r0 + CHUNK < rows:
        h2 = c2[q, pl.ds(r0 + 1, CHUNK), :]
    else:
        h2 = roll(k2, -1, 0)
    return SIG[0] + c1[q, here, :] + c1[q + 1, here, :] + k2 + h2 + k3 + roll(k3, -1, 1)


def fine_pre_kernel(own, coef1, far_raw, sib_raw, far, sib, u2, out_far, out_sib, f, c1, c2, c3, g, d, f1, u1, res, scr):
    below, above = sides(far, sib)
    below_raw, above_raw = sides(far_raw, sib_raw)
    for a, ref in enumerate((f, c1, c2, c3)):
        ref[1:5] = own[4 * a : 4 * a + 4]
    for a, ref, q, raw, rest in (
        [(a, ref, 0, below_raw, below) for a, ref in enumerate((f, c1, c2, c3))]
        + [(a, ref, 5, above_raw, above) for a, ref in enumerate((f, c1, c2, c3))]
        + [(4, c1, 6, above_raw, above)]
    ):
        halo_plane(ref, q, a, raw, rest)
    u1[0] = below(slice(80, 160))
    u1[7] = above(slice(80, 160))

    def smooth_first(q, carry):
        def rows(r0, n):
            here = pl.ds(r0, CHUNK)
            diag = diag_chunk(c1, c2, c3, q, r0, n)
            d[q, here, :] = diag
            inverse = 1.0 / diag
            g[q, here, :] = inverse
            u1[q + 1, here, :] = f[q, here, :] * inverse * (1.0 / THETA)

        chunked(80, rows)
        return carry

    lax.fori_loop(0, 6, smooth_first, 0)

    def smooth_second(q, carry):
        def rows(r0, n):
            here = pl.ds(r0, CHUNK)
            x, near = near_chunk(u1, q + 1, c1, c2, c3, q, r0, n)
            u2[q, here, :] = (1.0 + KEEP) * x + GAIN * (g[q, here, :] * (f[q, here, :] + near) - x)

        chunked(80, rows)
        return carry

    lax.fori_loop(0, 6, smooth_second, 0)

    def residual(q, carry):
        def rows(r0, n):
            here = pl.ds(r0, CHUNK)
            x, near = near_chunk(u2, q, c1, c2, c3, q, r0, n)
            res[q - 1, here, :] = f[q, here, :] + near - d[q, here, :] * x

        chunked(80, rows)
        return carry

    lax.fori_loop(1, 5, residual, 0)

    both = pairs_of_lanes(256, 128)
    sums = jnp.concatenate([res[0] + res[1], res[2] + res[3]], axis=0)
    coarse = 0.5 * pair_rows(mul(sums, both), scr)
    f1[0] = coarse[:40]
    f1[1] = coarse[40:]
    for p in range(2):
        face = coef1[1] if p == 0 else above(*block(0))
        inverse = 1.0 / diagonal(SIG[1], coef1[p], face, coef1[2 + p], coef1[4 + p])
        for out in (out_far, out_sib):
            out[p] = f1[p]
            out[2 + p] = inverse
    par = lax.rem(lax.axis_index("wide"), 2)
    for out, plane in ((out_far, 2 + par), (out_sib, 3 - par)):
        out[4] = u2[plane, 0:40, 0:128]
        out[5] = u2[plane, 0:40, 128:256]
        out[6] = u2[plane, 40:80, 0:128]
        out[7] = u2[plane, 40:80, 128:256]


def halo_plane(out, k, a, raw, rest):
    out[k, 0:8] = rest(slice(16 * a, 16 * a + 8))
    out[k, 8:72] = raw(a)
    out[k, 72:80] = rest(slice(16 * a + 8, 16 * a + 16))


def coarse_coef_kernel(coef1, far_raw, sib_raw, far, sib, w1, halo, out, scr):
    below, above = sides(far, sib)
    below_raw, above_raw = sides(far_raw, sib_raw)
    for a in range(4):
        halo_plane(halo, a, a, below_raw, below)
        halo_plane(halo, 4 + a, a, above_raw, above)
    halo_plane(halo, 8, 4, above_raw, above)
    for a in range(3):
        for p in range(2):
            w1[6 * a + p] = below(*block(2 * a + p))
            w1[6 * a + 2 + p] = coef1[2 * a + p]
            w1[6 * a + 4 + p] = above(*block(2 * a + p))
    k1 = jnp.concatenate([w1[2], w1[4]], axis=0)
    k2, k3 = w1[8] + w1[9], w1[14] + w1[15]
    both, alone = pairs_of_lanes(128, 64), pairs_of_lanes(128, 64, even=True)
    k1 = 0.25 * pair_rows(mul(k1, both), scr)
    k2 = 0.25 * pair_rows(mul(k2, both), scr, even=True)
    k3 = 0.25 * pair_rows(mul(k3, alone), scr)
    for k, x in enumerate((k1[2:18], k1[22:38], k2[2:18], k3[2:18])):
        out[8 * k : 8 * k + 8] = two_blocks(x)


def middle_pre_kernel(own, far, sib, w1, coefs, f, g, u2, f2, up, down, outer, u1, scr):
    below, above = sides(far, sib)
    for k, read in enumerate((below, own.__getitem__, above)):
        for p in range(2):
            f[2 * k + p] = read(p)
            g[2 * k + p] = read(2 + p)
    for k, read in enumerate((below, above)):
        outer[k, 0:40, 0:128] = read(4)
        outer[k, 0:40, 128:256] = read(5)
        outer[k, 40:80, 0:128] = read(6)
        outer[k, 40:80, 128:256] = read(7)
    for p in range(6):
        u1[p] = f[p] * g[p] * (1.0 / THETA)
    u2[0] = u1[0]
    u2[5] = u1[5]
    for p in range(1, 5):
        u2[p] = smooth_two(u1[p], u1[p - 1], u1[p + 1], f[p], g[p], w1[p], w1[p + 1], w1[6 + p], w1[12 + p])
    total = 0.0
    for p in (2, 3):
        k1, h1, k2, k3 = w1[p], w1[p + 1], w1[6 + p], w1[12 + p]
        near = gather_sum(u2[p - 1], u2[p], u2[p + 1], k1, h1, k2, k3)
        total = total + (f[p] + near - diagonal(SIG[1], k1, h1, k2, k3) * u2[p])
    coarse = 0.5 * pair_rows(mul(total, pairs_of_lanes(128, 64)), scr, 4, 16)
    f2[0:8] = two_blocks(coarse)
    f2[8:40] = coefs[...]
    for p in range(2):
        up[40 + 8 * p : 48 + 8 * p] = u2[2 + p, 28:36]
        down[40 + 8 * p : 48 + 8 * p] = u2[2 + p, 4:12]
    up[0:40] = f2[...]
    down[0:40] = f2[...]


def both_halves(x):
    return jnp.concatenate([spread_block(x, 0, 64), spread_block(x, 1, 64)], axis=0)


def coarse_start_kernel(f2, low, high, far, u2fine, own, msg):
    n = lax.axis_index("narrow")
    for piece, by in ((f2, 0), (high, 1), (far, 2), (low, 3)):
        at = pl.multiple_of(16 * lax.rem(n + by, 4), 16)
        for k in range(5):
            own[k, pl.ds(at, 16), :] = both_halves(piece[8 * k : 8 * k + 8])
    own[5] = 1.0 / diagonal(SIG[2], own[1], own[2], own[3], own[4])
    for k, plane in enumerate((0, 5, 1, 3, 4)):
        msg[32 * k : 32 * k + 32] = two_blocks(own[plane])
    for p in range(2):
        at = 160 + 40 * p
        msg[at : at + 40] = u2fine[2 + p]
        msg[at : at + 4] = low[44 + 8 * p : 48 + 8 * p]
        msg[at + 36 : at + 40] = high[40 + 8 * p : 44 + 8 * p]


def coarse_tiles_kernel(msg, sib, tiles, scr):
    odd = lax.rem(lax.axis_index("wide"), 2) == 1
    for a in range(3):
        here = slice(64 + 32 * a, 96 + 32 * a)
        x = jnp.where(odd, sib[here], msg[here]) if a == 0 else msg[here] + sib[here]
        scr[0:64, :] = 0.25 * mul(both_halves(x), pairs_of_lanes(128, 32, even=a == 2))
        tiles[a] = tile_of(scr, a == 1)


def tile_of(scr, even=False):
    block = iota((8, 128), 1) // 32
    packed = 0.0
    for q in range(4):
        part = scr[pl.ds(2 * q, 8, stride=8), :]
        if not even:
            part = part + scr[pl.ds(2 * q + 1, 8, stride=8), :]
        packed = jnp.where(block == q, part, packed)
    return packed


def coarse_swap_kernel(own, msg, sib, w1, out):
    out[0:32] = msg[0:32]
    out[32:128] = msg[64:160]
    out[128:160] = sib[0:32] * sib[32:64] * (1.0 / THETA)
    out[160:192] = two_blocks(own[2])
    out[192:272] = msg[160:240]
    par = lax.rem(lax.axis_index("wide"), 2)
    out[272:312] = sib[pl.ds(pl.multiple_of(160 + 40 * par, 8), 40), :]
    out[312:352] = w1[4]


def coarse_pre_kernel(own, msg, sib, near, other, w, u2, late, fine, u1):
    for p in range(2):
        fine[p] = sib[160 + 40 * p : 200 + 40 * p]
        fine[2 + p] = msg[160 + 40 * p : 200 + 40 * p]
    for p in range(4):
        fine[4 + p] = near[192 + 40 * p : 232 + 40 * p]
    odd = lax.rem(lax.axis_index("wide"), 2) == 1

    def below(k):
        here = slice(32 * k, 32 * k + 32)
        return both_halves(jnp.where(odd, other[here], near[here]))

    def above(k):
        here = slice(32 * k, 32 * k + 32)
        return both_halves(jnp.where(odd, near[here], other[here]))

    for a, (base, plane, slot) in enumerate(((0, 0, 0), (4, 5, None), (8, 1, 1), (13, 3, 2), (17, 4, 3))):
        mine, theirs = own[plane], both_halves(sib[32 * a : 32 * a + 32])
        w[base + 1] = jnp.where(odd, theirs, mine)
        w[base + 2] = jnp.where(odd, mine, theirs)
        if slot is not None:
            w[base] = below(slot)
            w[base + 3] = above(slot)
    w[12] = above(5)
    u1[0] = below(4)
    u1[5] = above(4)
    for k in (0, 3):
        w[4 + k] = 1.0 / diagonal(SIG[2], w[8 + k], w[9 + k], w[13 + k], w[17 + k])
    for k in range(4):
        u1[k + 1] = w[k] * w[4 + k] * (1.0 / THETA)
    for k in range(4):
        u2[k] = smooth_two(u1[k + 1], u1[k], u1[k + 2], w[k], w[4 + k], w[8 + k], w[9 + k], w[13 + k], w[17 + k])
    late[...] = two_blocks(jnp.where(odd, u2[1], u2[2]))


def coarse_send_kernel(w, u2, tiles, send, scr):
    odd = lax.rem(lax.axis_index("wide"), 2) == 1
    total = 0.0
    for k in (1, 2):
        args = (w[8 + k], w[9 + k], w[13 + k], w[17 + k])
        near = gather_sum(u2[k - 1], u2[k], u2[k + 1], *args)
        total = total + (w[k] + near - diagonal(SIG[2], *args) * u2[k])
    scr[0:64, :] = 0.5 * mul(total, pairs_of_lanes(128, 32))
    first = jnp.where(odd, tiles[1], tile_of(scr))
    second = jnp.where(odd, tiles[2], tiles[0])
    for k in range(send.shape[0]):
        send[k, 0] = first
        send[k, 1] = second


def packed_sum(below, x, above, c1, h1, c2, c3, width, blocks):
    lane = iota(x.shape, 2)
    block, inner = lane // width % blocks, lane % width

    def second_down(x):
        x = pltpu.roll(x, width, 2)
        return jnp.where(block == 0, pltpu.roll(x, 1, 1), x)

    def second_up(x):
        x = pltpu.roll(x, 128 - width, 2)
        return jnp.where(block == blocks - 1, pltpu.roll(x, 7, 1), x)

    def third_down(x):
        return jnp.where(inner == 0, pltpu.roll(x, 129 - width, 2), pltpu.roll(x, 1, 2))

    def third_up(x):
        return jnp.where(inner == width - 1, pltpu.roll(x, width - 1, 2), pltpu.roll(x, 127, 2))

    first = c1 * below + h1 * above
    second = c2 * second_down(x) + second_up(c2 * x)
    third = c3 * third_down(x) + third_up(c3 * x)
    return first + second + third


def packed_diagonal(sig, c1, h1, c2, c3, width, blocks):
    lane = iota(c1.shape, 2)
    block, inner = lane // width % blocks, lane % width
    h2 = pltpu.roll(c2, 128 - width, 2)
    h2 = jnp.where(block == blocks - 1, pltpu.roll(h2, 7, 1), h2)
    h3 = jnp.where(inner == width - 1, pltpu.roll(c3, width - 1, 2), pltpu.roll(c3, 127, 2))
    return sig + c1 + h1 + c2 + h2 + c3 + h3


def fold_matrix(even2=False, even3=False):
    k, j = iota((128, 128), 0), iota((128, 128), 1)
    k2, k3, j2, j3 = k // 32, k % 32, j // 16 % 2, j % 16
    hit2 = k2 == 2 * j2 if even2 else k2 // 2 == j2
    hit3 = k3 == 2 * j3 if even3 else k3 // 2 == j3
    return (hit2 & hit3).astype(F32)


def wrap(ref, count):
    ref[0] = ref[count]
    ref[count + 1] = ref[1]


def around(j, n):
    return lax.rem(j + n, n)


STEP = 32
THREE, FOUR = (32, 4), (16, 2)


def bottom_kernel(mine, theirs, e2,
                  f3, c1, c2, c3, d3, g3, u1, u2, res, f4, d1, d2, e3, g4, ua, ub, st, scr):
    n3, n4 = f3.shape[0], f4.shape[0]

    def loop(body):
        for j in range(0, n3, STEP):
            body(j)

    odd = lax.rem(lax.axis_index("wide"), 2) == 1

    def load(j):
        here = pl.ds(j, STEP)
        a, b, c, d = mine[here, 0], mine[here, 1], theirs[here, 0], theirs[here, 1]
        f3[here] = jnp.where(odd, c, a)
        c1[here] = jnp.where(odd, d, b)
        c2[here] = jnp.where(odd, a, c)
        c3[here] = jnp.where(odd, b, d)

    loop(load)
    c1[n3] = c1[0]

    def start(j):
        here = pl.ds(j, STEP)
        diag = packed_diagonal(SIG[3], c1[here], c1[pl.ds(j + 1, STEP)], c2[here], c3[here], *THREE)
        inverse = 1.0 / diag
        d3[here] = diag
        g3[here] = inverse
        u1[pl.ds(j + 1, STEP)] = f3[here] * inverse * (1.0 / THETA)

    loop(start)
    wrap(u1, n3)

    def near3(u, j):
        here = pl.ds(j, STEP)
        x = u[pl.ds(j + 1, STEP)]
        args = (c1[here], c1[pl.ds(j + 1, STEP)], c2[here], c3[here])
        return here, x, packed_sum(u[here], x, u[pl.ds(j + 2, STEP)], *args, *THREE)

    def pre(j):
        here, x, near = near3(u1, j)
        u2[pl.ds(j + 1, STEP)] = (1.0 + KEEP) * x + GAIN * (g3[here] * (f3[here] + near) - x)

    loop(pre)
    wrap(u2, n3)

    def residual(j):
        here, x, near = near3(u2, j)
        left = (f3[here] + near - d3[here] * x).reshape(STEP // 2, 2, 8, 128)
        res[pl.ds(j // 2, STEP // 2)] = left[:, 0] + left[:, 1]

    loop(residual)

    def fold(x, *even):
        return mul(x.reshape(8 * n4, 128), fold_matrix(*even)).reshape(n4, 8, 128)

    def halves(ref):
        x = ref[0:n3].reshape(n4, 2, 8, 128)
        return x[:, 0], x[:, 1]

    f4[...] = 0.5 * fold(res[...])
    d1[0:n4] = 0.25 * fold(halves(c1)[0])
    d1[n4] = d1[0]
    d2[...] = 0.25 * fold(sum(halves(c2)), True, False)
    e3[...] = 0.25 * fold(sum(halves(c3)), False, True)
    coefs4 = (d1[0:n4], d1[1 : n4 + 1], d2[...], e3[...])
    g4[...] = 1.0 / packed_diagonal(SIG[4], *coefs4, *FOUR)
    x = f4[...] * g4[...] * (1.0 / THETA)
    ua[1 : n4 + 1] = x
    wrap(ua, n4)
    st[...] = x
    src, dst = ua, ub
    for keep, gain in factors(4):
        x = src[1 : n4 + 1]
        near = packed_sum(src[0:n4], x, src[2 : n4 + 2], d1[0:n4], d1[1 : n4 + 1], d2[...], e3[...], *FOUR)
        step = keep * st[...] + gain * (g4[...] * (f4[...] + near) - x)
        st[...] = step
        dst[1 : n4 + 1] = x + step
        wrap(dst, n4)
        src, dst = dst, src

    j0 = around(lax.axis_index("wide") // 2 - 1, n3)
    k, j = iota((128, 128), 0), iota((128, 128), 1)
    unfold = (k == 16 * (j // 64) + j % 32 // 2).astype(F32)
    coarse = jnp.concatenate([src[1 + around(around(j0 - 2, n3) // 2 + m, n4)] for m in range(4)], axis=0)
    scr[0:32] = mul(coarse, unfold)
    shifted = lax.rem(around(j0 - 2, n3), 2)
    js = [around(j0 - 2 + m, n3) for m in range(7)]
    v = [u2[1 + js[m]] + scr[pl.ds(pl.multiple_of(8 * ((shifted + m) // 2), 8), 8), :] for m in range(7)]
    v = jnp.stack(v)

    def window(ref, first, count, by=0):
        return jnp.stack([ref[js[m] + by] for m in range(first, first + count)])

    def args(first, count):
        return window(c1, first, count), window(c1, first, count, 1), window(c2, first, count), window(c3, first, count)

    f, g = window(f3, 1, 5), window(g3, 1, 5)
    near = packed_sum(v[0:5], v[1:6], v[2:7], *args(1, 5), *THREE)
    w = v[1:6] + (1.0 / THETA) * (g * (f + near) - v[1:6])
    near = packed_sum(w[0:3], w[1:4], w[2:5], *args(2, 3), *THREE)
    x = w[1:4] + KEEP * (w[1:4] - v[2:5]) + GAIN * (g[1:4] * (f[1:4] + near) - w[1:4])
    x = x.reshape(24, 128)
    for q in range(4):
        fine = mul(x, (k == 32 * q + j % 64 // 2).astype(F32))
        e2[pl.ds(2 * q, 24, stride=8), :] = fine
        e2[pl.ds(2 * q + 1, 24, stride=8), :] = fine


def coarse_post_kernel(e2, win, u2, late, late_sib, out):
    below, above = sides(late, late_sib)
    v = [both_halves(below(...)), u2[0], u2[1], u2[2], u2[3], both_halves(above(...))]
    v = [v[m] + e2[64 * (m // 2) : 64 * (m // 2) + 64, :] for m in range(6)]

    def args(k):
        return win[k], win[4 + k], win[8 + k], win[9 + k], win[13 + k], win[17 + k]

    w = [first_post(v[m + 1], v[m], v[m + 2], *args(m)) for m in range(4)]
    for p in range(2):
        x = second_post(w[p + 1], v[p + 2], w[p], w[p + 2], *args(p + 1))
        out[p] = pltpu.roll(x, lax.rem(72 - 16 * lax.axis_index("narrow"), 64), 0)[0:32]


def middle_post_kernel(e2, far, u2, f, g, w1, own, edge, send, fine, c1, v, w):
    par = lax.rem(lax.axis_index("wide"), 2)
    odd = par == 1
    row, col = iota((40, 32), 0), iota((40, 32), 1)
    pick = (col == (row + 4) // 2 + 4).astype(F32)
    lanes = copies_of_lanes(128, 128)
    planes = (e2[0], e2[1], far[0], far[1])
    for k in range(4):
        fine[k] = mul(mul_left(pick, jnp.where(odd, planes[k], planes[(k + 2) % 4])), lanes)
    c1[0:6] = w1[0:6]
    c1[6] = u2[7]
    sibs, ours, next_chip = ([u2[k] for k in some] for some in ((0, 1), (2, 3), (4, 5, 6)))
    upper = sibs + ours + next_chip
    lower = [next_chip[2]] + next_chip[:2] + ours + sibs
    for i in range(7):
        v[i] = jnp.where(odd, upper[i], lower[i]) + fine[(i + 1 - par) // 2]

    def args(i):
        k = i - 1 + par
        return f[k], g[k], c1[k], c1[k + 1], w1[6 + k], w1[12 + k]

    for i in range(1, 6):
        w[i] = first_post(v[i], v[i - 1], v[i + 1], *args(i))
    out = [second_post(w[i], v[i], w[i - 1], w[i + 1], *args(i)) for i in (2, 3, 4)]
    own[0] = jnp.where(odd, out[0], out[1])
    own[1] = jnp.where(odd, out[1], out[2])
    edge[...] = jnp.where(odd, out[2], out[0])
    send[...] = jnp.where(odd, out[0], out[2])


def fine_post_kernel(e1, edge, other, outer, inner, low, high, halo, u2, result, f, c1, c2, c3, g, v, w, scr, out, sems):
    for a, ref in enumerate((f, c1, c2, c3)):
        ref[0] = halo[a]
        ref[5] = halo[4 + a]
        for p in range(4):
            ref[p + 1, 0:8] = low[4 * a + p]
            ref[p + 1, 8:72] = inner[4 * a + p]
            ref[p + 1, 72:80] = high[4 * a + p]
    c1[6] = halo[8]
    below, above = sides(edge, other)
    x = jnp.concatenate([below(...), e1[0], e1[1], above(...)], axis=0)
    for half in range(2):
        here = slice(128 * half, 128 * half + 128)
        row, col = iota((128, 128), 0), iota((128, 128), 1)
        fine = mul(x, (row == 64 * half + col // 2).astype(F32))
        scr[pl.ds(0, 160, stride=2), :] = fine
        scr[pl.ds(1, 160, stride=2), :] = fine
        for k in range(8):
            at = 80 * (k // 2)
            base = u2[k - 1, :, here] if 0 < k < 7 else outer[k // 7, :, here]
            v[k, :, here] = base + scr[at : at + 80, :]

    def post1(q, carry):
        def chunk(r0, n):
            here = pl.ds(r0, CHUNK)
            x, near = near_chunk(v, q + 1, c1, c2, c3, q, r0, n)
            inverse = 1.0 / diag_chunk(c1, c2, c3, q, r0, n)
            g[q, here, :] = inverse
            w[q + 1, here, :] = x + (1.0 / THETA) * (inverse * (f[q, here, :] + near) - x)

        chunked(80, chunk)
        return carry

    lax.fori_loop(0, 6, post1, 0)

    def post2(q, carry):
        for r0 in range(8, 72, CHUNK):
            here = pl.ds(r0, CHUNK)
            x, near = near_chunk(w, q + 1, c1, c2, c3, q, r0, 80)
            step = KEEP * (x - v[q + 1, here, :]) + GAIN * (g[q, here, :] * (f[q, here, :] + near) - x)
            out[q - 1, pl.ds(r0 - 8, CHUNK), :] = x + step
        return carry

    copies = []
    for p in range(4):
        post2(p + 1, 0)
        copies.append(pltpu.make_async_copy(out.at[pl.ds(p, 1)], result.at[pl.ds(p, 1)], sems.at[p]))
        copies[p].start()
    for copy in copies:
        copy.wait()


def shift(x, axis, by):
    count = lax.axis_size(axis)
    return lax.ppermute(x, axis, [(i, (i + by) % count) for i in range(count)])


def sibling(x):
    return lax.ppermute(x, "wide", [(i, i ^ 1) for i in range(lax.axis_size("wide"))])


def across(x):
    count = lax.axis_size("wide")
    return lax.ppermute(x, "wide", [(i, (i + 1 if i % 2 else i - 1) % count) for i in range(count)])


def body(source, coef_first, coef_second, coef_third):
    wide = lax.axis_size("wide")
    n3, n4 = wide // 2, wide // 4
    big = (80, 256)
    inputs = (source, coef_first, coef_second, coef_third)

    up, down, far_raw, sib_raw = call(
        start_kernel,
        [(16, 8, 256), (16, 8, 256), (5, 64, 256), (5, 64, 256)],
        [(2, 16, 8, 256), (2, 5, 64, 256), pltpu.SemaphoreType.DMA((2, 18))],
        {k: pltpu.HBM for k in range(4)},
        {k: pltpu.HBM for k in range(4)},
        limit=60,
    )(*inputs)
    far_raw, sib_raw = across(far_raw), sibling(sib_raw)
    low0, high0 = shift(up, "narrow", 1), shift(down, "narrow", -1)

    own, coef1, far, sib = call(
        pad_kernel, [(16,) + big, (6, 40, 128), (280, 256), (280, 256)], [(2,) + big, (168, 128)]
    )(jnp.concatenate(inputs, axis=0), low0, high0)
    far, sib = across(far), sibling(sib)

    windows = [(6,) + big, (7,) + big, (6,) + big, (6,) + big]
    u2, out_far, out_sib = call(
        fine_pre_kernel,
        [(6,) + big, (8, 40, 128), (8, 40, 128)],
        windows + [(6,) + big, (6,) + big, (2, 40, 128), (8,) + big, (4,) + big, (168, 128)],
        limit=6,
    )(own, coef1, far_raw, sib_raw, far, sib)
    far1, sib1 = across(out_far), sibling(out_sib)
    w1, halo, coefs = call(
        coarse_coef_kernel, [(18, 40, 128), (9,) + big, (32, 128)], [(88, 128)]
    )(coef1, far_raw, sib_raw, far, sib)

    six = (6, 40, 128)
    f1w, g1w, u2m, f2, up, down, outer = call(
        middle_pre_kernel, [six, six, six, (40, 128), (56, 128), (56, 128), (2,) + big], [six, (48, 128)]
    )(out_far, far1, sib1, w1, coefs)
    low, high, far = shift(up, "narrow", 1), shift(down, "narrow", -1), shift(f2, "narrow", 2)

    own2, msg = call(coarse_start_kernel, [(6, 64, 128), (240, 128)])(f2, low, high, far, u2m)
    sib = sibling(msg)
    (swap,) = call(coarse_swap_kernel, [(352, 128)])(own2, msg, sib, w1)
    near = across(swap)
    (tiles,) = call(coarse_tiles_kernel, [(3, 8, 128)], [(72, 128)])(msg, sib)
    near, tiles = lax.optimization_barrier((near, tiles))
    other = sibling(near)
    w2, u2w, late, fine1 = call(
        coarse_pre_kernel, [(21, 64, 128), (4, 64, 128), (32, 128), (8, 40, 128)], [(6, 64, 128)]
    )(own2, msg, sib, near, other)
    (send,) = call(coarse_send_kernel, [(n3, 2, 8, 128)], [(72, 128)])(w2, u2w, tiles)
    late = across(late)
    cores = [[k for k in range(wide) if k % 2 == c] for c in range(2)]
    parts = lax.all_to_all(send, "wide", split_axis=0, concat_axis=0, tiled=True, axis_index_groups=cores)
    parts, late = lax.optimization_barrier((parts, late))
    theirs, late_sib = sibling(parts), sibling(late)

    three, four = (n3, 8, 128), (n4, 8, 128)
    (fine2,) = call(
        bottom_kernel,
        [(200, 128)],
        [three, (n3 + 1, 8, 128), three, three, three, three, (n3 + 2, 8, 128), (n3 + 2, 8, 128), four, four]
        + [(n4 + 1, 8, 128), four, four, four, (n4 + 2, 8, 128), (n4 + 2, 8, 128), four, (32, 128)],
    )(parts, theirs)
    (e2,) = call(coarse_post_kernel, [(2, 32, 128)])(fine2, w2, u2w, late, late_sib)
    e2, *again = lax.optimization_barrier((e2,) + inputs)
    far = across(e2)

    e1, edge, send = call(
        middle_post_kernel,
        [(2, 40, 128), (40, 128), (40, 128)],
        [(4, 40, 128), (7, 40, 128), (7, 40, 128), (7, 40, 128)],
    )(e2, far, fine1, f1w, g1w, w1)
    other1 = sibling(send)

    (out,) = call(
        fine_post_kernel,
        [(4, 64, 256)],
        windows + [(6,) + big, (8,) + big, (8,) + big, (328, 128), (4, 64, 256), pltpu.SemaphoreType.DMA((4,))],
        out_places={0: pltpu.HBM},
        limit=6,
    )(e1, edge, other1, outer, jnp.concatenate(again, axis=0), low0, high0, halo, u2)
    return out


def solution(mesh):
    spec = P("wide", "narrow", None)
    return jax.shard_map(body, mesh=mesh, in_specs=(spec,) * 4, out_specs=spec, check_vma=False)
```
